32 devices in a mesh: row: 8 (over y, x, core), col: 4 (over z).
Axes of the slice: x: 2, y: 2, z: 4, core: 2. Of those that a mesh axis runs over, the one named last changes fastest.
Arguments:
- object_re: float32 [3072, 2048], P('row', 'col'), may hold values from -6 to 6
- object_im: float32 [3072, 2048], P('row', 'col'), may hold values from -6 to 6
- probe_re: float32 [256, 256], replicated, may hold values from -6 to 6
- probe_im: float32 [256, 256], replicated, may hold values from -6 to 6
- frames: bfloat16 [8, 4, 8, 256, 256], P('row', 'col'), may hold values from 0.049804688 to 20
- counts: int32 [8, 4], P('row', 'col'), may hold values from 1 to 8, as said below
- offsets: int32 [8, 4, 8, 2], P('row', 'col'), may hold values from -32 to 288, as said below
- frame_index: int32 [8, 4, 8], P('row', 'col'), may hold values from 0 to 7
Outputs:
- new_re: float32 [3072, 2048], P('row', 'col')
- new_im: float32 [3072, 2048], P('row', 'col')
The draws below stay inside these ranges and needn't reach their ends.
Inputs may be any that keep to these rules, and one draw needn't show every extreme that they name: `counts`: in every draw some tile has 8 positions and some tile has one. Row offsets are -32 plus multiples of 16, at most 160; column offsets likewise, at most 288; in every draw some live position has both offsets at the lowest value and some has both at the highest.
All inputs are finite; a program needn't handle non-finite values.
Results may differ from the reference program's by a relative error of at most 0.0003.
Values sent between devices are 32-bit elements; how exact they have to be, the bound alone decides.
No kernel may reach another device: no remote copies, remote signals or barrier semaphores. Data moves between devices by JAX's collectives and lax.ppermute only.
A program may use at most 64 MiB of HBM per device.

```python
import math
import jax
import jax.numpy as jnp
from jax import lax

TILE_R = 384
TILE_C = 512
P_SIZE = 256
HALO = 32
STEP = 16
MAXPOS = 8
FRAMES = 8
NR = 3072
NC = 2048
N_ROW = 8
N_COL = 4


def draw_counts(key, part):
    first_key, second_key, high_key, low_key = jax.random.split(jax.random.fold_in(key, 11), 4)
    first = jax.random.randint(first_key, (N_ROW * N_COL,), 0, MAXPOS)
    second = jax.random.randint(second_key, (N_ROW * N_COL,), 0, MAXPOS)
    counts = 1 + first * second // (MAXPOS - 1)
    high_spot = jax.random.randint(high_key, (), 0, N_ROW * N_COL)
    low_spot = (high_spot + 1 + jax.random.randint(low_key, (), 0, N_ROW * N_COL - 1)) % (N_ROW * N_COL)
    counts = counts.at[high_spot].set(MAXPOS).at[low_spot].set(1)
    return counts.reshape(N_ROW, N_COL).astype(jnp.int32)


def draw_offsets(key, part):
    row_key, col_key, low_key, high_key = jax.random.split(jax.random.fold_in(key, 23), 4)
    row_steps = (TILE_R - P_SIZE + 2 * HALO) // STEP + 1
    col_steps = (TILE_C - P_SIZE + 2 * HALO) // STEP + 1
    rows = -HALO + STEP * jax.random.randint(row_key, (N_ROW * N_COL, MAXPOS), 0, row_steps)
    cols = -HALO + STEP * jax.random.randint(col_key, (N_ROW * N_COL, MAXPOS), 0, col_steps)
    low_spot = jax.random.randint(low_key, (), 0, N_ROW * N_COL)
    high_spot = (low_spot + 1 + jax.random.randint(high_key, (), 0, N_ROW * N_COL - 1)) % (N_ROW * N_COL)
    rows = rows.at[low_spot, 0].set(-HALO).at[high_spot, 0].set(TILE_R - P_SIZE + HALO)
    cols = cols.at[low_spot, 0].set(-HALO).at[high_spot, 0].set(TILE_C - P_SIZE + HALO)
    both = jnp.stack([rows, cols], axis=-1)
    return both.reshape(N_ROW, N_COL, MAXPOS, 2).astype(jnp.int32)


def place_ends(values, own_key, smallest, largest):
    extent = values.shape
    index_at = [jax.random.randint(jax.random.fold_in(own_key, axis), (), 0, extent[axis]) for axis in range(len(extent))]
    values = values.at[tuple(index_at)].set(smallest)
    longest = extent.index(max(extent))
    index_at[longest] = (index_at[longest] + 1) % extent[longest]
    return values.at[tuple(index_at)].set(largest)


def block_levels(stream_key, shape, shards, low, high):
    level = 1.0
    for dim, parts in shards:
        steps = jax.random.uniform(jax.random.fold_in(jax.random.fold_in(stream_key, 6), dim), (parts,), jnp.float32, low / len(shards), high / len(shards))
        level = level * jnp.repeat(jnp.exp(steps), shape[dim] // parts).reshape((-1,) + (1,) * (len(shape) - 1 - dim))
    return level


def normal_values(stream_key, shape, spread, limit, cuts=(), kind=jnp.bfloat16):
    factor_of = block_levels(stream_key, shape, cuts, -0.22, 0.18) if cuts else 1.0
    drawn = jax.random.normal(stream_key, shape, jnp.float32) * spread * factor_of
    return jnp.minimum(jnp.maximum(drawn, -limit), limit).astype(kind)


def setup_inputs(seed: int = 0) -> dict:
    seeds = jax.random.split(jax.random.key(seed), 9)
    object_re = normal_values(seeds[0], (NR, NC), 1.0, 6.0, ((0, 8), (1, 4)), jnp.float32)
    object_im = normal_values(seeds[1], (NR, NC), 1.0, 6.0, ((0, 8), (1, 4)), jnp.float32)
    probe_re = normal_values(seeds[2], (P_SIZE, P_SIZE), 1.0, 6.0, (), jnp.float32)
    probe_im = normal_values(seeds[3], (P_SIZE, P_SIZE), 1.0, 6.0, (), jnp.float32)
    frames = jnp.clip(jnp.exp(math.log(20.0) - 5.9953784 * jax.random.uniform(seeds[4], (N_ROW, N_COL, FRAMES, P_SIZE, P_SIZE), jnp.float32) ** block_levels(seeds[4], (N_ROW, N_COL, FRAMES, P_SIZE, P_SIZE), ((0, 8), (1, 4)), -0.2, 0.2)), 0.049804688, 20.0).astype(jnp.bfloat16)
    counts = draw_counts(jax.random.fold_in(seeds[8], 71), 0)
    offsets = draw_offsets(jax.random.fold_in(seeds[8], 71), 0)
    frame_index = place_ends(jax.random.randint(seeds[7], (N_ROW, N_COL, MAXPOS), 0, FRAMES), jax.random.fold_in(seeds[7], 1), 0, FRAMES - 1).astype(jnp.int32)
    return dict(object_re=object_re, object_im=object_im, probe_re=probe_re, probe_im=probe_im, frames=frames, counts=counts, offsets=offsets, frame_index=frame_index)


floor_amp = 0.5
ridge = 1.0

def slot_gradient(patch_re, patch_im, probe, frame):
    patch = lax.complex(patch_re, patch_im)
    far = jnp.fft.fft2(probe * patch, norm='ortho')
    amplitude = jnp.abs(far)
    factor = 1.0 - jnp.sqrt(frame) / jnp.maximum(amplitude, floor_amp)
    back = jnp.fft.ifft2(far * factor, norm='ortho')
    grad = jnp.conj(probe) * back
    return (jnp.real(grad), jnp.imag(grad))

def reference(object_re, object_im, probe_re, probe_im, frames, counts, offsets, frame_index):
    pad_re = jnp.pad(object_re, HALO)
    pad_im = jnp.pad(object_im, HALO)
    probe = lax.complex(probe_re, probe_im)
    power = probe_re * probe_re + probe_im * probe_im
    zeros = jnp.zeros((3,) + pad_re.shape, object_re.dtype)

    def visit(acc, item):
        tile = item // MAXPOS
        slot = item % MAXPOS
        trow = tile // N_COL
        tcol = tile % N_COL
        live = (slot < counts[trow, tcol]).astype(object_re.dtype)
        row_start = (trow * TILE_R + offsets[trow, tcol, slot, 0] + HALO).astype(jnp.int32)
        col_start = (tcol * TILE_C + offsets[trow, tcol, slot, 1] + HALO).astype(jnp.int32)
        patch_re = lax.dynamic_slice(pad_re, (row_start, col_start), (P_SIZE, P_SIZE))
        patch_im = lax.dynamic_slice(pad_im, (row_start, col_start), (P_SIZE, P_SIZE))
        frame = frames[trow, tcol, frame_index[trow, tcol, slot]].astype(object_re.dtype)
        grad_re, grad_im = slot_gradient(patch_re, patch_im, probe, frame)
        term = jnp.stack([grad_re, grad_im, power]) * live
        start = (jnp.int32(0), row_start, col_start)
        acc = lax.dynamic_update_slice(acc, lax.dynamic_slice(acc, start, (3, P_SIZE, P_SIZE)) + term, start)
        return (acc, None)
    acc, _ = lax.scan(visit, zeros, jnp.arange(N_ROW * N_COL * MAXPOS, dtype=jnp.int32))
    inner = acc[:, HALO:HALO + NR, HALO:HALO + NC]
    denom = inner[2] + ridge
    return (object_re - inner[0] / denom, object_im - inner[1] / denom)
```

```python
import functools
import math

import jax
import jax.numpy as jnp
import ml_dtypes
import numpy as np
from jax import lax
from jax.experimental import pallas as pl
from jax.experimental.pallas import tpu as pltpu
from jax.sharding import PartitionSpec as P

P_SIZE = 256
HALF = P_SIZE // 2
HALO = 32
LANES = 128
GROUPS = LANES // HALO
PAIR = 2

floor_amp = 0.5
ridge = 1.0

VMEM = pl.BlockSpec(memory_space=pltpu.VMEM)
SMEM = pl.BlockSpec(memory_space=pltpu.SMEM)
ANY = pl.BlockSpec(memory_space=pl.ANY)
PARAMS = pltpu.CompilerParams(vmem_limit_bytes=48 * 1024 * 1024)


def transform_tables():
    index = np.arange(HALF)
    plain = []
    for parity in (0, 1):
        angle = 2.0 * math.pi / P_SIZE * (index[:, None] * (2 * index[None, :] + parity) % P_SIZE)
        cos, sin = np.cos(angle), np.sin(angle)
        plain.append(np.block([[cos, -sin], [sin, cos]]) / math.sqrt(P_SIZE))
    parts = []
    for table in plain + [t.T for t in plain]:
        high = table.astype(np.float32).astype(ml_dtypes.bfloat16)
        low = (table - high.astype(np.float64)).astype(np.float32).astype(ml_dtypes.bfloat16)
        parts += [high, low]
    order = np.concatenate([np.arange(0, P_SIZE, 2), np.arange(1, P_SIZE, 2)])
    sort = np.zeros((P_SIZE, P_SIZE), np.float32)
    sort[np.arange(P_SIZE), order] = 1.0
    parts += [sort.astype(ml_dtypes.bfloat16), sort.T.astype(ml_dtypes.bfloat16)]
    return np.stack(parts)


def lane_index(rows):
    return lax.broadcasted_iota(jnp.int32, (rows, LANES), 1)


def pack_lanes(ref, rows, first):
    lane = lane_index(rows)
    packed = None
    for g in range(GROUPS):
        part = ref[g * rows : (g + 1) * rows, :]
        if g:
            part = pltpu.roll(part, HALO * g, 1)
        low = (first + HALO * g) % LANES
        mine = (lane >= low) & (lane < low + HALO)
        packed = part if packed is None else jnp.where(mine, part, packed)
    return packed


def unpack_lanes(packed, group):
    return pltpu.roll(packed, LANES - HALO * group, 1) if group else packed


def split(x):
    high = x.astype(jnp.bfloat16)
    return high, (x - high.astype(jnp.float32)).astype(jnp.bfloat16)


def product(left, right):
    return jnp.dot(left, right, preferred_element_type=jnp.float32)


def times_table(x, table, which):
    high, low = split(x)
    t_high, t_low = table[2 * which], table[2 * which + 1]
    return product(high, t_high) + (product(high, t_low) + product(low, t_high))


def table_times(table, which, x):
    high, low = split(x)
    t_high, t_low = table[2 * which], table[2 * which + 1]
    return product(t_high, high) + (product(t_low, high) + product(t_high, low))


def beside(*blocks):
    return jnp.concatenate(blocks, axis=1)


def below(*blocks):
    return jnp.concatenate(blocks, axis=0)


def ends(x):
    return x[:, :HALF], x[:, HALF:]


def forward_columns(exit_re, exit_im, table):
    re_lo, re_hi = ends(exit_re)
    im_lo, im_hi = ends(exit_im)
    even = times_table(beside(re_lo + re_hi, im_lo + im_hi), table, 0)
    odd = times_table(beside(re_lo - re_hi, im_lo - im_hi), table, 1)
    return even, odd


def forward_rows(even, odd, table):
    out = []
    for parity in (0, 1):
        if parity == 0:
            se, so = even[:HALF] + even[HALF:], odd[:HALF] + odd[HALF:]
        else:
            se, so = even[:HALF] - even[HALF:], odd[:HALF] - odd[HALF:]
        e_re, e_im = ends(se)
        o_re, o_im = ends(so)
        out.append(table_times(table, 2 + parity, below(beside(e_re, o_re), beside(e_im, o_im))))
    return out


def residual(far, frame):
    out = []
    for parity in (0, 1):
        re, im = far[parity][:HALF], far[parity][HALF:]
        level = jnp.maximum(re * re + im * im, floor_amp * floor_amp)
        inten = frame[parity * HALF : (parity + 1) * HALF]
        factor = 1.0 - inten * lax.rsqrt(inten * level)
        out.append(below(re * factor, im * factor))
    return out


def back_rows(res, table):
    first = table_times(table, 0, res[0])
    second = table_times(table, 1, res[1])
    upper, lower = first + second, first - second
    out = []
    for cols in (slice(0, HALF), slice(HALF, P_SIZE)):
        out.append(
            below(
                beside(upper[:HALF, cols], upper[HALF:, cols]),
                beside(lower[:HALF, cols], lower[HALF:, cols]),
            )
        )
    return out


def back_columns(parts, table):
    even = times_table(parts[0], table, 2)
    odd = times_table(parts[1], table, 3)
    lo, hi = even + odd, even - odd
    return beside(lo[:, :HALF], hi[:, :HALF]), beside(lo[:, HALF:], hi[:, HALF:])


def window_kernel(
    counts, offsets, chosen, obj_re, obj_im, above, under, left, right,
    probe_re, probe_im, frames, table,
    acc_out, to_left, to_right,
    cells, acc, strip, sems,
):
    tile_r, tile_c = obj_re.shape
    rows = tile_r + 2 * HALO
    layers = acc.shape[0]
    inner = slice(HALO, HALO + tile_r)
    middle = slice(LANES, LANES + tile_c)
    copies = []
    for k, ref in enumerate((obj_re, obj_im)):
        copies.append(pltpu.make_async_copy(ref, cells.at[k, inner, middle], sems.at[3 * k]))
        copies.append(pltpu.make_async_copy(above.at[k], cells.at[k, 0:HALO, middle], sems.at[3 * k + 1]))
        copies.append(
            pltpu.make_async_copy(under.at[k], cells.at[k, rows - HALO : rows, middle], sems.at[3 * k + 2])
        )
    for copy in copies:
        copy.start()
    group_rows = 2 * rows // GROUPS
    for g in range(GROUPS):
        k, start = divmod(g * group_rows, rows)
        piece = slice(start, start + group_rows)
        cells[k, piece, 0:LANES] = unpack_lanes(left[...], g)
        cells[k, piece, LANES + tile_c :] = unpack_lanes(right[...], g)
    acc[...] = jnp.zeros_like(acc)
    for copy in copies:
        copy.wait()

    count = counts[0, 0]
    lane = lane_index(P_SIZE)

    def load(slot):
        row = pl.multiple_of(offsets[0, 0, slot, 0] + HALO, 16)
        col = offsets[0, 0, slot, 1] + LANES
        turn = lax.rem(col, LANES)
        base = pl.multiple_of(col - turn, LANES)
        keep = lane >= turn
        w_re = pltpu.roll(probe_re[...], turn, 1)
        w_im = pltpu.roll(probe_im[...], turn, 1)
        patch = []
        for k in (0, 1):
            block = cells[k, pl.ds(row, P_SIZE), pl.ds(base, 3 * LANES)]
            patch.append(
                beside(jnp.where(keep, block[:, :LANES], block[:, 2 * LANES :]), block[:, LANES : 2 * LANES])
            )
        exit_re = w_re * patch[0] - w_im * patch[1]
        exit_im = w_re * patch[1] + w_im * patch[0]
        return (row, base, keep, w_re, w_im), exit_re, exit_im

    def frame_of(slot):
        sort, unsort = table[8], table[9]
        half = product(sort, frames[chosen[0, 0, slot]]).astype(jnp.bfloat16)
        return product(half, unsort)

    def place(where, back_re, back_im):
        row, base, keep, w_re, w_im = where
        terms = (
            w_re * back_re + w_im * back_im,
            w_re * back_im - w_im * back_re,
            w_re * w_re + w_im * w_im,
        )
        for k in range(layers):
            lo, hi = ends(terms[k])
            parts = (jnp.where(keep, lo, 0.0), hi, jnp.where(keep, 0.0, lo))
            for t, part in enumerate(parts):
                acc[k, pl.ds(row, P_SIZE), pl.ds(base + t * LANES, LANES)] += part

    def step(pair, carry):
        slots = [jnp.minimum(pair * PAIR + i, count - 1) for i in range(PAIR)]
        frame = [frame_of(slot) for slot in slots]
        loaded = [load(slot) for slot in slots]
        state = [forward_columns(x[1], x[2], table) for x in loaded]
        state = [forward_rows(*x, table) for x in state]
        state = [residual(x, f) for x, f in zip(state, frame)]
        state = [back_rows(x, table) for x in state]
        state = [back_columns(x, table) for x in state]
        place(loaded[0][0], *state[0])
        for i in range(1, PAIR):
            pl.when(pair * PAIR + i < count)(functools.partial(place, loaded[i][0], *state[i]))
        return carry

    lax.fori_loop(0, (count + PAIR - 1) // PAIR, step, 0)

    out = pltpu.make_async_copy(acc.at[:, :, middle], acc_out, sems.at[0])
    out.start()
    group_rows = layers * rows // GROUPS
    for tile, first, dest in ((0, LANES - HALO, to_left), (LANES + tile_c, 0, to_right)):
        for k in range(layers):
            strip[k * rows : (k + 1) * rows, :] = acc[k, :, tile : tile + LANES]
        dest[...] = pack_lanes(strip, group_rows, first)
    out.wait()


def column_strips(obj_re, obj_im, above, under, to_left, to_right, strip, sems):
    tile_r, tile_c = obj_re.shape
    rows = tile_r + 2 * HALO
    copies = []
    for side, start in ((0, 0), (1, tile_c - LANES)):
        cols = slice(start, start + LANES)
        for k, ref in enumerate((obj_re, obj_im)):
            top = k * rows
            base = 6 * side + 3 * k
            copies += [
                pltpu.make_async_copy(above.at[k, :, cols], strip.at[side, top : top + HALO], sems.at[base]),
                pltpu.make_async_copy(
                    ref.at[:, cols], strip.at[side, top + HALO : top + HALO + tile_r], sems.at[base + 1]
                ),
                pltpu.make_async_copy(
                    under.at[k, :, cols], strip.at[side, top + rows - HALO : top + rows], sems.at[base + 2]
                ),
            ]
    for copy in copies:
        copy.start()
    for copy in copies:
        copy.wait()
    group_rows = 2 * rows // GROUPS
    to_left[...] = pack_lanes(strip.at[0], group_rows, 0)
    to_right[...] = pack_lanes(strip.at[1], group_rows, LANES - HALO)


def add_side_strips(add, packed, layers, rows, first):
    group_rows = layers * rows // GROUPS
    lane = lane_index(group_rows)
    mine = (lane >= first) & (lane < first + HALO)
    for g in range(GROUPS):
        part = jnp.where(mine, unpack_lanes(packed, g), 0.0)
        done = 0
        while done < group_rows:
            layer, row = divmod(g * group_rows + done, rows)
            size = min(group_rows - done, rows - row)
            add(layer, row, part[done : done + size])
            done += size


def row_strips(acc, from_left, from_right, up, down, whole):
    layers, rows, width = acc.shape
    whole[...] = acc[...]
    for packed, first, col in ((from_left, 0, 0), (from_right, LANES - HALO, width - LANES)):

        def add(layer, row, part):
            whole[layer, row : row + part.shape[0], col : col + LANES] += part

        add_side_strips(add, packed[...], layers, rows, first)
    up[...] = whole[:, 0:HALO, :]
    down[...] = whole[:, rows - HALO : rows, :]


def finish(whole, from_above, from_under, obj_re, obj_im, new_re, new_im):
    layers, rows, width = whole.shape
    tile_r = rows - 2 * HALO
    for start, size, extra in (
        (0, HALO, from_above),
        (HALO, tile_r - 2 * HALO, None),
        (tile_r - HALO, HALO, from_under),
    ):
        part = [whole[k, HALO + start : HALO + start + size, :] for k in range(layers)]
        if extra is not None:
            part = [part[k] + extra[k] for k in range(layers)]
        scale = 1.0 / (part[2] + ridge)
        new_re[start : start + size, :] = obj_re[start : start + size, :] - part[0] * scale
        new_im[start : start + size, :] = obj_im[start : start + size, :] - part[1] * scale


def passed_along(shard, axis, by):
    devices = lax.axis_size(axis)
    pairs = [(i, i + by) for i in range(devices) if 0 <= i + by < devices]
    return lax.ppermute(shard, axis, pairs)


def f32(*shape):
    return jax.ShapeDtypeStruct(shape, jnp.float32)


def shards(object_re, object_im, probe_re, probe_im, frames, counts, offsets, frame_index):
    tile_r, tile_c = object_re.shape
    rows = tile_r + 2 * HALO
    layers = 3
    table = jnp.asarray(transform_tables())

    stacked_top = jnp.stack([object_re[:HALO], object_im[:HALO]])
    stacked_end = jnp.stack([object_re[tile_r - HALO :], object_im[tile_r - HALO :]])
    above = passed_along(stacked_end, "row", 1)
    under = passed_along(stacked_top, "row", -1)

    strip_rows = 2 * rows // GROUPS
    to_left, to_right = pl.pallas_call(
        column_strips,
        out_shape=(f32(strip_rows, LANES), f32(strip_rows, LANES)),
        in_specs=[ANY] * 4,
        out_specs=(VMEM, VMEM),
        scratch_shapes=[pltpu.VMEM((2, 2 * rows, LANES), jnp.float32), pltpu.SemaphoreType.DMA((12,))],
        compiler_params=PARAMS,
        name="column_strips",
    )(object_re, object_im, above, under)
    left = passed_along(to_right, "col", 1)
    right = passed_along(to_left, "col", -1)

    spill_rows = layers * rows // GROUPS
    acc, to_left, to_right = pl.pallas_call(
        window_kernel,
        out_shape=(f32(layers, rows, tile_c), f32(spill_rows, LANES), f32(spill_rows, LANES)),
        in_specs=[SMEM] * 3 + [ANY] * 4 + [VMEM] * 6,
        out_specs=(ANY, VMEM, VMEM),
        scratch_shapes=[
            pltpu.VMEM((2, rows, tile_c + 2 * LANES), jnp.float32),
            pltpu.VMEM((layers, rows, tile_c + 2 * LANES), jnp.float32),
            pltpu.VMEM((layers * rows, LANES), jnp.float32),
            pltpu.SemaphoreType.DMA((6,)),
        ],
        compiler_params=PARAMS,
        name="windows",
    )(
        counts, offsets, frame_index, object_re, object_im, above, under, left, right,
        probe_re, probe_im, frames.reshape(frames.shape[2:]), table,
    )
    from_right = passed_along(to_left, "col", -1)
    from_left = passed_along(to_right, "col", 1)

    up, down, whole = pl.pallas_call(
        row_strips,
        out_shape=(f32(layers, HALO, tile_c), f32(layers, HALO, tile_c), f32(layers, rows, tile_c)),
        in_specs=[VMEM] * 3,
        out_specs=(VMEM,) * 3,
        compiler_params=PARAMS,
        name="row_strips",
    )(acc, from_left, from_right)
    from_under = passed_along(up, "row", -1)
    from_above = passed_along(down, "row", 1)

    return pl.pallas_call(
        finish,
        out_shape=(f32(tile_r, tile_c), f32(tile_r, tile_c)),
        in_specs=[VMEM] * 5,
        out_specs=(VMEM, VMEM),
        compiler_params=PARAMS,
        name="finish",
    )(whole, from_above, from_under, object_re, object_im)


def solution(mesh):
    return jax.shard_map(
        shards,
        mesh=mesh,
        in_specs=(
            P("row", "col"),
            P("row", "col"),
            P(),
            P(),
            P("row", "col", None, None, None),
            P("row", "col"),
            P("row", "col", None, None),
            P("row", "col", None),
        ),
        out_specs=(P("row", "col"), P("row", "col")),
        check_vma=False,
    )
```

```python
import functools
import math

import jax
import jax.numpy as jnp
import ml_dtypes
import numpy as np
from jax import lax
from jax.experimental import pallas as pl
from jax.experimental.pallas import tpu as pltpu
from jax.sharding import PartitionSpec as P

P_SIZE = 256
HALF = P_SIZE // 2
HALO = 32
LANES = 128
GROUPS = LANES // HALO
PAIR = 2

floor_amp = 0.5
ridge = 1.0

VMEM = pl.BlockSpec(memory_space=pltpu.VMEM)
SMEM = pl.BlockSpec(memory_space=pltpu.SMEM)
ANY = pl.BlockSpec(memory_space=pltpu.HBM)
PARAMS = pltpu.CompilerParams(vmem_limit_bytes=60 * 1024 * 1024)


def transform_tables():
    index = np.arange(HALF)
    plain = []
    for parity in (0, 1):
        angle = 2.0 * math.pi / P_SIZE * (index[:, None] * (2 * index[None, :] + parity) % P_SIZE)
        cos, sin = np.cos(angle), np.sin(angle)
        plain.append(np.block([[cos, -sin], [sin, cos]]) / math.sqrt(P_SIZE))
    parts = []
    for table in plain + [t.T for t in plain]:
        high = table.astype(np.float32).astype(ml_dtypes.bfloat16)
        low = (table - high.astype(np.float64)).astype(np.float32).astype(ml_dtypes.bfloat16)
        parts += [high, low]
    order = np.concatenate([np.arange(0, P_SIZE, 2), np.arange(1, P_SIZE, 2)])
    sort = np.zeros((P_SIZE, P_SIZE), np.float32)
    sort[np.arange(P_SIZE), order] = 1.0
    parts += [sort.astype(ml_dtypes.bfloat16), sort.T.astype(ml_dtypes.bfloat16)]
    return np.stack(parts)


def lane_index(rows):
    return lax.broadcasted_iota(jnp.int32, (rows, LANES), 1)


def pack_lanes(ref, rows, first):
    lane = lane_index(rows)
    packed = None
    for g in range(GROUPS):
        part = ref[g * rows : (g + 1) * rows, :]
        if g:
            part = pltpu.roll(part, HALO * g, 1)
        low = (first + HALO * g) % LANES
        mine = (lane >= low) & (lane < low + HALO)
        packed = part if packed is None else jnp.where(mine, part, packed)
    return packed


def unpack_lanes(packed, group):
    return pltpu.roll(packed, LANES - HALO * group, 1) if group else packed


def split(x):
    high = x.astype(jnp.bfloat16)
    return high, (x - high.astype(jnp.float32)).astype(jnp.bfloat16)


def product(left, right):
    return jnp.dot(left, right, preferred_element_type=jnp.float32)


def times_table(x, table, which):
    high, low = split(x)
    t_high, t_low = table[2 * which], table[2 * which + 1]
    return product(high, t_high) + (product(high, t_low) + product(low, t_high))


def table_times(table, which, x):
    high, low = split(x)
    t_high, t_low = table[2 * which], table[2 * which + 1]
    return product(t_high, high) + (product(t_low, high) + product(t_high, low))


def beside(*blocks):
    return jnp.concatenate(blocks, axis=1)


def below(*blocks):
    return jnp.concatenate(blocks, axis=0)


def ends(x):
    return x[:, :HALF], x[:, HALF:]


def forward_columns(exit_re, exit_im, table):
    re_lo, re_hi = ends(exit_re)
    im_lo, im_hi = ends(exit_im)
    even = times_table(beside(re_lo + re_hi, im_lo + im_hi), table, 0)
    odd = times_table(beside(re_lo - re_hi, im_lo - im_hi), table, 1)
    return even, odd


def forward_rows(even, odd, table):
    out = []
    for parity in (0, 1):
        if parity == 0:
            se, so = even[:HALF] + even[HALF:], odd[:HALF] + odd[HALF:]
        else:
            se, so = even[:HALF] - even[HALF:], odd[:HALF] - odd[HALF:]
        e_re, e_im = ends(se)
        o_re, o_im = ends(so)
        out.append(table_times(table, 2 + parity, below(beside(e_re, o_re), beside(e_im, o_im))))
    return out


def residual(far, frame):
    out = []
    for parity in (0, 1):
        re, im = far[parity][:HALF], far[parity][HALF:]
        level = jnp.maximum(re * re + im * im, floor_amp * floor_amp)
        inten = frame[parity * HALF : (parity + 1) * HALF]
        factor = 1.0 - inten * lax.rsqrt(inten * level)
        out.append(below(re * factor, im * factor))
    return out


def back_rows(res, table):
    first = table_times(table, 0, res[0])
    second = table_times(table, 1, res[1])
    upper, lower = first + second, first - second
    out = []
    for cols in (slice(0, HALF), slice(HALF, P_SIZE)):
        out.append(
            below(
                beside(upper[:HALF, cols], upper[HALF:, cols]),
                beside(lower[:HALF, cols], lower[HALF:, cols]),
            )
        )
    return out


def back_columns(parts, table):
    even = times_table(parts[0], table, 2)
    odd = times_table(parts[1], table, 3)
    lo, hi = even + odd, even - odd
    return beside(lo[:, :HALF], hi[:, :HALF]), beside(lo[:, HALF:], hi[:, HALF:])


def window_kernel(
    counts, offsets, chosen, obj_re, obj_im, above, under, left, right,
    probe_re_far, probe_im_far, frames_far, table_far,
    acc_out, to_left, to_right,
    cells, acc, strip, probe_re, probe_im, frames, table, sems,
):
    tile_r, tile_c = obj_re.shape
    rows = tile_r + 2 * HALO
    layers = acc.shape[0]
    inner = slice(HALO, HALO + tile_r)
    middle = slice(LANES, LANES + tile_c)
    copies = []
    for k, ref in enumerate((obj_re, obj_im)):
        copies.append(pltpu.make_async_copy(ref, cells.at[k, inner, middle], sems.at[3 * k]))
        copies.append(pltpu.make_async_copy(above.at[k], cells.at[k, 0:HALO, middle], sems.at[3 * k + 1]))
        copies.append(
            pltpu.make_async_copy(under.at[k], cells.at[k, rows - HALO : rows, middle], sems.at[3 * k + 2])
        )
    pairs = ((table_far, table), (probe_re_far, probe_re), (probe_im_far, probe_im), (frames_far, frames))
    for i, (far, near) in enumerate(pairs):
        copies.append(pltpu.make_async_copy(far, near, sems.at[6 + i]))
    for copy in copies:
        copy.start()
    group_rows = 2 * rows // GROUPS
    for g in range(GROUPS):
        k, start = divmod(g * group_rows, rows)
        piece = slice(start, start + group_rows)
        cells[k, piece, 0:LANES] = unpack_lanes(left[...], g)
        cells[k, piece, LANES + tile_c :] = unpack_lanes(right[...], g)
    acc[...] = jnp.zeros_like(acc)
    for copy in copies:
        copy.wait()

    count = counts[0, 0]
    lane = lane_index(P_SIZE)

    def load(slot):
        row = pl.multiple_of(offsets[0, 0, slot, 0] + HALO, 16)
        col = offsets[0, 0, slot, 1] + LANES
        turn = lax.rem(col, LANES)
        base = pl.multiple_of(col - turn, LANES)
        keep = lane >= turn
        w_re = pltpu.roll(probe_re[...], turn, 1)
        w_im = pltpu.roll(probe_im[...], turn, 1)
        patch = []
        for k in (0, 1):
            block = cells[k, pl.ds(row, P_SIZE), pl.ds(base, 3 * LANES)]
            patch.append(
                beside(jnp.where(keep, block[:, :LANES], block[:, 2 * LANES :]), block[:, LANES : 2 * LANES])
            )
        exit_re = w_re * patch[0] - w_im * patch[1]
        exit_im = w_re * patch[1] + w_im * patch[0]
        return (row, base, keep, w_re, w_im), exit_re, exit_im

    def frame_of(slot):
        sort, unsort = table[8], table[9]
        half = product(sort, frames[chosen[0, 0, slot]]).astype(jnp.bfloat16)
        return product(half, unsort)

    def place(where, back_re, back_im):
        row, base, keep, w_re, w_im = where
        terms = (
            w_re * back_re + w_im * back_im,
            w_re * back_im - w_im * back_re,
            w_re * w_re + w_im * w_im,
        )
        for k in range(layers):
            lo, hi = ends(terms[k])
            parts = (jnp.where(keep, lo, 0.0), hi, jnp.where(keep, 0.0, lo))
            for t, part in enumerate(parts):
                acc[k, pl.ds(row, P_SIZE), pl.ds(base + t * LANES, LANES)] += part

    def step(pair, carry):
        slots = [jnp.minimum(pair * PAIR + i, count - 1) for i in range(PAIR)]
        frame = [frame_of(slot) for slot in slots]
        loaded = [load(slot) for slot in slots]
        state = [forward_columns(x[1], x[2], table) for x in loaded]
        state = [forward_rows(*x, table) for x in state]
        state = [residual(x, f) for x, f in zip(state, frame)]
        state = [back_rows(x, table) for x in state]
        state = [back_columns(x, table) for x in state]
        place(loaded[0][0], *state[0])
        for i in range(1, PAIR):
            pl.when(pair * PAIR + i < count)(functools.partial(place, loaded[i][0], *state[i]))
        return carry

    lax.fori_loop(0, (count + PAIR - 1) // PAIR, step, 0)

    out = pltpu.make_async_copy(acc.at[:, :, middle], acc_out, sems.at[0])
    out.start()
    group_rows = layers * rows // GROUPS
    for tile, first, dest in ((0, LANES - HALO, to_left), (LANES + tile_c, 0, to_right)):
        for k in range(layers):
            strip[k * rows : (k + 1) * rows, :] = acc[k, :, tile : tile + LANES]
        dest[...] = pack_lanes(strip, group_rows, first)
    out.wait()


def column_strips(obj_re, obj_im, above, under, to_left, to_right, strip, sems):
    tile_r, tile_c = obj_re.shape
    rows = tile_r + 2 * HALO
    copies = []
    for side, start in ((0, 0), (1, tile_c - LANES)):
        cols = slice(start, start + LANES)
        for k, ref in enumerate((obj_re, obj_im)):
            top = k * rows
            base = 6 * side + 3 * k
            copies += [
                pltpu.make_async_copy(above.at[k, :, cols], strip.at[side, top : top + HALO], sems.at[base]),
                pltpu.make_async_copy(
                    ref.at[:, cols], strip.at[side, top + HALO : top + HALO + tile_r], sems.at[base + 1]
                ),
                pltpu.make_async_copy(
                    under.at[k, :, cols], strip.at[side, top + rows - HALO : top + rows], sems.at[base + 2]
                ),
            ]
    for copy in copies:
        copy.start()
    for copy in copies:
        copy.wait()
    group_rows = 2 * rows // GROUPS
    to_left[...] = pack_lanes(strip.at[0], group_rows, 0)
    to_right[...] = pack_lanes(strip.at[1], group_rows, LANES - HALO)


def add_side_strips(add, packed, layers, rows, first):
    group_rows = layers * rows // GROUPS
    lane = lane_index(group_rows)
    mine = (lane >= first) & (lane < first + HALO)
    for g in range(GROUPS):
        part = jnp.where(mine, unpack_lanes(packed, g), 0.0)
        done = 0
        while done < group_rows:
            layer, row = divmod(g * group_rows + done, rows)
            size = min(group_rows - done, rows - row)
            add(layer, row, part[done : done + size])
            done += size


def row_strips(acc, from_left, from_right, up, down, whole):
    layers, rows, width = acc.shape
    whole[...] = acc[...]
    for packed, first, col in ((from_left, 0, 0), (from_right, LANES - HALO, width - LANES)):

        def add(layer, row, part):
            whole[layer, row : row + part.shape[0], col : col + LANES] += part

        add_side_strips(add, packed[...], layers, rows, first)
    up[...] = whole[:, 0:HALO, :]
    down[...] = whole[:, rows - HALO : rows, :]


def finish(whole, from_above, from_under, obj_re, obj_im, new_re, new_im):
    layers, rows, width = whole.shape
    tile_r = rows - 2 * HALO
    for start, size, extra in (
        (0, HALO, from_above),
        (HALO, tile_r - 2 * HALO, None),
        (tile_r - HALO, HALO, from_under),
    ):
        part = [whole[k, HALO + start : HALO + start + size, :] for k in range(layers)]
        if extra is not None:
            part = [part[k] + extra[k] for k in range(layers)]
        scale = 1.0 / (part[2] + ridge)
        new_re[start : start + size, :] = obj_re[start : start + size, :] - part[0] * scale
        new_im[start : start + size, :] = obj_im[start : start + size, :] - part[1] * scale


def passed_along(shard, axis, by):
    devices = lax.axis_size(axis)
    pairs = [(i, i + by) for i in range(devices) if 0 <= i + by < devices]
    return lax.ppermute(shard, axis, pairs)


def swapped(first, last, axis):
    devices = lax.axis_size(axis)
    index = lax.axis_index(axis)
    odd = index % 2
    inner = [[i, i + 1] for i in range(0, devices, 2)]
    outer = [[i, (i + 1) % devices] for i in range(1, devices, 2)]
    by_inner = lax.all_gather(jnp.where(odd == 1, first, last), axis, axis_index_groups=inner)
    by_outer = lax.all_gather(jnp.where(odd == 1, last, first), axis, axis_index_groups=outer)
    from_inner = jnp.where(odd == 1, by_inner[0], by_inner[1])
    from_outer = jnp.where(odd == 1, by_outer[1], by_outer[0])
    before = jnp.where(odd == 1, from_inner, jnp.where(index > 0, from_outer, 0.0))
    after = jnp.where(odd == 1, jnp.where(index < devices - 1, from_outer, 0.0), from_inner)
    return before, after


def f32(*shape):
    return jax.ShapeDtypeStruct(shape, jnp.float32)


def shards(object_re, object_im, probe_re, probe_im, frames, counts, offsets, frame_index):
    tile_r, tile_c = object_re.shape
    rows = tile_r + 2 * HALO
    layers = 3
    table = jnp.asarray(transform_tables())

    stacked_top = jnp.stack([object_re[:HALO], object_im[:HALO]])
    stacked_end = jnp.stack([object_re[tile_r - HALO :], object_im[tile_r - HALO :]])
    above, under = swapped(stacked_top, stacked_end, "row")

    strip_rows = 2 * rows // GROUPS
    to_left, to_right = pl.pallas_call(
        column_strips,
        out_shape=(f32(strip_rows, LANES), f32(strip_rows, LANES)),
        in_specs=[ANY] * 4,
        out_specs=(VMEM, VMEM),
        scratch_shapes=[pltpu.VMEM((2, 2 * rows, LANES), jnp.float32), pltpu.SemaphoreType.DMA((12,))],
        compiler_params=PARAMS,
        name="column_strips",
    )(object_re, object_im, above, under)
    left = passed_along(to_right, "col", 1)
    right = passed_along(to_left, "col", -1)

    spill_rows = layers * rows // GROUPS
    acc, to_left, to_right = pl.pallas_call(
        window_kernel,
        out_shape=(f32(layers, rows, tile_c), f32(spill_rows, LANES), f32(spill_rows, LANES)),
        in_specs=[SMEM] * 3 + [ANY] * 4 + [VMEM] * 2 + [ANY] * 4,
        out_specs=(ANY, VMEM, VMEM),
        scratch_shapes=[
            pltpu.VMEM((2, rows, tile_c + 2 * LANES), jnp.float32),
            pltpu.VMEM((layers, rows, tile_c + 2 * LANES), jnp.float32),
            pltpu.VMEM((layers * rows, LANES), jnp.float32),
            pltpu.VMEM(probe_re.shape, jnp.float32),
            pltpu.VMEM(probe_im.shape, jnp.float32),
            pltpu.VMEM(frames.shape[2:], frames.dtype),
            pltpu.VMEM(table.shape, table.dtype),
            pltpu.SemaphoreType.DMA((10,)),
        ],
        compiler_params=PARAMS,
        name="windows",
    )(
        counts, offsets, frame_index, object_re, object_im, above, under, left, right,
        probe_re, probe_im, frames.reshape(frames.shape[2:]), table,
    )
    from_right = passed_along(to_left, "col", -1)
    from_left = passed_along(to_right, "col", 1)

    up, down, whole = pl.pallas_call(
        row_strips,
        out_shape=(f32(layers, HALO, tile_c), f32(layers, HALO, tile_c), f32(layers, rows, tile_c)),
        in_specs=[VMEM] * 3,
        out_specs=(VMEM,) * 3,
        compiler_params=PARAMS,
        name="row_strips",
    )(acc, from_left, from_right)
    from_above, from_under = swapped(up, down, "row")

    return pl.pallas_call(
        finish,
        out_shape=(f32(tile_r, tile_c), f32(tile_r, tile_c)),
        in_specs=[VMEM] * 5,
        out_specs=(VMEM, VMEM),
        compiler_params=PARAMS,
        name="finish",
    )(whole, from_above, from_under, object_re, object_im)


def solution(mesh):
    return jax.shard_map(
        shards,
        mesh=mesh,
        in_specs=(
            P("row", "col"),
            P("row", "col"),
            P(),
            P(),
            P("row", "col", None, None, None),
            P("row", "col"),
            P("row", "col", None, None),
            P("row", "col", None),
        ),
        out_specs=(P("row", "col"), P("row", "col")),
        check_vma=False,
    )
```

```python
import functools
import math

import jax
import jax.numpy as jnp
import ml_dtypes
import numpy as np
from jax import lax
from jax.experimental import pallas as pl
from jax.experimental.pallas import tpu as pltpu
from jax.sharding import PartitionSpec as P

P_SIZE = 256
HALF = P_SIZE // 2
HALO = 32
LANES = 128
GROUPS = LANES // HALO
PAIR = 2

floor_amp = 0.5
ridge = 1.0

VMEM = pl.BlockSpec(memory_space=pltpu.VMEM)
SMEM = pl.BlockSpec(memory_space=pltpu.SMEM)
HBM = pl.BlockSpec(memory_space=pltpu.HBM)
PARAMS = pltpu.CompilerParams(vmem_limit_bytes=40 * 1024 * 1024)
ALONE = pltpu.CompilerParams(vmem_limit_bytes=60 * 1024 * 1024)
BUSY = pl.CostEstimate(flops=4_000_000_000, bytes_accessed=8_000_000, transcendentals=0)


def transform_tables():
    index = np.arange(HALF)
    plain = []
    for parity in (0, 1):
        angle = 2.0 * math.pi / P_SIZE * (index[:, None] * (2 * index[None, :] + parity) % P_SIZE)
        cos, sin = np.cos(angle), np.sin(angle)
        plain.append(np.block([[cos, -sin], [sin, cos]]) / math.sqrt(P_SIZE))
    parts = []
    for table in plain + [t.T for t in plain]:
        high = table.astype(np.float32).astype(ml_dtypes.bfloat16)
        low = (table - high.astype(np.float64)).astype(np.float32).astype(ml_dtypes.bfloat16)
        parts += [high, low]
    order = np.concatenate([np.arange(0, P_SIZE, 2), np.arange(1, P_SIZE, 2)])
    sort = np.zeros((P_SIZE, P_SIZE), np.float32)
    sort[np.arange(P_SIZE), order] = 1.0
    parts += [sort.astype(ml_dtypes.bfloat16), sort.T.astype(ml_dtypes.bfloat16)]
    return np.stack(parts)


def lane_index(rows):
    return lax.broadcasted_iota(jnp.int32, (rows, LANES), 1)


def pack_lanes(ref, rows, first):
    lane = lane_index(rows)
    packed = None
    for g in range(GROUPS):
        part = ref[g * rows : (g + 1) * rows, :]
        if g:
            part = pltpu.roll(part, HALO * g, 1)
        low = (first + HALO * g) % LANES
        mine = (lane >= low) & (lane < low + HALO)
        packed = part if packed is None else jnp.where(mine, part, packed)
    return packed


def unpack_lanes(packed, group):
    return pltpu.roll(packed, LANES - HALO * group, 1) if group else packed


def split(x):
    high = x.astype(jnp.bfloat16)
    return high, (x - high.astype(jnp.float32)).astype(jnp.bfloat16)


def product(left, right):
    return jnp.dot(left, right, preferred_element_type=jnp.float32)


def times_table(x, table, which):
    high, low = split(x)
    t_high, t_low = table[2 * which], table[2 * which + 1]
    return product(high, t_high) + (product(high, t_low) + product(low, t_high))


def table_times(table, which, x):
    high, low = split(x)
    t_high, t_low = table[2 * which], table[2 * which + 1]
    return product(t_high, high) + (product(t_low, high) + product(t_high, low))


def beside(*blocks):
    return jnp.concatenate(blocks, axis=1)


def below(*blocks):
    return jnp.concatenate(blocks, axis=0)


def ends(x):
    return x[:, :HALF], x[:, HALF:]


def forward_columns(exit_re, exit_im, table):
    re_lo, re_hi = ends(exit_re)
    im_lo, im_hi = ends(exit_im)
    even = times_table(beside(re_lo + re_hi, im_lo + im_hi), table, 0)
    odd = times_table(beside(re_lo - re_hi, im_lo - im_hi), table, 1)
    return even, odd


def forward_rows(even, odd, table):
    out = []
    for parity in (0, 1):
        if parity == 0:
            se, so = even[:HALF] + even[HALF:], odd[:HALF] + odd[HALF:]
        else:
            se, so = even[:HALF] - even[HALF:], odd[:HALF] - odd[HALF:]
        e_re, e_im = ends(se)
        o_re, o_im = ends(so)
        out.append(table_times(table, 2 + parity, below(beside(e_re, o_re), beside(e_im, o_im))))
    return out


def residual(far, frame):
    out = []
    for parity in (0, 1):
        re, im = far[parity][:HALF], far[parity][HALF:]
        level = jnp.maximum(re * re + im * im, floor_amp * floor_amp)
        inten = frame[parity * HALF : (parity + 1) * HALF]
        factor = 1.0 - inten * lax.rsqrt(inten * level)
        out.append(below(re * factor, im * factor))
    return out


def back_rows(res, table):
    first = table_times(table, 0, res[0])
    second = table_times(table, 1, res[1])
    upper, lower = first + second, first - second
    out = []
    for cols in (slice(0, HALF), slice(HALF, P_SIZE)):
        out.append(
            below(
                beside(upper[:HALF, cols], upper[HALF:, cols]),
                beside(lower[:HALF, cols], lower[HALF:, cols]),
            )
        )
    return out


def back_columns(parts, table):
    even = times_table(parts[0], table, 2)
    odd = times_table(parts[1], table, 3)
    lo, hi = even + odd, even - odd
    return beside(lo[:, :HALF], hi[:, :HALF]), beside(lo[:, HALF:], hi[:, HALF:])


def is_odd(axis):
    return lax.rem(lax.axis_index(axis), 2) == 1


def fetch(pairs, sems):
    copies = [pltpu.make_async_copy(far, near, sems.at[i]) for i, (far, near) in enumerate(pairs)]
    for copy in copies:
        copy.start()
    return copies


def finish_all(copies):
    for copy in copies:
        copy.wait()


def row_edges(obj_re, obj_im, to_inner, to_outer, sems):
    tile_r = obj_re.shape[0]
    odd = is_odd("row")
    low = pl.multiple_of(jnp.where(odd, 0, tile_r - HALO), 16)
    high = pl.multiple_of(jnp.where(odd, tile_r - HALO, 0), 16)
    pairs = []
    for k, ref in enumerate((obj_re, obj_im)):
        pairs.append((ref.at[pl.ds(high, HALO)], to_outer.at[k]))
        pairs.append((ref.at[pl.ds(low, HALO)], to_inner.at[k]))
    finish_all(fetch(pairs, sems))


def window_place(offsets, slot):
    row = pl.multiple_of(offsets[0, 0, slot, 0] + HALO, 16)
    col = offsets[0, 0, slot, 1] + LANES
    turn = lax.rem(col, LANES)
    return row, pl.multiple_of(col - turn, LANES), turn


def add_window(acc, layer, where, keep, term):
    row, base, _ = where
    lo, hi = ends(term)
    for t, part in enumerate((jnp.where(keep, lo, 0.0), hi, jnp.where(keep, 0.0, lo))):
        acc[layer, pl.ds(row, P_SIZE), pl.ds(base + t * LANES, LANES)] += part


def load_state(
    counts, offsets, obj_re, obj_im, probe_re_far, probe_im_far, frames_far, table_far,
    cells, acc, probe_re, probe_im, frames, table, power, sems,
):
    tile_r, tile_c = obj_re.shape
    inner = slice(HALO, HALO + tile_r)
    middle = slice(LANES, LANES + tile_c)
    copies = fetch(
        (
            (probe_re_far, probe_re),
            (probe_im_far, probe_im),
            (obj_re, cells.at[0, inner, middle]),
            (obj_im, cells.at[1, inner, middle]),
            (table_far, table),
            (frames_far, frames),
        ),
        sems,
    )
    acc[...] = jnp.zeros_like(acc)
    finish_all(copies[:2])
    power[...] = probe_re[...] * probe_re[...] + probe_im[...] * probe_im[...]
    lane = lane_index(P_SIZE)

    def step(slot, carry):
        where = window_place(offsets, slot)
        add_window(acc, 2, where, lane >= where[2], pltpu.roll(power[...], where[2], 1))
        return carry

    lax.fori_loop(0, counts[0, 0], step, 0)
    finish_all(copies[2:])


def fill_strip(strip, parts):
    done = 0
    for part in parts:
        strip[done : done + part.shape[0], :] = part
        done += part.shape[0]


def send_columns(to_left, to_right, to_inner, to_outer):
    odd = is_odd("col")
    to_inner[...] = jnp.where(odd, to_left, to_right)
    to_outer[...] = jnp.where(odd, to_right, to_left)


def received(by_inner, by_outer, axis):
    odd = is_odd(axis)
    before = jnp.where(odd, by_inner[0], by_outer[...])
    after = jnp.where(odd, by_outer[...], by_inner[1])
    return before, after


def pieces(packed, layers, rows):
    group_rows = layers * rows // GROUPS
    for g in range(GROUPS):
        part = unpack_lanes(packed, g)
        done = 0
        while done < group_rows:
            layer, row = divmod(g * group_rows + done, rows)
            size = min(group_rows - done, rows - row)
            yield layer, row, part[done : done + size]
            done += size


def row_halos(cells_in, acc, by_inner, by_outer, cells, to_inner, to_outer, strip):
    rows, width = acc.shape[1:]
    middle = slice(LANES, width - LANES)
    before, after = received(by_inner, by_outer, "row")
    for k in (0, 1):
        cells[k, 0:HALO, middle] = before[k]
        cells[k, rows - HALO : rows, middle] = after[k]
    group_rows = 3 * rows // GROUPS
    first, last = slice(LANES, 2 * LANES), slice(width - 2 * LANES, width - LANES)
    fill_strip(strip, (cells[0, :, first], cells[1, :, first], pltpu.roll(acc[2, :, 0:LANES], HALO, 1)))
    to_left = pack_lanes(strip, group_rows, 0)
    fill_strip(strip, (cells[0, :, last], cells[1, :, last], pltpu.roll(acc[2, :, width - LANES :], LANES - HALO, 1)))
    to_right = pack_lanes(strip, group_rows, LANES - HALO)
    send_columns(to_left, to_right, to_inner, to_outer)


def run_windows(wanted, counts, offsets, chosen, cells, acc, probe_re, probe_im, frames, table, order):
    tile_c = cells.shape[2] - 2 * LANES
    count = counts[0, 0]
    slots = range(offsets.shape[2])
    over = []
    for slot in slots:
        col = offsets[0, 0, slot, 1]
        over.append((col < 0) | (col > tile_c - P_SIZE))
    total = jnp.int32(0)
    for slot in slots:
        total += ((slot < count) & ~over[slot]).astype(jnp.int32)
    limit = jnp.where(total <= PAIR, total, jnp.where(total <= 2 * PAIR, PAIR, 2 * PAIR))
    seen, found = jnp.int32(0), jnp.int32(0)
    for slot in slots:
        live = slot < count
        mine = live & wanted(over[slot], seen, limit)

        @pl.when(mine)
        def _():
            order[found] = slot

        seen += (live & ~over[slot]).astype(jnp.int32)
        found += mine.astype(jnp.int32)

    lane = lane_index(P_SIZE)

    def load(slot):
        where = row, base, turn = window_place(offsets, slot)
        keep = lane >= turn
        w_re = pltpu.roll(probe_re[...], turn, 1)
        w_im = pltpu.roll(probe_im[...], turn, 1)
        patch = []
        for k in (0, 1):
            block = cells[k, pl.ds(row, P_SIZE), pl.ds(base, 3 * LANES)]
            patch.append(
                beside(jnp.where(keep, block[:, :LANES], block[:, 2 * LANES :]), block[:, LANES : 2 * LANES])
            )
        exit_re = w_re * patch[0] - w_im * patch[1]
        exit_im = w_re * patch[1] + w_im * patch[0]
        return (where, keep, w_re, w_im), exit_re, exit_im

    def frame_of(slot):
        sort, unsort = table[8], table[9]
        half = product(sort, frames[chosen[0, 0, slot]]).astype(jnp.bfloat16)
        return product(half, unsort)

    def place(at, back_re, back_im):
        where, keep, w_re, w_im = at
        add_window(acc, 0, where, keep, w_re * back_re + w_im * back_im)
        add_window(acc, 1, where, keep, w_re * back_im - w_im * back_re)

    def step(group):
        frame = [frame_of(slot) for slot in group]
        loaded = [load(slot) for slot in group]
        state = [forward_columns(x[1], x[2], table) for x in loaded]
        state = [forward_rows(*x, table) for x in state]
        state = [residual(x, f) for x, f in zip(state, frame)]
        state = [back_rows(x, table) for x in state]
        state = [back_columns(x, table) for x in state]
        for x, back in zip(loaded, state):
            place(x[0], *back)

    def pair_step(pair, carry):
        step([order[pair * PAIR + i] for i in range(PAIR)])
        return carry

    lax.fori_loop(0, found // PAIR, pair_step, 0)

    @pl.when(found % PAIR == 1)
    def _():
        step([order[found - 1]])


def windows_before(counts, offsets, chosen, cells, acc_in, probe_re, probe_im, frames, table, acc, order):
    run_windows(
        lambda over, seen, limit: ~over & (seen < limit),
        counts, offsets, chosen, cells, acc, probe_re, probe_im, frames, table, order,
    )


def windows_after(counts, offsets, chosen, cells, acc_in, probe_re, probe_im, frames, table, acc, order):
    run_windows(
        lambda over, seen, limit: ~over & (seen >= limit),
        counts, offsets, chosen, cells, acc, probe_re, probe_im, frames, table, order,
    )


def windows_over_edge(
    counts, offsets, chosen, cells_in, acc_in, probe_re, probe_im, frames, table, by_inner, by_outer,
    cells, acc, to_inner, to_outer, order, strip,
):
    rows, width = acc.shape[1:]
    before, after = received(by_inner, by_outer, "col")
    lane = lane_index(rows)[0:1]
    for layer, row, part in pieces(before, 3, rows):
        here = slice(row, row + part.shape[0])
        if layer < 2:
            cells[layer, here, 0:LANES] = part
        else:
            spilled = pltpu.roll(part, HALO, 1)
            acc[2, here, LANES : 2 * LANES] += jnp.where(lane < HALO, spilled, 0.0)
    for layer, row, part in pieces(after, 3, rows):
        here = slice(row, row + part.shape[0])
        if layer < 2:
            cells[layer, here, width - LANES :] = part
        else:
            spilled = pltpu.roll(part, LANES - HALO, 1)
            acc[2, here, width - 2 * LANES : width - LANES] += jnp.where(lane >= LANES - HALO, spilled, 0.0)
    run_windows(
        lambda over, seen, limit: over,
        counts, offsets, chosen, cells, acc, probe_re, probe_im, frames, table, order,
    )
    group_rows = 2 * rows // GROUPS
    fill_strip(strip, (acc[0, :, 0:LANES], acc[1, :, 0:LANES]))
    to_left = pack_lanes(strip, group_rows, LANES - HALO)
    fill_strip(strip, (acc[0, :, width - LANES :], acc[1, :, width - LANES :]))
    to_right = pack_lanes(strip, group_rows, 0)
    send_columns(to_left, to_right, to_inner, to_outer)


def row_spill(acc_in, by_inner, by_outer, acc, to_inner, to_outer):
    layers, rows, width = acc.shape
    before, after = received(by_inner, by_outer, "col")
    lane = lane_index(rows)[0:1]
    for layer, row, part in pieces(before, 2, rows):
        here = slice(row, row + part.shape[0])
        acc[layer, here, LANES : 2 * LANES] += jnp.where(lane < HALO, part, 0.0)
    for layer, row, part in pieces(after, 2, rows):
        here = slice(row, row + part.shape[0])
        acc[layer, here, width - 2 * LANES : width - LANES] += jnp.where(lane >= LANES - HALO, part, 0.0)
    odd = is_odd("row")
    for k in range(layers):
        up = acc[k, 0:HALO, LANES : width - LANES]
        down = acc[k, rows - HALO : rows, LANES : width - LANES]
        to_inner[k] = jnp.where(odd, up, down)
        to_outer[k] = jnp.where(odd, down, up)


def finish(cells, acc, by_inner, by_outer, new_re, new_im):
    layers, rows, width = acc.shape
    tile_r = rows - 2 * HALO
    middle = slice(LANES, width - LANES)
    before, after = received(by_inner, by_outer, "row")
    for start, size, extra in (
        (0, HALO, before),
        (HALO, tile_r - 2 * HALO, None),
        (tile_r - HALO, HALO, after),
    ):
        here = slice(HALO + start, HALO + start + size)
        part = [acc[k, here, middle] for k in range(layers)]
        if extra is not None:
            part = [part[k] + extra[k] for k in range(layers)]
        scale = 1.0 / (part[2] + ridge)
        new_re[start : start + size, :] = cells[0, here, middle] - part[0] * scale
        new_im[start : start + size, :] = cells[1, here, middle] - part[1] * scale


def swap(to_inner, to_outer, axis):
    devices = lax.axis_size(axis)
    groups = [[i, i + 1] for i in range(0, devices, 2)]
    pairs = [(i, i + 1) for i in range(1, devices - 1, 2)]
    by_inner = lax.all_gather(to_inner, axis, axis_index_groups=groups)
    by_outer = lax.ppermute(to_outer, axis, pairs + [(j, i) for i, j in pairs])
    return by_inner, by_outer


def f32(*shape):
    return jax.ShapeDtypeStruct(shape, jnp.float32)


def shards(object_re, object_im, probe_re, probe_im, frames, counts, offsets, frame_index):
    tile_r, tile_c = object_re.shape
    rows, width = tile_r + 2 * HALO, tile_c + 2 * LANES
    layers = 3
    slots = offsets.shape[2]
    table = jnp.asarray(transform_tables())
    frames = frames.reshape(frames.shape[2:])
    cells_shape, acc_shape = f32(2, rows, width), f32(layers, rows, width)
    dma = pltpu.SemaphoreType.DMA

    edge = f32(2, HALO, tile_c)
    to_inner, to_outer = pl.pallas_call(
        row_edges,
        out_shape=(edge, edge),
        in_specs=[HBM] * 2,
        out_specs=(VMEM, VMEM),
        scratch_shapes=[dma((4,))],
        compiler_params=ALONE,
        name="row_edges",
    )(object_re, object_im)
    by_inner, by_outer = swap(to_inner, to_outer, "row")

    cells, acc, *fixed = pl.pallas_call(
        load_state,
        out_shape=(
            cells_shape, acc_shape, f32(*probe_re.shape), f32(*probe_im.shape),
            jax.ShapeDtypeStruct(frames.shape, frames.dtype), jax.ShapeDtypeStruct(table.shape, table.dtype),
        ),
        in_specs=[SMEM] * 2 + [HBM] * 6,
        out_specs=(VMEM,) * 6,
        scratch_shapes=[pltpu.VMEM(probe_re.shape, jnp.float32), dma((6,))],
        compiler_params=PARAMS,
        cost_estimate=BUSY,
        name="load_state",
    )(counts, offsets, object_re, object_im, probe_re, probe_im, frames, table)

    strip = pltpu.VMEM((3 * rows, LANES), jnp.float32)
    packed = f32(3 * rows // GROUPS, LANES)
    cells, to_inner, to_outer = pl.pallas_call(
        row_halos,
        out_shape=(cells_shape, packed, packed),
        in_specs=[VMEM] * 4,
        out_specs=(VMEM,) * 3,
        scratch_shapes=[strip],
        input_output_aliases={0: 0},
        compiler_params=PARAMS,
        name="row_halos",
    )(cells, acc, by_inner, by_outer)
    by_inner, by_outer = swap(to_inner, to_outer, "col")

    order = pltpu.SMEM((slots,), jnp.int32)
    scalars = (counts, offsets, frame_index)
    acc = pl.pallas_call(
        windows_before,
        out_shape=acc_shape,
        in_specs=[SMEM] * 3 + [VMEM] * 6,
        out_specs=VMEM,
        scratch_shapes=[order],
        input_output_aliases={4: 0},
        compiler_params=PARAMS,
        cost_estimate=BUSY,
        name="windows_before",
    )(*scalars, cells, acc, *fixed)

    packed = f32(2 * rows // GROUPS, LANES)
    cells, acc, to_inner, to_outer = pl.pallas_call(
        windows_over_edge,
        out_shape=(cells_shape, acc_shape, packed, packed),
        in_specs=[SMEM] * 3 + [VMEM] * 8,
        out_specs=(VMEM,) * 4,
        scratch_shapes=[order, strip],
        input_output_aliases={3: 0, 4: 1},
        compiler_params=PARAMS,
        cost_estimate=BUSY,
        name="windows_over_edge",
    )(*scalars, cells, acc, *fixed, by_inner, by_outer)
    by_inner, by_outer = swap(to_inner, to_outer, "col")

    acc = pl.pallas_call(
        windows_after,
        out_shape=acc_shape,
        in_specs=[SMEM] * 3 + [VMEM] * 6,
        out_specs=VMEM,
        scratch_shapes=[order],
        input_output_aliases={4: 0},
        compiler_params=PARAMS,
        cost_estimate=BUSY,
        name="windows_after",
    )(*scalars, cells, acc, *fixed)

    edge = f32(layers, HALO, tile_c)
    acc, to_inner, to_outer = pl.pallas_call(
        row_spill,
        out_shape=(acc_shape, edge, edge),
        in_specs=[VMEM] * 3,
        out_specs=(VMEM,) * 3,
        input_output_aliases={0: 0},
        compiler_params=PARAMS,
        name="row_spill",
    )(acc, by_inner, by_outer)
    by_inner, by_outer = swap(to_inner, to_outer, "row")

    return pl.pallas_call(
        finish,
        out_shape=(f32(tile_r, tile_c), f32(tile_r, tile_c)),
        in_specs=[VMEM] * 4,
        out_specs=(VMEM, VMEM),
        compiler_params=PARAMS,
        name="finish",
    )(cells, acc, by_inner, by_outer)


def solution(mesh):
    return jax.shard_map(
        shards,
        mesh=mesh,
        in_specs=(
            P("row", "col"),
            P("row", "col"),
            P(),
            P(),
            P("row", "col", None, None, None),
            P("row", "col"),
            P("row", "col", None, None),
            P("row", "col", None),
        ),
        out_specs=(P("row", "col"), P("row", "col")),
        check_vma=False,
    )
```

```python
import functools
import math

import jax
import jax.numpy as jnp
import ml_dtypes
import numpy as np
from jax import lax
from jax.experimental import pallas as pl
from jax.experimental.pallas import tpu as pltpu
from jax.sharding import PartitionSpec as P

P_SIZE = 256
HALF = P_SIZE // 2
HALO = 32
LANES = 128
GROUPS = LANES // HALO
PAIR = 2

floor_amp = 0.5
ridge = 1.0

VMEM = pl.BlockSpec(memory_space=pltpu.VMEM)
SMEM = pl.BlockSpec(memory_space=pltpu.SMEM)
HBM = pl.BlockSpec(memory_space=pltpu.HBM)
PARAMS = pltpu.CompilerParams(vmem_limit_bytes=40 * 1024 * 1024)
BUSY = pl.CostEstimate(flops=4_000_000_000, bytes_accessed=8_000_000, transcendentals=0)


def transform_tables():
    index = np.arange(HALF)
    plain = []
    for parity in (0, 1):
        angle = 2.0 * math.pi / P_SIZE * (index[:, None] * (2 * index[None, :] + parity) % P_SIZE)
        cos, sin = np.cos(angle), np.sin(angle)
        plain.append(np.block([[cos, -sin], [sin, cos]]) / math.sqrt(P_SIZE))
    parts = []
    for table in plain + [t.T for t in plain]:
        high = table.astype(np.float32).astype(ml_dtypes.bfloat16)
        low = (table - high.astype(np.float64)).astype(np.float32).astype(ml_dtypes.bfloat16)
        parts += [high, low]
    order = np.concatenate([np.arange(0, P_SIZE, 2), np.arange(1, P_SIZE, 2)])
    sort = np.zeros((P_SIZE, P_SIZE), np.float32)
    sort[np.arange(P_SIZE), order] = 1.0
    parts += [sort.astype(ml_dtypes.bfloat16), sort.T.astype(ml_dtypes.bfloat16)]
    return np.stack(parts)


def lane_index(rows):
    return lax.broadcasted_iota(jnp.int32, (rows, LANES), 1)


def pack_lanes(ref, rows, first):
    lane = lane_index(rows)
    packed = None
    for g in range(GROUPS):
        part = ref[g * rows : (g + 1) * rows, :]
        if g:
            part = pltpu.roll(part, HALO * g, 1)
        low = (first + HALO * g) % LANES
        mine = (lane >= low) & (lane < low + HALO)
        packed = part if packed is None else jnp.where(mine, part, packed)
    return packed


def unpack_lanes(packed, group):
    return pltpu.roll(packed, LANES - HALO * group, 1) if group else packed


def split(x):
    high = x.astype(jnp.bfloat16)
    return high, (x - high.astype(jnp.float32)).astype(jnp.bfloat16)


def product(left, right):
    return jnp.dot(left, right, preferred_element_type=jnp.float32)


def times_table(x, table, which):
    high, low = split(x)
    t_high, t_low = table[2 * which], table[2 * which + 1]
    return product(high, t_high) + (product(high, t_low) + product(low, t_high))


def table_times(table, which, x):
    high, low = split(x)
    t_high, t_low = table[2 * which], table[2 * which + 1]
    return product(t_high, high) + (product(t_low, high) + product(t_high, low))


def beside(*blocks):
    return jnp.concatenate(blocks, axis=1)


def below(*blocks):
    return jnp.concatenate(blocks, axis=0)


def ends(x):
    return x[:, :HALF], x[:, HALF:]


def forward_columns(exit_re, exit_im, table):
    re_lo, re_hi = ends(exit_re)
    im_lo, im_hi = ends(exit_im)
    even = times_table(beside(re_lo + re_hi, im_lo + im_hi), table, 0)
    odd = times_table(beside(re_lo - re_hi, im_lo - im_hi), table, 1)
    return even, odd


def forward_rows(even, odd, table):
    out = []
    for parity in (0, 1):
        if parity == 0:
            se, so = even[:HALF] + even[HALF:], odd[:HALF] + odd[HALF:]
        else:
            se, so = even[:HALF] - even[HALF:], odd[:HALF] - odd[HALF:]
        e_re, e_im = ends(se)
        o_re, o_im = ends(so)
        out.append(table_times(table, 2 + parity, below(beside(e_re, o_re), beside(e_im, o_im))))
    return out


def residual(far, frame):
    out = []
    for parity in (0, 1):
        re, im = far[parity][:HALF], far[parity][HALF:]
        level = jnp.maximum(re * re + im * im, floor_amp * floor_amp)
        inten = frame[parity * HALF : (parity + 1) * HALF]
        factor = 1.0 - inten * lax.rsqrt(inten * level)
        out.append(below(re * factor, im * factor))
    return out


def back_rows(res, table):
    first = table_times(table, 0, res[0])
    second = table_times(table, 1, res[1])
    upper, lower = first + second, first - second
    out = []
    for cols in (slice(0, HALF), slice(HALF, P_SIZE)):
        out.append(
            below(
                beside(upper[:HALF, cols], upper[HALF:, cols]),
                beside(lower[:HALF, cols], lower[HALF:, cols]),
            )
        )
    return out


def back_columns(parts, table):
    even = times_table(parts[0], table, 2)
    odd = times_table(parts[1], table, 3)
    lo, hi = even + odd, even - odd
    return beside(lo[:, :HALF], hi[:, :HALF]), beside(lo[:, HALF:], hi[:, HALF:])


def is_odd(axis):
    return lax.rem(lax.axis_index(axis), 2) == 1


def fetch(pairs, sems):
    copies = [pltpu.make_async_copy(far, near, sems.at[i]) for i, (far, near) in enumerate(pairs)]
    for copy in copies:
        copy.start()
    return copies


def finish_all(copies):
    for copy in copies:
        copy.wait()


def row_edges(obj_re, obj_im, to_inner, to_outer, sems):
    tile_r = obj_re.shape[0]
    odd = is_odd("row")
    low = pl.multiple_of(jnp.where(odd, 0, tile_r - HALO), 16)
    high = pl.multiple_of(jnp.where(odd, tile_r - HALO, 0), 16)
    pairs = []
    for k, ref in enumerate((obj_re, obj_im)):
        pairs.append((ref.at[pl.ds(high, HALO)], to_outer.at[k]))
        pairs.append((ref.at[pl.ds(low, HALO)], to_inner.at[k]))
    finish_all(fetch(pairs, sems))


def window_place(offsets, slot):
    row = pl.multiple_of(offsets[0, 0, slot, 0] + HALO, 16)
    col = offsets[0, 0, slot, 1] + LANES
    turn = lax.rem(col, LANES)
    return row, pl.multiple_of(col - turn, LANES), turn


def add_window(acc, layer, where, keep, term):
    row, base, _ = where
    lo, hi = ends(term)
    for t, part in enumerate((jnp.where(keep, lo, 0.0), hi, jnp.where(keep, 0.0, lo))):
        acc[layer, pl.ds(row, P_SIZE), pl.ds(base + t * LANES, LANES)] += part


def load_state(
    obj_re, obj_im, probe_re_far, probe_im_far, frames_far, table_far,
    cells, probe_re, probe_im, frames, table, sems,
):
    tile_r, tile_c = obj_re.shape
    inner = slice(HALO, HALO + tile_r)
    middle = slice(LANES, LANES + tile_c)
    copies = fetch(
        (
            (probe_re_far, probe_re),
            (probe_im_far, probe_im),
            (obj_re, cells.at[0, inner, middle]),
            (obj_im, cells.at[1, inner, middle]),
            (table_far, table),
            (frames_far, frames),
        ),
        sems,
    )
    finish_all(copies)


def fill_strip(strip, parts):
    done = 0
    for part in parts:
        strip[done : done + part.shape[0], :] = part
        done += part.shape[0]


def send_columns(to_left, to_right, to_inner, to_outer):
    odd = is_odd("col")
    to_inner[...] = jnp.where(odd, to_left, to_right)
    to_outer[...] = jnp.where(odd, to_right, to_left)


def received(by_inner, by_outer, axis):
    odd = is_odd(axis)
    if len(by_inner.shape) > len(by_outer.shape):
        before, after = by_inner[0], by_inner[1]
    else:
        before = after = by_inner[...]
    return jnp.where(odd, before, by_outer[...]), jnp.where(odd, by_outer[...], after)


def pieces(packed, layers, rows):
    group_rows = layers * rows // GROUPS
    for g in range(GROUPS):
        part = unpack_lanes(packed, g)
        done = 0
        while done < group_rows:
            layer, row = divmod(g * group_rows + done, rows)
            size = min(group_rows - done, rows - row)
            yield layer, row, part[done : done + size]
            done += size


def row_halos(cells_in, by_inner, by_outer, cells, to_inner, to_outer, strip):
    rows, width = cells.shape[1:]
    middle = slice(LANES, width - LANES)
    before, after = received(by_inner, by_outer, "row")
    for k in (0, 1):
        cells[k, 0:HALO, middle] = before[k]
        cells[k, rows - HALO : rows, middle] = after[k]
    group_rows = 2 * rows // GROUPS
    first, last = slice(LANES, 2 * LANES), slice(width - 2 * LANES, width - LANES)
    fill_strip(strip, (cells[0, :, first], cells[1, :, first]))
    to_left = pack_lanes(strip, group_rows, 0)
    fill_strip(strip, (cells[0, :, last], cells[1, :, last]))
    to_right = pack_lanes(strip, group_rows, LANES - HALO)
    send_columns(to_left, to_right, to_inner, to_outer)


def run_windows(wanted, counts, offsets, chosen, cells, acc, probe_re, probe_im, frames, table, order):
    tile_c = cells.shape[2] - 2 * LANES
    count = counts[0, 0]
    slots = range(offsets.shape[2])
    over = []
    for slot in slots:
        col = offsets[0, 0, slot, 1]
        over.append((col < 0) | (col > tile_c - P_SIZE))
    total = jnp.int32(0)
    for slot in slots:
        total += ((slot < count) & ~over[slot]).astype(jnp.int32)
    limit = jnp.where(total <= PAIR, total, jnp.where(total <= 2 * PAIR, PAIR, 2 * PAIR))
    seen, found = jnp.int32(0), jnp.int32(0)
    for slot in slots:
        live = slot < count
        mine = live & wanted(over[slot], seen, limit)

        @pl.when(mine)
        def _():
            order[found] = slot

        seen += (live & ~over[slot]).astype(jnp.int32)
        found += mine.astype(jnp.int32)

    lane = lane_index(P_SIZE)

    def load(slot):
        where = row, base, turn = window_place(offsets, slot)
        keep = lane >= turn
        w_re = pltpu.roll(probe_re[...], turn, 1)
        w_im = pltpu.roll(probe_im[...], turn, 1)
        patch = []
        for k in (0, 1):
            block = cells[k, pl.ds(row, P_SIZE), pl.ds(base, 3 * LANES)]
            patch.append(
                beside(jnp.where(keep, block[:, :LANES], block[:, 2 * LANES :]), block[:, LANES : 2 * LANES])
            )
        exit_re = w_re * patch[0] - w_im * patch[1]
        exit_im = w_re * patch[1] + w_im * patch[0]
        return (where, keep, w_re, w_im), exit_re, exit_im

    def frame_of(slot):
        sort, unsort = table[8], table[9]
        half = product(sort, frames[chosen[0, 0, slot]]).astype(jnp.bfloat16)
        return product(half, unsort)

    def place(at, back_re, back_im):
        where, keep, w_re, w_im = at
        add_window(acc, 0, where, keep, w_re * back_re + w_im * back_im)
        add_window(acc, 1, where, keep, w_re * back_im - w_im * back_re)

    def step(group):
        frame = [frame_of(slot) for slot in group]
        loaded = [load(slot) for slot in group]
        state = [forward_columns(x[1], x[2], table) for x in loaded]
        state = [forward_rows(*x, table) for x in state]
        state = [residual(x, f) for x, f in zip(state, frame)]
        state = [back_rows(x, table) for x in state]
        state = [back_columns(x, table) for x in state]
        for x, back in zip(loaded, state):
            place(x[0], *back)

    def pair_step(pair, carry):
        step([order[pair * PAIR + i] for i in range(PAIR)])
        return carry

    lax.fori_loop(0, found // PAIR, pair_step, 0)

    @pl.when(found % PAIR == 1)
    def _():
        step([order[found - 1]])


def windows_before(counts, offsets, chosen, cells, probe_re, probe_im, frames, table, acc, order, power):
    acc[...] = jnp.zeros_like(acc)
    power[...] = probe_re[...] * probe_re[...] + probe_im[...] * probe_im[...]
    lane = lane_index(P_SIZE)

    def step(slot, carry):
        where = window_place(offsets, slot)
        add_window(acc, 2, where, lane >= where[2], pltpu.roll(power[...], where[2], 1))
        return carry

    lax.fori_loop(0, counts[0, 0], step, 0)
    run_windows(
        lambda over, seen, limit: ~over & (seen < limit),
        counts, offsets, chosen, cells, acc, probe_re, probe_im, frames, table, order,
    )


def windows_after(counts, offsets, chosen, cells, acc_in, probe_re, probe_im, frames, table, acc, order):
    run_windows(
        lambda over, seen, limit: ~over & (seen >= limit),
        counts, offsets, chosen, cells, acc, probe_re, probe_im, frames, table, order,
    )


def windows_over_edge(
    counts, offsets, chosen, cells_in, acc_in, probe_re, probe_im, frames, table, by_inner, by_outer,
    cells, acc, to_inner, to_outer, order, strip,
):
    rows, width = acc.shape[1:]
    before, after = received(by_inner, by_outer, "col")
    for layer, row, part in pieces(before, 2, rows):
        cells[layer, row : row + part.shape[0], 0:LANES] = part
    for layer, row, part in pieces(after, 2, rows):
        cells[layer, row : row + part.shape[0], width - LANES :] = part
    run_windows(
        lambda over, seen, limit: over,
        counts, offsets, chosen, cells, acc, probe_re, probe_im, frames, table, order,
    )
    layers = acc.shape[0]
    group_rows = layers * rows // GROUPS
    fill_strip(strip, [acc[k, :, 0:LANES] for k in range(layers)])
    to_left = pack_lanes(strip, group_rows, LANES - HALO)
    fill_strip(strip, [acc[k, :, width - LANES :] for k in range(layers)])
    to_right = pack_lanes(strip, group_rows, 0)
    send_columns(to_left, to_right, to_inner, to_outer)


def row_spill(acc_in, by_inner, by_outer, acc, to_inner, to_outer):
    layers, rows, width = acc.shape
    before, after = received(by_inner, by_outer, "col")
    lane = lane_index(rows)[0:1]
    for layer, row, part in pieces(before, layers, rows):
        here = slice(row, row + part.shape[0])
        acc[layer, here, LANES : 2 * LANES] += jnp.where(lane < HALO, part, 0.0)
    for layer, row, part in pieces(after, layers, rows):
        here = slice(row, row + part.shape[0])
        acc[layer, here, width - 2 * LANES : width - LANES] += jnp.where(lane >= LANES - HALO, part, 0.0)
    odd = is_odd("row")
    for k in range(layers):
        up = acc[k, 0:HALO, LANES : width - LANES]
        down = acc[k, rows - HALO : rows, LANES : width - LANES]
        to_inner[k] = jnp.where(odd, up, down)
        to_outer[k] = jnp.where(odd, down, up)


def finish(cells, acc, by_inner, by_outer, new_re, new_im):
    layers, rows, width = acc.shape
    tile_r = rows - 2 * HALO
    middle = slice(LANES, width - LANES)
    before, after = received(by_inner, by_outer, "row")
    for start, size, extra in (
        (0, HALO, before),
        (HALO, tile_r - 2 * HALO, None),
        (tile_r - HALO, HALO, after),
    ):
        here = slice(HALO + start, HALO + start + size)
        part = [acc[k, here, middle] for k in range(layers)]
        if extra is not None:
            part = [part[k] + extra[k] for k in range(layers)]
        scale = 1.0 / (part[2] + ridge)
        new_re[start : start + size, :] = cells[0, here, middle] - part[0] * scale
        new_im[start : start + size, :] = cells[1, here, middle] - part[1] * scale


def swap(to_inner, to_outer, axis, gather):
    devices = lax.axis_size(axis)
    inner = [(i, i + 1) for i in range(0, devices, 2)]
    outer = [(i, i + 1) for i in range(1, devices - 1, 2)]
    by_outer = lax.ppermute(to_outer, axis, outer + [(j, i) for i, j in outer])
    if gather:
        by_inner = lax.all_gather(to_inner, axis, axis_index_groups=[list(pair) for pair in inner])
    else:
        by_inner = lax.ppermute(to_inner, axis, inner + [(j, i) for i, j in inner])
    return by_inner, by_outer


def far(x):
    return pltpu.with_memory_space_constraint(x, pltpu.HBM)


def f32(*shape):
    return jax.ShapeDtypeStruct(shape, jnp.float32)


def shards(object_re, object_im, probe_re, probe_im, frames, counts, offsets, frame_index):
    tile_r, tile_c = object_re.shape
    rows, width = tile_r + 2 * HALO, tile_c + 2 * LANES
    layers = 3
    slots = offsets.shape[2]
    table = jnp.asarray(transform_tables())
    frames = frames.reshape(frames.shape[2:])
    cells_shape, acc_shape = f32(2, rows, width), f32(layers, rows, width)
    dma = pltpu.SemaphoreType.DMA

    edge = f32(2, HALO, tile_c)
    to_inner, to_outer = pl.pallas_call(
        row_edges,
        out_shape=(edge, edge),
        in_specs=[HBM] * 2,
        out_specs=(HBM, VMEM),
        scratch_shapes=[dma((4,))],
        compiler_params=PARAMS,
        name="row_edges",
    )(far(object_re), far(object_im))
    by_inner, by_outer = swap(to_inner, to_outer, "row", True)

    cells, *fixed = pl.pallas_call(
        load_state,
        out_shape=(
            cells_shape, f32(*probe_re.shape), f32(*probe_im.shape),
            jax.ShapeDtypeStruct(frames.shape, frames.dtype), jax.ShapeDtypeStruct(table.shape, table.dtype),
        ),
        in_specs=[HBM] * 6,
        out_specs=(VMEM,) * 5,
        scratch_shapes=[dma((6,))],
        compiler_params=PARAMS,
        cost_estimate=BUSY,
        name="load_state",
    )(*map(far, (object_re, object_im, probe_re, probe_im, frames, table)))

    strip = pltpu.VMEM((layers * rows, LANES), jnp.float32)
    packed = f32(2 * rows // GROUPS, LANES)
    cells, to_inner, to_outer = pl.pallas_call(
        row_halos,
        out_shape=(cells_shape, packed, packed),
        in_specs=[VMEM] * 3,
        out_specs=(VMEM,) * 3,
        scratch_shapes=[strip],
        input_output_aliases={0: 0},
        compiler_params=PARAMS,
        name="row_halos",
    )(cells, by_inner, by_outer)
    by_inner, by_outer = swap(to_inner, to_outer, "col", False)

    order = pltpu.SMEM((slots,), jnp.int32)
    scalars = (counts, offsets, frame_index)
    acc = pl.pallas_call(
        windows_before,
        out_shape=acc_shape,
        in_specs=[SMEM] * 3 + [VMEM] * 5,
        out_specs=VMEM,
        scratch_shapes=[order, pltpu.VMEM(probe_re.shape, jnp.float32)],
        compiler_params=PARAMS,
        cost_estimate=BUSY,
        name="windows_before",
    )(*scalars, cells, *fixed)

    packed = f32(layers * rows // GROUPS, LANES)
    cells, acc, to_inner, to_outer = pl.pallas_call(
        windows_over_edge,
        out_shape=(cells_shape, acc_shape, packed, packed),
        in_specs=[SMEM] * 3 + [VMEM] * 8,
        out_specs=(VMEM,) * 4,
        scratch_shapes=[order, strip],
        input_output_aliases={3: 0, 4: 1},
        compiler_params=PARAMS,
        cost_estimate=BUSY,
        name="windows_over_edge",
    )(*scalars, cells, acc, *fixed, by_inner, by_outer)
    by_inner, by_outer = swap(to_inner, to_outer, "col", False)

    acc = pl.pallas_call(
        windows_after,
        out_shape=acc_shape,
        in_specs=[SMEM] * 3 + [VMEM] * 6,
        out_specs=VMEM,
        scratch_shapes=[order],
        input_output_aliases={4: 0},
        compiler_params=PARAMS,
        cost_estimate=BUSY,
        name="windows_after",
    )(*scalars, cells, acc, *fixed)

    edge = f32(layers, HALO, tile_c)
    acc, to_inner, to_outer = pl.pallas_call(
        row_spill,
        out_shape=(acc_shape, edge, edge),
        in_specs=[VMEM] * 3,
        out_specs=(VMEM,) * 3,
        input_output_aliases={0: 0},
        compiler_params=PARAMS,
        name="row_spill",
    )(acc, by_inner, by_outer)
    by_inner, by_outer = swap(to_inner, to_outer, "row", True)

    return pl.pallas_call(
        finish,
        out_shape=(f32(tile_r, tile_c), f32(tile_r, tile_c)),
        in_specs=[VMEM] * 4,
        out_specs=(VMEM, VMEM),
        compiler_params=PARAMS,
        name="finish",
    )(cells, acc, by_inner, by_outer)


def solution(mesh):
    return jax.shard_map(
        shards,
        mesh=mesh,
        in_specs=(
            P("row", "col"),
            P("row", "col"),
            P(),
            P(),
            P("row", "col", None, None, None),
            P("row", "col"),
            P("row", "col", None, None),
            P("row", "col", None),
        ),
        out_specs=(P("row", "col"), P("row", "col")),
        check_vma=False,
    )
```

```python
import functools
import math

import jax
import jax.numpy as jnp
import ml_dtypes
import numpy as np
from jax import lax
from jax.experimental import pallas as pl
from jax.experimental.pallas import tpu as pltpu
from jax.sharding import PartitionSpec as P

P_SIZE = 256
HALF = P_SIZE // 2
HALO = 32
LANES = 128
GROUPS = LANES // HALO
PAIR = 2

floor_amp = 0.5
ridge = 1.0

VMEM = pl.BlockSpec(memory_space=pltpu.VMEM)
SMEM = pl.BlockSpec(memory_space=pltpu.SMEM)
HBM = pl.BlockSpec(memory_space=pltpu.HBM)
PARAMS = pltpu.CompilerParams(vmem_limit_bytes=32 * 1024 * 1024)
SMALL = pltpu.CompilerParams(vmem_limit_bytes=16 * 1024 * 1024)
BUSY = pl.CostEstimate(flops=4_000_000_000, bytes_accessed=8_000_000, transcendentals=0)


def transform_tables():
    index = np.arange(HALF)
    plain = []
    for parity in (0, 1):
        angle = 2.0 * math.pi / P_SIZE * (index[:, None] * (2 * index[None, :] + parity) % P_SIZE)
        cos, sin = np.cos(angle), np.sin(angle)
        plain.append(np.block([[cos, -sin], [sin, cos]]) / math.sqrt(P_SIZE))
    parts = []
    for table in plain + [t.T for t in plain]:
        high = table.astype(np.float32).astype(ml_dtypes.bfloat16)
        low = (table - high.astype(np.float64)).astype(np.float32).astype(ml_dtypes.bfloat16)
        parts += [high, low]
    order = np.concatenate([np.arange(0, P_SIZE, 2), np.arange(1, P_SIZE, 2)])
    sort = np.zeros((P_SIZE, P_SIZE), np.float32)
    sort[np.arange(P_SIZE), order] = 1.0
    parts += [sort.astype(ml_dtypes.bfloat16), sort.T.astype(ml_dtypes.bfloat16)]
    return np.stack(parts)


def lane_index(rows):
    return lax.broadcasted_iota(jnp.int32, (rows, LANES), 1)


def pack_lanes(ref, rows, first):
    lane = lane_index(rows)
    packed = None
    for g in range(GROUPS):
        part = ref[g * rows : (g + 1) * rows, :]
        if g:
            part = pltpu.roll(part, HALO * g, 1)
        low = (first + HALO * g) % LANES
        mine = (lane >= low) & (lane < low + HALO)
        packed = part if packed is None else jnp.where(mine, part, packed)
    return packed


def unpack_lanes(packed, group):
    return pltpu.roll(packed, LANES - HALO * group, 1) if group else packed


def split(x):
    high = x.astype(jnp.bfloat16)
    return high, (x - high.astype(jnp.float32)).astype(jnp.bfloat16)


def product(left, right):
    return jnp.dot(left, right, preferred_element_type=jnp.float32)


def times_table(x, table, which):
    high, low = split(x)
    t_high, t_low = table[2 * which], table[2 * which + 1]
    return product(high, t_high) + (product(high, t_low) + product(low, t_high))


def table_times(table, which, x):
    high, low = split(x)
    t_high, t_low = table[2 * which], table[2 * which + 1]
    return product(t_high, high) + (product(t_low, high) + product(t_high, low))


def beside(*blocks):
    return jnp.concatenate(blocks, axis=1)


def below(*blocks):
    return jnp.concatenate(blocks, axis=0)


def ends(x):
    return x[:, :HALF], x[:, HALF:]


def forward_columns(exit_re, exit_im, table):
    re_lo, re_hi = ends(exit_re)
    im_lo, im_hi = ends(exit_im)
    even = times_table(beside(re_lo + re_hi, im_lo + im_hi), table, 0)
    odd = times_table(beside(re_lo - re_hi, im_lo - im_hi), table, 1)
    return even, odd


def forward_rows(even, odd, table):
    out = []
    for parity in (0, 1):
        if parity == 0:
            se, so = even[:HALF] + even[HALF:], odd[:HALF] + odd[HALF:]
        else:
            se, so = even[:HALF] - even[HALF:], odd[:HALF] - odd[HALF:]
        e_re, e_im = ends(se)
        o_re, o_im = ends(so)
        out.append(table_times(table, 2 + parity, below(beside(e_re, o_re), beside(e_im, o_im))))
    return out


def residual(far, frame):
    out = []
    for parity in (0, 1):
        re, im = far[parity][:HALF], far[parity][HALF:]
        level = jnp.maximum(re * re + im * im, floor_amp * floor_amp)
        inten = frame[parity * HALF : (parity + 1) * HALF]
        factor = 1.0 - inten * lax.rsqrt(inten * level)
        out.append(below(re * factor, im * factor))
    return out


def back_rows(res, table):
    first = table_times(table, 0, res[0])
    second = table_times(table, 1, res[1])
    upper, lower = first + second, first - second
    out = []
    for cols in (slice(0, HALF), slice(HALF, P_SIZE)):
        out.append(
            below(
                beside(upper[:HALF, cols], upper[HALF:, cols]),
                beside(lower[:HALF, cols], lower[HALF:, cols]),
            )
        )
    return out


def back_columns(parts, table):
    even = times_table(parts[0], table, 2)
    odd = times_table(parts[1], table, 3)
    lo, hi = even + odd, even - odd
    return beside(lo[:, :HALF], hi[:, :HALF]), beside(lo[:, HALF:], hi[:, HALF:])


def is_odd(axis):
    return lax.rem(lax.axis_index(axis), 2) == 1


def fetch(pairs, sems):
    copies = [pltpu.make_async_copy(far, near, sems.at[i]) for i, (far, near) in enumerate(pairs)]
    for copy in copies:
        copy.start()
    return copies


def finish_all(copies):
    for copy in copies:
        copy.wait()


def row_edges(obj_re, obj_im, to_inner, to_outer, sems):
    tile_r = obj_re.shape[0]
    odd = is_odd("row")
    low = pl.multiple_of(jnp.where(odd, 0, tile_r - HALO), 16)
    high = pl.multiple_of(jnp.where(odd, tile_r - HALO, 0), 16)
    pairs = []
    for k, ref in enumerate((obj_re, obj_im)):
        pairs.append((ref.at[pl.ds(high, HALO)], to_outer.at[k]))
        pairs.append((ref.at[pl.ds(low, HALO)], to_inner.at[k]))
    finish_all(fetch(pairs, sems))


def window_place(offsets, slot):
    row = pl.multiple_of(offsets[0, 0, 0, slot] + HALO, 16)
    col = offsets[0, 0, 1, slot] + LANES
    turn = lax.rem(col, LANES)
    return row, pl.multiple_of(col - turn, LANES), turn


def add_window(acc, layer, where, keep, term):
    row, base, _ = where
    lo, hi = ends(term)
    for t, part in enumerate((jnp.where(keep, lo, 0.0), hi, jnp.where(keep, 0.0, lo))):
        acc[layer, pl.ds(row, P_SIZE), pl.ds(base + t * LANES, LANES)] += part


def load_object(obj_re, obj_im, cells, sems):
    tile_r, tile_c = obj_re.shape
    inner = slice(HALO, HALO + tile_r)
    middle = slice(LANES, LANES + tile_c)
    finish_all(fetch([(ref, cells.at[k, inner, middle]) for k, ref in enumerate((obj_re, obj_im))], sems))


def fill_strip(strip, parts):
    done = 0
    for part in parts:
        strip[done : done + part.shape[0], :] = part
        done += part.shape[0]


def send_columns(to_left, to_right, to_inner, to_outer):
    odd = is_odd("col")
    to_inner[...] = jnp.where(odd, to_left, to_right)
    to_outer[...] = jnp.where(odd, to_right, to_left)


def received(by_inner, by_outer, axis):
    odd = is_odd(axis)
    if len(by_inner.shape) > len(by_outer.shape):
        before, after = by_inner[0], by_inner[1]
    else:
        before = after = by_inner[...]
    return jnp.where(odd, before, by_outer[...]), jnp.where(odd, by_outer[...], after)


def pieces(packed, layers, rows):
    group_rows = layers * rows // GROUPS
    for g in range(GROUPS):
        part = unpack_lanes(packed, g)
        done = 0
        while done < group_rows:
            layer, row = divmod(g * group_rows + done, rows)
            size = min(group_rows - done, rows - row)
            yield layer, row, part[done : done + size]
            done += size


def row_halos(cells_in, by_inner, by_outer, cells, to_inner, to_outer, strip):
    rows, width = cells.shape[1:]
    middle = slice(LANES, width - LANES)
    before, after = received(by_inner, by_outer, "row")
    for k in (0, 1):
        cells[k, 0:HALO, middle] = before[k]
        cells[k, rows - HALO : rows, middle] = after[k]
    group_rows = 2 * rows // GROUPS
    first, last = slice(LANES, 2 * LANES), slice(width - 2 * LANES, width - LANES)
    fill_strip(strip, (cells[0, :, first], cells[1, :, first]))
    to_left = pack_lanes(strip, group_rows, 0)
    fill_strip(strip, (cells[0, :, last], cells[1, :, last]))
    to_right = pack_lanes(strip, group_rows, LANES - HALO)
    send_columns(to_left, to_right, to_inner, to_outer)


def run_windows(wanted, counts, offsets, chosen, cells, acc, probe_re, probe_im, table, frames, order):
    tile_c = cells.shape[2] - 2 * LANES
    count = counts[0, 0]
    slots = range(offsets.shape[3])
    over = []
    for slot in slots:
        col = offsets[0, 0, 1, slot]
        over.append((col < 0) | (col > tile_c - P_SIZE))
    total = jnp.int32(0)
    for slot in slots:
        total += ((slot < count) & ~over[slot]).astype(jnp.int32)
    limit = jnp.where(total < len(slots) - 1, PAIR, 2 * PAIR)
    seen, found = jnp.int32(0), jnp.int32(0)
    for slot in slots:
        live = slot < count
        mine = live & wanted(over[slot], seen, limit)

        @pl.when(mine)
        def _():
            order[found] = slot

        seen += (live & ~over[slot]).astype(jnp.int32)
        found += mine.astype(jnp.int32)

    lane = lane_index(P_SIZE)

    def load(slot):
        where = row, base, turn = window_place(offsets, slot)
        keep = lane >= turn
        w_re = pltpu.roll(probe_re[...], turn, 1)
        w_im = pltpu.roll(probe_im[...], turn, 1)
        patch = []
        for k in (0, 1):
            block = cells[k, pl.ds(row, P_SIZE), pl.ds(base, 3 * LANES)]
            patch.append(
                beside(jnp.where(keep, block[:, :LANES], block[:, 2 * LANES :]), block[:, LANES : 2 * LANES])
            )
        exit_re = w_re * patch[0] - w_im * patch[1]
        exit_im = w_re * patch[1] + w_im * patch[0]
        return (where, keep, w_re, w_im), exit_re, exit_im

    def frame_of(slot):
        sort, unsort = table[8], table[9]
        half = product(sort, frames[chosen[0, 0, slot]]).astype(jnp.bfloat16)
        return product(half, unsort)

    def place(at, back_re, back_im):
        where, keep, w_re, w_im = at
        add_window(acc, 0, where, keep, w_re * back_re + w_im * back_im)
        add_window(acc, 1, where, keep, w_re * back_im - w_im * back_re)

    def step(group):
        frame = [frame_of(slot) for slot in group]
        loaded = [load(slot) for slot in group]
        state = [forward_columns(x[1], x[2], table) for x in loaded]
        state = [forward_rows(*x, table) for x in state]
        state = [residual(x, f) for x, f in zip(state, frame)]
        state = [back_rows(x, table) for x in state]
        state = [back_columns(x, table) for x in state]
        for x, back in zip(loaded, state):
            place(x[0], *back)

    def pair_step(pair, carry):
        step([order[pair * PAIR + i] for i in range(PAIR)])
        return carry

    lax.fori_loop(0, found // PAIR, pair_step, 0)

    @pl.when(found % PAIR == 1)
    def _():
        step([order[found - 1]])


def windows_before(
    counts, offsets, chosen, cells, probe_re_far, probe_im_far, table_far, frames_far,
    acc, probe_re, probe_im, table, frames, order, power, sems,
):
    far_near = ((probe_re_far, probe_re), (probe_im_far, probe_im), (table_far, table), (frames_far, frames))
    copies = fetch(far_near, sems)
    acc[...] = jnp.zeros_like(acc)
    finish_all(copies[:2])
    power[...] = probe_re[...] * probe_re[...] + probe_im[...] * probe_im[...]
    lane = lane_index(P_SIZE)

    def step(slot, carry):
        where = window_place(offsets, slot)
        add_window(acc, 2, where, lane >= where[2], pltpu.roll(power[...], where[2], 1))
        return carry

    lax.fori_loop(0, counts[0, 0], step, 0)
    finish_all(copies[2:])
    run_windows(
        lambda over, seen, limit: ~over & (seen < limit),
        counts, offsets, chosen, cells, acc, probe_re, probe_im, table, frames, order,
    )


def windows_after(counts, offsets, chosen, cells, acc_in, probe_re, probe_im, table, frames, acc, order):
    run_windows(
        lambda over, seen, limit: ~over & (seen >= limit),
        counts, offsets, chosen, cells, acc, probe_re, probe_im, table, frames, order,
    )


def windows_over_edge(
    counts, offsets, chosen, cells_in, acc_in, probe_re, probe_im, table, frames, by_inner, by_outer,
    cells, acc, to_inner, to_outer, order, strip,
):
    rows, width = acc.shape[1:]
    before, after = received(by_inner, by_outer, "col")
    for layer, row, part in pieces(before, 2, rows):
        cells[layer, row : row + part.shape[0], 0:LANES] = part
    for layer, row, part in pieces(after, 2, rows):
        cells[layer, row : row + part.shape[0], width - LANES :] = part
    run_windows(
        lambda over, seen, limit: over,
        counts, offsets, chosen, cells, acc, probe_re, probe_im, table, frames, order,
    )
    layers = acc.shape[0]
    group_rows = layers * rows // GROUPS
    fill_strip(strip, [acc[k, :, 0:LANES] for k in range(layers)])
    to_left = pack_lanes(strip, group_rows, LANES - HALO)
    fill_strip(strip, [acc[k, :, width - LANES :] for k in range(layers)])
    to_right = pack_lanes(strip, group_rows, 0)
    send_columns(to_left, to_right, to_inner, to_outer)


def row_spill(acc_in, by_inner, by_outer, acc, to_inner, to_outer):
    layers, rows, width = acc.shape
    before, after = received(by_inner, by_outer, "col")
    lane = lane_index(rows)[0:1]
    for layer, row, part in pieces(before, layers, rows):
        here = slice(row, row + part.shape[0])
        acc[layer, here, LANES : 2 * LANES] += jnp.where(lane < HALO, part, 0.0)
    for layer, row, part in pieces(after, layers, rows):
        here = slice(row, row + part.shape[0])
        acc[layer, here, width - 2 * LANES : width - LANES] += jnp.where(lane >= LANES - HALO, part, 0.0)
    odd = is_odd("row")
    for k in range(layers):
        up = acc[k, 0:HALO, LANES : width - LANES]
        down = acc[k, rows - HALO : rows, LANES : width - LANES]
        to_inner[k] = jnp.where(odd, up, down)
        to_outer[k] = jnp.where(odd, down, up)


def new_rows(cells, acc, extra, start, size, new_re, new_im):
    here = slice(HALO + start, HALO + start + size)
    middle = slice(LANES, acc.shape[2] - LANES)
    part = [acc[k, here, middle] for k in range(acc.shape[0])]
    if extra is not None:
        part = [part[k] + extra[k] for k in range(acc.shape[0])]
    scale = 1.0 / (part[2] + ridge)
    new_re[start : start + size, :] = cells[0, here, middle] - part[0] * scale
    new_im[start : start + size, :] = cells[1, here, middle] - part[1] * scale


def finish_inner(cells, acc, new_re, new_im, near_re, near_im, sems):
    tile_r = near_re.shape[0]
    new_rows(cells, acc, None, HALO, tile_r - 2 * HALO, near_re, near_im)
    rows = slice(HALO, tile_r - HALO)
    finish_all(fetch([(near_re.at[rows], new_re.at[rows]), (near_im.at[rows], new_im.at[rows])], sems))


def finish_edges(cells, acc, by_inner, by_outer, re_in, im_in, new_re, new_im, near_re, near_im, sems):
    tile_r = near_re.shape[0]
    copies = []
    for i, (start, extra) in enumerate(zip((0, tile_r - HALO), received(by_inner, by_outer, "row"))):
        new_rows(cells, acc, extra, start, HALO, near_re, near_im)
        rows = slice(start, start + HALO)
        pairs = ((near_re.at[rows], new_re.at[rows]), (near_im.at[rows], new_im.at[rows]))
        copies += fetch(pairs, sems.at[2 * i : 2 * i + 2])
    finish_all(copies)


def swap(to_inner, to_outer, axis, gather):
    devices = lax.axis_size(axis)
    inner = [(i, i + 1) for i in range(0, devices, 2)]
    outer = [(i, i + 1) for i in range(1, devices - 1, 2)]
    by_outer = lax.ppermute(to_outer, axis, outer + [(j, i) for i, j in outer])
    if gather:
        by_inner = lax.all_gather(to_inner, axis, axis_index_groups=[list(pair) for pair in inner])
    else:
        by_inner = lax.ppermute(to_inner, axis, inner + [(j, i) for i, j in inner])
    return by_inner, by_outer


def far(x):
    return pltpu.with_memory_space_constraint(x, pltpu.HBM)


def f32(*shape):
    return jax.ShapeDtypeStruct(shape, jnp.float32)


def shards(object_re, object_im, probe_re, probe_im, frames, counts, offsets, frame_index):
    tile_r, tile_c = object_re.shape
    rows, width = tile_r + 2 * HALO, tile_c + 2 * LANES
    layers = 3
    slots = offsets.shape[2]
    table = jnp.asarray(transform_tables())
    frames = frames.reshape(frames.shape[2:])
    cells_shape, acc_shape = f32(2, rows, width), f32(layers, rows, width)
    dma = pltpu.SemaphoreType.DMA

    edge = f32(2, HALO, tile_c)
    to_inner, to_outer = pl.pallas_call(
        row_edges,
        out_shape=(edge, edge),
        in_specs=[HBM] * 2,
        out_specs=(HBM, VMEM),
        scratch_shapes=[dma((4,))],
        compiler_params=SMALL,
        name="row_edges",
    )(far(object_re), far(object_im))
    by_inner, by_outer = swap(to_inner, to_outer, "row", True)

    cells = pl.pallas_call(
        load_object,
        out_shape=cells_shape,
        in_specs=[HBM] * 2,
        out_specs=VMEM,
        scratch_shapes=[dma((2,))],
        compiler_params=SMALL,
        cost_estimate=BUSY,
        name="load_object",
    )(far(object_re), far(object_im))

    strip = pltpu.VMEM((layers * rows, LANES), jnp.float32)
    packed = f32(2 * rows // GROUPS, LANES)
    cells, to_inner, to_outer = pl.pallas_call(
        row_halos,
        out_shape=(cells_shape, packed, packed),
        in_specs=[VMEM] * 3,
        out_specs=(VMEM,) * 3,
        scratch_shapes=[strip],
        input_output_aliases={0: 0},
        compiler_params=SMALL,
        name="row_halos",
    )(cells, by_inner, by_outer)
    by_inner, by_outer = swap(to_inner, to_outer, "col", False)

    order = pltpu.SMEM((slots,), jnp.int32)
    scalars = (counts, jnp.swapaxes(offsets, 2, 3), frame_index)
    acc, *fixed = pl.pallas_call(
        windows_before,
        out_shape=(
            acc_shape, f32(*probe_re.shape), f32(*probe_im.shape),
            jax.ShapeDtypeStruct(table.shape, table.dtype), jax.ShapeDtypeStruct(frames.shape, frames.dtype),
        ),
        in_specs=[SMEM] * 3 + [VMEM] + [HBM] * 4,
        out_specs=(VMEM,) * 5,
        scratch_shapes=[order, pltpu.VMEM(probe_re.shape, jnp.float32), dma((4,))],
        compiler_params=PARAMS,
        cost_estimate=BUSY,
        name="windows_before",
    )(*scalars, cells, *map(far, (probe_re, probe_im, table, frames)))

    packed = f32(layers * rows // GROUPS, LANES)
    cells, acc, to_inner, to_outer = pl.pallas_call(
        windows_over_edge,
        out_shape=(cells_shape, acc_shape, packed, packed),
        in_specs=[SMEM] * 3 + [VMEM] * 8,
        out_specs=(VMEM,) * 4,
        scratch_shapes=[order, strip],
        input_output_aliases={3: 0, 4: 1},
        compiler_params=PARAMS,
        cost_estimate=BUSY,
        name="windows_over_edge",
    )(*scalars, cells, acc, *fixed, by_inner, by_outer)
    by_inner, by_outer = swap(to_inner, to_outer, "col", False)

    acc = pl.pallas_call(
        windows_after,
        out_shape=acc_shape,
        in_specs=[SMEM] * 3 + [VMEM] * 6,
        out_specs=VMEM,
        scratch_shapes=[order],
        input_output_aliases={4: 0},
        compiler_params=PARAMS,
        cost_estimate=BUSY,
        name="windows_after",
    )(*scalars, cells, acc, *fixed)

    edge = f32(layers, HALO, tile_c)
    acc, to_inner, to_outer = pl.pallas_call(
        row_spill,
        out_shape=(acc_shape, edge, edge),
        in_specs=[VMEM] * 3,
        out_specs=(VMEM,) * 3,
        input_output_aliases={0: 0},
        compiler_params=SMALL,
        name="row_spill",
    )(acc, by_inner, by_outer)
    by_inner, by_outer = swap(to_inner, to_outer, "row", True)

    near = [pltpu.VMEM((tile_r, tile_c), jnp.float32)] * 2
    new = (f32(tile_r, tile_c), f32(tile_r, tile_c))
    new_re, new_im = pl.pallas_call(
        finish_inner,
        out_shape=new,
        in_specs=[VMEM] * 2,
        out_specs=(HBM, HBM),
        scratch_shapes=near + [dma((2,))],
        compiler_params=SMALL,
        cost_estimate=BUSY,
        name="finish_inner",
    )(cells, acc)
    return pl.pallas_call(
        finish_edges,
        out_shape=new,
        in_specs=[VMEM] * 4 + [HBM] * 2,
        out_specs=(HBM, HBM),
        scratch_shapes=near + [dma((4,))],
        input_output_aliases={4: 0, 5: 1},
        compiler_params=SMALL,
        name="finish_edges",
    )(cells, acc, by_inner, by_outer, far(new_re), far(new_im))


def solution(mesh):
    return jax.shard_map(
        shards,
        mesh=mesh,
        in_specs=(
            P("row", "col"),
            P("row", "col"),
            P(),
            P(),
            P("row", "col", None, None, None),
            P("row", "col"),
            P("row", "col", None, None),
            P("row", "col", None),
        ),
        out_specs=(P("row", "col"), P("row", "col")),
        check_vma=False,
    )
```

```python
import functools
import math

import jax
import jax.numpy as jnp
import ml_dtypes
import numpy as np
from jax import lax
from jax.experimental import pallas as pl
from jax.experimental.pallas import tpu as pltpu
from jax.sharding import PartitionSpec as P

P_SIZE = 256
HALF = P_SIZE // 2
HALO = 32
LANES = 128
GROUPS = LANES // HALO
MARKS = 8
PAIR = 2

floor_amp = 0.5
ridge = 1.0

VMEM = pl.BlockSpec(memory_space=pltpu.VMEM)
SMEM = pl.BlockSpec(memory_space=pltpu.SMEM)
HBM = pl.BlockSpec(memory_space=pltpu.HBM)
PARAMS = pltpu.CompilerParams(vmem_limit_bytes=32 * 1024 * 1024)
SMALL = pltpu.CompilerParams(vmem_limit_bytes=16 * 1024 * 1024)
BUSY = pl.CostEstimate(flops=4_000_000_000, bytes_accessed=8_000_000, transcendentals=0)


def transform_tables():
    index = np.arange(HALF)
    plain = []
    for parity in (0, 1):
        angle = 2.0 * math.pi / P_SIZE * (index[:, None] * (2 * index[None, :] + parity) % P_SIZE)
        cos, sin = np.cos(angle), np.sin(angle)
        plain.append(np.block([[cos, -sin], [sin, cos]]) / math.sqrt(P_SIZE))
    parts = []
    for table in plain + [t.T for t in plain]:
        high = table.astype(np.float32).astype(ml_dtypes.bfloat16)
        low = (table - high.astype(np.float64)).astype(np.float32).astype(ml_dtypes.bfloat16)
        parts += [high, low]
    order = np.concatenate([np.arange(0, P_SIZE, 2), np.arange(1, P_SIZE, 2)])
    sort = np.zeros((P_SIZE, P_SIZE), np.float32)
    sort[np.arange(P_SIZE), order] = 1.0
    parts += [sort.astype(ml_dtypes.bfloat16), sort.T.astype(ml_dtypes.bfloat16)]
    return np.stack(parts)


def lane_index(rows):
    return lax.broadcasted_iota(jnp.int32, (rows, LANES), 1)


def pack_lanes(ref, rows, first):
    lane = lane_index(rows)
    packed = None
    for g in range(GROUPS):
        part = ref[g * rows : (g + 1) * rows, :]
        if g:
            part = pltpu.roll(part, HALO * g, 1)
        low = (first + HALO * g) % LANES
        mine = (lane >= low) & (lane < low + HALO)
        packed = part if packed is None else jnp.where(mine, part, packed)
    return packed


def unpack_lanes(packed, group):
    return pltpu.roll(packed, LANES - HALO * group, 1) if group else packed


def split(x):
    high = x.astype(jnp.bfloat16)
    return high, (x - high.astype(jnp.float32)).astype(jnp.bfloat16)


def product(left, right):
    return jnp.dot(left, right, preferred_element_type=jnp.float32)


def times_table(x, table, which):
    high, low = split(x)
    t_high, t_low = table[2 * which], table[2 * which + 1]
    return product(high, t_high) + (product(high, t_low) + product(low, t_high))


def table_times(table, which, x):
    high, low = split(x)
    t_high, t_low = table[2 * which], table[2 * which + 1]
    return product(t_high, high) + (product(t_low, high) + product(t_high, low))


def beside(*blocks):
    return jnp.concatenate(blocks, axis=1)


def below(*blocks):
    return jnp.concatenate(blocks, axis=0)


def ends(x):
    return x[:, :HALF], x[:, HALF:]


def forward_columns(exit_re, exit_im, table):
    re_lo, re_hi = ends(exit_re)
    im_lo, im_hi = ends(exit_im)
    even = times_table(beside(re_lo + re_hi, im_lo + im_hi), table, 0)
    odd = times_table(beside(re_lo - re_hi, im_lo - im_hi), table, 1)
    return even, odd


def forward_rows(even, odd, table):
    out = []
    for parity in (0, 1):
        if parity == 0:
            se, so = even[:HALF] + even[HALF:], odd[:HALF] + odd[HALF:]
        else:
            se, so = even[:HALF] - even[HALF:], odd[:HALF] - odd[HALF:]
        e_re, e_im = ends(se)
        o_re, o_im = ends(so)
        out.append(table_times(table, 2 + parity, below(beside(e_re, o_re), beside(e_im, o_im))))
    return out


def residual(far, frame):
    out = []
    for parity in (0, 1):
        re, im = far[parity][:HALF], far[parity][HALF:]
        level = jnp.maximum(re * re + im * im, floor_amp * floor_amp)
        inten = frame[parity * HALF : (parity + 1) * HALF]
        factor = 1.0 - inten * lax.rsqrt(inten * level)
        out.append(below(re * factor, im * factor))
    return out


def back_rows(res, table):
    first = table_times(table, 0, res[0])
    second = table_times(table, 1, res[1])
    upper, lower = first + second, first - second
    out = []
    for cols in (slice(0, HALF), slice(HALF, P_SIZE)):
        out.append(
            below(
                beside(upper[:HALF, cols], upper[HALF:, cols]),
                beside(lower[:HALF, cols], lower[HALF:, cols]),
            )
        )
    return out


def back_columns(parts, table):
    even = times_table(parts[0], table, 2)
    odd = times_table(parts[1], table, 3)
    lo, hi = even + odd, even - odd
    return beside(lo[:, :HALF], hi[:, :HALF]), beside(lo[:, HALF:], hi[:, HALF:])


def is_odd(axis):
    return lax.rem(lax.axis_index(axis), 2) == 1


def fetch(pairs, sems):
    copies = [pltpu.make_async_copy(far, near, sems.at[i]) for i, (far, near) in enumerate(pairs)]
    for copy in copies:
        copy.start()
    return copies


def finish_all(copies):
    for copy in copies:
        copy.wait()


def row_edges(counts, obj_re, obj_im, offsets, to_inner, to_outer, marked, places, sems):
    tile_r = obj_re.shape[0]
    odd = is_odd("row")
    low = pl.multiple_of(jnp.where(odd, 0, tile_r - HALO), 16)
    high = pl.multiple_of(jnp.where(odd, tile_r - HALO, 0), 16)
    pairs = [(offsets, places)]
    for k, ref in enumerate((obj_re, obj_im)):
        rows = slice(k * HALO, (k + 1) * HALO)
        pairs.append((ref.at[pl.ds(high, HALO)], to_outer.at[rows]))
        pairs.append((ref.at[pl.ds(low, HALO)], to_inner.at[rows]))
    copies = fetch(pairs, sems)
    finish_all(copies[:1])
    place = places[0, 0]
    live = lax.broadcasted_iota(jnp.int32, place.shape, 1) < counts[0, 0]
    place = jnp.where(live, place, 2 * tile_r)
    marked[0, 0] = place
    for message in (to_inner, to_outer):
        message[2 * HALO : 2 * HALO + 2, 0 : place.shape[1]] = place.astype(jnp.float32)
    finish_all(copies[1:])


def window_place(offsets, slot):
    row = pl.multiple_of(offsets[0, 0, 0, slot] + HALO, 16)
    col = offsets[0, 0, 1, slot] + LANES
    turn = lax.rem(col, LANES)
    return row, pl.multiple_of(col - turn, LANES), turn


def add_window(acc, layer, where, keep, term, tiles=(0, 1, 2)):
    row, base, _ = where
    lo, hi = ends(term)
    parts = (jnp.where(keep, lo, 0.0), hi, jnp.where(keep, 0.0, lo))
    for t in tiles:
        acc[layer, pl.ds(row, term.shape[0]), pl.ds(base + t * LANES, LANES)] += parts[t]


def load_state(
    obj_re, obj_im, probe_re_far, probe_im_far, table_far, frames_far,
    cells, probe_re, probe_im, table, frames, sems,
):
    tile_r, tile_c = obj_re.shape
    inner = slice(HALO, HALO + tile_r)
    middle = slice(LANES, LANES + tile_c)
    pairs = (
        (table_far, table),
        (frames_far, frames),
        (obj_re, cells.at[0, inner, middle]),
        (obj_im, cells.at[1, inner, middle]),
        (probe_re_far, probe_re),
        (probe_im_far, probe_im),
    )
    finish_all(fetch(pairs, sems))


def fill_strip(strip, parts):
    done = 0
    for part in parts:
        strip[done : done + part.shape[0], :] = part
        done += part.shape[0]


def send_columns(to_left, to_right, to_inner, to_outer):
    odd = is_odd("col")
    to_inner[0 : to_left.shape[0], :] = jnp.where(odd, to_left, to_right)
    to_outer[0 : to_left.shape[0], :] = jnp.where(odd, to_right, to_left)


def received(by_inner, by_outer, axis):
    odd = is_odd(axis)
    if len(by_inner.shape) > len(by_outer.shape):
        before, after = by_inner[0], by_inner[1]
    else:
        before = after = by_inner[...]
    return jnp.where(odd, before, by_outer[...]), jnp.where(odd, by_outer[...], after)


def pieces(packed, layers, rows):
    group_rows = layers * rows // GROUPS
    for g in range(GROUPS):
        part = unpack_lanes(packed, g)
        done = 0
        while done < group_rows:
            layer, row = divmod(g * group_rows + done, rows)
            size = min(group_rows - done, rows - row)
            yield layer, row, part[done : done + size]
            done += size


def row_halos(cells_in, own, by_inner, by_outer, cells, marks, to_inner, to_outer, strip):
    rows, width = cells.shape[1:]
    middle = slice(LANES, width - LANES)
    before, after = received(by_inner, by_outer, "row")
    for k in (0, 1):
        cells[k, 0:HALO, middle] = before[k * HALO : (k + 1) * HALO]
        cells[k, rows - HALO : rows, middle] = after[k * HALO : (k + 1) * HALO]
    first_mark = 2 * HALO
    for i, message in enumerate((own[...], before, after)):
        marks[2 * i : 2 * i + 2, :] = message[first_mark : first_mark + 2, 0:LANES]
    group_rows = 2 * rows // GROUPS
    first, last = slice(LANES, 2 * LANES), slice(width - 2 * LANES, width - LANES)
    fill_strip(strip, (cells[0, :, first], cells[1, :, first]))
    to_left = pack_lanes(strip, group_rows, 0)
    fill_strip(strip, (cells[0, :, last], cells[1, :, last]))
    to_right = pack_lanes(strip, group_rows, LANES - HALO)
    send_columns(to_left, to_right, to_inner, to_outer)
    to_inner[group_rows:, :] = marks[...]
    to_outer[group_rows:, :] = marks[...]


def live_slots(offsets, cells):
    tile_r = cells.shape[1] - 2 * HALO
    count = jnp.int32(0)
    for slot in range(offsets.shape[3]):
        count += (offsets[0, 0, 0, slot] < tile_r).astype(jnp.int32)
    return count


def run_windows(wanted, offsets, chosen, cells, acc, probe_re, probe_im, table, frames, order):
    tile_c = cells.shape[2] - 2 * LANES
    count = live_slots(offsets, cells)
    slots = range(offsets.shape[3])
    over = []
    for slot in slots:
        col = offsets[0, 0, 1, slot]
        over.append((col < 0) | (col > tile_c - P_SIZE))
    total = jnp.int32(0)
    for slot in slots:
        total += ((slot < count) & ~over[slot]).astype(jnp.int32)
    limit = jnp.where(total < len(slots) - 1, PAIR, 2 * PAIR)
    seen, found = jnp.int32(0), jnp.int32(0)
    for slot in slots:
        live = slot < count
        mine = live & wanted(over[slot], seen, limit)

        @pl.when(mine)
        def _():
            order[found] = slot

        seen += (live & ~over[slot]).astype(jnp.int32)
        found += mine.astype(jnp.int32)

    lane = lane_index(P_SIZE)

    def load(slot):
        where = row, base, turn = window_place(offsets, slot)
        keep = lane >= turn
        w_re = pltpu.roll(probe_re[...], turn, 1)
        w_im = pltpu.roll(probe_im[...], turn, 1)
        patch = []
        for k in (0, 1):
            block = cells[k, pl.ds(row, P_SIZE), pl.ds(base, 3 * LANES)]
            patch.append(
                beside(jnp.where(keep, block[:, :LANES], block[:, 2 * LANES :]), block[:, LANES : 2 * LANES])
            )
        exit_re = w_re * patch[0] - w_im * patch[1]
        exit_im = w_re * patch[1] + w_im * patch[0]
        return (where, keep, w_re, w_im), exit_re, exit_im

    def frame_of(slot):
        sort, unsort = table[8], table[9]
        half = product(sort, frames[chosen[0, 0, slot]]).astype(jnp.bfloat16)
        return product(half, unsort)

    def place(at, back_re, back_im):
        where, keep, w_re, w_im = at
        add_window(acc, 0, where, keep, w_re * back_re + w_im * back_im)
        add_window(acc, 1, where, keep, w_re * back_im - w_im * back_re)

    def step(group):
        frame = [frame_of(slot) for slot in group]
        loaded = [load(slot) for slot in group]
        state = [forward_columns(x[1], x[2], table) for x in loaded]
        state = [forward_rows(*x, table) for x in state]
        state = [residual(x, f) for x, f in zip(state, frame)]
        state = [back_rows(x, table) for x in state]
        state = [back_columns(x, table) for x in state]
        for x, back in zip(loaded, state):
            place(x[0], *back)

    def pair_step(pair, carry):
        step([order[pair * PAIR + i] for i in range(PAIR)])
        return carry

    lax.fori_loop(0, found // PAIR, pair_step, 0)

    @pl.when(found % PAIR == 1)
    def _():
        step([order[found - 1]])


def windows_before(
    offsets, chosen, cells, probe_re, probe_im, table, frames, acc, order, power,
):
    acc[...] = jnp.zeros_like(acc)
    power[...] = probe_re[...] * probe_re[...] + probe_im[...] * probe_im[...]
    lane = lane_index(P_SIZE)

    def step(slot, carry):
        where = window_place(offsets, slot)
        add_window(acc, 2, where, lane >= where[2], pltpu.roll(power[...], where[2], 1))
        return carry

    lax.fori_loop(0, live_slots(offsets, cells), step, 0)
    run_windows(
        lambda over, seen, limit: ~over & (seen < limit),
        offsets, chosen, cells, acc, probe_re, probe_im, table, frames, order,
    )


def add_neighbours_light(places, acc, power):
    rows, width = acc.shape[1:]
    tile_r, tile_c = rows - 2 * HALO, width - 2 * LANES
    for right in (-1, 0, 1):
        for i, down in enumerate((0, -1, 1)):
            if not right and not down:
                continue
            first, last = {-1: (P_SIZE - HALO, P_SIZE), 0: (0, P_SIZE), 1: (0, HALO)}[down]
            tiles = {-1: (2,), 0: (0, 1, 2), 1: (0,)}[right]
            lane = lane_index(last - first)

            def step(slot, carry):
                row, col = places[right + 1, 2 * i, slot], places[right + 1, 2 * i + 1, slot]
                reaches = row < tile_r
                if down < 0:
                    reaches &= row > tile_r - P_SIZE
                if down > 0:
                    reaches &= row < 0
                if right < 0:
                    reaches &= col > tile_c - P_SIZE
                if right > 0:
                    reaches &= col < 0

                @pl.when(reaches)
                def _():
                    turn = lax.rem(col + LANES, LANES)
                    at = pl.multiple_of(row + HALO + (down * tile_r + first), 16)
                    base = pl.multiple_of(col + LANES - turn + right * tile_c, LANES)
                    part = pltpu.roll(power[first:last, :], turn, 1)
                    add_window(acc, 2, (at, base, turn), lane >= turn, part, tiles)

                return carry

            lax.fori_loop(0, MARKS, step, 0)


def windows_after(
    offsets, chosen, cells, acc_in, probe_re, probe_im, table, frames, marks, by_inner, by_outer,
    acc, order, power, whole, places, sem,
):
    before, after = received(by_inner, by_outer, "col")
    for i, part in enumerate((before[-MARKS:], marks[...], after[-MARKS:])):
        whole[i] = part.astype(jnp.int32)
    copy = pltpu.make_async_copy(whole, places, sem)
    copy.start()
    power[...] = probe_re[...] * probe_re[...] + probe_im[...] * probe_im[...]
    copy.wait()
    add_neighbours_light(places, acc, power)
    run_windows(
        lambda over, seen, limit: ~over & (seen >= limit),
        offsets, chosen, cells, acc, probe_re, probe_im, table, frames, order,
    )


def windows_over_edge(
    offsets, chosen, cells_in, acc_in, probe_re, probe_im, table, frames, by_inner, by_outer,
    cells, acc, to_inner, to_outer, order, strip,
):
    rows, width = acc.shape[1:]
    before, after = received(by_inner, by_outer, "col")
    for layer, row, part in pieces(before, 2, rows):
        cells[layer, row : row + part.shape[0], 0:LANES] = part
    for layer, row, part in pieces(after, 2, rows):
        cells[layer, row : row + part.shape[0], width - LANES :] = part
    run_windows(
        lambda over, seen, limit: over,
        offsets, chosen, cells, acc, probe_re, probe_im, table, frames, order,
    )
    group_rows = 2 * rows // GROUPS
    fill_strip(strip, (acc[0, :, 0:LANES], acc[1, :, 0:LANES]))
    to_left = pack_lanes(strip, group_rows, LANES - HALO)
    fill_strip(strip, (acc[0, :, width - LANES :], acc[1, :, width - LANES :]))
    to_right = pack_lanes(strip, group_rows, 0)
    send_columns(to_left, to_right, to_inner, to_outer)


def row_spill(acc_in, by_inner, by_outer, acc, to_inner, to_outer):
    rows, width = acc.shape[1:]
    before, after = received(by_inner, by_outer, "col")
    lane = lane_index(rows)[0:1]
    for layer, row, part in pieces(before, 2, rows):
        here = slice(row, row + part.shape[0])
        acc[layer, here, LANES : 2 * LANES] += jnp.where(lane < HALO, part, 0.0)
    for layer, row, part in pieces(after, 2, rows):
        here = slice(row, row + part.shape[0])
        acc[layer, here, width - 2 * LANES : width - LANES] += jnp.where(lane >= LANES - HALO, part, 0.0)
    odd = is_odd("row")
    for k in (0, 1):
        up = acc[k, 0:HALO, LANES : width - LANES]
        down = acc[k, rows - HALO : rows, LANES : width - LANES]
        to_inner[k] = jnp.where(odd, up, down)
        to_outer[k] = jnp.where(odd, down, up)


def new_rows(cells, acc, extra, start, size, new_re, new_im):
    here = slice(HALO + start, HALO + start + size)
    middle = slice(LANES, acc.shape[2] - LANES)
    part = [acc[k, here, middle] for k in range(acc.shape[0])]
    if extra is not None:
        part[:2] = [part[k] + extra[k] for k in (0, 1)]
    scale = 1.0 / (part[2] + ridge)
    new_re[start : start + size, :] = cells[0, here, middle] - part[0] * scale
    new_im[start : start + size, :] = cells[1, here, middle] - part[1] * scale


def finish_inner(cells, acc, new_re, new_im, near_re, near_im, sems):
    tile_r = near_re.shape[0]
    new_rows(cells, acc, None, HALO, tile_r - 2 * HALO, near_re, near_im)
    rows = slice(HALO, tile_r - HALO)
    finish_all(fetch([(near_re.at[rows], new_re.at[rows]), (near_im.at[rows], new_im.at[rows])], sems))


def finish_edges(cells, acc, by_inner, by_outer, re_in, im_in, new_re, new_im, near_re, near_im, sems):
    tile_r = near_re.shape[0]
    copies = []
    for i, (start, extra) in enumerate(zip((0, tile_r - HALO), received(by_inner, by_outer, "row"))):
        new_rows(cells, acc, extra, start, HALO, near_re, near_im)
        rows = slice(start, start + HALO)
        pairs = ((near_re.at[rows], new_re.at[rows]), (near_im.at[rows], new_im.at[rows]))
        copies += fetch(pairs, sems.at[2 * i : 2 * i + 2])
    finish_all(copies)


def swap(to_inner, to_outer, axis, gather):
    devices = lax.axis_size(axis)
    inner = [(i, i + 1) for i in range(0, devices, 2)]
    outer = [(i, i + 1) for i in range(1, devices - 1, 2)]
    by_outer = lax.ppermute(to_outer, axis, outer + [(j, i) for i, j in outer])
    if gather:
        by_inner = lax.all_gather(to_inner, axis, axis_index_groups=[list(pair) for pair in inner])
    else:
        by_inner = lax.ppermute(to_inner, axis, inner + [(j, i) for i, j in inner])
    return by_inner, by_outer


def far(x):
    return pltpu.with_memory_space_constraint(x, pltpu.HBM)


def f32(*shape):
    return jax.ShapeDtypeStruct(shape, jnp.float32)


def shards(object_re, object_im, probe_re, probe_im, frames, counts, offsets, frame_index):
    tile_r, tile_c = object_re.shape
    rows, width = tile_r + 2 * HALO, tile_c + 2 * LANES
    layers = 3
    slots = offsets.shape[2]
    table = jnp.asarray(transform_tables())
    frames = frames.reshape(frames.shape[2:])
    cells_shape, acc_shape = f32(2, rows, width), f32(layers, rows, width)
    dma = pltpu.SemaphoreType.DMA

    places = jnp.swapaxes(offsets, 2, 3)
    edge = f32(2 * HALO + MARKS, tile_c)
    to_inner, to_outer, marked = pl.pallas_call(
        row_edges,
        out_shape=(edge, edge, jax.ShapeDtypeStruct(places.shape, jnp.int32)),
        in_specs=[SMEM] + [HBM] * 3,
        out_specs=(VMEM, VMEM, VMEM),
        scratch_shapes=[pltpu.VMEM(places.shape, jnp.int32), dma((5,))],
        compiler_params=SMALL,
        name="row_edges",
    )(counts, far(object_re), far(object_im), far(places))
    by_inner, by_outer = swap(to_inner, to_outer, "row", True)

    cells, *fixed = pl.pallas_call(
        load_state,
        out_shape=(
            cells_shape, f32(*probe_re.shape), f32(*probe_im.shape),
            jax.ShapeDtypeStruct(table.shape, table.dtype), jax.ShapeDtypeStruct(frames.shape, frames.dtype),
        ),
        in_specs=[HBM] * 6,
        out_specs=(VMEM,) * 5,
        scratch_shapes=[dma((6,))],
        compiler_params=SMALL,
        cost_estimate=BUSY,
        name="load_state",
    )(*map(far, (object_re, object_im, probe_re, probe_im, table, frames)))

    strip = pltpu.VMEM((2 * rows, LANES), jnp.float32)
    packed = f32(2 * rows // GROUPS + MARKS, LANES)
    cells, marks, to_inner, to_outer = pl.pallas_call(
        row_halos,
        out_shape=(cells_shape, f32(MARKS, LANES), packed, packed),
        in_specs=[VMEM] * 4,
        out_specs=(VMEM,) * 4,
        scratch_shapes=[strip],
        input_output_aliases={0: 0},
        compiler_params=SMALL,
        name="row_halos",
    )(cells, to_outer, by_inner, by_outer)
    edges = swap(to_inner, to_outer, "col", False)

    order = pltpu.SMEM((slots,), jnp.int32)
    scalars = (marked, frame_index)
    acc = pl.pallas_call(
        windows_before,
        out_shape=acc_shape,
        in_specs=[SMEM] * 2 + [VMEM] * 5,
        out_specs=VMEM,
        scratch_shapes=[order, pltpu.VMEM(probe_re.shape, jnp.float32)],
        compiler_params=PARAMS,
        cost_estimate=BUSY,
        name="windows_before",
    )(*scalars, cells, *fixed)

    packed = f32(2 * rows // GROUPS, LANES)
    cells, acc, to_inner, to_outer = pl.pallas_call(
        windows_over_edge,
        out_shape=(cells_shape, acc_shape, packed, packed),
        in_specs=[SMEM] * 2 + [VMEM] * 8,
        out_specs=(VMEM,) * 4,
        scratch_shapes=[order, strip],
        input_output_aliases={2: 0, 3: 1},
        compiler_params=PARAMS,
        cost_estimate=BUSY,
        name="windows_over_edge",
    )(*scalars, cells, acc, *fixed, *edges)
    by_inner, by_outer = swap(to_inner, to_outer, "col", False)

    acc = pl.pallas_call(
        windows_after,
        out_shape=acc_shape,
        in_specs=[SMEM] * 2 + [VMEM] * 9,
        out_specs=VMEM,
        scratch_shapes=[
            order, pltpu.VMEM(probe_re.shape, jnp.float32),
            pltpu.VMEM((3, MARKS, LANES), jnp.int32), pltpu.SMEM((3, MARKS, LANES), jnp.int32), dma(()),
        ],
        input_output_aliases={3: 0},
        compiler_params=PARAMS,
        cost_estimate=BUSY,
        name="windows_after",
    )(*scalars, cells, acc, *fixed, marks, *edges)

    edge = f32(2, HALO, tile_c)
    acc, to_inner, to_outer = pl.pallas_call(
        row_spill,
        out_shape=(acc_shape, edge, edge),
        in_specs=[VMEM] * 3,
        out_specs=(VMEM,) * 3,
        input_output_aliases={0: 0},
        compiler_params=SMALL,
        name="row_spill",
    )(acc, by_inner, by_outer)
    by_inner, by_outer = swap(to_inner, to_outer, "row", True)

    near = [pltpu.VMEM((tile_r, tile_c), jnp.float32)] * 2
    new = (f32(tile_r, tile_c), f32(tile_r, tile_c))
    new_re, new_im = pl.pallas_call(
        finish_inner,
        out_shape=new,
        in_specs=[VMEM] * 2,
        out_specs=(HBM, HBM),
        scratch_shapes=near + [dma((2,))],
        compiler_params=SMALL,
        cost_estimate=BUSY,
        name="finish_inner",
    )(cells, acc)
    return pl.pallas_call(
        finish_edges,
        out_shape=new,
        in_specs=[VMEM] * 4 + [HBM] * 2,
        out_specs=(HBM, HBM),
        scratch_shapes=near + [dma((4,))],
        input_output_aliases={4: 0, 5: 1},
        compiler_params=SMALL,
        name="finish_edges",
    )(cells, acc, by_inner, by_outer, far(new_re), far(new_im))


def solution(mesh):
    return jax.shard_map(
        shards,
        mesh=mesh,
        in_specs=(
            P("row", "col"),
            P("row", "col"),
            P(),
            P(),
            P("row", "col", None, None, None),
            P("row", "col"),
            P("row", "col", None, None),
            P("row", "col", None),
        ),
        out_specs=(P("row", "col"), P("row", "col")),
        check_vma=False,
    )
```

```python
import functools
import math

import jax
import jax.numpy as jnp
import ml_dtypes
import numpy as np
from jax import lax
from jax.experimental import pallas as pl
from jax.experimental.pallas import tpu as pltpu
from jax.sharding import PartitionSpec as P

P_SIZE = 256
HALF = P_SIZE // 2
HALO = 32
LANES = 128
GROUPS = LANES // HALO
MARKS = 8
PAIR = 2

floor_amp = 0.5
ridge = 1.0

VMEM = pl.BlockSpec(memory_space=pltpu.VMEM)
SMEM = pl.BlockSpec(memory_space=pltpu.SMEM)
HBM = pl.BlockSpec(memory_space=pltpu.HBM)
PARAMS = pltpu.CompilerParams(vmem_limit_bytes=32 * 1024 * 1024)
SMALL = pltpu.CompilerParams(vmem_limit_bytes=16 * 1024 * 1024)
BUSY = pl.CostEstimate(flops=4_000_000_000, bytes_accessed=8_000_000, transcendentals=0)


def transform_tables():
    index = np.arange(HALF)
    plain = []
    for parity in (0, 1):
        angle = 2.0 * math.pi / P_SIZE * (index[:, None] * (2 * index[None, :] + parity) % P_SIZE)
        cos, sin = np.cos(angle), np.sin(angle)
        plain.append(np.block([[cos, -sin], [sin, cos]]) / math.sqrt(P_SIZE))
    parts = []
    for table in plain + [t.T for t in plain]:
        high = table.astype(np.float32).astype(ml_dtypes.bfloat16)
        low = (table - high.astype(np.float64)).astype(np.float32).astype(ml_dtypes.bfloat16)
        parts += [high, low]
    order = np.concatenate([np.arange(0, P_SIZE, 2), np.arange(1, P_SIZE, 2)])
    sort = np.zeros((P_SIZE, P_SIZE), np.float32)
    sort[np.arange(P_SIZE), order] = 1.0
    parts += [sort.astype(ml_dtypes.bfloat16), sort.T.astype(ml_dtypes.bfloat16)]
    return np.stack(parts)


def lane_index(rows):
    return lax.broadcasted_iota(jnp.int32, (rows, LANES), 1)


def pack_lanes(ref, rows, first):
    lane = lane_index(rows)
    packed = None
    for g in range(GROUPS):
        part = ref[g * rows : (g + 1) * rows, :]
        if g:
            part = pltpu.roll(part, HALO * g, 1)
        low = (first + HALO * g) % LANES
        mine = (lane >= low) & (lane < low + HALO)
        packed = part if packed is None else jnp.where(mine, part, packed)
    return packed


def unpack_lanes(packed, group):
    return pltpu.roll(packed, LANES - HALO * group, 1) if group else packed


def split(x):
    high = x.astype(jnp.bfloat16)
    return high, (x - high.astype(jnp.float32)).astype(jnp.bfloat16)


def product(left, right):
    return jnp.dot(left, right, preferred_element_type=jnp.float32)


def times_table(x, table, which):
    high, low = split(x)
    t_high, t_low = table[2 * which], table[2 * which + 1]
    return product(high, t_high) + (product(high, t_low) + product(low, t_high))


def table_times(table, which, x):
    high, low = split(x)
    t_high, t_low = table[2 * which], table[2 * which + 1]
    return product(t_high, high) + (product(t_low, high) + product(t_high, low))


def beside(*blocks):
    return jnp.concatenate(blocks, axis=1)


def below(*blocks):
    return jnp.concatenate(blocks, axis=0)


def ends(x):
    return x[:, :HALF], x[:, HALF:]


def forward_columns(exit_re, exit_im, table):
    re_lo, re_hi = ends(exit_re)
    im_lo, im_hi = ends(exit_im)
    even = times_table(beside(re_lo + re_hi, im_lo + im_hi), table, 0)
    odd = times_table(beside(re_lo - re_hi, im_lo - im_hi), table, 1)
    return even, odd


def forward_rows(even, odd, table):
    out = []
    for parity in (0, 1):
        if parity == 0:
            se, so = even[:HALF] + even[HALF:], odd[:HALF] + odd[HALF:]
        else:
            se, so = even[:HALF] - even[HALF:], odd[:HALF] - odd[HALF:]
        e_re, e_im = ends(se)
        o_re, o_im = ends(so)
        out.append(table_times(table, 2 + parity, below(beside(e_re, o_re), beside(e_im, o_im))))
    return out


def residual(far, frame):
    out = []
    for parity in (0, 1):
        re, im = far[parity][:HALF], far[parity][HALF:]
        level = jnp.maximum(re * re + im * im, floor_amp * floor_amp)
        inten = frame[parity * HALF : (parity + 1) * HALF]
        factor = 1.0 - inten * lax.rsqrt(inten * level)
        out.append(below(re * factor, im * factor))
    return out


def back_rows(res, table):
    first = table_times(table, 0, res[0])
    second = table_times(table, 1, res[1])
    upper, lower = first + second, first - second
    out = []
    for cols in (slice(0, HALF), slice(HALF, P_SIZE)):
        out.append(
            below(
                beside(upper[:HALF, cols], upper[HALF:, cols]),
                beside(lower[:HALF, cols], lower[HALF:, cols]),
            )
        )
    return out


def back_columns(parts, table):
    even = times_table(parts[0], table, 2)
    odd = times_table(parts[1], table, 3)
    lo, hi = even + odd, even - odd
    return beside(lo[:, :HALF], hi[:, :HALF]), beside(lo[:, HALF:], hi[:, HALF:])


def is_odd(axis):
    return lax.rem(lax.axis_index(axis), 2) == 1


def fetch(pairs, sems):
    copies = [pltpu.make_async_copy(far, near, sems.at[i]) for i, (far, near) in enumerate(pairs)]
    for copy in copies:
        copy.start()
    return copies


def finish_all(copies):
    for copy in copies:
        copy.wait()


def row_edges(counts, obj_re, obj_im, offsets, chosen, to_inner, to_outer, marked, places, frame_of, sems):
    tile_r = obj_re.shape[0]
    odd = is_odd("row")
    low = pl.multiple_of(jnp.where(odd, 0, tile_r - HALO), 16)
    high = pl.multiple_of(jnp.where(odd, tile_r - HALO, 0), 16)
    pairs = [(offsets, places), (chosen, frame_of)]
    for k, ref in enumerate((obj_re, obj_im)):
        rows = slice(k * HALO, (k + 1) * HALO)
        pairs.append((ref.at[pl.ds(high, HALO)], to_outer.at[rows]))
        pairs.append((ref.at[pl.ds(low, HALO)], to_inner.at[rows]))
    copies = fetch(pairs, sems)
    finish_all(copies[:2])
    place = places[0, 0]
    live = lax.broadcasted_iota(jnp.int32, place.shape, 1) < counts[0, 0]
    place = jnp.where(live, place, 2 * tile_r)
    marked[0:2, :] = place
    marked[2:3, :] = frame_of[0]
    for message in (to_inner, to_outer):
        message[2 * HALO : 2 * HALO + 2, 0 : place.shape[1]] = place.astype(jnp.float32)
    finish_all(copies[2:])


def window_place(slots, slot):
    row = pl.multiple_of(slots[0, slot] + HALO, 16)
    col = slots[1, slot] + LANES
    turn = lax.rem(col, LANES)
    return row, pl.multiple_of(col - turn, LANES), turn


def add_window(acc, layer, where, keep, term, tiles=(0, 1, 2)):
    row, base, _ = where
    lo, hi = ends(term)
    parts = (jnp.where(keep, lo, 0.0), hi, jnp.where(keep, 0.0, lo))
    for t in tiles:
        acc[layer, pl.ds(row, term.shape[0]), pl.ds(base + t * LANES, LANES)] += parts[t]


def load_state(
    obj_re, obj_im, probe_re_far, probe_im_far, table_far, frames_far,
    cells, probe_re, probe_im, table, frames, sems,
):
    tile_r, tile_c = obj_re.shape
    inner = slice(HALO, HALO + tile_r)
    middle = slice(LANES, LANES + tile_c)
    pairs = (
        (table_far, table),
        (frames_far, frames),
        (obj_re, cells.at[0, inner, middle]),
        (obj_im, cells.at[1, inner, middle]),
        (probe_re_far, probe_re),
        (probe_im_far, probe_im),
    )
    finish_all(fetch(pairs, sems))


def fill_strip(strip, parts):
    done = 0
    for part in parts:
        strip[done : done + part.shape[0], :] = part
        done += part.shape[0]


def send_columns(to_left, to_right, to_inner, to_outer):
    odd = is_odd("col")
    to_inner[0 : to_left.shape[0], :] = jnp.where(odd, to_left, to_right)
    to_outer[0 : to_left.shape[0], :] = jnp.where(odd, to_right, to_left)


def received(by_inner, by_outer, axis):
    odd = is_odd(axis)
    if len(by_inner.shape) > len(by_outer.shape):
        before, after = by_inner[0], by_inner[1]
    else:
        before = after = by_inner[...]
    return jnp.where(odd, before, by_outer[...]), jnp.where(odd, by_outer[...], after)


def pieces(packed, layers, rows):
    group_rows = layers * rows // GROUPS
    for g in range(GROUPS):
        part = unpack_lanes(packed, g)
        done = 0
        while done < group_rows:
            layer, row = divmod(g * group_rows + done, rows)
            size = min(group_rows - done, rows - row)
            yield layer, row, part[done : done + size]
            done += size


def row_halos(cells_in, own, by_inner, by_outer, cells, marks, to_inner, to_outer, strip):
    rows, width = cells.shape[1:]
    middle = slice(LANES, width - LANES)
    before, after = received(by_inner, by_outer, "row")
    for k in (0, 1):
        cells[k, 0:HALO, middle] = before[k * HALO : (k + 1) * HALO]
        cells[k, rows - HALO : rows, middle] = after[k * HALO : (k + 1) * HALO]
    first_mark = 2 * HALO
    for i, message in enumerate((own[...], before, after)):
        marks[2 * i : 2 * i + 2, :] = message[first_mark : first_mark + 2, 0:LANES]
    group_rows = 2 * rows // GROUPS
    first, last = slice(LANES, 2 * LANES), slice(width - 2 * LANES, width - LANES)
    fill_strip(strip, (cells[0, :, first], cells[1, :, first]))
    to_left = pack_lanes(strip, group_rows, 0)
    fill_strip(strip, (cells[0, :, last], cells[1, :, last]))
    to_right = pack_lanes(strip, group_rows, LANES - HALO)
    send_columns(to_left, to_right, to_inner, to_outer)
    to_inner[group_rows:, :] = marks[...]
    to_outer[group_rows:, :] = marks[...]


def live_slots(slots, cells):
    tile_r = cells.shape[1] - 2 * HALO
    count = jnp.int32(0)
    for slot in range(slots.shape[1]):
        count += (slots[0, slot] < tile_r).astype(jnp.int32)
    return count


def run_windows(wanted, slots, cells, acc, probe_re, probe_im, table, frames, order):
    tile_c = cells.shape[2] - 2 * LANES
    count = live_slots(slots, cells)
    every = range(slots.shape[1])
    over = []
    for slot in every:
        col = slots[1, slot]
        over.append((col < 0) | (col > tile_c - P_SIZE))
    total = jnp.int32(0)
    for slot in every:
        total += ((slot < count) & ~over[slot]).astype(jnp.int32)
    limit = jnp.where(total < len(every) - 1, PAIR, 2 * PAIR)
    seen, found = jnp.int32(0), jnp.int32(0)
    for slot in every:
        live = slot < count
        mine = live & wanted(over[slot], seen, limit)

        @pl.when(mine)
        def _():
            order[found] = slot

        seen += (live & ~over[slot]).astype(jnp.int32)
        found += mine.astype(jnp.int32)

    lane = lane_index(P_SIZE)

    def load(slot):
        where = row, base, turn = window_place(slots, slot)
        keep = lane >= turn
        w_re = pltpu.roll(probe_re[...], turn, 1)
        w_im = pltpu.roll(probe_im[...], turn, 1)
        patch = []
        for k in (0, 1):
            block = cells[k, pl.ds(row, P_SIZE), pl.ds(base, 3 * LANES)]
            patch.append(
                beside(jnp.where(keep, block[:, :LANES], block[:, 2 * LANES :]), block[:, LANES : 2 * LANES])
            )
        exit_re = w_re * patch[0] - w_im * patch[1]
        exit_im = w_re * patch[1] + w_im * patch[0]
        return (where, keep, w_re, w_im), exit_re, exit_im

    def frame_of(slot):
        sort, unsort = table[8], table[9]
        half = product(sort, frames[slots[2, slot]]).astype(jnp.bfloat16)
        return product(half, unsort)

    def place(at, back_re, back_im):
        where, keep, w_re, w_im = at
        add_window(acc, 0, where, keep, w_re * back_re + w_im * back_im)
        add_window(acc, 1, where, keep, w_re * back_im - w_im * back_re)

    def step(group):
        frame = [frame_of(slot) for slot in group]
        loaded = [load(slot) for slot in group]
        state = [forward_columns(x[1], x[2], table) for x in loaded]
        state = [forward_rows(*x, table) for x in state]
        state = [residual(x, f) for x, f in zip(state, frame)]
        state = [back_rows(x, table) for x in state]
        state = [back_columns(x, table) for x in state]
        for x, back in zip(loaded, state):
            place(x[0], *back)

    def pair_step(pair, carry):
        step([order[pair * PAIR + i] for i in range(PAIR)])
        return carry

    lax.fori_loop(0, found // PAIR, pair_step, 0)

    @pl.when(found % PAIR == 1)
    def _():
        step([order[found - 1]])


def windows_before(
    slots, cells, probe_re, probe_im, table, frames, acc, order, power,
):
    acc[...] = jnp.zeros_like(acc)
    power[...] = probe_re[...] * probe_re[...] + probe_im[...] * probe_im[...]
    lane = lane_index(P_SIZE)

    def step(slot, carry):
        where = window_place(slots, slot)
        add_window(acc, 2, where, lane >= where[2], pltpu.roll(power[...], where[2], 1))
        return carry

    lax.fori_loop(0, live_slots(slots, cells), step, 0)
    run_windows(
        lambda over, seen, limit: ~over & (seen < limit),
        slots, cells, acc, probe_re, probe_im, table, frames, order,
    )


def reaching(place, right, tile_r, tile_c):
    shape = place.shape
    index = lax.broadcasted_iota(jnp.int32, shape, 0)
    lane = lax.broadcasted_iota(jnp.int32, shape, 1)
    col = pltpu.roll(place, shape[0] - 1, 0)
    low = jnp.where(index == 2, tile_r - P_SIZE, -tile_r).astype(jnp.float32)
    high = jnp.where(index == 4, 0, tile_r).astype(jnp.float32)
    reaches = (lane < MARKS) & (index % 2 == 0) & (index < 6) & (place > low) & (place < high)
    if right < 0:
        reaches &= col > tile_c - P_SIZE
    if right > 0:
        reaches &= col < 0
    bit = lax.shift_left(jnp.ones(shape, jnp.int32), jnp.minimum(lane, MARKS)).astype(jnp.float32)
    bits = jnp.sum(jnp.where(reaches, bit, 0.0), axis=1, keepdims=True)
    return jnp.where(lane < MARKS, place, bits).astype(jnp.int32)


def add_neighbours_light(places, acc, power):
    rows, width = acc.shape[1:]
    tile_r, tile_c = rows - 2 * HALO, width - 2 * LANES
    for right in (-1, 0, 1):
        for i, down in enumerate((0, -1, 1)):
            if not right and not down:
                continue
            first, last = {-1: (P_SIZE - HALO, P_SIZE), 0: (0, P_SIZE), 1: (0, HALO)}[down]
            tiles = {-1: (2,), 0: (0, 1, 2), 1: (0,)}[right]
            lane = lane_index(last - first)
            bits = places[right + 1, 2 * i, MARKS]

            def step(slot, carry):
                row, col = places[right + 1, 2 * i, slot], places[right + 1, 2 * i + 1, slot]

                @pl.when(lax.shift_right_logical(bits, slot) % 2 == 1)
                def _():
                    turn = lax.rem(col + LANES, LANES)
                    at = pl.multiple_of(row + HALO + (down * tile_r + first), 16)
                    base = pl.multiple_of(col + LANES - turn + right * tile_c, LANES)
                    part = pltpu.roll(power[first:last, :], turn, 1)
                    add_window(acc, 2, (at, base, turn), lane >= turn, part, tiles)

                return carry

            @pl.when(bits != 0)
            def _():
                lax.fori_loop(0, MARKS, step, 0)


def windows_after(
    slots, cells, acc_in, probe_re, probe_im, table, frames, marks, by_inner, by_outer,
    acc, order, power, whole, places, sem,
):
    rows, width = acc.shape[1:]
    before, after = received(by_inner, by_outer, "col")
    for i, part in enumerate((before[-MARKS:], marks[...], after[-MARKS:])):
        whole[i] = reaching(part, i - 1, rows - 2 * HALO, width - 2 * LANES)
    copy = pltpu.make_async_copy(whole, places, sem)
    copy.start()
    power[...] = probe_re[...] * probe_re[...] + probe_im[...] * probe_im[...]
    run_windows(
        lambda over, seen, limit: ~over & (seen >= limit),
        slots, cells, acc, probe_re, probe_im, table, frames, order,
    )
    copy.wait()
    add_neighbours_light(places, acc, power)


def windows_over_edge(
    slots, cells_in, acc_in, probe_re, probe_im, table, frames, by_inner, by_outer,
    cells, acc, to_inner, to_outer, order, strip,
):
    rows, width = acc.shape[1:]
    before, after = received(by_inner, by_outer, "col")
    for layer, row, part in pieces(before, 2, rows):
        cells[layer, row : row + part.shape[0], 0:LANES] = part
    for layer, row, part in pieces(after, 2, rows):
        cells[layer, row : row + part.shape[0], width - LANES :] = part
    run_windows(
        lambda over, seen, limit: over,
        slots, cells, acc, probe_re, probe_im, table, frames, order,
    )
    group_rows = 2 * rows // GROUPS
    fill_strip(strip, (acc[0, :, 0:LANES], acc[1, :, 0:LANES]))
    to_left = pack_lanes(strip, group_rows, LANES - HALO)
    fill_strip(strip, (acc[0, :, width - LANES :], acc[1, :, width - LANES :]))
    to_right = pack_lanes(strip, group_rows, 0)
    send_columns(to_left, to_right, to_inner, to_outer)


def row_spill(acc_in, by_inner, by_outer, acc, to_inner, to_outer):
    rows, width = acc.shape[1:]
    before, after = received(by_inner, by_outer, "col")
    lane = lane_index(rows)[0:1]
    for layer, row, part in pieces(before, 2, rows):
        here = slice(row, row + part.shape[0])
        acc[layer, here, LANES : 2 * LANES] += jnp.where(lane < HALO, part, 0.0)
    for layer, row, part in pieces(after, 2, rows):
        here = slice(row, row + part.shape[0])
        acc[layer, here, width - 2 * LANES : width - LANES] += jnp.where(lane >= LANES - HALO, part, 0.0)
    odd = is_odd("row")
    for k in (0, 1):
        up = acc[k, 0:HALO, LANES : width - LANES]
        down = acc[k, rows - HALO : rows, LANES : width - LANES]
        to_inner[k] = jnp.where(odd, up, down)
        to_outer[k] = jnp.where(odd, down, up)


def new_rows(cells, acc, extra, start, size, new_re, new_im):
    here = slice(HALO + start, HALO + start + size)
    middle = slice(LANES, acc.shape[2] - LANES)
    part = [acc[k, here, middle] for k in range(acc.shape[0])]
    if extra is not None:
        part[:2] = [part[k] + extra[k] for k in (0, 1)]
    scale = 1.0 / (part[2] + ridge)
    new_re[start : start + size, :] = cells[0, here, middle] - part[0] * scale
    new_im[start : start + size, :] = cells[1, here, middle] - part[1] * scale


def finish_inner(cells, acc, new_re, new_im, near_re, near_im, sems):
    tile_r = near_re.shape[0]
    new_rows(cells, acc, None, HALO, tile_r - 2 * HALO, near_re, near_im)
    rows = slice(HALO, tile_r - HALO)
    finish_all(fetch([(near_re.at[rows], new_re.at[rows]), (near_im.at[rows], new_im.at[rows])], sems))


def finish_edges(cells, acc, by_inner, by_outer, re_in, im_in, new_re, new_im, near_re, near_im, sems):
    tile_r = near_re.shape[0]
    copies = []
    for i, (start, extra) in enumerate(zip((0, tile_r - HALO), received(by_inner, by_outer, "row"))):
        new_rows(cells, acc, extra, start, HALO, near_re, near_im)
        rows = slice(start, start + HALO)
        pairs = ((near_re.at[rows], new_re.at[rows]), (near_im.at[rows], new_im.at[rows]))
        copies += fetch(pairs, sems.at[2 * i : 2 * i + 2])
    finish_all(copies)


def swap(to_inner, to_outer, axis, gather):
    devices = lax.axis_size(axis)
    inner = [(i, i + 1) for i in range(0, devices, 2)]
    outer = [(i, i + 1) for i in range(1, devices - 1, 2)]
    by_outer = lax.ppermute(to_outer, axis, outer + [(j, i) for i, j in outer])
    if gather:
        by_inner = lax.all_gather(to_inner, axis, axis_index_groups=[list(pair) for pair in inner])
    else:
        by_inner = lax.ppermute(to_inner, axis, inner + [(j, i) for i, j in inner])
    return by_inner, by_outer


def far(x):
    return pltpu.with_memory_space_constraint(x, pltpu.HBM)


def f32(*shape):
    return jax.ShapeDtypeStruct(shape, jnp.float32)


def shards(object_re, object_im, probe_re, probe_im, frames, counts, offsets, frame_index):
    tile_r, tile_c = object_re.shape
    rows, width = tile_r + 2 * HALO, tile_c + 2 * LANES
    layers = 3
    slots = offsets.shape[2]
    table = jnp.asarray(transform_tables())
    frames = frames.reshape(frames.shape[2:])
    cells_shape, acc_shape = f32(2, rows, width), f32(layers, rows, width)
    dma = pltpu.SemaphoreType.DMA

    places = jnp.swapaxes(offsets, 2, 3)
    edge = f32(2 * HALO + MARKS, tile_c)
    to_inner, to_outer, marked = pl.pallas_call(
        row_edges,
        out_shape=(edge, edge, jax.ShapeDtypeStruct((3, slots), jnp.int32)),
        in_specs=[SMEM] + [HBM] * 4,
        out_specs=(VMEM, VMEM, VMEM),
        scratch_shapes=[
            pltpu.VMEM(places.shape, jnp.int32), pltpu.VMEM(frame_index.shape, jnp.int32), dma((6,)),
        ],
        compiler_params=SMALL,
        name="row_edges",
    )(counts, far(object_re), far(object_im), far(places), far(frame_index))
    by_inner, by_outer = swap(to_inner, to_outer, "row", True)

    cells, *fixed = pl.pallas_call(
        load_state,
        out_shape=(
            cells_shape, f32(*probe_re.shape), f32(*probe_im.shape),
            jax.ShapeDtypeStruct(table.shape, table.dtype), jax.ShapeDtypeStruct(frames.shape, frames.dtype),
        ),
        in_specs=[HBM] * 6,
        out_specs=(VMEM,) * 5,
        scratch_shapes=[dma((6,))],
        compiler_params=SMALL,
        cost_estimate=BUSY,
        name="load_state",
    )(*map(far, (object_re, object_im, probe_re, probe_im, table, frames)))

    strip = pltpu.VMEM((2 * rows, LANES), jnp.float32)
    packed = f32(2 * rows // GROUPS + MARKS, LANES)
    cells, marks, to_inner, to_outer = pl.pallas_call(
        row_halos,
        out_shape=(cells_shape, f32(MARKS, LANES), packed, packed),
        in_specs=[VMEM] * 4,
        out_specs=(VMEM,) * 4,
        scratch_shapes=[strip],
        input_output_aliases={0: 0},
        compiler_params=SMALL,
        name="row_halos",
    )(cells, to_outer, by_inner, by_outer)
    edges = swap(to_inner, to_outer, "col", False)

    order = pltpu.SMEM((slots,), jnp.int32)
    acc = pl.pallas_call(
        windows_before,
        out_shape=acc_shape,
        in_specs=[SMEM] + [VMEM] * 5,
        out_specs=VMEM,
        scratch_shapes=[order, pltpu.VMEM(probe_re.shape, jnp.float32)],
        compiler_params=PARAMS,
        cost_estimate=BUSY,
        name="windows_before",
    )(marked, cells, *fixed)

    packed = f32(2 * rows // GROUPS, LANES)
    cells, acc, to_inner, to_outer = pl.pallas_call(
        windows_over_edge,
        out_shape=(cells_shape, acc_shape, packed, packed),
        in_specs=[SMEM] + [VMEM] * 8,
        out_specs=(VMEM,) * 4,
        scratch_shapes=[order, strip],
        input_output_aliases={1: 0, 2: 1},
        compiler_params=PARAMS,
        cost_estimate=BUSY,
        name="windows_over_edge",
    )(marked, cells, acc, *fixed, *edges)
    by_inner, by_outer = swap(to_inner, to_outer, "col", False)

    acc = pl.pallas_call(
        windows_after,
        out_shape=acc_shape,
        in_specs=[SMEM] + [VMEM] * 9,
        out_specs=VMEM,
        scratch_shapes=[
            order, pltpu.VMEM(probe_re.shape, jnp.float32),
            pltpu.VMEM((3, MARKS, LANES), jnp.int32), pltpu.SMEM((3, MARKS, LANES), jnp.int32), dma(()),
        ],
        input_output_aliases={2: 0},
        compiler_params=PARAMS,
        cost_estimate=BUSY,
        name="windows_after",
    )(marked, cells, acc, *fixed, marks, *edges)

    edge = f32(2, HALO, tile_c)
    acc, to_inner, to_outer = pl.pallas_call(
        row_spill,
        out_shape=(acc_shape, edge, edge),
        in_specs=[VMEM] * 3,
        out_specs=(VMEM,) * 3,
        input_output_aliases={0: 0},
        compiler_params=SMALL,
        name="row_spill",
    )(acc, by_inner, by_outer)
    by_inner, by_outer = swap(to_inner, to_outer, "row", True)

    near = [pltpu.VMEM((tile_r, tile_c), jnp.float32)] * 2
    new = (f32(tile_r, tile_c), f32(tile_r, tile_c))
    new_re, new_im = pl.pallas_call(
        finish_inner,
        out_shape=new,
        in_specs=[VMEM] * 2,
        out_specs=(HBM, HBM),
        scratch_shapes=near + [dma((2,))],
        compiler_params=SMALL,
        cost_estimate=BUSY,
        name="finish_inner",
    )(cells, acc)
    return pl.pallas_call(
        finish_edges,
        out_shape=new,
        in_specs=[VMEM] * 4 + [HBM] * 2,
        out_specs=(HBM, HBM),
        scratch_shapes=near + [dma((4,))],
        input_output_aliases={4: 0, 5: 1},
        compiler_params=SMALL,
        name="finish_edges",
    )(cells, acc, by_inner, by_outer, far(new_re), far(new_im))


def solution(mesh):
    return jax.shard_map(
        shards,
        mesh=mesh,
        in_specs=(
            P("row", "col"),
            P("row", "col"),
            P(),
            P(),
            P("row", "col", None, None, None),
            P("row", "col"),
            P("row", "col", None, None),
            P("row", "col", None),
        ),
        out_specs=(P("row", "col"), P("row", "col")),
        check_vma=False,
    )
```

```python
import functools
import math

import jax
import jax.numpy as jnp
import ml_dtypes
import numpy as np
from jax import lax
from jax.experimental import pallas as pl
from jax.experimental.pallas import tpu as pltpu
from jax.sharding import PartitionSpec as P

P_SIZE = 256
HALF = P_SIZE // 2
HALO = 32
LANES = 128
GROUPS = LANES // HALO
MARKS = 8
PAIR = 2

floor_amp = 0.5
ridge = 1.0

VMEM = pl.BlockSpec(memory_space=pltpu.VMEM)
SMEM = pl.BlockSpec(memory_space=pltpu.SMEM)
HBM = pl.BlockSpec(memory_space=pltpu.HBM)
PARAMS = pltpu.CompilerParams(vmem_limit_bytes=32 * 1024 * 1024)
SMALL = pltpu.CompilerParams(vmem_limit_bytes=16 * 1024 * 1024)
BUSY = pl.CostEstimate(flops=4_000_000_000, bytes_accessed=8_000_000, transcendentals=0)


def transform_tables():
    index = np.arange(HALF)
    plain = []
    for parity in (0, 1):
        angle = 2.0 * math.pi / P_SIZE * (index[:, None] * (2 * index[None, :] + parity) % P_SIZE)
        cos, sin = np.cos(angle), np.sin(angle)
        plain.append(np.block([[cos, -sin], [sin, cos]]) / math.sqrt(P_SIZE))
    parts = []
    for table in plain + [t.T for t in plain]:
        high = table.astype(np.float32).astype(ml_dtypes.bfloat16)
        low = (table - high.astype(np.float64)).astype(np.float32).astype(ml_dtypes.bfloat16)
        parts += [high, low]
    order = np.concatenate([np.arange(0, P_SIZE, 2), np.arange(1, P_SIZE, 2)])
    sort = np.zeros((P_SIZE, P_SIZE), np.float32)
    sort[np.arange(P_SIZE), order] = 1.0
    parts += [sort.astype(ml_dtypes.bfloat16), sort.T.astype(ml_dtypes.bfloat16)]
    return np.stack(parts)


def lane_index(rows):
    return lax.broadcasted_iota(jnp.int32, (rows, LANES), 1)


def pack_lanes(ref, rows, first):
    lane = lane_index(rows)
    packed = None
    for g in range(GROUPS):
        part = ref[g * rows : (g + 1) * rows, :]
        if g:
            part = pltpu.roll(part, HALO * g, 1)
        low = (first + HALO * g) % LANES
        mine = (lane >= low) & (lane < low + HALO)
        packed = part if packed is None else jnp.where(mine, part, packed)
    return packed


def unpack_lanes(packed, group):
    return pltpu.roll(packed, LANES - HALO * group, 1) if group else packed


def split(x):
    high = x.astype(jnp.bfloat16)
    return high, (x - high.astype(jnp.float32)).astype(jnp.bfloat16)


def product(left, right):
    return jnp.dot(left, right, preferred_element_type=jnp.float32)


def times_table(x, table, which):
    high, low = split(x)
    t_high, t_low = table[2 * which], table[2 * which + 1]
    return product(high, t_high) + (product(high, t_low) + product(low, t_high))


def table_times(table, which, x):
    high, low = split(x)
    t_high, t_low = table[2 * which], table[2 * which + 1]
    return product(t_high, high) + (product(t_low, high) + product(t_high, low))


def beside(*blocks):
    return jnp.concatenate(blocks, axis=1)


def below(*blocks):
    return jnp.concatenate(blocks, axis=0)


def ends(x):
    return x[:, :HALF], x[:, HALF:]


def forward_columns(exit_re, exit_im, table):
    re_lo, re_hi = ends(exit_re)
    im_lo, im_hi = ends(exit_im)
    even = times_table(beside(re_lo + re_hi, im_lo + im_hi), table, 0)
    odd = times_table(beside(re_lo - re_hi, im_lo - im_hi), table, 1)
    return even, odd


def forward_rows(even, odd, table):
    out = []
    for parity in (0, 1):
        if parity == 0:
            se, so = even[:HALF] + even[HALF:], odd[:HALF] + odd[HALF:]
        else:
            se, so = even[:HALF] - even[HALF:], odd[:HALF] - odd[HALF:]
        e_re, e_im = ends(se)
        o_re, o_im = ends(so)
        out.append(table_times(table, 2 + parity, below(beside(e_re, o_re), beside(e_im, o_im))))
    return out


def residual(far, frame):
    out = []
    for parity in (0, 1):
        re, im = far[parity][:HALF], far[parity][HALF:]
        level = jnp.maximum(re * re + im * im, floor_amp * floor_amp)
        inten = frame[parity * HALF : (parity + 1) * HALF]
        factor = 1.0 - inten * lax.rsqrt(inten * level)
        out.append(below(re * factor, im * factor))
    return out


def back_rows(res, table):
    first = table_times(table, 0, res[0])
    second = table_times(table, 1, res[1])
    upper, lower = first + second, first - second
    out = []
    for cols in (slice(0, HALF), slice(HALF, P_SIZE)):
        out.append(
            below(
                beside(upper[:HALF, cols], upper[HALF:, cols]),
                beside(lower[:HALF, cols], lower[HALF:, cols]),
            )
        )
    return out


def back_columns(parts, table):
    even = times_table(parts[0], table, 2)
    odd = times_table(parts[1], table, 3)
    lo, hi = even + odd, even - odd
    return beside(lo[:, :HALF], hi[:, :HALF]), beside(lo[:, HALF:], hi[:, HALF:])


def is_odd(axis):
    return lax.rem(lax.axis_index(axis), 2) == 1


def fetch(pairs, sems):
    copies = [pltpu.make_async_copy(far, near, sems.at[i]) for i, (far, near) in enumerate(pairs)]
    for copy in copies:
        copy.start()
    return copies


def finish_all(copies):
    for copy in copies:
        copy.wait()


def row_edges(counts, obj_re, obj_im, offsets, chosen, to_inner, to_outer, marked, places, frame_of, sems):
    tile_r = obj_re.shape[0]
    odd = is_odd("row")
    low = pl.multiple_of(jnp.where(odd, 0, tile_r - HALO), 16)
    high = pl.multiple_of(jnp.where(odd, tile_r - HALO, 0), 16)
    pairs = [(offsets, places), (chosen, frame_of)]
    for k, ref in enumerate((obj_re, obj_im)):
        rows = slice(k * HALO, (k + 1) * HALO)
        pairs.append((ref.at[pl.ds(high, HALO)], to_outer.at[rows]))
        pairs.append((ref.at[pl.ds(low, HALO)], to_inner.at[rows]))
    copies = fetch(pairs, sems)
    finish_all(copies[:2])
    place = places[0, 0]
    live = lax.broadcasted_iota(jnp.int32, place.shape, 1) < counts[0, 0]
    place = jnp.where(live, place, 2 * tile_r)
    marked[0:2, :] = place
    marked[2:3, :] = frame_of[0]
    for message in (to_inner, to_outer):
        message[2 * HALO : 2 * HALO + 2, 0 : place.shape[1]] = place.astype(jnp.float32)
    finish_all(copies[2:])


def window_place(slots, slot):
    row = pl.multiple_of(slots[0, slot] + HALO, 16)
    col = slots[1, slot] + LANES
    turn = lax.rem(col, LANES)
    return row, pl.multiple_of(col - turn, LANES), turn


def add_window(acc, layer, where, keep, term, tiles=(0, 1, 2)):
    row, base, _ = where
    lo, hi = ends(term)
    parts = (jnp.where(keep, lo, 0.0), hi, jnp.where(keep, 0.0, lo))
    for t in tiles:
        acc[layer, pl.ds(row, term.shape[0]), pl.ds(base + t * LANES, LANES)] += parts[t]


def load_state(
    obj_re, obj_im, probe_re_far, probe_im_far, table_far, frames_far,
    cells, probe_re, probe_im, table, frames, sems,
):
    tile_r, tile_c = obj_re.shape
    inner = slice(HALO, HALO + tile_r)
    middle = slice(LANES, LANES + tile_c)
    pairs = (
        (table_far, table),
        (frames_far, frames),
        (obj_re, cells.at[0, inner, middle]),
        (obj_im, cells.at[1, inner, middle]),
        (probe_re_far, probe_re),
        (probe_im_far, probe_im),
    )
    finish_all(fetch(pairs, sems))


def fill_strip(strip, parts):
    done = 0
    for part in parts:
        strip[done : done + part.shape[0], :] = part
        done += part.shape[0]


def send_columns(to_left, to_right, to_inner, to_outer):
    odd = is_odd("col")
    to_inner[0 : to_left.shape[0], :] = jnp.where(odd, to_left, to_right)
    to_outer[0 : to_left.shape[0], :] = jnp.where(odd, to_right, to_left)


def received(by_inner, by_outer, axis):
    odd = is_odd(axis)
    index = lax.axis_index(axis)
    inside = (index > 0) & (index < lax.axis_size(axis) - 1)
    by_outer = jnp.where(inside, by_outer[...], 0.0)
    if len(by_inner.shape) > len(by_outer.shape):
        before, after = by_inner[0], by_inner[1]
    else:
        before = after = by_inner[...]
    return jnp.where(odd, before, by_outer), jnp.where(odd, by_outer, after)


def pieces(packed, layers, rows):
    group_rows = layers * rows // GROUPS
    for g in range(GROUPS):
        part = unpack_lanes(packed, g)
        done = 0
        while done < group_rows:
            layer, row = divmod(g * group_rows + done, rows)
            size = min(group_rows - done, rows - row)
            yield layer, row, part[done : done + size]
            done += size


def row_halos(cells_in, own, by_inner, by_outer, cells, marks, to_inner, to_outer, strip):
    rows, width = cells.shape[1:]
    middle = slice(LANES, width - LANES)
    before, after = received(by_inner, by_outer, "row")
    for k in (0, 1):
        cells[k, 0:HALO, middle] = before[k * HALO : (k + 1) * HALO]
        cells[k, rows - HALO : rows, middle] = after[k * HALO : (k + 1) * HALO]
    first_mark = 2 * HALO
    for i, message in enumerate((own[...], before, after)):
        marks[2 * i : 2 * i + 2, :] = message[first_mark : first_mark + 2, 0:LANES]
    group_rows = 2 * rows // GROUPS
    first, last = slice(LANES, 2 * LANES), slice(width - 2 * LANES, width - LANES)
    fill_strip(strip, (cells[0, :, first], cells[1, :, first]))
    to_left = pack_lanes(strip, group_rows, 0)
    fill_strip(strip, (cells[0, :, last], cells[1, :, last]))
    to_right = pack_lanes(strip, group_rows, LANES - HALO)
    send_columns(to_left, to_right, to_inner, to_outer)
    to_inner[group_rows:, :] = marks[...]
    to_outer[group_rows:, :] = marks[...]


def live_slots(slots, cells):
    tile_r = cells.shape[1] - 2 * HALO
    count = jnp.int32(0)
    for slot in range(slots.shape[1]):
        count += (slots[0, slot] < tile_r).astype(jnp.int32)
    return count


def run_windows(wanted, slots, cells, acc, probe_re, probe_im, table, frames, order):
    tile_c = cells.shape[2] - 2 * LANES
    count = live_slots(slots, cells)
    every = range(slots.shape[1])
    over = []
    for slot in every:
        col = slots[1, slot]
        over.append((col < 0) | (col > tile_c - P_SIZE))
    total = jnp.int32(0)
    for slot in every:
        total += ((slot < count) & ~over[slot]).astype(jnp.int32)
    limit = jnp.where(total < len(every) - 1, PAIR, 2 * PAIR)
    seen, found = jnp.int32(0), jnp.int32(0)
    for slot in every:
        live = slot < count
        mine = live & wanted(over[slot], seen, limit)

        @pl.when(mine)
        def _():
            order[found] = slot

        seen += (live & ~over[slot]).astype(jnp.int32)
        found += mine.astype(jnp.int32)

    lane = lane_index(P_SIZE)

    def load(slot):
        where = row, base, turn = window_place(slots, slot)
        keep = lane >= turn
        w_re = pltpu.roll(probe_re[...], turn, 1)
        w_im = pltpu.roll(probe_im[...], turn, 1)
        patch = []
        for k in (0, 1):
            block = cells[k, pl.ds(row, P_SIZE), pl.ds(base, 3 * LANES)]
            patch.append(
                beside(jnp.where(keep, block[:, :LANES], block[:, 2 * LANES :]), block[:, LANES : 2 * LANES])
            )
        exit_re = w_re * patch[0] - w_im * patch[1]
        exit_im = w_re * patch[1] + w_im * patch[0]
        return (where, keep, w_re, w_im), exit_re, exit_im

    def frame_of(slot):
        sort, unsort = table[8], table[9]
        half = product(sort, frames[slots[2, slot]]).astype(jnp.bfloat16)
        return product(half, unsort)

    def place(at, back_re, back_im):
        where, keep, w_re, w_im = at
        add_window(acc, 0, where, keep, w_re * back_re + w_im * back_im)
        add_window(acc, 1, where, keep, w_re * back_im - w_im * back_re)

    def step(group):
        frame = [frame_of(slot) for slot in group]
        loaded = [load(slot) for slot in group]
        state = [forward_columns(x[1], x[2], table) for x in loaded]
        state = [forward_rows(*x, table) for x in state]
        state = [residual(x, f) for x, f in zip(state, frame)]
        state = [back_rows(x, table) for x in state]
        state = [back_columns(x, table) for x in state]
        for x, back in zip(loaded, state):
            place(x[0], *back)

    def pair_step(pair, carry):
        step([order[pair * PAIR + i] for i in range(PAIR)])
        return carry

    lax.fori_loop(0, found // PAIR, pair_step, 0)

    @pl.when(found % PAIR == 1)
    def _():
        step([order[found - 1]])


def windows_before(
    slots, cells, probe_re, probe_im, table, frames, acc, order, power,
):
    acc[...] = jnp.zeros_like(acc)
    power[...] = probe_re[...] * probe_re[...] + probe_im[...] * probe_im[...]
    lane = lane_index(P_SIZE)

    def step(slot, carry):
        where = window_place(slots, slot)
        add_window(acc, 2, where, lane >= where[2], pltpu.roll(power[...], where[2], 1))
        return carry

    lax.fori_loop(0, live_slots(slots, cells), step, 0)
    run_windows(
        lambda over, seen, limit: ~over & (seen < limit),
        slots, cells, acc, probe_re, probe_im, table, frames, order,
    )


def reaching(place, right, tile_r, tile_c):
    shape = place.shape
    index = lax.broadcasted_iota(jnp.int32, shape, 0)
    lane = lax.broadcasted_iota(jnp.int32, shape, 1)
    col = pltpu.roll(place, shape[0] - 1, 0)
    low = jnp.where(index == 2, tile_r - P_SIZE, -tile_r).astype(jnp.float32)
    high = jnp.where(index == 4, 0, tile_r).astype(jnp.float32)
    reaches = (lane < MARKS) & (index % 2 == 0) & (index < 6) & (place > low) & (place < high)
    if right < 0:
        reaches &= col > tile_c - P_SIZE
    if right > 0:
        reaches &= col < 0
    bit = lax.shift_left(jnp.ones(shape, jnp.int32), jnp.minimum(lane, MARKS)).astype(jnp.float32)
    bits = jnp.sum(jnp.where(reaches, bit, 0.0), axis=1, keepdims=True)
    return jnp.where(lane < MARKS, place, bits).astype(jnp.int32)


def add_neighbours_light(places, acc, power):
    rows, width = acc.shape[1:]
    tile_r, tile_c = rows - 2 * HALO, width - 2 * LANES
    for right in (-1, 0, 1):
        for i, down in enumerate((0, -1, 1)):
            if not right and not down:
                continue
            first, last = {-1: (P_SIZE - HALO, P_SIZE), 0: (0, P_SIZE), 1: (0, HALO)}[down]
            tiles = {-1: (2,), 0: (0, 1, 2), 1: (0,)}[right]
            lane = lane_index(last - first)
            bits = places[right + 1, 2 * i, MARKS]

            def step(slot, carry):
                row, col = places[right + 1, 2 * i, slot], places[right + 1, 2 * i + 1, slot]

                @pl.when(lax.shift_right_logical(bits, slot) % 2 == 1)
                def _():
                    turn = lax.rem(col + LANES, LANES)
                    at = pl.multiple_of(row + HALO + (down * tile_r + first), 16)
                    base = pl.multiple_of(col + LANES - turn + right * tile_c, LANES)
                    part = pltpu.roll(power[first:last, :], turn, 1)
                    add_window(acc, 2, (at, base, turn), lane >= turn, part, tiles)

                return carry

            @pl.when(bits != 0)
            def _():
                lax.fori_loop(0, MARKS, step, 0)


def windows_after(
    slots, cells, acc_in, probe_re, probe_im, table, frames, marks, by_inner, by_outer,
    acc, order, power, whole, places, sem,
):
    rows, width = acc.shape[1:]
    before, after = received(by_inner, by_outer, "col")
    for i, part in enumerate((before[-MARKS:], marks[...], after[-MARKS:])):
        whole[i] = reaching(part, i - 1, rows - 2 * HALO, width - 2 * LANES)
    copy = pltpu.make_async_copy(whole, places, sem)
    copy.start()
    power[...] = probe_re[...] * probe_re[...] + probe_im[...] * probe_im[...]
    run_windows(
        lambda over, seen, limit: ~over & (seen >= limit),
        slots, cells, acc, probe_re, probe_im, table, frames, order,
    )
    copy.wait()
    add_neighbours_light(places, acc, power)


def windows_over_edge(
    slots, cells_in, acc_in, probe_re, probe_im, table, frames, by_inner, by_outer,
    cells, acc, to_inner, to_outer, order, strip,
):
    rows, width = acc.shape[1:]
    before, after = received(by_inner, by_outer, "col")
    for layer, row, part in pieces(before, 2, rows):
        cells[layer, row : row + part.shape[0], 0:LANES] = part
    for layer, row, part in pieces(after, 2, rows):
        cells[layer, row : row + part.shape[0], width - LANES :] = part
    run_windows(
        lambda over, seen, limit: over,
        slots, cells, acc, probe_re, probe_im, table, frames, order,
    )
    group_rows = 2 * rows // GROUPS
    fill_strip(strip, (acc[0, :, 0:LANES], acc[1, :, 0:LANES]))
    to_left = pack_lanes(strip, group_rows, LANES - HALO)
    fill_strip(strip, (acc[0, :, width - LANES :], acc[1, :, width - LANES :]))
    to_right = pack_lanes(strip, group_rows, 0)
    send_columns(to_left, to_right, to_inner, to_outer)


def row_spill(acc_in, by_inner, by_outer, acc, to_inner, to_outer):
    rows, width = acc.shape[1:]
    before, after = received(by_inner, by_outer, "col")
    lane = lane_index(rows)[0:1]
    for layer, row, part in pieces(before, 2, rows):
        here = slice(row, row + part.shape[0])
        acc[layer, here, LANES : 2 * LANES] += jnp.where(lane < HALO, part, 0.0)
    for layer, row, part in pieces(after, 2, rows):
        here = slice(row, row + part.shape[0])
        acc[layer, here, width - 2 * LANES : width - LANES] += jnp.where(lane >= LANES - HALO, part, 0.0)
    odd = is_odd("row")
    for k in (0, 1):
        up = acc[k, 0:HALO, LANES : width - LANES]
        down = acc[k, rows - HALO : rows, LANES : width - LANES]
        to_inner[k] = jnp.where(odd, up, down)
        to_outer[k] = jnp.where(odd, down, up)


def new_rows(cells, acc, extra, start, size, new_re, new_im):
    here = slice(HALO + start, HALO + start + size)
    middle = slice(LANES, acc.shape[2] - LANES)
    part = [acc[k, here, middle] for k in range(acc.shape[0])]
    if extra is not None:
        part[:2] = [part[k] + extra[k] for k in (0, 1)]
    scale = 1.0 / (part[2] + ridge)
    new_re[start : start + size, :] = cells[0, here, middle] - part[0] * scale
    new_im[start : start + size, :] = cells[1, here, middle] - part[1] * scale


def finish_inner(cells, acc, new_re, new_im, near_re, near_im, sems):
    tile_r = near_re.shape[0]
    new_rows(cells, acc, None, HALO, tile_r - 2 * HALO, near_re, near_im)
    rows = slice(HALO, tile_r - HALO)
    finish_all(fetch([(near_re.at[rows], new_re.at[rows]), (near_im.at[rows], new_im.at[rows])], sems))


def finish_edges(cells, acc, by_inner, by_outer, re_in, im_in, new_re, new_im, near_re, near_im, sems):
    tile_r = near_re.shape[0]
    copies = []
    for i, (start, extra) in enumerate(zip((0, tile_r - HALO), received(by_inner, by_outer, "row"))):
        new_rows(cells, acc, extra, start, HALO, near_re, near_im)
        rows = slice(start, start + HALO)
        pairs = ((near_re.at[rows], new_re.at[rows]), (near_im.at[rows], new_im.at[rows]))
        copies += fetch(pairs, sems.at[2 * i : 2 * i + 2])
    finish_all(copies)


def swap(to_inner, to_outer, axis, gather):
    devices = lax.axis_size(axis)
    inner = [(i, i + 1) for i in range(0, devices, 2)]
    outer = [(i, i + 1) for i in range(1, devices - 1, 2)]
    ends = [(0, 0), (devices - 1, devices - 1)]
    by_outer = lax.ppermute(to_outer, axis, outer + [(j, i) for i, j in outer] + ends)
    if gather:
        by_inner = lax.all_gather(to_inner, axis, axis_index_groups=[list(pair) for pair in inner])
    else:
        by_inner = lax.ppermute(to_inner, axis, inner + [(j, i) for i, j in inner])
    return by_inner, by_outer


def far(x):
    return pltpu.with_memory_space_constraint(x, pltpu.HBM)


def f32(*shape):
    return jax.ShapeDtypeStruct(shape, jnp.float32)


def shards(object_re, object_im, probe_re, probe_im, frames, counts, offsets, frame_index):
    tile_r, tile_c = object_re.shape
    rows, width = tile_r + 2 * HALO, tile_c + 2 * LANES
    layers = 3
    slots = offsets.shape[2]
    table = jnp.asarray(transform_tables())
    frames = frames.reshape(frames.shape[2:])
    cells_shape, acc_shape = f32(2, rows, width), f32(layers, rows, width)
    dma = pltpu.SemaphoreType.DMA

    places = jnp.swapaxes(offsets, 2, 3)
    edge = f32(2 * HALO + MARKS, tile_c)
    to_inner, to_outer, marked = pl.pallas_call(
        row_edges,
        out_shape=(edge, edge, jax.ShapeDtypeStruct((3, slots), jnp.int32)),
        in_specs=[SMEM] + [HBM] * 4,
        out_specs=(VMEM, VMEM, VMEM),
        scratch_shapes=[
            pltpu.VMEM(places.shape, jnp.int32), pltpu.VMEM(frame_index.shape, jnp.int32), dma((6,)),
        ],
        compiler_params=SMALL,
        name="row_edges",
    )(counts, far(object_re), far(object_im), far(places), far(frame_index))
    by_inner, by_outer = swap(to_inner, to_outer, "row", True)

    cells, *fixed = pl.pallas_call(
        load_state,
        out_shape=(
            cells_shape, f32(*probe_re.shape), f32(*probe_im.shape),
            jax.ShapeDtypeStruct(table.shape, table.dtype), jax.ShapeDtypeStruct(frames.shape, frames.dtype),
        ),
        in_specs=[HBM] * 6,
        out_specs=(VMEM,) * 5,
        scratch_shapes=[dma((6,))],
        compiler_params=SMALL,
        cost_estimate=BUSY,
        name="load_state",
    )(*map(far, (object_re, object_im, probe_re, probe_im, table, frames)))

    strip = pltpu.VMEM((2 * rows, LANES), jnp.float32)
    packed = f32(2 * rows // GROUPS + MARKS, LANES)
    cells, marks, to_inner, to_outer = pl.pallas_call(
        row_halos,
        out_shape=(cells_shape, f32(MARKS, LANES), packed, packed),
        in_specs=[VMEM] * 4,
        out_specs=(VMEM,) * 4,
        scratch_shapes=[strip],
        input_output_aliases={0: 0},
        compiler_params=SMALL,
        name="row_halos",
    )(cells, to_outer, by_inner, by_outer)
    edges = swap(to_inner, to_outer, "col", False)

    order = pltpu.SMEM((slots,), jnp.int32)
    acc = pl.pallas_call(
        windows_before,
        out_shape=acc_shape,
        in_specs=[SMEM] + [VMEM] * 5,
        out_specs=VMEM,
        scratch_shapes=[order, pltpu.VMEM(probe_re.shape, jnp.float32)],
        compiler_params=PARAMS,
        cost_estimate=BUSY,
        name="windows_before",
    )(marked, cells, *fixed)

    packed = f32(2 * rows // GROUPS, LANES)
    cells, acc, to_inner, to_outer = pl.pallas_call(
        windows_over_edge,
        out_shape=(cells_shape, acc_shape, packed, packed),
        in_specs=[SMEM] + [VMEM] * 8,
        out_specs=(VMEM,) * 4,
        scratch_shapes=[order, strip],
        input_output_aliases={1: 0, 2: 1},
        compiler_params=PARAMS,
        cost_estimate=BUSY,
        name="windows_over_edge",
    )(marked, cells, acc, *fixed, *edges)
    by_inner, by_outer = swap(to_inner, to_outer, "col", False)

    acc = pl.pallas_call(
        windows_after,
        out_shape=acc_shape,
        in_specs=[SMEM] + [VMEM] * 9,
        out_specs=VMEM,
        scratch_shapes=[
            order, pltpu.VMEM(probe_re.shape, jnp.float32),
            pltpu.VMEM((3, MARKS, LANES), jnp.int32), pltpu.SMEM((3, MARKS, LANES), jnp.int32), dma(()),
        ],
        input_output_aliases={2: 0},
        compiler_params=PARAMS,
        cost_estimate=BUSY,
        name="windows_after",
    )(marked, cells, acc, *fixed, marks, *edges)

    edge = f32(2, HALO, tile_c)
    acc, to_inner, to_outer = pl.pallas_call(
        row_spill,
        out_shape=(acc_shape, edge, edge),
        in_specs=[VMEM] * 3,
        out_specs=(VMEM,) * 3,
        input_output_aliases={0: 0},
        compiler_params=SMALL,
        name="row_spill",
    )(acc, by_inner, by_outer)
    by_inner, by_outer = swap(to_inner, to_outer, "row", True)

    near = [pltpu.VMEM((tile_r, tile_c), jnp.float32)] * 2
    new = (f32(tile_r, tile_c), f32(tile_r, tile_c))
    new_re, new_im = pl.pallas_call(
        finish_inner,
        out_shape=new,
        in_specs=[VMEM] * 2,
        out_specs=(HBM, HBM),
        scratch_shapes=near + [dma((2,))],
        compiler_params=SMALL,
        cost_estimate=BUSY,
        name="finish_inner",
    )(cells, acc)
    return pl.pallas_call(
        finish_edges,
        out_shape=new,
        in_specs=[VMEM] * 4 + [HBM] * 2,
        out_specs=(HBM, HBM),
        scratch_shapes=near + [dma((4,))],
        input_output_aliases={4: 0, 5: 1},
        compiler_params=SMALL,
        name="finish_edges",
    )(cells, acc, by_inner, by_outer, far(new_re), far(new_im))


def solution(mesh):
    return jax.shard_map(
        shards,
        mesh=mesh,
        in_specs=(
            P("row", "col"),
            P("row", "col"),
            P(),
            P(),
            P("row", "col", None, None, None),
            P("row", "col"),
            P("row", "col", None, None),
            P("row", "col", None),
        ),
        out_specs=(P("row", "col"), P("row", "col")),
        check_vma=False,
    )
```

```python
import functools
import math

import jax
import jax.numpy as jnp
import ml_dtypes
import numpy as np
from jax import lax
from jax.experimental import pallas as pl
from jax.experimental.pallas import tpu as pltpu
from jax.sharding import PartitionSpec as P

P_SIZE = 256
HALF = P_SIZE // 2
HALO = 32
LANES = 128
GROUPS = LANES // HALO
MARKS = 8
PAIR = 2

floor_amp = 0.5
ridge = 1.0

VMEM = pl.BlockSpec(memory_space=pltpu.VMEM)
SMEM = pl.BlockSpec(memory_space=pltpu.SMEM)
HBM = pl.BlockSpec(memory_space=pltpu.HBM)
PARAMS = pltpu.CompilerParams(vmem_limit_bytes=32 * 1024 * 1024)
SMALL = pltpu.CompilerParams(vmem_limit_bytes=16 * 1024 * 1024)
BUSY = pl.CostEstimate(flops=4_000_000_000, bytes_accessed=8_000_000, transcendentals=0)


def transform_tables():
    index = np.arange(HALF)
    plain = []
    for parity in (0, 1):
        angle = 2.0 * math.pi / P_SIZE * (index[:, None] * (2 * index[None, :] + parity) % P_SIZE)
        cos, sin = np.cos(angle), np.sin(angle)
        plain.append(np.block([[cos, -sin], [sin, cos]]) / math.sqrt(P_SIZE))
    parts = []
    for table in plain + [t.T for t in plain]:
        high = table.astype(np.float32).astype(ml_dtypes.bfloat16)
        low = (table - high.astype(np.float64)).astype(np.float32).astype(ml_dtypes.bfloat16)
        parts += [high, low]
    order = np.concatenate([np.arange(0, P_SIZE, 2), np.arange(1, P_SIZE, 2)])
    sort = np.zeros((P_SIZE, P_SIZE), np.float32)
    sort[np.arange(P_SIZE), order] = 1.0
    parts += [sort.astype(ml_dtypes.bfloat16), sort.T.astype(ml_dtypes.bfloat16)]
    return np.stack(parts)


def lane_index(rows):
    return lax.broadcasted_iota(jnp.int32, (rows, LANES), 1)


def pack_lanes(ref, rows, first):
    lane = lane_index(rows)
    packed = None
    for g in range(GROUPS):
        part = ref[g * rows : (g + 1) * rows, :]
        if g:
            part = pltpu.roll(part, HALO * g, 1)
        low = (first + HALO * g) % LANES
        mine = (lane >= low) & (lane < low + HALO)
        packed = part if packed is None else jnp.where(mine, part, packed)
    return packed


def unpack_lanes(packed, group):
    return pltpu.roll(packed, LANES - HALO * group, 1) if group else packed


def split(x):
    high = x.astype(jnp.bfloat16)
    return high, (x - high.astype(jnp.float32)).astype(jnp.bfloat16)


def product(left, right):
    return jnp.dot(left, right, preferred_element_type=jnp.float32)


def times_table(x, table, which):
    high, low = split(x)
    t_high, t_low = table[2 * which], table[2 * which + 1]
    return product(high, t_high) + (product(high, t_low) + product(low, t_high))


def table_times(table, which, x):
    high, low = split(x)
    t_high, t_low = table[2 * which], table[2 * which + 1]
    return product(t_high, high) + (product(t_low, high) + product(t_high, low))


def beside(*blocks):
    return jnp.concatenate(blocks, axis=1)


def below(*blocks):
    return jnp.concatenate(blocks, axis=0)


def ends(x):
    return x[:, :HALF], x[:, HALF:]


def forward_columns(exit_re, exit_im, table):
    re_lo, re_hi = ends(exit_re)
    im_lo, im_hi = ends(exit_im)
    even = times_table(beside(re_lo + re_hi, im_lo + im_hi), table, 0)
    odd = times_table(beside(re_lo - re_hi, im_lo - im_hi), table, 1)
    return even, odd


def forward_rows(even, odd, table):
    out = []
    for parity in (0, 1):
        if parity == 0:
            se, so = even[:HALF] + even[HALF:], odd[:HALF] + odd[HALF:]
        else:
            se, so = even[:HALF] - even[HALF:], odd[:HALF] - odd[HALF:]
        e_re, e_im = ends(se)
        o_re, o_im = ends(so)
        out.append(table_times(table, 2 + parity, below(beside(e_re, o_re), beside(e_im, o_im))))
    return out


def residual(far, frame):
    out = []
    for parity in (0, 1):
        re, im = far[parity][:HALF], far[parity][HALF:]
        level = jnp.maximum(re * re + im * im, floor_amp * floor_amp)
        inten = frame[parity * HALF : (parity + 1) * HALF]
        factor = 1.0 - inten * lax.rsqrt(inten * level)
        out.append(below(re * factor, im * factor))
    return out


def back_rows(res, table):
    first = table_times(table, 0, res[0])
    second = table_times(table, 1, res[1])
    upper, lower = first + second, first - second
    out = []
    for cols in (slice(0, HALF), slice(HALF, P_SIZE)):
        out.append(
            below(
                beside(upper[:HALF, cols], upper[HALF:, cols]),
                beside(lower[:HALF, cols], lower[HALF:, cols]),
            )
        )
    return out


def back_columns(parts, table):
    even = times_table(parts[0], table, 2)
    odd = times_table(parts[1], table, 3)
    lo, hi = even + odd, even - odd
    return beside(lo[:, :HALF], hi[:, :HALF]), beside(lo[:, HALF:], hi[:, HALF:])


def is_odd(axis):
    return lax.rem(lax.axis_index(axis), 2) == 1


def fetch(pairs, sems):
    copies = [pltpu.make_async_copy(far, near, sems.at[i]) for i, (far, near) in enumerate(pairs)]
    for copy in copies:
        copy.start()
    return copies


def finish_all(copies):
    for copy in copies:
        copy.wait()


def row_edges(counts, obj_re, obj_im, offsets, chosen, to_inner, to_outer, marked, places, frame_of, sems):
    tile_r = obj_re.shape[0]
    odd = is_odd("row")
    low = pl.multiple_of(jnp.where(odd, 0, tile_r - HALO), 16)
    high = pl.multiple_of(jnp.where(odd, tile_r - HALO, 0), 16)
    pairs = [(offsets, places), (chosen, frame_of)]
    for k, ref in enumerate((obj_re, obj_im)):
        rows = slice(k * HALO, (k + 1) * HALO)
        pairs.append((ref.at[pl.ds(high, HALO)], to_outer.at[rows]))
        pairs.append((ref.at[pl.ds(low, HALO)], to_inner.at[rows]))
    copies = fetch(pairs, sems)
    finish_all(copies[:2])
    place = places[0, 0]
    live = lax.broadcasted_iota(jnp.int32, place.shape, 1) < counts[0, 0]
    place = jnp.where(live, place, 2 * tile_r)
    marked[0:2, :] = place
    marked[2:3, :] = frame_of[0]
    for message in (to_inner, to_outer):
        message[2 * HALO : 2 * HALO + 2, 0 : place.shape[1]] = place.astype(jnp.float32)
    finish_all(copies[2:])


def window_place(slots, slot):
    row = pl.multiple_of(slots[0, slot] + HALO, 16)
    col = slots[1, slot] + LANES
    turn = lax.rem(col, LANES)
    return row, pl.multiple_of(col - turn, LANES), turn


def add_window(acc, layer, where, keep, term, tiles=(0, 1, 2)):
    row, base, _ = where
    lo, hi = ends(term)
    parts = (jnp.where(keep, lo, 0.0), hi, jnp.where(keep, 0.0, lo))
    for t in tiles:
        acc[layer, pl.ds(row, term.shape[0]), pl.ds(base + t * LANES, LANES)] += parts[t]


def load_state(
    obj_re, obj_im, probe_re_far, probe_im_far, table_far, frames_far,
    cells, probe_re, probe_im, table, frames, sems,
):
    tile_r, tile_c = obj_re.shape
    inner = slice(HALO, HALO + tile_r)
    middle = slice(LANES, LANES + tile_c)
    pairs = (
        (table_far, table),
        (frames_far, frames),
        (obj_re, cells.at[0, inner, middle]),
        (obj_im, cells.at[1, inner, middle]),
        (probe_re_far, probe_re),
        (probe_im_far, probe_im),
    )
    finish_all(fetch(pairs, sems))


def fill_strip(strip, parts):
    done = 0
    for part in parts:
        strip[done : done + part.shape[0], :] = part
        done += part.shape[0]


def send_columns(to_left, to_right, to_inner, to_outer):
    odd = is_odd("col")
    to_inner[0 : to_left.shape[0], :] = jnp.where(odd, to_left, to_right)
    to_outer[0 : to_left.shape[0], :] = jnp.where(odd, to_right, to_left)


def received(by_inner, by_outer, axis):
    odd = is_odd(axis)
    index = lax.axis_index(axis)
    inside = (index > 0) & (index < lax.axis_size(axis) - 1)
    by_outer = jnp.where(inside, by_outer[...], 0.0)
    if len(by_inner.shape) > len(by_outer.shape):
        before, after = by_inner[0], by_inner[1]
    else:
        before = after = by_inner[...]
    return jnp.where(odd, before, by_outer), jnp.where(odd, by_outer, after)


def pieces(packed, layers, rows):
    group_rows = layers * rows // GROUPS
    for g in range(GROUPS):
        part = unpack_lanes(packed, g)
        done = 0
        while done < group_rows:
            layer, row = divmod(g * group_rows + done, rows)
            size = min(group_rows - done, rows - row)
            yield layer, row, part[done : done + size]
            done += size


def row_halos(cells_in, own, by_inner, by_outer, cells, marks, to_inner, to_outer, strip):
    rows, width = cells.shape[1:]
    middle = slice(LANES, width - LANES)
    before, after = received(by_inner, by_outer, "row")
    for k in (0, 1):
        cells[k, 0:HALO, middle] = before[k * HALO : (k + 1) * HALO]
        cells[k, rows - HALO : rows, middle] = after[k * HALO : (k + 1) * HALO]
    first_mark = 2 * HALO
    for i, message in enumerate((own[...], before, after)):
        marks[2 * i : 2 * i + 2, :] = message[first_mark : first_mark + 2, 0:LANES]
    group_rows = 2 * rows // GROUPS
    first, last = slice(LANES, 2 * LANES), slice(width - 2 * LANES, width - LANES)
    fill_strip(strip, (cells[0, :, first], cells[1, :, first]))
    to_left = pack_lanes(strip, group_rows, 0)
    fill_strip(strip, (cells[0, :, last], cells[1, :, last]))
    to_right = pack_lanes(strip, group_rows, LANES - HALO)
    send_columns(to_left, to_right, to_inner, to_outer)
    to_inner[group_rows:, :] = marks[...]
    to_outer[group_rows:, :] = marks[...]


def live_slots(slots, cells):
    tile_r = cells.shape[1] - 2 * HALO
    count = jnp.int32(0)
    for slot in range(slots.shape[1]):
        count += (slots[0, slot] < tile_r).astype(jnp.int32)
    return count


def run_windows(wanted, slots, cells, acc, probe_re, probe_im, table, frames, order):
    tile_c = cells.shape[2] - 2 * LANES
    count = live_slots(slots, cells)
    every = range(slots.shape[1])
    over = []
    for slot in every:
        col = slots[1, slot]
        over.append((col < 0) | (col > tile_c - P_SIZE))
    total = jnp.int32(0)
    for slot in every:
        total += ((slot < count) & ~over[slot]).astype(jnp.int32)
    limit = jnp.where(total < len(every) - 1, PAIR, 2 * PAIR)
    seen, found = jnp.int32(0), jnp.int32(0)
    for slot in every:
        live = slot < count
        mine = live & wanted(over[slot], seen, limit)

        @pl.when(mine)
        def _():
            order[found] = slot

        seen += (live & ~over[slot]).astype(jnp.int32)
        found += mine.astype(jnp.int32)

    lane = lane_index(P_SIZE)

    def load(slot):
        where = row, base, turn = window_place(slots, slot)
        keep = lane >= turn
        w_re = pltpu.roll(probe_re[...], turn, 1)
        w_im = pltpu.roll(probe_im[...], turn, 1)
        patch = []
        for k in (0, 1):
            block = cells[k, pl.ds(row, P_SIZE), pl.ds(base, 3 * LANES)]
            patch.append(
                beside(jnp.where(keep, block[:, :LANES], block[:, 2 * LANES :]), block[:, LANES : 2 * LANES])
            )
        exit_re = w_re * patch[0] - w_im * patch[1]
        exit_im = w_re * patch[1] + w_im * patch[0]
        return (where, keep, w_re, w_im), exit_re, exit_im

    def frame_of(slot):
        sort, unsort = table[8], table[9]
        half = product(sort, frames[slots[2, slot]]).astype(jnp.bfloat16)
        return product(half, unsort)

    def place(at, back_re, back_im):
        where, keep, w_re, w_im = at
        add_window(acc, 0, where, keep, w_re * back_re + w_im * back_im)
        add_window(acc, 1, where, keep, w_re * back_im - w_im * back_re)

    def step(group):
        frame = [frame_of(slot) for slot in group]
        loaded = [load(slot) for slot in group]
        state = [forward_columns(x[1], x[2], table) for x in loaded]
        state = [forward_rows(*x, table) for x in state]
        state = [residual(x, f) for x, f in zip(state, frame)]
        state = [back_rows(x, table) for x in state]
        state = [back_columns(x, table) for x in state]
        for x, back in zip(loaded, state):
            place(x[0], *back)

    def pair_step(pair, carry):
        step([order[pair * PAIR + i] for i in range(PAIR)])
        return carry

    lax.fori_loop(0, found // PAIR, pair_step, 0)

    @pl.when(found % PAIR == 1)
    def _():
        step([order[found - 1]])


def windows_before(
    slots, cells, probe_re, probe_im, table, frames, acc, order, power,
):
    acc[...] = jnp.zeros_like(acc)
    power[...] = probe_re[...] * probe_re[...] + probe_im[...] * probe_im[...]
    lane = lane_index(P_SIZE)

    def step(slot, carry):
        where = window_place(slots, slot)
        add_window(acc, 2, where, lane >= where[2], pltpu.roll(power[...], where[2], 1))
        return carry

    lax.fori_loop(0, live_slots(slots, cells), step, 0)
    run_windows(
        lambda over, seen, limit: ~over & (seen < limit),
        slots, cells, acc, probe_re, probe_im, table, frames, order,
    )


def reaching(place, right, tile_r, tile_c):
    shape = place.shape
    index = lax.broadcasted_iota(jnp.int32, shape, 0)
    lane = lax.broadcasted_iota(jnp.int32, shape, 1)
    col = pltpu.roll(place, shape[0] - 1, 0)
    low = jnp.where(index == 2, tile_r - P_SIZE, -tile_r).astype(jnp.float32)
    high = jnp.where(index == 4, 0, tile_r).astype(jnp.float32)
    reaches = (lane < MARKS) & (index % 2 == 0) & (index < 6) & (place > low) & (place < high)
    if right < 0:
        reaches &= col > tile_c - P_SIZE
    if right > 0:
        reaches &= col < 0
    bit = lax.shift_left(jnp.ones(shape, jnp.int32), jnp.minimum(lane, MARKS)).astype(jnp.float32)
    bits = jnp.sum(jnp.where(reaches, bit, 0.0), axis=1, keepdims=True)
    return jnp.where(lane < MARKS, place, bits).astype(jnp.int32)


def add_neighbours_light(places, acc, power):
    rows, width = acc.shape[1:]
    tile_r, tile_c = rows - 2 * HALO, width - 2 * LANES
    for right in (-1, 0, 1):
        for i, down in enumerate((0, -1, 1)):
            if not right and not down:
                continue
            first, last = {-1: (P_SIZE - HALO, P_SIZE), 0: (0, P_SIZE), 1: (0, HALO)}[down]
            tiles = {-1: (2,), 0: (0, 1, 2), 1: (0,)}[right]
            lane = lane_index(last - first)
            bits = places[right + 1, 2 * i, MARKS]

            def step(slot, carry):
                row, col = places[right + 1, 2 * i, slot], places[right + 1, 2 * i + 1, slot]

                @pl.when(lax.shift_right_logical(bits, slot) % 2 == 1)
                def _():
                    turn = lax.rem(col + LANES, LANES)
                    at = pl.multiple_of(row + HALO + (down * tile_r + first), 16)
                    base = pl.multiple_of(col + LANES - turn + right * tile_c, LANES)
                    part = pltpu.roll(power[first:last, :], turn, 1)
                    add_window(acc, 2, (at, base, turn), lane >= turn, part, tiles)

                return carry

            @pl.when(bits != 0)
            def _():
                lax.fori_loop(0, MARKS, step, 0)


def windows_after(
    slots, cells, acc_in, probe_re, probe_im, table, frames, marks, by_inner, by_outer,
    acc, order, power, whole, places, sem,
):
    rows, width = acc.shape[1:]
    before, after = received(by_inner, by_outer, "col")
    for i, part in enumerate((before[-MARKS:], marks[...], after[-MARKS:])):
        whole[i] = reaching(part, i - 1, rows - 2 * HALO, width - 2 * LANES)
    copy = pltpu.make_async_copy(whole, places, sem)
    copy.start()
    power[...] = probe_re[...] * probe_re[...] + probe_im[...] * probe_im[...]
    run_windows(
        lambda over, seen, limit: ~over & (seen >= limit),
        slots, cells, acc, probe_re, probe_im, table, frames, order,
    )
    copy.wait()
    add_neighbours_light(places, acc, power)


def windows_over_edge(
    slots, cells_in, acc_in, probe_re, probe_im, table, frames, by_inner, by_outer,
    cells, acc, to_inner, to_outer, order, strip,
):
    rows, width = acc.shape[1:]
    before, after = received(by_inner, by_outer, "col")
    for layer, row, part in pieces(before, 2, rows):
        cells[layer, row : row + part.shape[0], 0:LANES] = part
    for layer, row, part in pieces(after, 2, rows):
        cells[layer, row : row + part.shape[0], width - LANES :] = part
    run_windows(
        lambda over, seen, limit: over,
        slots, cells, acc, probe_re, probe_im, table, frames, order,
    )
    group_rows = 2 * rows // GROUPS
    fill_strip(strip, (acc[0, :, 0:LANES], acc[1, :, 0:LANES]))
    to_left = pack_lanes(strip, group_rows, LANES - HALO)
    fill_strip(strip, (acc[0, :, width - LANES :], acc[1, :, width - LANES :]))
    to_right = pack_lanes(strip, group_rows, 0)
    send_columns(to_left, to_right, to_inner, to_outer)


def row_spill(acc_in, by_inner, by_outer, acc, to_inner, to_outer):
    rows, width = acc.shape[1:]
    before, after = received(by_inner, by_outer, "col")
    lane = lane_index(rows)[0:1]
    for layer, row, part in pieces(before, 2, rows):
        here = slice(row, row + part.shape[0])
        acc[layer, here, LANES : 2 * LANES] += jnp.where(lane < HALO, part, 0.0)
    for layer, row, part in pieces(after, 2, rows):
        here = slice(row, row + part.shape[0])
        acc[layer, here, width - 2 * LANES : width - LANES] += jnp.where(lane >= LANES - HALO, part, 0.0)
    odd = is_odd("row")
    for k in (0, 1):
        up = acc[k, 0:HALO, LANES : width - LANES]
        down = acc[k, rows - HALO : rows, LANES : width - LANES]
        to_inner[k] = jnp.where(odd, up, down)
        to_outer[k] = jnp.where(odd, down, up)


def new_rows(cells, acc, extra, start, size, new_re, new_im):
    here = slice(HALO + start, HALO + start + size)
    middle = slice(LANES, acc.shape[2] - LANES)
    part = [acc[k, here, middle] for k in range(acc.shape[0])]
    if extra is not None:
        part[:2] = [part[k] + extra[k] for k in (0, 1)]
    scale = 1.0 / (part[2] + ridge)
    new_re[start : start + size, :] = cells[0, here, middle] - part[0] * scale
    new_im[start : start + size, :] = cells[1, here, middle] - part[1] * scale


def finish_inner(cells, acc, new_re, new_im, near_re, near_im, sems):
    tile_r = near_re.shape[0]
    new_rows(cells, acc, None, HALO, tile_r - 2 * HALO, near_re, near_im)
    rows = slice(HALO, tile_r - HALO)
    finish_all(fetch([(near_re.at[rows], new_re.at[rows]), (near_im.at[rows], new_im.at[rows])], sems))


def finish_edges(cells, acc, by_inner, by_outer, re_in, im_in, new_re, new_im, near_re, near_im, sems):
    tile_r = near_re.shape[0]
    copies = []
    for i, (start, extra) in enumerate(zip((0, tile_r - HALO), received(by_inner, by_outer, "row"))):
        new_rows(cells, acc, extra, start, HALO, near_re, near_im)
        rows = slice(start, start + HALO)
        pairs = ((near_re.at[rows], new_re.at[rows]), (near_im.at[rows], new_im.at[rows]))
        copies += fetch(pairs, sems.at[2 * i : 2 * i + 2])
    finish_all(copies)


def swap(to_inner, to_outer, axis, gather):
    devices = lax.axis_size(axis)
    inner = [(i, i + 1) for i in range(0, devices, 2)]
    partner = {i: i + 1 if i % 2 else i - 1 for i in range(1, devices - 1)}
    n_row, n_col = lax.axis_size("row"), lax.axis_size("col")
    pairs = []
    for row in range(n_row):
        for col in range(n_col):
            if axis == "row":
                there = (partner[row], col) if row in partner else (row, col ^ 1)
            else:
                there = (row, partner[col]) if col in partner else (row ^ 1, col)
            pairs.append((row * n_col + col, there[0] * n_col + there[1]))
    by_outer = lax.ppermute(to_outer, ("row", "col"), pairs)
    if gather:
        by_inner = lax.all_gather(to_inner, axis, axis_index_groups=[list(pair) for pair in inner])
    else:
        by_inner = lax.ppermute(to_inner, axis, inner + [(j, i) for i, j in inner])
    return by_inner, by_outer


def far(x):
    return pltpu.with_memory_space_constraint(x, pltpu.HBM)


def f32(*shape):
    return jax.ShapeDtypeStruct(shape, jnp.float32)


def shards(object_re, object_im, probe_re, probe_im, frames, counts, offsets, frame_index):
    tile_r, tile_c = object_re.shape
    rows, width = tile_r + 2 * HALO, tile_c + 2 * LANES
    layers = 3
    slots = offsets.shape[2]
    table = jnp.asarray(transform_tables())
    frames = frames.reshape(frames.shape[2:])
    cells_shape, acc_shape = f32(2, rows, width), f32(layers, rows, width)
    dma = pltpu.SemaphoreType.DMA

    places = jnp.swapaxes(offsets, 2, 3)
    edge = f32(2 * HALO + MARKS, tile_c)
    to_inner, to_outer, marked = pl.pallas_call(
        row_edges,
        out_shape=(edge, edge, jax.ShapeDtypeStruct((3, slots), jnp.int32)),
        in_specs=[SMEM] + [HBM] * 4,
        out_specs=(VMEM, VMEM, VMEM),
        scratch_shapes=[
            pltpu.VMEM(places.shape, jnp.int32), pltpu.VMEM(frame_index.shape, jnp.int32), dma((6,)),
        ],
        compiler_params=SMALL,
        name="row_edges",
    )(counts, far(object_re), far(object_im), far(places), far(frame_index))
    by_inner, by_outer = swap(to_inner, to_outer, "row", True)

    cells, *fixed = pl.pallas_call(
        load_state,
        out_shape=(
            cells_shape, f32(*probe_re.shape), f32(*probe_im.shape),
            jax.ShapeDtypeStruct(table.shape, table.dtype), jax.ShapeDtypeStruct(frames.shape, frames.dtype),
        ),
        in_specs=[HBM] * 6,
        out_specs=(VMEM,) * 5,
        scratch_shapes=[dma((6,))],
        compiler_params=SMALL,
        cost_estimate=BUSY,
        name="load_state",
    )(*map(far, (object_re, object_im, probe_re, probe_im, table, frames)))

    strip = pltpu.VMEM((2 * rows, LANES), jnp.float32)
    packed = f32(2 * rows // GROUPS + MARKS, LANES)
    cells, marks, to_inner, to_outer = pl.pallas_call(
        row_halos,
        out_shape=(cells_shape, f32(MARKS, LANES), packed, packed),
        in_specs=[VMEM] * 4,
        out_specs=(VMEM,) * 4,
        scratch_shapes=[strip],
        input_output_aliases={0: 0},
        compiler_params=SMALL,
        name="row_halos",
    )(cells, to_outer, by_inner, by_outer)
    edges = swap(to_inner, to_outer, "col", False)

    order = pltpu.SMEM((slots,), jnp.int32)
    acc = pl.pallas_call(
        windows_before,
        out_shape=acc_shape,
        in_specs=[SMEM] + [VMEM] * 5,
        out_specs=VMEM,
        scratch_shapes=[order, pltpu.VMEM(probe_re.shape, jnp.float32)],
        compiler_params=PARAMS,
        cost_estimate=BUSY,
        name="windows_before",
    )(marked, cells, *fixed)

    packed = f32(2 * rows // GROUPS, LANES)
    cells, acc, to_inner, to_outer = pl.pallas_call(
        windows_over_edge,
        out_shape=(cells_shape, acc_shape, packed, packed),
        in_specs=[SMEM] + [VMEM] * 8,
        out_specs=(VMEM,) * 4,
        scratch_shapes=[order, strip],
        input_output_aliases={1: 0, 2: 1},
        compiler_params=PARAMS,
        cost_estimate=BUSY,
        name="windows_over_edge",
    )(marked, cells, acc, *fixed, *edges)
    by_inner, by_outer = swap(to_inner, to_outer, "col", False)

    acc = pl.pallas_call(
        windows_after,
        out_shape=acc_shape,
        in_specs=[SMEM] + [VMEM] * 9,
        out_specs=VMEM,
        scratch_shapes=[
            order, pltpu.VMEM(probe_re.shape, jnp.float32),
            pltpu.VMEM((3, MARKS, LANES), jnp.int32), pltpu.SMEM((3, MARKS, LANES), jnp.int32), dma(()),
        ],
        input_output_aliases={2: 0},
        compiler_params=PARAMS,
        cost_estimate=BUSY,
        name="windows_after",
    )(marked, cells, acc, *fixed, marks, *edges)

    edge = f32(2, HALO, tile_c)
    acc, to_inner, to_outer = pl.pallas_call(
        row_spill,
        out_shape=(acc_shape, edge, edge),
        in_specs=[VMEM] * 3,
        out_specs=(VMEM,) * 3,
        input_output_aliases={0: 0},
        compiler_params=SMALL,
        name="row_spill",
    )(acc, by_inner, by_outer)
    by_inner, by_outer = swap(to_inner, to_outer, "row", True)

    near = [pltpu.VMEM((tile_r, tile_c), jnp.float32)] * 2
    new = (f32(tile_r, tile_c), f32(tile_r, tile_c))
    new_re, new_im = pl.pallas_call(
        finish_inner,
        out_shape=new,
        in_specs=[VMEM] * 2,
        out_specs=(HBM, HBM),
        scratch_shapes=near + [dma((2,))],
        compiler_params=SMALL,
        cost_estimate=BUSY,
        name="finish_inner",
    )(cells, acc)
    return pl.pallas_call(
        finish_edges,
        out_shape=new,
        in_specs=[VMEM] * 4 + [HBM] * 2,
        out_specs=(HBM, HBM),
        scratch_shapes=near + [dma((4,))],
        input_output_aliases={4: 0, 5: 1},
        compiler_params=SMALL,
        name="finish_edges",
    )(cells, acc, by_inner, by_outer, far(new_re), far(new_im))


def solution(mesh):
    return jax.shard_map(
        shards,
        mesh=mesh,
        in_specs=(
            P("row", "col"),
            P("row", "col"),
            P(),
            P(),
            P("row", "col", None, None, None),
            P("row", "col"),
            P("row", "col", None, None),
            P("row", "col", None),
        ),
        out_specs=(P("row", "col"), P("row", "col")),
        check_vma=False,
    )
```

```python
import functools
import math

import jax
import jax.numpy as jnp
import ml_dtypes
import numpy as np
from jax import lax
from jax.experimental import pallas as pl
from jax.experimental.pallas import tpu as pltpu
from jax.sharding import PartitionSpec as P

P_SIZE = 256
HALF = P_SIZE // 2
HALO = 32
LANES = 128
GROUPS = LANES // HALO
MARKS = 8
INNER, OUTER = 0, 1
KINDS = (
    ("row", OUTER), ("row", INNER), ("col", OUTER), ("col", INNER),
    ("up", OUTER), ("down", OUTER), ("up", INNER), ("down", INNER),
)
SLOPE = {"down": 1, "up": -1}
SIDES = tuple((down, right) for down in (-1, 0, 1) for right in (-1, 0, 1) if down or right)
PAIR = 2

floor_amp = 0.5
ridge = 1.0

VMEM = pl.BlockSpec(memory_space=pltpu.VMEM)
SMEM = pl.BlockSpec(memory_space=pltpu.SMEM)
HBM = pl.BlockSpec(memory_space=pltpu.HBM)
PARAMS = pltpu.CompilerParams(vmem_limit_bytes=32 * 1024 * 1024)
SMALL = pltpu.CompilerParams(vmem_limit_bytes=16 * 1024 * 1024)
BUSY = pl.CostEstimate(flops=4_000_000_000, bytes_accessed=8_000_000, transcendentals=0)


def transform_tables():
    index = np.arange(HALF)
    plain = []
    for parity in (0, 1):
        angle = 2.0 * math.pi / P_SIZE * (index[:, None] * (2 * index[None, :] + parity) % P_SIZE)
        cos, sin = np.cos(angle), np.sin(angle)
        plain.append(np.block([[cos, -sin], [sin, cos]]) / math.sqrt(P_SIZE))
    parts = []
    for table in plain + [t.T for t in plain]:
        high = table.astype(np.float32).astype(ml_dtypes.bfloat16)
        low = (table - high.astype(np.float64)).astype(np.float32).astype(ml_dtypes.bfloat16)
        parts += [high, low]
    order = np.concatenate([np.arange(0, P_SIZE, 2), np.arange(1, P_SIZE, 2)])
    sort = np.zeros((P_SIZE, P_SIZE), np.float32)
    sort[np.arange(P_SIZE), order] = 1.0
    parts += [sort.astype(ml_dtypes.bfloat16), sort.T.astype(ml_dtypes.bfloat16)]
    return np.stack(parts)


def lane_index(rows):
    return lax.broadcasted_iota(jnp.int32, (rows, LANES), 1)


def pack_lanes(ref, rows, first):
    lane = lane_index(rows)
    packed = None
    for g in range(GROUPS):
        part = ref[g * rows : (g + 1) * rows, :]
        if g:
            part = pltpu.roll(part, HALO * g, 1)
        low = (first + HALO * g) % LANES
        mine = (lane >= low) & (lane < low + HALO)
        packed = part if packed is None else jnp.where(mine, part, packed)
    return packed


def unpack_lanes(packed, group):
    return pltpu.roll(packed, LANES - HALO * group, 1) if group else packed


def split(x):
    high = x.astype(jnp.bfloat16)
    return high, (x - high.astype(jnp.float32)).astype(jnp.bfloat16)


def product(left, right):
    return jnp.dot(left, right, preferred_element_type=jnp.float32)


def times_table(x, table, which):
    high, low = split(x)
    t_high, t_low = table[2 * which], table[2 * which + 1]
    return product(high, t_high) + (product(high, t_low) + product(low, t_high))


def table_times(table, which, x):
    high, low = split(x)
    t_high, t_low = table[2 * which], table[2 * which + 1]
    return product(t_high, high) + (product(t_low, high) + product(t_high, low))


def beside(*blocks):
    return jnp.concatenate(blocks, axis=1)


def below(*blocks):
    return jnp.concatenate(blocks, axis=0)


def ends(x):
    return x[:, :HALF], x[:, HALF:]


def forward_columns(exit_re, exit_im, table):
    re_lo, re_hi = ends(exit_re)
    im_lo, im_hi = ends(exit_im)
    even = times_table(beside(re_lo + re_hi, im_lo + im_hi), table, 0)
    odd = times_table(beside(re_lo - re_hi, im_lo - im_hi), table, 1)
    return even, odd


def forward_rows(even, odd, table):
    out = []
    for parity in (0, 1):
        if parity == 0:
            se, so = even[:HALF] + even[HALF:], odd[:HALF] + odd[HALF:]
        else:
            se, so = even[:HALF] - even[HALF:], odd[:HALF] - odd[HALF:]
        e_re, e_im = ends(se)
        o_re, o_im = ends(so)
        out.append(table_times(table, 2 + parity, below(beside(e_re, o_re), beside(e_im, o_im))))
    return out


def residual(far, frame):
    out = []
    for parity in (0, 1):
        re, im = far[parity][:HALF], far[parity][HALF:]
        level = jnp.maximum(re * re + im * im, floor_amp * floor_amp)
        inten = frame[parity * HALF : (parity + 1) * HALF]
        factor = 1.0 - inten * lax.rsqrt(inten * level)
        out.append(below(re * factor, im * factor))
    return out


def back_rows(res, table):
    first = table_times(table, 0, res[0])
    second = table_times(table, 1, res[1])
    upper, lower = first + second, first - second
    out = []
    for cols in (slice(0, HALF), slice(HALF, P_SIZE)):
        out.append(
            below(
                beside(upper[:HALF, cols], upper[HALF:, cols]),
                beside(lower[:HALF, cols], lower[HALF:, cols]),
            )
        )
    return out


def back_columns(parts, table):
    even = times_table(parts[0], table, 2)
    odd = times_table(parts[1], table, 3)
    lo, hi = even + odd, even - odd
    return beside(lo[:, :HALF], hi[:, :HALF]), beside(lo[:, HALF:], hi[:, HALF:])


def is_odd(axis):
    return lax.rem(lax.axis_index(axis), 2) == 1


def fetch(pairs, sems):
    copies = [pltpu.make_async_copy(far, near, sems.at[i]) for i, (far, near) in enumerate(pairs)]
    for copy in copies:
        copy.start()
    return copies


def finish_all(copies):
    for copy in copies:
        copy.wait()


def window_place(slots, slot):
    row = pl.multiple_of(slots[0, slot] + HALO, 16)
    col = slots[1, slot] + LANES
    turn = lax.rem(col, LANES)
    return row, pl.multiple_of(col - turn, LANES), turn


def add_window(acc, layer, where, keep, term, tiles=(0, 1, 2)):
    row, base, _ = where
    lo, hi = ends(term)
    parts = (jnp.where(keep, lo, 0.0), hi, jnp.where(keep, 0.0, lo))
    for t in tiles:
        acc[layer, pl.ds(row, term.shape[0]), pl.ds(base + t * LANES, LANES)] += parts[t]


def fill_strip(strip, parts):
    done = 0
    for part in parts:
        strip[done : done + part.shape[0], :] = part
        done += part.shape[0]


def pieces(packed, layers, rows):
    group_rows = layers * rows // GROUPS
    for g in range(GROUPS):
        part = unpack_lanes(packed, g)
        done = 0
        while done < group_rows:
            layer, row = divmod(g * group_rows + done, rows)
            size = min(group_rows - done, rows - row)
            yield layer, row, part[done : done + size]
            done += size


def turns(strips, kind):
    name, place = kind
    if name == "col":
        odd, side = is_odd("col"), (0, -1)
    else:
        odd, side = is_odd("row"), (-1, -SLOPE.get(name, 0))
    other = (-side[0], -side[1])
    if place == OUTER:
        side, other = other, side
    return jnp.where(odd, strips[side], strips[other])


def arrived(messages, side):
    down, right = side
    name = "col" if not down else "row" if not right else "down" if down == right else "up"
    odd = is_odd("col" if name == "col" else "row")
    first = (right if name == "col" else down) < 0
    inner, outer = messages[KINDS.index((name, INNER))][...], messages[KINDS.index((name, OUTER))][...]
    came = jnp.where(odd, inner, outer) if first else jnp.where(odd, outer, inner)
    row, col = lax.axis_index("row") + down, lax.axis_index("col") + right
    there = (row >= 0) & (row < lax.axis_size("row")) & (col >= 0) & (col < lax.axis_size("col"))
    return jnp.where(there, came, 0.0)


def edge_strips(field, strip, reach):
    rows, width = field.shape[1:]
    tile_r, tile_c = rows - 2 * HALO, width - 2 * LANES
    tops = {-1: 0 if reach else HALO, 0: HALO, 1: tile_r + HALO if reach else tile_r}
    tiles = {-1: 0 if reach else LANES, 1: tile_c + LANES if reach else tile_c}
    lanes = {-1: LANES - HALO if reach else 0, 1: 0 if reach else LANES - HALO}
    strips = {}
    for down, right in SIDES:
        size = HALO if down else tile_r
        here = slice(tops[down], tops[down] + size)
        if not right:
            strips[down, right] = below(*(field[k, here, LANES : LANES + tile_c] for k in (0, 1)))
            continue
        tile = slice(tiles[right], tiles[right] + LANES)
        fill_strip(strip, [field[k, here, tile] for k in (0, 1)])
        strips[down, right] = pack_lanes(strip, 2 * size // GROUPS, lanes[right])
    return strips


def edges(counts, obj_re, obj_im, offsets, chosen, *refs):
    cells, slots, *messages = refs[: 2 + len(KINDS)]
    places, frame_of, marks, strip, sems = refs[2 + len(KINDS) :]
    tile_r, tile_c = obj_re.shape
    inner, middle = slice(HALO, HALO + tile_r), slice(LANES, LANES + tile_c)
    pairs = [(offsets, places), (chosen, frame_of)]
    pairs += [(ref, cells.at[k, inner, middle]) for k, ref in enumerate((obj_re, obj_im))]
    copies = fetch(pairs, sems)
    finish_all(copies[:2])
    place = places[0, 0]
    live = lax.broadcasted_iota(jnp.int32, place.shape, 1) < counts[0, 0]
    place = jnp.where(live, place, 2 * tile_r)
    slots[0:2, :] = place
    slots[2:3, :] = frame_of[0]
    marks[...] = jnp.zeros_like(marks)
    marks[0:2, 0 : place.shape[1]] = place.astype(jnp.float32)
    finish_all(copies[2:])
    strips = edge_strips(cells, strip, False)
    for kind, message in zip(KINDS, messages):
        data = turns(strips, kind)
        message[0 : data.shape[0], :] = data
        message[data.shape[0] :, 0:LANES] = marks[...]


def live_slots(slots, cells):
    tile_r = cells.shape[1] - 2 * HALO
    count = jnp.int32(0)
    for slot in range(slots.shape[1]):
        count += (slots[0, slot] < tile_r).astype(jnp.int32)
    return count


def run_windows(wanted, slots, cells, acc, probe_re, probe_im, table, frames, order):
    tile_r, tile_c = cells.shape[1] - 2 * HALO, cells.shape[2] - 2 * LANES
    count = live_slots(slots, cells)
    every = range(slots.shape[1])
    over = []
    for slot in every:
        row, col = slots[0, slot], slots[1, slot]
        over.append((row < 0) | (row > tile_r - P_SIZE) | (col < 0) | (col > tile_c - P_SIZE))
    total = jnp.int32(0)
    for slot in every:
        total += ((slot < count) & ~over[slot]).astype(jnp.int32)
    limit = jnp.where(total <= 2 * PAIR, PAIR, 2 * PAIR)
    seen, found = jnp.int32(0), jnp.int32(0)
    for slot in every:
        live = slot < count
        mine = live & wanted(over[slot], seen, limit)

        @pl.when(mine)
        def _():
            order[found] = slot

        seen += (live & ~over[slot]).astype(jnp.int32)
        found += mine.astype(jnp.int32)

    lane = lane_index(P_SIZE)

    def load(slot):
        where = row, base, turn = window_place(slots, slot)
        keep = lane >= turn
        w_re = pltpu.roll(probe_re[...], turn, 1)
        w_im = pltpu.roll(probe_im[...], turn, 1)
        patch = []
        for k in (0, 1):
            block = cells[k, pl.ds(row, P_SIZE), pl.ds(base, 3 * LANES)]
            patch.append(
                beside(jnp.where(keep, block[:, :LANES], block[:, 2 * LANES :]), block[:, LANES : 2 * LANES])
            )
        exit_re = w_re * patch[0] - w_im * patch[1]
        exit_im = w_re * patch[1] + w_im * patch[0]
        return (where, keep, w_re, w_im), exit_re, exit_im

    def frame_of(slot):
        sort, unsort = table[8], table[9]
        half = product(sort, frames[slots[2, slot]]).astype(jnp.bfloat16)
        return product(half, unsort)

    def place(at, back_re, back_im):
        where, keep, w_re, w_im = at
        add_window(acc, 0, where, keep, w_re * back_re + w_im * back_im)
        add_window(acc, 1, where, keep, w_re * back_im - w_im * back_re)

    def step(group):
        frame = [frame_of(slot) for slot in group]
        loaded = [load(slot) for slot in group]
        state = [forward_columns(x[1], x[2], table) for x in loaded]
        state = [forward_rows(*x, table) for x in state]
        state = [residual(x, f) for x, f in zip(state, frame)]
        state = [back_rows(x, table) for x in state]
        state = [back_columns(x, table) for x in state]
        for x, back in zip(loaded, state):
            place(x[0], *back)

    def pair_step(pair, carry):
        step([order[pair * PAIR + i] for i in range(PAIR)])
        return carry

    lax.fori_loop(0, found // PAIR, pair_step, 0)

    @pl.when(found % PAIR == 1)
    def _():
        step([order[found - 1]])


def windows_inside(
    slots, cells, probe_re_far, probe_im_far, table_far, frames_far,
    acc, probe_re, probe_im, table, frames, order, power, sems,
):
    far_near = ((probe_re_far, probe_re), (probe_im_far, probe_im), (table_far, table), (frames_far, frames))
    copies = fetch(far_near, sems)
    acc[...] = jnp.zeros_like(acc)
    finish_all(copies[:2])
    power[...] = probe_re[...] * probe_re[...] + probe_im[...] * probe_im[...]
    lane = lane_index(P_SIZE)

    def step(slot, carry):
        where = window_place(slots, slot)
        add_window(acc, 2, where, lane >= where[2], pltpu.roll(power[...], where[2], 1))
        return carry

    lax.fori_loop(0, live_slots(slots, cells), step, 0)
    finish_all(copies[2:])
    run_windows(
        lambda over, seen, limit: ~over & (seen < limit),
        slots, cells, acc, probe_re, probe_im, table, frames, order,
    )


def windows_over_edges(slots, cells_in, acc_in, probe_re, probe_im, table, frames, *refs):
    messages = refs[: len(KINDS)]
    cells, acc, *out = refs[len(KINDS) : 2 * len(KINDS) + 2]
    order, strip = refs[2 * len(KINDS) + 2 :]
    rows, width = acc.shape[1:]
    tile_r, tile_c = rows - 2 * HALO, width - 2 * LANES
    for down, right in SIDES:
        came = arrived(messages, (down, right))
        size = HALO if down else tile_r
        top = {-1: 0, 0: HALO, 1: HALO + tile_r}[down]
        if not right:
            for k in (0, 1):
                cells[k, top : top + size, LANES : LANES + tile_c] = came[k * size : (k + 1) * size]
            continue
        tile = slice(0, LANES) if right < 0 else slice(width - LANES, width)
        for k, row, part in pieces(came[:-MARKS], 2, size):
            cells[k, top + row : top + row + part.shape[0], tile] = part
    run_windows(
        lambda over, seen, limit: over,
        slots, cells, acc, probe_re, probe_im, table, frames, order,
    )
    strips = edge_strips(acc, strip, True)
    for kind, message in zip(KINDS, out):
        message[...] = turns(strips, kind)


def reaching(place, down, right, tile_r, tile_c):
    shape = place.shape
    index = lax.broadcasted_iota(jnp.int32, shape, 0)
    lane = lax.broadcasted_iota(jnp.int32, shape, 1)
    col = pltpu.roll(place, shape[0] - 1, 0)
    reaches = (lane < MARKS) & (index == 0) & (place < tile_r)
    if down < 0:
        reaches &= place > tile_r - P_SIZE
    if down > 0:
        reaches &= place < 0
    if right < 0:
        reaches &= col > tile_c - P_SIZE
    if right > 0:
        reaches &= col < 0
    bit = lax.shift_left(jnp.ones(shape, jnp.int32), jnp.minimum(lane, MARKS)).astype(jnp.float32)
    bits = jnp.sum(jnp.where(reaches, bit, 0.0), axis=1, keepdims=True)
    return jnp.where(lane < MARKS, place, bits).astype(jnp.int32)


def add_neighbours_light(places, acc, power):
    rows, width = acc.shape[1:]
    tile_r, tile_c = rows - 2 * HALO, width - 2 * LANES
    for i, (down, right) in enumerate(SIDES):
        first, last = {-1: (P_SIZE - HALO, P_SIZE), 0: (0, P_SIZE), 1: (0, HALO)}[down]
        tiles = {-1: (2,), 0: (0, 1, 2), 1: (0,)}[right]
        lane = lane_index(last - first)
        bits = places[i, 0, MARKS]

        def step(slot, carry):
            row, col = places[i, 0, slot], places[i, 1, slot]

            @pl.when(lax.shift_right_logical(bits, slot) % 2 == 1)
            def _():
                turn = lax.rem(col + LANES, LANES)
                at = pl.multiple_of(row + HALO + (down * tile_r + first), 16)
                base = pl.multiple_of(col + LANES - turn + right * tile_c, LANES)
                part = pltpu.roll(power[first:last, :], turn, 1)
                add_window(acc, 2, (at, base, turn), lane >= turn, part, tiles)

            return carry

        @pl.when(bits != 0)
        def _():
            lax.fori_loop(0, MARKS, step, 0)


def windows_rest(slots, cells, acc_in, probe_re, probe_im, table, frames, *refs):
    messages = refs[: len(KINDS)]
    acc, order, power, whole, places, sem = refs[len(KINDS) :]
    rows, width = acc.shape[1:]
    tails = [message.at[message.shape[0] - MARKS :, 0:LANES] for message in messages]
    for i, side in enumerate(SIDES):
        whole[i] = reaching(arrived(tails, side), *side, rows - 2 * HALO, width - 2 * LANES)
    copy = pltpu.make_async_copy(whole, places, sem)
    copy.start()
    power[...] = probe_re[...] * probe_re[...] + probe_im[...] * probe_im[...]
    run_windows(
        lambda over, seen, limit: ~over & (seen >= limit),
        slots, cells, acc, probe_re, probe_im, table, frames, order,
    )
    copy.wait()
    add_neighbours_light(places, acc, power)


def finish(cells, acc_in, *refs):
    messages = refs[: len(KINDS)]
    acc, new_re, new_im, near_re, near_im, sems = refs[len(KINDS) :]
    rows, width = acc.shape[1:]
    tile_r, tile_c = rows - 2 * HALO, width - 2 * LANES
    middle = slice(LANES, LANES + tile_c)
    lane = lane_index(rows)[0:1]
    for down, right in SIDES:
        came = arrived(messages, (down, right))
        size = HALO if down else tile_r
        top = tile_r if down > 0 else HALO
        if not right:
            for k in (0, 1):
                acc[k, top : top + size, middle] += came[k * size : (k + 1) * size]
            continue
        tile = slice(LANES, 2 * LANES) if right < 0 else slice(width - 2 * LANES, width - LANES)
        mine = lane < HALO if right < 0 else lane >= LANES - HALO
        for k, row, part in pieces(came, 2, size):
            acc[k, top + row : top + row + part.shape[0], tile] += jnp.where(mine, part, 0.0)
    chunk = tile_r // 3
    copies = []
    for i in range(3):
        here, there = slice(HALO + i * chunk, HALO + (i + 1) * chunk), slice(i * chunk, (i + 1) * chunk)
        scale = 1.0 / (acc[2, here, middle] + ridge)
        near_re[there, :] = cells[0, here, middle] - acc[0, here, middle] * scale
        near_im[there, :] = cells[1, here, middle] - acc[1, here, middle] * scale
        pairs = ((near_re.at[there], new_re.at[there]), (near_im.at[there], new_im.at[there]))
        copies += fetch(pairs, sems.at[2 * i : 2 * i + 2])
    finish_all(copies)


def partners(kind, n_row, n_col):
    name, place = kind
    pairs = []
    for row in range(n_row):
        for col in range(n_col):
            index, count = (col, n_col) if name == "col" else (row, n_row)
            beside_me = index ^ 1 if place == INNER else index + 1 if index % 2 else index - 1
            if not 0 <= beside_me < count:
                there = (row ^ 1, col) if name == "col" else (row, col ^ 1)
            elif name == "col":
                there = (row, beside_me)
            else:
                there = (beside_me, (col + SLOPE.get(name, 0) * (beside_me - row)) % n_col)
            pairs.append((row * n_col + col, there[0] * n_col + there[1]))
    return pairs


def exchange(messages):
    n_row, n_col = lax.axis_size("row"), lax.axis_size("col")
    return [
        lax.ppermute(message, ("row", "col"), partners(kind, n_row, n_col))
        for kind, message in zip(KINDS, messages)
    ]


def far(x):
    return pltpu.with_memory_space_constraint(x, pltpu.HBM)


def f32(*shape):
    return jax.ShapeDtypeStruct(shape, jnp.float32)


def message_shapes(tile_r, tile_c, marks):
    sizes = {"row": (2 * HALO, tile_c), "col": (2 * tile_r // GROUPS, LANES)}
    corner = (2 * HALO // GROUPS, LANES)
    return [f32(sizes.get(name, corner)[0] + marks, sizes.get(name, corner)[1]) for name, _ in KINDS]


def shards(object_re, object_im, probe_re, probe_im, frames, counts, offsets, frame_index):
    tile_r, tile_c = object_re.shape
    rows, width = tile_r + 2 * HALO, tile_c + 2 * LANES
    layers = 3
    slots = offsets.shape[2]
    table = jnp.asarray(transform_tables())
    frames = frames.reshape(frames.shape[2:])
    cells_shape, acc_shape = f32(2, rows, width), f32(layers, rows, width)
    dma = pltpu.SemaphoreType.DMA
    strip = pltpu.VMEM((2 * tile_r, LANES), jnp.float32)
    order = pltpu.SMEM((slots,), jnp.int32)
    power = pltpu.VMEM(probe_re.shape, jnp.float32)
    kinds = len(KINDS)

    places = jnp.swapaxes(offsets, 2, 3)
    cells, slots_at, *messages = pl.pallas_call(
        edges,
        out_shape=(
            cells_shape, jax.ShapeDtypeStruct((3, slots), jnp.int32), *message_shapes(tile_r, tile_c, MARKS),
        ),
        in_specs=[SMEM] + [HBM] * 4,
        out_specs=(VMEM,) * (2 + kinds),
        scratch_shapes=[
            pltpu.VMEM(places.shape, jnp.int32), pltpu.VMEM(frame_index.shape, jnp.int32),
            pltpu.VMEM((MARKS, LANES), jnp.float32), strip, dma((4,)),
        ],
        compiler_params=SMALL,
        name="edges",
    )(counts, far(object_re), far(object_im), far(places), far(frame_index))
    came = exchange(messages)

    acc, *fixed = pl.pallas_call(
        windows_inside,
        out_shape=(
            acc_shape, f32(*probe_re.shape), f32(*probe_im.shape),
            jax.ShapeDtypeStruct(table.shape, table.dtype), jax.ShapeDtypeStruct(frames.shape, frames.dtype),
        ),
        in_specs=[SMEM, VMEM] + [HBM] * 4,
        out_specs=(VMEM,) * 5,
        scratch_shapes=[order, power, dma((4,))],
        compiler_params=PARAMS,
        cost_estimate=BUSY,
        name="windows_inside",
    )(slots_at, cells, *map(far, (probe_re, probe_im, table, frames)))

    cells, acc, *messages = pl.pallas_call(
        windows_over_edges,
        out_shape=(cells_shape, acc_shape, *message_shapes(tile_r, tile_c, 0)),
        in_specs=[SMEM] + [VMEM] * (6 + kinds),
        out_specs=(VMEM,) * (2 + kinds),
        scratch_shapes=[order, strip],
        input_output_aliases={1: 0, 2: 1},
        compiler_params=PARAMS,
        cost_estimate=BUSY,
        name="windows_over_edges",
    )(slots_at, cells, acc, *fixed, *came)
    back = exchange(messages)

    acc = pl.pallas_call(
        windows_rest,
        out_shape=acc_shape,
        in_specs=[SMEM] + [VMEM] * (6 + kinds),
        out_specs=VMEM,
        scratch_shapes=[
            order, power, pltpu.VMEM((len(SIDES), MARKS, LANES), jnp.int32),
            pltpu.SMEM((len(SIDES), MARKS, LANES), jnp.int32), dma(()),
        ],
        input_output_aliases={2: 0},
        compiler_params=PARAMS,
        cost_estimate=BUSY,
        name="windows_rest",
    )(slots_at, cells, acc, *fixed, *came)

    near = pltpu.VMEM((tile_r, tile_c), jnp.float32)
    _, new_re, new_im = pl.pallas_call(
        finish,
        out_shape=(acc_shape, f32(tile_r, tile_c), f32(tile_r, tile_c)),
        in_specs=[VMEM] * (2 + kinds),
        out_specs=(VMEM, HBM, HBM),
        scratch_shapes=[near, near, dma((6,))],
        input_output_aliases={1: 0},
        compiler_params=SMALL,
        name="finish",
    )(cells, acc, *back)
    return new_re, new_im


def solution(mesh):
    return jax.shard_map(
        shards,
        mesh=mesh,
        in_specs=(
            P("row", "col"),
            P("row", "col"),
            P(),
            P(),
            P("row", "col", None, None, None),
            P("row", "col"),
            P("row", "col", None, None),
            P("row", "col", None),
        ),
        out_specs=(P("row", "col"), P("row", "col")),
        check_vma=False,
    )
```

```python
import functools
import math

import jax
import jax.numpy as jnp
import ml_dtypes
import numpy as np
from jax import lax
from jax.experimental import pallas as pl
from jax.experimental.pallas import tpu as pltpu
from jax.sharding import PartitionSpec as P

P_SIZE = 256
HALF = P_SIZE // 2
HALO = 32
LANES = 128
GROUPS = LANES // HALO
MARKS = 8
PAIR = 2

floor_amp = 0.5
ridge = 1.0

VMEM = pl.BlockSpec(memory_space=pltpu.VMEM)
SMEM = pl.BlockSpec(memory_space=pltpu.SMEM)
HBM = pl.BlockSpec(memory_space=pltpu.HBM)
PARAMS = pltpu.CompilerParams(vmem_limit_bytes=32 * 1024 * 1024)
SMALL = pltpu.CompilerParams(vmem_limit_bytes=16 * 1024 * 1024)
BUSY = pl.CostEstimate(flops=4_000_000_000, bytes_accessed=8_000_000, transcendentals=0)


def transform_tables():
    index = np.arange(HALF)
    plain = []
    for parity in (0, 1):
        angle = 2.0 * math.pi / P_SIZE * (index[:, None] * (2 * index[None, :] + parity) % P_SIZE)
        cos, sin = np.cos(angle), np.sin(angle)
        plain.append(np.block([[cos, -sin], [sin, cos]]) / math.sqrt(P_SIZE))
    parts = []
    for table in plain + [t.T for t in plain]:
        high = table.astype(np.float32).astype(ml_dtypes.bfloat16)
        low = (table - high.astype(np.float64)).astype(np.float32).astype(ml_dtypes.bfloat16)
        parts += [high, low]
    order = np.concatenate([np.arange(0, P_SIZE, 2), np.arange(1, P_SIZE, 2)])
    sort = np.zeros((P_SIZE, P_SIZE), np.float32)
    sort[np.arange(P_SIZE), order] = 1.0
    parts += [sort.astype(ml_dtypes.bfloat16), sort.T.astype(ml_dtypes.bfloat16)]
    return np.stack(parts)


def lane_index(rows):
    return lax.broadcasted_iota(jnp.int32, (rows, LANES), 1)


def pack_lanes(ref, rows, first):
    lane = lane_index(rows)
    packed = None
    for g in range(GROUPS):
        part = ref[g * rows : (g + 1) * rows, :]
        if g:
            part = pltpu.roll(part, HALO * g, 1)
        low = (first + HALO * g) % LANES
        mine = (lane >= low) & (lane < low + HALO)
        packed = part if packed is None else jnp.where(mine, part, packed)
    return packed


def unpack_lanes(packed, group):
    return pltpu.roll(packed, LANES - HALO * group, 1) if group else packed


def split(x):
    high = x.astype(jnp.bfloat16)
    return high, (x - high.astype(jnp.float32)).astype(jnp.bfloat16)


def product(left, right):
    return jnp.dot(left, right, preferred_element_type=jnp.float32)


def times_table(x, table, which):
    high, low = split(x)
    t_high, t_low = table[2 * which], table[2 * which + 1]
    return product(beside(high, high, low), below(t_high, t_low, t_high))


def table_times(table, which, x):
    high, low = split(x)
    t_high, t_low = table[2 * which], table[2 * which + 1]
    return product(beside(t_high, t_low, t_high), below(high, high, low))


def beside(*blocks):
    return jnp.concatenate(blocks, axis=1)


def below(*blocks):
    return jnp.concatenate(blocks, axis=0)


def ends(x):
    return x[:, :HALF], x[:, HALF:]


def forward_columns(exit_re, exit_im, table):
    re_lo, re_hi = ends(exit_re)
    im_lo, im_hi = ends(exit_im)
    even = times_table(beside(re_lo + re_hi, im_lo + im_hi), table, 0)
    odd = times_table(beside(re_lo - re_hi, im_lo - im_hi), table, 1)
    return even, odd


def forward_rows(even, odd, table):
    out = []
    for parity in (0, 1):
        if parity == 0:
            se, so = even[:HALF] + even[HALF:], odd[:HALF] + odd[HALF:]
        else:
            se, so = even[:HALF] - even[HALF:], odd[:HALF] - odd[HALF:]
        e_re, e_im = ends(se)
        o_re, o_im = ends(so)
        out.append(table_times(table, 2 + parity, below(beside(e_re, o_re), beside(e_im, o_im))))
    return out


def residual(far, frame):
    out = []
    for parity in (0, 1):
        re, im = far[parity][:HALF], far[parity][HALF:]
        level = jnp.maximum(re * re + im * im, floor_amp * floor_amp)
        inten = frame[parity * HALF : (parity + 1) * HALF]
        factor = 1.0 - inten * lax.rsqrt(inten * level)
        out.append(below(re * factor, im * factor))
    return out


def back_rows(res, table):
    first = table_times(table, 0, res[0])
    second = table_times(table, 1, res[1])
    upper, lower = first + second, first - second
    out = []
    for cols in (slice(0, HALF), slice(HALF, P_SIZE)):
        out.append(
            below(
                beside(upper[:HALF, cols], upper[HALF:, cols]),
                beside(lower[:HALF, cols], lower[HALF:, cols]),
            )
        )
    return out


def back_columns(parts, table):
    even = times_table(parts[0], table, 2)
    odd = times_table(parts[1], table, 3)
    lo, hi = even + odd, even - odd
    return beside(lo[:, :HALF], hi[:, :HALF]), beside(lo[:, HALF:], hi[:, HALF:])


def is_odd(axis):
    return lax.rem(lax.axis_index(axis), 2) == 1


def fetch(pairs, sems):
    copies = [pltpu.make_async_copy(far, near, sems.at[i]) for i, (far, near) in enumerate(pairs)]
    for copy in copies:
        copy.start()
    return copies


def finish_all(copies):
    for copy in copies:
        copy.wait()


def row_edges(counts, obj_re, obj_im, offsets, chosen, to_inner, to_outer, marked, places, frame_of, sems):
    tile_r = obj_re.shape[0]
    odd = is_odd("row")
    low = pl.multiple_of(jnp.where(odd, 0, tile_r - HALO), 16)
    high = pl.multiple_of(jnp.where(odd, tile_r - HALO, 0), 16)
    pairs = [(offsets, places), (chosen, frame_of)]
    for k, ref in enumerate((obj_re, obj_im)):
        rows = slice(k * HALO, (k + 1) * HALO)
        pairs.append((ref.at[pl.ds(high, HALO)], to_outer.at[rows]))
        pairs.append((ref.at[pl.ds(low, HALO)], to_inner.at[rows]))
    copies = fetch(pairs, sems)
    finish_all(copies[:2])
    place = places[0, 0]
    live = lax.broadcasted_iota(jnp.int32, place.shape, 1) < counts[0, 0]
    place = jnp.where(live, place, 2 * tile_r)
    marked[0:2, :] = place
    marked[2:3, :] = frame_of[0]
    for message in (to_inner, to_outer):
        message[2 * HALO : 2 * HALO + 2, 0 : place.shape[1]] = place.astype(jnp.float32)
    finish_all(copies[2:])


def window_place(slots, slot):
    row = pl.multiple_of(slots[0, slot] + HALO, 16)
    col = slots[1, slot] + LANES
    turn = lax.rem(col, LANES)
    return row, pl.multiple_of(col - turn, LANES), turn


def add_window(acc, layer, where, keep, term, tiles=(0, 1, 2)):
    row, base, _ = where
    lo, hi = ends(term)
    parts = (jnp.where(keep, lo, 0.0), hi, jnp.where(keep, 0.0, lo))
    for t in tiles:
        acc[layer, pl.ds(row, term.shape[0]), pl.ds(base + t * LANES, LANES)] += parts[t]


def load_state(
    obj_re, obj_im, probe_re_far, probe_im_far, table_far, frames_far,
    cells, probe_re, probe_im, table, frames, sems,
):
    tile_r, tile_c = obj_re.shape
    inner = slice(HALO, HALO + tile_r)
    middle = slice(LANES, LANES + tile_c)
    pairs = (
        (table_far, table),
        (frames_far, frames),
        (obj_re, cells.at[0, inner, middle]),
        (obj_im, cells.at[1, inner, middle]),
        (probe_re_far, probe_re),
        (probe_im_far, probe_im),
    )
    copies = fetch(pairs, sems)
    finish_all(copies[:2])

    def sort(i, carry):
        half = product(table[8], frames[i]).astype(jnp.bfloat16)
        frames[i] = product(half, table[9]).astype(jnp.bfloat16)
        return carry

    lax.fori_loop(0, frames.shape[0], sort, 0, unroll=2)
    finish_all(copies[2:])


def fill_strip(strip, parts):
    done = 0
    for part in parts:
        strip[done : done + part.shape[0], :] = part
        done += part.shape[0]


def send_columns(to_left, to_right, to_inner, to_outer):
    odd = is_odd("col")
    to_inner[0 : to_left.shape[0], :] = jnp.where(odd, to_left, to_right)
    to_outer[0 : to_left.shape[0], :] = jnp.where(odd, to_right, to_left)


def received(by_inner, by_outer, axis):
    odd = is_odd(axis)
    index = lax.axis_index(axis)
    inside = (index > 0) & (index < lax.axis_size(axis) - 1)
    by_outer = jnp.where(inside, by_outer[...], 0.0)
    if len(by_inner.shape) > len(by_outer.shape):
        before, after = by_inner[0], by_inner[1]
    else:
        before = after = by_inner[...]
    return jnp.where(odd, before, by_outer), jnp.where(odd, by_outer, after)


def pieces(packed, layers, rows):
    group_rows = layers * rows // GROUPS
    for g in range(GROUPS):
        part = unpack_lanes(packed, g)
        done = 0
        while done < group_rows:
            layer, row = divmod(g * group_rows + done, rows)
            size = min(group_rows - done, rows - row)
            yield layer, row, part[done : done + size]
            done += size


def row_halos(cells_in, own, by_inner, by_outer, cells, marks, to_inner, to_outer, strip):
    rows, width = cells.shape[1:]
    middle = slice(LANES, width - LANES)
    before, after = received(by_inner, by_outer, "row")
    for k in (0, 1):
        cells[k, 0:HALO, middle] = before[k * HALO : (k + 1) * HALO]
        cells[k, rows - HALO : rows, middle] = after[k * HALO : (k + 1) * HALO]
    first_mark = 2 * HALO
    for i, message in enumerate((own[...], before, after)):
        marks[2 * i : 2 * i + 2, :] = message[first_mark : first_mark + 2, 0:LANES]
    group_rows = 2 * rows // GROUPS
    first, last = slice(LANES, 2 * LANES), slice(width - 2 * LANES, width - LANES)
    fill_strip(strip, (cells[0, :, first], cells[1, :, first]))
    to_left = pack_lanes(strip, group_rows, 0)
    fill_strip(strip, (cells[0, :, last], cells[1, :, last]))
    to_right = pack_lanes(strip, group_rows, LANES - HALO)
    send_columns(to_left, to_right, to_inner, to_outer)
    to_inner[group_rows:, :] = marks[...]
    to_outer[group_rows:, :] = marks[...]


def live_slots(slots, cells):
    tile_r = cells.shape[1] - 2 * HALO
    count = jnp.int32(0)
    for slot in range(slots.shape[1]):
        count += (slots[0, slot] < tile_r).astype(jnp.int32)
    return count


def run_windows(wanted, slots, cells, acc, probe_re, probe_im, table, frames, order):
    tile_c = cells.shape[2] - 2 * LANES
    count = live_slots(slots, cells)
    every = range(slots.shape[1])
    over = []
    for slot in every:
        col = slots[1, slot]
        over.append((col < 0) | (col > tile_c - P_SIZE))
    total = jnp.int32(0)
    for slot in every:
        total += ((slot < count) & ~over[slot]).astype(jnp.int32)
    limit = jnp.where(total < len(every) - 1, PAIR, 2 * PAIR)
    seen, found = jnp.int32(0), jnp.int32(0)
    for slot in every:
        live = slot < count
        mine = live & wanted(over[slot], seen, limit)

        @pl.when(mine)
        def _():
            order[found] = slot

        seen += (live & ~over[slot]).astype(jnp.int32)
        found += mine.astype(jnp.int32)

    lane = lane_index(P_SIZE)

    def load(slot):
        where = row, base, turn = window_place(slots, slot)
        keep = lane >= turn
        w_re = pltpu.roll(probe_re[...], turn, 1)
        w_im = pltpu.roll(probe_im[...], turn, 1)
        patch = []
        for k in (0, 1):
            block = cells[k, pl.ds(row, P_SIZE), pl.ds(base, 3 * LANES)]
            patch.append(
                beside(jnp.where(keep, block[:, :LANES], block[:, 2 * LANES :]), block[:, LANES : 2 * LANES])
            )
        exit_re = w_re * patch[0] - w_im * patch[1]
        exit_im = w_re * patch[1] + w_im * patch[0]
        return (where, keep, w_re, w_im), exit_re, exit_im

    def frame_of(slot):
        return frames[slots[2, slot]].astype(jnp.float32)

    def place(at, back_re, back_im):
        where, keep, w_re, w_im = at
        add_window(acc, 0, where, keep, w_re * back_re + w_im * back_im)
        add_window(acc, 1, where, keep, w_re * back_im - w_im * back_re)

    def step(group):
        frame = [frame_of(slot) for slot in group]
        loaded = [load(slot) for slot in group]
        state = [forward_columns(x[1], x[2], table) for x in loaded]
        state = [forward_rows(*x, table) for x in state]
        state = [residual(x, f) for x, f in zip(state, frame)]
        state = [back_rows(x, table) for x in state]
        state = [back_columns(x, table) for x in state]
        for x, back in zip(loaded, state):
            place(x[0], *back)

    def pair_step(pair, carry):
        step([order[pair * PAIR + i] for i in range(PAIR)])
        return carry

    lax.fori_loop(0, found // PAIR, pair_step, 0)

    @pl.when(found % PAIR == 1)
    def _():
        step([order[found - 1]])


def windows_before(
    slots, cells, probe_re, probe_im, table, frames, acc, order, power,
):
    acc[...] = jnp.zeros_like(acc)
    power[...] = probe_re[...] * probe_re[...] + probe_im[...] * probe_im[...]
    lane = lane_index(P_SIZE)

    def step(slot, carry):
        where = window_place(slots, slot)
        add_window(acc, 2, where, lane >= where[2], pltpu.roll(power[...], where[2], 1))
        return carry

    lax.fori_loop(0, live_slots(slots, cells), step, 0)
    run_windows(
        lambda over, seen, limit: ~over & (seen < limit),
        slots, cells, acc, probe_re, probe_im, table, frames, order,
    )


def reaching(place, right, tile_r, tile_c):
    shape = place.shape
    index = lax.broadcasted_iota(jnp.int32, shape, 0)
    lane = lax.broadcasted_iota(jnp.int32, shape, 1)
    col = pltpu.roll(place, shape[0] - 1, 0)
    low = jnp.where(index == 2, tile_r - P_SIZE, -tile_r).astype(jnp.float32)
    high = jnp.where(index == 4, 0, tile_r).astype(jnp.float32)
    reaches = (lane < MARKS) & (index % 2 == 0) & (index < 6) & (place > low) & (place < high)
    if right < 0:
        reaches &= col > tile_c - P_SIZE
    if right > 0:
        reaches &= col < 0
    bit = lax.shift_left(jnp.ones(shape, jnp.int32), jnp.minimum(lane, MARKS)).astype(jnp.float32)
    bits = jnp.sum(jnp.where(reaches, bit, 0.0), axis=1, keepdims=True)
    return jnp.where(lane < MARKS, place, bits).astype(jnp.int32)


def add_neighbours_light(places, acc, power):
    rows, width = acc.shape[1:]
    tile_r, tile_c = rows - 2 * HALO, width - 2 * LANES
    for right in (-1, 0, 1):
        for i, down in enumerate((0, -1, 1)):
            if not right and not down:
                continue
            first, last = {-1: (P_SIZE - HALO, P_SIZE), 0: (0, P_SIZE), 1: (0, HALO)}[down]
            tiles = {-1: (2,), 0: (0, 1, 2), 1: (0,)}[right]
            lane = lane_index(last - first)
            bits = places[right + 1, 2 * i, MARKS]

            def step(slot, carry):
                row, col = places[right + 1, 2 * i, slot], places[right + 1, 2 * i + 1, slot]

                @pl.when(lax.shift_right_logical(bits, slot) % 2 == 1)
                def _():
                    turn = lax.rem(col + LANES, LANES)
                    at = pl.multiple_of(row + HALO + (down * tile_r + first), 16)
                    base = pl.multiple_of(col + LANES - turn + right * tile_c, LANES)
                    part = pltpu.roll(power[first:last, :], turn, 1)
                    add_window(acc, 2, (at, base, turn), lane >= turn, part, tiles)

                return carry

            @pl.when(bits != 0)
            def _():
                lax.fori_loop(0, MARKS, step, 0)


def windows_after(
    slots, cells, acc_in, probe_re, probe_im, table, frames, marks, by_inner, by_outer,
    acc, order, power, whole, places, sem,
):
    rows, width = acc.shape[1:]
    before, after = received(by_inner, by_outer, "col")
    for i, part in enumerate((before[-MARKS:], marks[...], after[-MARKS:])):
        whole[i] = reaching(part, i - 1, rows - 2 * HALO, width - 2 * LANES)
    copy = pltpu.make_async_copy(whole, places, sem)
    copy.start()
    power[...] = probe_re[...] * probe_re[...] + probe_im[...] * probe_im[...]
    run_windows(
        lambda over, seen, limit: ~over & (seen >= limit),
        slots, cells, acc, probe_re, probe_im, table, frames, order,
    )
    copy.wait()
    add_neighbours_light(places, acc, power)


def windows_over_edge(
    slots, cells_in, acc_in, probe_re, probe_im, table, frames, by_inner, by_outer,
    cells, acc, to_inner, to_outer, order, strip,
):
    rows, width = acc.shape[1:]
    before, after = received(by_inner, by_outer, "col")
    for layer, row, part in pieces(before, 2, rows):
        cells[layer, row : row + part.shape[0], 0:LANES] = part
    for layer, row, part in pieces(after, 2, rows):
        cells[layer, row : row + part.shape[0], width - LANES :] = part
    run_windows(
        lambda over, seen, limit: over,
        slots, cells, acc, probe_re, probe_im, table, frames, order,
    )
    group_rows = 2 * rows // GROUPS
    fill_strip(strip, (acc[0, :, 0:LANES], acc[1, :, 0:LANES]))
    to_left = pack_lanes(strip, group_rows, LANES - HALO)
    fill_strip(strip, (acc[0, :, width - LANES :], acc[1, :, width - LANES :]))
    to_right = pack_lanes(strip, group_rows, 0)
    send_columns(to_left, to_right, to_inner, to_outer)


def row_spill(acc_in, by_inner, by_outer, acc, to_inner, to_outer):
    rows, width = acc.shape[1:]
    before, after = received(by_inner, by_outer, "col")
    lane = lane_index(rows)[0:1]
    for layer, row, part in pieces(before, 2, rows):
        here = slice(row, row + part.shape[0])
        acc[layer, here, LANES : 2 * LANES] += jnp.where(lane < HALO, part, 0.0)
    for layer, row, part in pieces(after, 2, rows):
        here = slice(row, row + part.shape[0])
        acc[layer, here, width - 2 * LANES : width - LANES] += jnp.where(lane >= LANES - HALO, part, 0.0)
    odd = is_odd("row")
    for k in (0, 1):
        up = acc[k, 0:HALO, LANES : width - LANES]
        down = acc[k, rows - HALO : rows, LANES : width - LANES]
        to_inner[k] = jnp.where(odd, up, down)
        to_outer[k] = jnp.where(odd, down, up)


def new_rows(cells, acc, extra, start, size, new_re, new_im):
    here = slice(HALO + start, HALO + start + size)
    middle = slice(LANES, acc.shape[2] - LANES)
    part = [acc[k, here, middle] for k in range(acc.shape[0])]
    if extra is not None:
        part[:2] = [part[k] + extra[k] for k in (0, 1)]
    scale = 1.0 / (part[2] + ridge)
    new_re[start : start + size, :] = cells[0, here, middle] - part[0] * scale
    new_im[start : start + size, :] = cells[1, here, middle] - part[1] * scale


def finish_inner(cells, acc, new_re, new_im, near_re, near_im, sems):
    tile_r = near_re.shape[0]
    new_rows(cells, acc, None, HALO, tile_r - 2 * HALO, near_re, near_im)
    rows = slice(HALO, tile_r - HALO)
    finish_all(fetch([(near_re.at[rows], new_re.at[rows]), (near_im.at[rows], new_im.at[rows])], sems))


def finish_edges(cells, acc, by_inner, by_outer, re_in, im_in, new_re, new_im, near_re, near_im, sems):
    tile_r = near_re.shape[0]
    copies = []
    for i, (start, extra) in enumerate(zip((0, tile_r - HALO), received(by_inner, by_outer, "row"))):
        new_rows(cells, acc, extra, start, HALO, near_re, near_im)
        rows = slice(start, start + HALO)
        pairs = ((near_re.at[rows], new_re.at[rows]), (near_im.at[rows], new_im.at[rows]))
        copies += fetch(pairs, sems.at[2 * i : 2 * i + 2])
    finish_all(copies)


def swap(to_inner, to_outer, axis, gather):
    devices = lax.axis_size(axis)
    inner = [(i, i + 1) for i in range(0, devices, 2)]
    partner = {i: i + 1 if i % 2 else i - 1 for i in range(1, devices - 1)}
    n_row, n_col = lax.axis_size("row"), lax.axis_size("col")
    pairs = []
    for row in range(n_row):
        for col in range(n_col):
            if axis == "row":
                there = (partner[row], col) if row in partner else (row, col ^ 1)
            else:
                there = (row, partner[col]) if col in partner else (row ^ 1, col)
            pairs.append((row * n_col + col, there[0] * n_col + there[1]))
    by_outer = lax.ppermute(to_outer, ("row", "col"), pairs)
    if gather:
        by_inner = lax.all_gather(to_inner, axis, axis_index_groups=[list(pair) for pair in inner])
    else:
        by_inner = lax.ppermute(to_inner, axis, inner + [(j, i) for i, j in inner])
    return by_inner, by_outer


def far(x):
    return pltpu.with_memory_space_constraint(x, pltpu.HBM)


def f32(*shape):
    return jax.ShapeDtypeStruct(shape, jnp.float32)


def shards(object_re, object_im, probe_re, probe_im, frames, counts, offsets, frame_index):
    tile_r, tile_c = object_re.shape
    rows, width = tile_r + 2 * HALO, tile_c + 2 * LANES
    layers = 3
    slots = offsets.shape[2]
    table = jnp.asarray(transform_tables())
    frames = frames.reshape(frames.shape[2:])
    cells_shape, acc_shape = f32(2, rows, width), f32(layers, rows, width)
    dma = pltpu.SemaphoreType.DMA

    places = jnp.swapaxes(offsets, 2, 3)
    edge = f32(2 * HALO + MARKS, tile_c)
    to_inner, to_outer, marked = pl.pallas_call(
        row_edges,
        out_shape=(edge, edge, jax.ShapeDtypeStruct((3, slots), jnp.int32)),
        in_specs=[SMEM] + [HBM] * 4,
        out_specs=(VMEM, VMEM, VMEM),
        scratch_shapes=[
            pltpu.VMEM(places.shape, jnp.int32), pltpu.VMEM(frame_index.shape, jnp.int32), dma((6,)),
        ],
        compiler_params=SMALL,
        name="row_edges",
    )(counts, far(object_re), far(object_im), far(places), far(frame_index))
    by_inner, by_outer = swap(to_inner, to_outer, "row", True)

    cells, *fixed = pl.pallas_call(
        load_state,
        out_shape=(
            cells_shape, f32(*probe_re.shape), f32(*probe_im.shape),
            jax.ShapeDtypeStruct(table.shape, table.dtype), jax.ShapeDtypeStruct(frames.shape, frames.dtype),
        ),
        in_specs=[HBM] * 6,
        out_specs=(VMEM,) * 5,
        scratch_shapes=[dma((6,))],
        compiler_params=SMALL,
        cost_estimate=BUSY,
        name="load_state",
    )(*map(far, (object_re, object_im, probe_re, probe_im, table, frames)))

    strip = pltpu.VMEM((2 * rows, LANES), jnp.float32)
    packed = f32(2 * rows // GROUPS + MARKS, LANES)
    cells, marks, to_inner, to_outer = pl.pallas_call(
        row_halos,
        out_shape=(cells_shape, f32(MARKS, LANES), packed, packed),
        in_specs=[VMEM] * 4,
        out_specs=(VMEM,) * 4,
        scratch_shapes=[strip],
        input_output_aliases={0: 0},
        compiler_params=SMALL,
        name="row_halos",
    )(cells, to_outer, by_inner, by_outer)
    edges = swap(to_inner, to_outer, "col", False)

    order = pltpu.SMEM((slots,), jnp.int32)
    acc = pl.pallas_call(
        windows_before,
        out_shape=acc_shape,
        in_specs=[SMEM] + [VMEM] * 5,
        out_specs=VMEM,
        scratch_shapes=[order, pltpu.VMEM(probe_re.shape, jnp.float32)],
        compiler_params=PARAMS,
        cost_estimate=BUSY,
        name="windows_before",
    )(marked, cells, *fixed)

    packed = f32(2 * rows // GROUPS, LANES)
    cells, acc, to_inner, to_outer = pl.pallas_call(
        windows_over_edge,
        out_shape=(cells_shape, acc_shape, packed, packed),
        in_specs=[SMEM] + [VMEM] * 8,
        out_specs=(VMEM,) * 4,
        scratch_shapes=[order, strip],
        input_output_aliases={1: 0, 2: 1},
        compiler_params=PARAMS,
        cost_estimate=BUSY,
        name="windows_over_edge",
    )(marked, cells, acc, *fixed, *edges)
    by_inner, by_outer = swap(to_inner, to_outer, "col", False)

    acc = pl.pallas_call(
        windows_after,
        out_shape=acc_shape,
        in_specs=[SMEM] + [VMEM] * 9,
        out_specs=VMEM,
        scratch_shapes=[
            order, pltpu.VMEM(probe_re.shape, jnp.float32),
            pltpu.VMEM((3, MARKS, LANES), jnp.int32), pltpu.SMEM((3, MARKS, LANES), jnp.int32), dma(()),
        ],
        input_output_aliases={2: 0},
        compiler_params=PARAMS,
        cost_estimate=BUSY,
        name="windows_after",
    )(marked, cells, acc, *fixed, marks, *edges)

    edge = f32(2, HALO, tile_c)
    acc, to_inner, to_outer = pl.pallas_call(
        row_spill,
        out_shape=(acc_shape, edge, edge),
        in_specs=[VMEM] * 3,
        out_specs=(VMEM,) * 3,
        input_output_aliases={0: 0},
        compiler_params=SMALL,
        name="row_spill",
    )(acc, by_inner, by_outer)
    by_inner, by_outer = swap(to_inner, to_outer, "row", True)

    near = [pltpu.VMEM((tile_r, tile_c), jnp.float32)] * 2
    new = (f32(tile_r, tile_c), f32(tile_r, tile_c))
    new_re, new_im = pl.pallas_call(
        finish_inner,
        out_shape=new,
        in_specs=[VMEM] * 2,
        out_specs=(HBM, HBM),
        scratch_shapes=near + [dma((2,))],
        compiler_params=SMALL,
        cost_estimate=BUSY,
        name="finish_inner",
    )(cells, acc)
    return pl.pallas_call(
        finish_edges,
        out_shape=new,
        in_specs=[VMEM] * 4 + [HBM] * 2,
        out_specs=(HBM, HBM),
        scratch_shapes=near + [dma((4,))],
        input_output_aliases={4: 0, 5: 1},
        compiler_params=SMALL,
        name="finish_edges",
    )(cells, acc, by_inner, by_outer, far(new_re), far(new_im))


def solution(mesh):
    return jax.shard_map(
        shards,
        mesh=mesh,
        in_specs=(
            P("row", "col"),
            P("row", "col"),
            P(),
            P(),
            P("row", "col", None, None, None),
            P("row", "col"),
            P("row", "col", None, None),
            P("row", "col", None),
        ),
        out_specs=(P("row", "col"), P("row", "col")),
        check_vma=False,
    )
```

```python
import functools
import math

import jax
import jax.numpy as jnp
import ml_dtypes
import numpy as np
from jax import lax
from jax.experimental import pallas as pl
from jax.experimental.pallas import tpu as pltpu
from jax.sharding import PartitionSpec as P

P_SIZE = 256
HALF = P_SIZE // 2
HALO = 32
LANES = 128
GROUPS = LANES // HALO
MARKS = 8
PAIR = 2

floor_amp = 0.5
ridge = 1.0

VMEM = pl.BlockSpec(memory_space=pltpu.VMEM)
SMEM = pl.BlockSpec(memory_space=pltpu.SMEM)
HBM = pl.BlockSpec(memory_space=pltpu.HBM)
PARAMS = pltpu.CompilerParams(vmem_limit_bytes=32 * 1024 * 1024)
SMALL = pltpu.CompilerParams(vmem_limit_bytes=16 * 1024 * 1024)
BUSY = pl.CostEstimate(flops=4_000_000_000, bytes_accessed=8_000_000, transcendentals=0)


def transform_tables():
    index = np.arange(HALF)
    plain = []
    for parity in (0, 1):
        angle = 2.0 * math.pi / P_SIZE * (index[:, None] * (2 * index[None, :] + parity) % P_SIZE)
        cos, sin = np.cos(angle), np.sin(angle)
        plain.append(np.block([[cos, -sin], [sin, cos]]) / math.sqrt(P_SIZE))
    parts = []
    for table in plain + [t.T for t in plain]:
        high = table.astype(np.float32).astype(ml_dtypes.bfloat16)
        low = (table - high.astype(np.float64)).astype(np.float32).astype(ml_dtypes.bfloat16)
        parts += [high, low]
    order = np.concatenate([np.arange(0, P_SIZE, 2), np.arange(1, P_SIZE, 2)])
    sort = np.zeros((P_SIZE, P_SIZE), np.float32)
    sort[np.arange(P_SIZE), order] = 1.0
    parts += [sort.astype(ml_dtypes.bfloat16), sort.T.astype(ml_dtypes.bfloat16)]
    return np.stack(parts)


def lane_index(rows):
    return lax.broadcasted_iota(jnp.int32, (rows, LANES), 1)


def pack_lanes(ref, rows, first):
    lane = lane_index(rows)
    packed = None
    for g in range(GROUPS):
        part = ref[g * rows : (g + 1) * rows, :]
        if g:
            part = pltpu.roll(part, HALO * g, 1)
        low = (first + HALO * g) % LANES
        mine = (lane >= low) & (lane < low + HALO)
        packed = part if packed is None else jnp.where(mine, part, packed)
    return packed


def unpack_lanes(packed, group):
    return pltpu.roll(packed, LANES - HALO * group, 1) if group else packed


def split(x):
    high = x.astype(jnp.bfloat16)
    return high, (x - high.astype(jnp.float32)).astype(jnp.bfloat16)


def product(left, right):
    return jnp.dot(left, right, preferred_element_type=jnp.float32)


def times_table(x, table, which):
    high, low = split(x)
    t_high, t_low = table[2 * which], table[2 * which + 1]
    return product(beside(high, high, low), below(t_high, t_low, t_high))


def table_times(table, which, x):
    high, low = split(x)
    t_high, t_low = table[2 * which], table[2 * which + 1]
    return product(beside(t_high, t_low, t_high), below(high, high, low))


def beside(*blocks):
    return jnp.concatenate(blocks, axis=1)


def below(*blocks):
    return jnp.concatenate(blocks, axis=0)


def ends(x):
    return x[:, :HALF], x[:, HALF:]


def forward_columns(exit_re, exit_im, table):
    re_lo, re_hi = ends(exit_re)
    im_lo, im_hi = ends(exit_im)
    even = times_table(beside(re_lo + re_hi, im_lo + im_hi), table, 0)
    odd = times_table(beside(re_lo - re_hi, im_lo - im_hi), table, 1)
    return even, odd


def forward_rows(even, odd, table):
    out = []
    for parity in (0, 1):
        if parity == 0:
            se, so = even[:HALF] + even[HALF:], odd[:HALF] + odd[HALF:]
        else:
            se, so = even[:HALF] - even[HALF:], odd[:HALF] - odd[HALF:]
        e_re, e_im = ends(se)
        o_re, o_im = ends(so)
        out.append(table_times(table, 2 + parity, below(beside(e_re, o_re), beside(e_im, o_im))))
    return out


def residual(far, frame):
    out = []
    for parity in (0, 1):
        re, im = far[parity][:HALF], far[parity][HALF:]
        level = jnp.maximum(re * re + im * im, floor_amp * floor_amp)
        inten = frame[parity * HALF : (parity + 1) * HALF]
        factor = 1.0 - inten * lax.rsqrt(inten * level)
        out.append(below(re * factor, im * factor))
    return out


def back_rows(res, table):
    first = table_times(table, 0, res[0])
    second = table_times(table, 1, res[1])
    upper, lower = first + second, first - second
    out = []
    for cols in (slice(0, HALF), slice(HALF, P_SIZE)):
        out.append(
            below(
                beside(upper[:HALF, cols], upper[HALF:, cols]),
                beside(lower[:HALF, cols], lower[HALF:, cols]),
            )
        )
    return out


def back_columns(parts, table):
    even = times_table(parts[0], table, 2)
    odd = times_table(parts[1], table, 3)
    lo, hi = even + odd, even - odd
    return beside(lo[:, :HALF], hi[:, :HALF]), beside(lo[:, HALF:], hi[:, HALF:])


def is_odd(axis):
    return lax.rem(lax.axis_index(axis), 2) == 1


def fetch(pairs, sems):
    copies = [pltpu.make_async_copy(far, near, sems.at[i]) for i, (far, near) in enumerate(pairs)]
    for copy in copies:
        copy.start()
    return copies


def finish_all(copies):
    for copy in copies:
        copy.wait()


def row_edges(counts, obj_re, obj_im, offsets, chosen, to_inner, to_outer, marked, places, frame_of, sems):
    tile_r = obj_re.shape[0]
    odd = is_odd("row")
    low = pl.multiple_of(jnp.where(odd, 0, tile_r - HALO), 16)
    high = pl.multiple_of(jnp.where(odd, tile_r - HALO, 0), 16)
    pairs = [(offsets, places), (chosen, frame_of)]
    for k, ref in enumerate((obj_re, obj_im)):
        rows = slice(k * HALO, (k + 1) * HALO)
        pairs.append((ref.at[pl.ds(high, HALO)], to_outer.at[rows]))
        pairs.append((ref.at[pl.ds(low, HALO)], to_inner.at[rows]))
    copies = fetch(pairs, sems)
    finish_all(copies[:2])
    place = places[0, 0]
    live = lax.broadcasted_iota(jnp.int32, place.shape, 1) < counts[0, 0]
    place = jnp.where(live, place, 2 * tile_r)
    marked[0:2, :] = place
    marked[2:3, :] = frame_of[0]
    for message in (to_inner, to_outer):
        message[2 * HALO : 2 * HALO + 2, 0 : place.shape[1]] = place.astype(jnp.float32)
    finish_all(copies[2:])


def window_place(slots, slot):
    row = pl.multiple_of(slots[0, slot] + HALO, 16)
    col = slots[1, slot] + LANES
    turn = lax.rem(col, LANES)
    return row, pl.multiple_of(col - turn, LANES), turn


def add_window(acc, layer, where, keep, term, tiles=(0, 1, 2)):
    row, base, _ = where
    lo, hi = ends(term)
    parts = (jnp.where(keep, lo, 0.0), hi, jnp.where(keep, 0.0, lo))
    for t in tiles:
        acc[layer, pl.ds(row, term.shape[0]), pl.ds(base + t * LANES, LANES)] += parts[t]


def fill_strip(strip, parts):
    done = 0
    for part in parts:
        strip[done : done + part.shape[0], :] = part
        done += part.shape[0]


def send_columns(to_left, to_right, to_inner, to_outer):
    odd = is_odd("col")
    to_inner[0 : to_left.shape[0], :] = jnp.where(odd, to_left, to_right)
    to_outer[0 : to_left.shape[0], :] = jnp.where(odd, to_right, to_left)


def received(by_inner, by_outer, axis):
    odd = is_odd(axis)
    index = lax.axis_index(axis)
    inside = (index > 0) & (index < lax.axis_size(axis) - 1)
    by_outer = jnp.where(inside, by_outer[...], 0.0)
    by_inner = by_inner[...]
    return jnp.where(odd, by_inner, by_outer), jnp.where(odd, by_outer, by_inner)


def pieces(packed, layers, rows):
    group_rows = layers * rows // GROUPS
    for g in range(GROUPS):
        part = unpack_lanes(packed, g)
        done = 0
        while done < group_rows:
            layer, row = divmod(g * group_rows + done, rows)
            size = min(group_rows - done, rows - row)
            yield layer, row, part[done : done + size]
            done += size


def row_halos(cells_in, own, by_inner, by_outer, cells, marks, to_inner, to_outer, strip):
    rows, width = cells.shape[1:]
    middle = slice(LANES, width - LANES)
    before, after = received(by_inner, by_outer, "row")
    for k in (0, 1):
        cells[k, 0:HALO, middle] = before[k * HALO : (k + 1) * HALO]
        cells[k, rows - HALO : rows, middle] = after[k * HALO : (k + 1) * HALO]
    first_mark = 2 * HALO
    for i, message in enumerate((own[...], before, after)):
        marks[2 * i : 2 * i + 2, :] = message[first_mark : first_mark + 2, 0:LANES]
    group_rows = 2 * rows // GROUPS
    first, last = slice(LANES, 2 * LANES), slice(width - 2 * LANES, width - LANES)
    fill_strip(strip, (cells[0, :, first], cells[1, :, first]))
    to_left = pack_lanes(strip, group_rows, 0)
    fill_strip(strip, (cells[0, :, last], cells[1, :, last]))
    to_right = pack_lanes(strip, group_rows, LANES - HALO)
    send_columns(to_left, to_right, to_inner, to_outer)
    to_inner[group_rows:, :] = marks[...]
    to_outer[group_rows:, :] = marks[...]


def live_slots(slots, cells):
    tile_r = cells.shape[1] - 2 * HALO
    count = jnp.int32(0)
    for slot in range(slots.shape[1]):
        count += (slots[0, slot] < tile_r).astype(jnp.int32)
    return count


FIRST, BEFORE, OVER, AFTER, LAST = range(5)


def run_windows(phase, slots, cells, acc, probe_re, probe_im, table, frames, order):
    tile_r, tile_c = cells.shape[1] - 2 * HALO, cells.shape[2] - 2 * LANES
    count = live_slots(slots, cells)
    kinds = []
    n_inside, n_row = jnp.int32(0), jnp.int32(0)
    for slot in range(slots.shape[1]):
        row, col = slots[0, slot], slots[1, slot]
        live = slot < count
        over_col = (col < 0) | (col > tile_c - P_SIZE)
        over_row = (row < 0) | (row > tile_r - P_SIZE)
        inside, by_row = live & ~over_col & ~over_row, live & ~over_col & over_row
        kinds.append((live & over_col, inside, by_row, n_inside, n_row))
        n_inside += inside.astype(jnp.int32)
        n_row += by_row.astype(jnp.int32)
    first = jnp.minimum(n_inside, PAIR)
    rest = n_inside - first + n_row
    last = jnp.clip(rest - 2 * PAIR, 0, jnp.minimum(n_inside - first, PAIR))
    before = jnp.minimum(rest - last, PAIR)
    found = jnp.int32(0)
    for slot, (over, inside, by_row, inside_rank, row_rank) in enumerate(kinds):
        rank = jnp.where(by_row, row_rank, n_row + inside_rank - first)
        later = by_row | (inside & (inside_rank >= first))
        mine = {
            FIRST: lambda: inside & (inside_rank < first),
            BEFORE: lambda: later & (rank < before),
            OVER: lambda: over,
            AFTER: lambda: later & (rank >= before) & (rank < rest - last),
            LAST: lambda: later & (rank >= rest - last),
        }[phase]()

        @pl.when(mine)
        def _():
            order[found] = slot

        found += mine.astype(jnp.int32)

    lane = lane_index(P_SIZE)

    def load(slot):
        where = row, base, turn = window_place(slots, slot)
        keep = lane >= turn
        w_re = pltpu.roll(probe_re[...], turn, 1)
        w_im = pltpu.roll(probe_im[...], turn, 1)
        patch = []
        for k in (0, 1):
            block = cells[k, pl.ds(row, P_SIZE), pl.ds(base, 3 * LANES)]
            patch.append(
                beside(jnp.where(keep, block[:, :LANES], block[:, 2 * LANES :]), block[:, LANES : 2 * LANES])
            )
        exit_re = w_re * patch[0] - w_im * patch[1]
        exit_im = w_re * patch[1] + w_im * patch[0]
        return (where, keep, w_re, w_im), exit_re, exit_im

    def frame_of(slot):
        half = product(table[8], frames[slots[2, slot]]).astype(jnp.bfloat16)
        return product(half, table[9])

    def place(at, back_re, back_im):
        where, keep, w_re, w_im = at
        add_window(acc, 0, where, keep, w_re * back_re + w_im * back_im)
        add_window(acc, 1, where, keep, w_re * back_im - w_im * back_re)

    def step(group):
        frame = [frame_of(slot) for slot in group]
        loaded = [load(slot) for slot in group]
        state = [forward_columns(x[1], x[2], table) for x in loaded]
        state = [forward_rows(*x, table) for x in state]
        state = [residual(x, f) for x, f in zip(state, frame)]
        state = [back_rows(x, table) for x in state]
        state = [back_columns(x, table) for x in state]
        for x, back in zip(loaded, state):
            place(x[0], *back)

    def pair_step(pair, carry):
        step([order[pair * PAIR + i] for i in range(PAIR)])
        return carry

    lax.fori_loop(0, found // PAIR, pair_step, 0)

    @pl.when(found % PAIR == 1)
    def _():
        step([order[found - 1]])


def windows_first(
    slots, obj_re, obj_im, probe_re_far, probe_im_far, table_far, frames_far,
    cells, acc, probe_re, probe_im, table, frames, order, sems,
):
    tile_r, tile_c = obj_re.shape
    inner = slice(HALO, HALO + tile_r)
    middle = slice(LANES, LANES + tile_c)
    pairs = (
        (table_far, table),
        (frames_far, frames),
        (obj_re, cells.at[0, inner, middle]),
        (obj_im, cells.at[1, inner, middle]),
        (probe_re_far, probe_re),
        (probe_im_far, probe_im),
    )
    copies = fetch(pairs, sems)
    acc[...] = jnp.zeros_like(acc)
    finish_all(copies)
    run_windows(FIRST, slots, cells, acc, probe_re, probe_im, table, frames, order)


def windows_before(
    slots, cells, acc_in, probe_re, probe_im, table, frames, acc, order, power,
):
    power[...] = probe_re[...] * probe_re[...] + probe_im[...] * probe_im[...]
    lane = lane_index(P_SIZE)

    def step(slot, carry):
        where = window_place(slots, slot)
        add_window(acc, 2, where, lane >= where[2], pltpu.roll(power[...], where[2], 1))
        return carry

    lax.fori_loop(0, live_slots(slots, cells), step, 0)
    run_windows(BEFORE, slots, cells, acc, probe_re, probe_im, table, frames, order)


def reaching(place, right, tile_r, tile_c):
    shape = place.shape
    index = lax.broadcasted_iota(jnp.int32, shape, 0)
    lane = lax.broadcasted_iota(jnp.int32, shape, 1)
    col = pltpu.roll(place, shape[0] - 1, 0)
    low = jnp.where(index == 2, tile_r - P_SIZE, -tile_r).astype(jnp.float32)
    high = jnp.where(index == 4, 0, tile_r).astype(jnp.float32)
    reaches = (lane < MARKS) & (index % 2 == 0) & (index < 6) & (place > low) & (place < high)
    if right < 0:
        reaches &= col > tile_c - P_SIZE
    if right > 0:
        reaches &= col < 0
    bit = lax.shift_left(jnp.ones(shape, jnp.int32), jnp.minimum(lane, MARKS)).astype(jnp.float32)
    bits = jnp.sum(jnp.where(reaches, bit, 0.0), axis=1, keepdims=True)
    return jnp.where(lane < MARKS, place, bits).astype(jnp.int32)


def add_neighbours_light(places, acc, power):
    rows, width = acc.shape[1:]
    tile_r, tile_c = rows - 2 * HALO, width - 2 * LANES
    for right in (-1, 0, 1):
        for i, down in enumerate((0, -1, 1)):
            if not right and not down:
                continue
            first, last = {-1: (P_SIZE - HALO, P_SIZE), 0: (0, P_SIZE), 1: (0, HALO)}[down]
            tiles = {-1: (2,), 0: (0, 1, 2), 1: (0,)}[right]
            lane = lane_index(last - first)
            bits = places[right + 1, 2 * i, MARKS]

            def step(slot, carry):
                row, col = places[right + 1, 2 * i, slot], places[right + 1, 2 * i + 1, slot]

                @pl.when(lax.shift_right_logical(bits, slot) % 2 == 1)
                def _():
                    turn = lax.rem(col + LANES, LANES)
                    at = pl.multiple_of(row + HALO + (down * tile_r + first), 16)
                    base = pl.multiple_of(col + LANES - turn + right * tile_c, LANES)
                    part = pltpu.roll(power[first:last, :], turn, 1)
                    add_window(acc, 2, (at, base, turn), lane >= turn, part, tiles)

                return carry

            @pl.when(bits != 0)
            def _():
                lax.fori_loop(0, MARKS, step, 0)


def windows_after(
    slots, cells, acc_in, probe_re, probe_im, table, frames, marks, by_inner, by_outer,
    acc, order, power, whole, places, sem,
):
    rows, width = acc.shape[1:]
    before, after = received(by_inner, by_outer, "col")
    for i, part in enumerate((before[-MARKS:], marks[...], after[-MARKS:])):
        whole[i] = reaching(part, i - 1, rows - 2 * HALO, width - 2 * LANES)
    copy = pltpu.make_async_copy(whole, places, sem)
    copy.start()
    power[...] = probe_re[...] * probe_re[...] + probe_im[...] * probe_im[...]
    run_windows(AFTER, slots, cells, acc, probe_re, probe_im, table, frames, order)
    copy.wait()
    add_neighbours_light(places, acc, power)


def windows_over_edge(
    slots, cells_in, acc_in, probe_re, probe_im, table, frames, by_inner, by_outer,
    cells, acc, to_inner, to_outer, order, strip,
):
    rows, width = acc.shape[1:]
    before, after = received(by_inner, by_outer, "col")
    for layer, row, part in pieces(before, 2, rows):
        cells[layer, row : row + part.shape[0], 0:LANES] = part
    for layer, row, part in pieces(after, 2, rows):
        cells[layer, row : row + part.shape[0], width - LANES :] = part
    run_windows(OVER, slots, cells, acc, probe_re, probe_im, table, frames, order)
    group_rows = 2 * rows // GROUPS
    fill_strip(strip, (acc[0, :, 0:LANES], acc[1, :, 0:LANES]))
    to_left = pack_lanes(strip, group_rows, LANES - HALO)
    fill_strip(strip, (acc[0, :, width - LANES :], acc[1, :, width - LANES :]))
    to_right = pack_lanes(strip, group_rows, 0)
    send_columns(to_left, to_right, to_inner, to_outer)


def row_spill(acc_in, by_inner, by_outer, acc, to_inner, to_outer):
    rows, width = acc.shape[1:]
    before, after = received(by_inner, by_outer, "col")
    lane = lane_index(rows)[0:1]
    for layer, row, part in pieces(before, 2, rows):
        here = slice(row, row + part.shape[0])
        acc[layer, here, LANES : 2 * LANES] += jnp.where(lane < HALO, part, 0.0)
    for layer, row, part in pieces(after, 2, rows):
        here = slice(row, row + part.shape[0])
        acc[layer, here, width - 2 * LANES : width - LANES] += jnp.where(lane >= LANES - HALO, part, 0.0)
    odd = is_odd("row")
    for k in (0, 1):
        up = acc[k, 0:HALO, LANES : width - LANES]
        down = acc[k, rows - HALO : rows, LANES : width - LANES]
        to_inner[k] = jnp.where(odd, up, down)
        to_outer[k] = jnp.where(odd, down, up)


def new_rows(cells, acc, extra, start, size, new_re, new_im):
    here = slice(HALO + start, HALO + start + size)
    middle = slice(LANES, acc.shape[2] - LANES)
    part = [acc[k, here, middle] for k in range(acc.shape[0])]
    if extra is not None:
        part[:2] = [part[k] + extra[k] for k in (0, 1)]
    scale = 1.0 / (part[2] + ridge)
    new_re[start : start + size, :] = cells[0, here, middle] - part[0] * scale
    new_im[start : start + size, :] = cells[1, here, middle] - part[1] * scale


def finish_inner(
    slots, cells, acc_in, probe_re, probe_im, table, frames, acc, new_re, new_im, order, near_re, near_im, sems,
):
    run_windows(LAST, slots, cells, acc, probe_re, probe_im, table, frames, order)
    tile_r = near_re.shape[0]
    new_rows(cells, acc, None, HALO, tile_r - 2 * HALO, near_re, near_im)
    rows = slice(HALO, tile_r - HALO)
    finish_all(fetch([(near_re.at[rows], new_re.at[rows]), (near_im.at[rows], new_im.at[rows])], sems))


def finish_edges(cells, acc, by_inner, by_outer, re_in, im_in, new_re, new_im, near_re, near_im, sems):
    tile_r = near_re.shape[0]
    copies = []
    for i, (start, extra) in enumerate(zip((0, tile_r - HALO), received(by_inner, by_outer, "row"))):
        new_rows(cells, acc, extra, start, HALO, near_re, near_im)
        rows = slice(start, start + HALO)
        pairs = ((near_re.at[rows], new_re.at[rows]), (near_im.at[rows], new_im.at[rows]))
        copies += fetch(pairs, sems.at[2 * i : 2 * i + 2])
    finish_all(copies)


def swap(to_inner, to_outer, axis):
    devices = lax.axis_size(axis)
    inner = [(i, i + 1) for i in range(0, devices, 2)]
    partner = {i: i + 1 if i % 2 else i - 1 for i in range(1, devices - 1)}
    n_row, n_col = lax.axis_size("row"), lax.axis_size("col")
    pairs = []
    for row in range(n_row):
        for col in range(n_col):
            if axis == "row":
                there = (partner[row], col) if row in partner else (row, col ^ 1)
            else:
                there = (row, partner[col]) if col in partner else (row ^ 1, col)
            pairs.append((row * n_col + col, there[0] * n_col + there[1]))
    by_outer = lax.ppermute(to_outer, ("row", "col"), pairs)
    by_inner = lax.ppermute(to_inner, axis, inner + [(j, i) for i, j in inner])
    return by_inner, by_outer


def far(x):
    return pltpu.with_memory_space_constraint(x, pltpu.HBM)


def f32(*shape):
    return jax.ShapeDtypeStruct(shape, jnp.float32)


def shards(object_re, object_im, probe_re, probe_im, frames, counts, offsets, frame_index):
    tile_r, tile_c = object_re.shape
    rows, width = tile_r + 2 * HALO, tile_c + 2 * LANES
    layers = 3
    slots = offsets.shape[2]
    table = jnp.asarray(transform_tables())
    frames = frames.reshape(frames.shape[2:])
    cells_shape, acc_shape = f32(2, rows, width), f32(layers, rows, width)
    dma = pltpu.SemaphoreType.DMA

    places = jnp.swapaxes(offsets, 2, 3)
    edge = f32(2 * HALO + MARKS, tile_c)
    to_inner, to_outer, marked = pl.pallas_call(
        row_edges,
        out_shape=(edge, edge, jax.ShapeDtypeStruct((3, slots), jnp.int32)),
        in_specs=[SMEM] + [HBM] * 4,
        out_specs=(VMEM, VMEM, VMEM),
        scratch_shapes=[
            pltpu.VMEM(places.shape, jnp.int32), pltpu.VMEM(frame_index.shape, jnp.int32), dma((6,)),
        ],
        compiler_params=SMALL,
        name="row_edges",
    )(counts, far(object_re), far(object_im), far(places), far(frame_index))
    by_inner, by_outer = swap(to_inner, to_outer, "row")

    order = pltpu.SMEM((slots,), jnp.int32)
    cells, acc, *fixed = pl.pallas_call(
        windows_first,
        out_shape=(
            cells_shape, acc_shape, f32(*probe_re.shape), f32(*probe_im.shape),
            jax.ShapeDtypeStruct(table.shape, table.dtype), jax.ShapeDtypeStruct(frames.shape, frames.dtype),
        ),
        in_specs=[SMEM] + [HBM] * 6,
        out_specs=(VMEM,) * 6,
        scratch_shapes=[order, dma((6,))],
        compiler_params=PARAMS,
        cost_estimate=BUSY,
        name="windows_first",
    )(marked, *map(far, (object_re, object_im, probe_re, probe_im, table, frames)))

    strip = pltpu.VMEM((2 * rows, LANES), jnp.float32)
    packed = f32(2 * rows // GROUPS + MARKS, LANES)
    cells, marks, to_inner, to_outer = pl.pallas_call(
        row_halos,
        out_shape=(cells_shape, f32(MARKS, LANES), packed, packed),
        in_specs=[VMEM] * 4,
        out_specs=(VMEM,) * 4,
        scratch_shapes=[strip],
        input_output_aliases={0: 0},
        compiler_params=SMALL,
        name="row_halos",
    )(cells, to_outer, by_inner, by_outer)
    edges = swap(to_inner, to_outer, "col")

    acc = pl.pallas_call(
        windows_before,
        out_shape=acc_shape,
        in_specs=[SMEM] + [VMEM] * 6,
        out_specs=VMEM,
        scratch_shapes=[order, pltpu.VMEM(probe_re.shape, jnp.float32)],
        input_output_aliases={2: 0},
        compiler_params=PARAMS,
        cost_estimate=BUSY,
        name="windows_before",
    )(marked, cells, acc, *fixed)

    packed = f32(2 * rows // GROUPS, LANES)
    cells, acc, to_inner, to_outer = pl.pallas_call(
        windows_over_edge,
        out_shape=(cells_shape, acc_shape, packed, packed),
        in_specs=[SMEM] + [VMEM] * 8,
        out_specs=(VMEM,) * 4,
        scratch_shapes=[order, strip],
        input_output_aliases={1: 0, 2: 1},
        compiler_params=PARAMS,
        cost_estimate=BUSY,
        name="windows_over_edge",
    )(marked, cells, acc, *fixed, *edges)
    by_inner, by_outer = swap(to_inner, to_outer, "col")

    acc = pl.pallas_call(
        windows_after,
        out_shape=acc_shape,
        in_specs=[SMEM] + [VMEM] * 9,
        out_specs=VMEM,
        scratch_shapes=[
            order, pltpu.VMEM(probe_re.shape, jnp.float32),
            pltpu.VMEM((3, MARKS, LANES), jnp.int32), pltpu.SMEM((3, MARKS, LANES), jnp.int32), dma(()),
        ],
        input_output_aliases={2: 0},
        compiler_params=PARAMS,
        cost_estimate=BUSY,
        name="windows_after",
    )(marked, cells, acc, *fixed, marks, *edges)

    edge = f32(2, HALO, tile_c)
    acc, to_inner, to_outer = pl.pallas_call(
        row_spill,
        out_shape=(acc_shape, edge, edge),
        in_specs=[VMEM] * 3,
        out_specs=(VMEM,) * 3,
        input_output_aliases={0: 0},
        compiler_params=SMALL,
        name="row_spill",
    )(acc, by_inner, by_outer)
    by_inner, by_outer = swap(to_inner, to_outer, "row")

    near = [pltpu.VMEM((tile_r, tile_c), jnp.float32)] * 2
    new = (f32(tile_r, tile_c), f32(tile_r, tile_c))
    acc, new_re, new_im = pl.pallas_call(
        finish_inner,
        out_shape=(acc_shape, *new),
        in_specs=[SMEM] + [VMEM] * 6,
        out_specs=(VMEM, HBM, HBM),
        scratch_shapes=[order] + near + [dma((2,))],
        input_output_aliases={2: 0},
        compiler_params=PARAMS,
        cost_estimate=BUSY,
        name="finish_inner",
    )(marked, cells, acc, *fixed)
    return pl.pallas_call(
        finish_edges,
        out_shape=new,
        in_specs=[VMEM] * 4 + [HBM] * 2,
        out_specs=(HBM, HBM),
        scratch_shapes=near + [dma((4,))],
        input_output_aliases={4: 0, 5: 1},
        compiler_params=SMALL,
        name="finish_edges",
    )(cells, acc, by_inner, by_outer, far(new_re), far(new_im))


def solution(mesh):
    return jax.shard_map(
        shards,
        mesh=mesh,
        in_specs=(
            P("row", "col"),
            P("row", "col"),
            P(),
            P(),
            P("row", "col", None, None, None),
            P("row", "col"),
            P("row", "col", None, None),
            P("row", "col", None),
        ),
        out_specs=(P("row", "col"), P("row", "col")),
        check_vma=False,
    )
```

```python
import functools
import math

import jax
import jax.numpy as jnp
import ml_dtypes
import numpy as np
from jax import lax
from jax.experimental import pallas as pl
from jax.experimental.pallas import tpu as pltpu
from jax.sharding import PartitionSpec as P

P_SIZE = 256
HALF = P_SIZE // 2
HALO = 32
LANES = 128
GROUPS = LANES // HALO
MARKS = 8
PAIR = 2

floor_amp = 0.5
ridge = 1.0

VMEM = pl.BlockSpec(memory_space=pltpu.VMEM)
SMEM = pl.BlockSpec(memory_space=pltpu.SMEM)
HBM = pl.BlockSpec(memory_space=pltpu.HBM)
PARAMS = pltpu.CompilerParams(vmem_limit_bytes=32 * 1024 * 1024)
SMALL = pltpu.CompilerParams(vmem_limit_bytes=16 * 1024 * 1024)
BUSY = pl.CostEstimate(flops=4_000_000_000, bytes_accessed=8_000_000, transcendentals=0)


def transform_tables():
    index = np.arange(HALF)
    plain = []
    for parity in (0, 1):
        angle = 2.0 * math.pi / P_SIZE * (index[:, None] * (2 * index[None, :] + parity) % P_SIZE)
        cos, sin = np.cos(angle), np.sin(angle)
        plain.append(np.block([[cos, -sin], [sin, cos]]) / math.sqrt(P_SIZE))
    parts = []
    for table in plain + [t.T for t in plain]:
        high = table.astype(np.float32).astype(ml_dtypes.bfloat16)
        low = (table - high.astype(np.float64)).astype(np.float32).astype(ml_dtypes.bfloat16)
        parts += [high, low]
    order = np.concatenate([np.arange(0, P_SIZE, 2), np.arange(1, P_SIZE, 2)])
    sort = np.zeros((P_SIZE, P_SIZE), np.float32)
    sort[np.arange(P_SIZE), order] = 1.0
    parts += [sort.astype(ml_dtypes.bfloat16), sort.T.astype(ml_dtypes.bfloat16)]
    return np.stack(parts)


def lane_index(rows):
    return lax.broadcasted_iota(jnp.int32, (rows, LANES), 1)


def pack_lanes(field, top, size, tile, first):
    half = size // 2
    lane = lane_index(half)
    packed = None
    for g in range(GROUPS):
        start = top + g % 2 * half
        part = field[g // 2, start : start + half, tile]
        if g:
            part = pltpu.roll(part, HALO * g, 1)
        low = (first + HALO * g) % LANES
        mine = (lane >= low) & (lane < low + HALO)
        packed = part if packed is None else jnp.where(mine, part, packed)
    return packed


def unpack_lanes(packed, group):
    return pltpu.roll(packed, LANES - HALO * group, 1) if group else packed


def split(x):
    high = x.astype(jnp.bfloat16)
    return high, (x - high.astype(jnp.float32)).astype(jnp.bfloat16)


def product(left, right):
    return jnp.dot(left, right, preferred_element_type=jnp.float32)


def times_table(x, table, which):
    high, low = split(x)
    t_high, t_low = table[2 * which], table[2 * which + 1]
    return product(beside(high, high, low), below(t_high, t_low, t_high))


def table_times(table, which, x):
    high, low = split(x)
    t_high, t_low = table[2 * which], table[2 * which + 1]
    return product(beside(t_high, t_low, t_high), below(high, high, low))


def beside(*blocks):
    return jnp.concatenate(blocks, axis=1)


def below(*blocks):
    return jnp.concatenate(blocks, axis=0)


def ends(x):
    return x[:, :HALF], x[:, HALF:]


def forward_columns(exit_re, exit_im, table):
    re_lo, re_hi = ends(exit_re)
    im_lo, im_hi = ends(exit_im)
    even = times_table(beside(re_lo + re_hi, im_lo + im_hi), table, 0)
    odd = times_table(beside(re_lo - re_hi, im_lo - im_hi), table, 1)
    return even, odd


def forward_rows(even, odd, table):
    out = []
    for parity in (0, 1):
        if parity == 0:
            se, so = even[:HALF] + even[HALF:], odd[:HALF] + odd[HALF:]
        else:
            se, so = even[:HALF] - even[HALF:], odd[:HALF] - odd[HALF:]
        e_re, e_im = ends(se)
        o_re, o_im = ends(so)
        out.append(table_times(table, 2 + parity, below(beside(e_re, o_re), beside(e_im, o_im))))
    return out


def residual(far, frame):
    out = []
    for parity in (0, 1):
        re, im = far[parity][:HALF], far[parity][HALF:]
        level = jnp.maximum(re * re + im * im, floor_amp * floor_amp)
        inten = frame[parity * HALF : (parity + 1) * HALF]
        factor = 1.0 - inten * lax.rsqrt(inten * level)
        out.append(below(re * factor, im * factor))
    return out


def back_rows(res, table):
    first = table_times(table, 0, res[0])
    second = table_times(table, 1, res[1])
    upper, lower = first + second, first - second
    out = []
    for cols in (slice(0, HALF), slice(HALF, P_SIZE)):
        out.append(
            below(
                beside(upper[:HALF, cols], upper[HALF:, cols]),
                beside(lower[:HALF, cols], lower[HALF:, cols]),
            )
        )
    return out


def back_columns(parts, table):
    even = times_table(parts[0], table, 2)
    odd = times_table(parts[1], table, 3)
    lo, hi = even + odd, even - odd
    return beside(lo[:, :HALF], hi[:, :HALF]), beside(lo[:, HALF:], hi[:, HALF:])


def is_odd(axis):
    return lax.rem(lax.axis_index(axis), 2) == 1


def fetch(pairs, sems):
    copies = [pltpu.make_async_copy(far, near, sems.at[i]) for i, (far, near) in enumerate(pairs)]
    for copy in copies:
        copy.start()
    return copies


def finish_all(copies):
    for copy in copies:
        copy.wait()


def row_edges(counts, obj_re, obj_im, offsets, chosen, to_inner, to_outer, marked, places, frame_of, sems):
    tile_r = obj_re.shape[0]
    odd = is_odd("row")
    low = pl.multiple_of(jnp.where(odd, 0, tile_r - HALO), 16)
    high = pl.multiple_of(jnp.where(odd, tile_r - HALO, 0), 16)
    pairs = [(offsets, places), (chosen, frame_of)]
    for k, ref in enumerate((obj_re, obj_im)):
        rows = slice(k * HALO, (k + 1) * HALO)
        pairs.append((ref.at[pl.ds(high, HALO)], to_outer.at[rows]))
        pairs.append((ref.at[pl.ds(low, HALO)], to_inner.at[rows]))
    copies = fetch(pairs, sems)
    finish_all(copies[:2])
    place = places[0, 0]
    live = lax.broadcasted_iota(jnp.int32, place.shape, 1) < counts[0, 0]
    place = jnp.where(live, place, 2 * tile_r)
    marked[0:2, :] = place
    marked[2:3, :] = frame_of[0]
    for message in (to_inner, to_outer):
        message[2 * HALO : 2 * HALO + 2, 0 : place.shape[1]] = place.astype(jnp.float32)
    finish_all(copies[2:])


def window_place(slots, slot):
    row = pl.multiple_of(slots[0, slot] + HALO, 16)
    col = slots[1, slot] + LANES
    turn = lax.rem(col, LANES)
    return row, pl.multiple_of(col - turn, LANES), turn


def add_window(acc, layer, where, keep, term, tiles=(0, 1, 2)):
    row, base, _ = where
    lo, hi = ends(term)
    parts = (jnp.where(keep, lo, 0.0), hi, jnp.where(keep, 0.0, lo))
    for t in tiles:
        acc[layer, pl.ds(row, term.shape[0]), pl.ds(base + t * LANES, LANES)] += parts[t]


def send_columns(to_left, to_right, to_inner, to_outer):
    odd = is_odd("col")
    to_inner[0 : to_left.shape[0], :] = jnp.where(odd, to_left, to_right)
    to_outer[0 : to_left.shape[0], :] = jnp.where(odd, to_right, to_left)


def received(by_inner, by_outer, axis):
    odd = is_odd(axis)
    index = lax.axis_index(axis)
    inside = (index > 0) & (index < lax.axis_size(axis) - 1)
    by_outer = jnp.where(inside, by_outer[...], 0.0)
    by_inner = by_inner[...]
    return jnp.where(odd, by_inner, by_outer), jnp.where(odd, by_outer, by_inner)


def pieces(packed, size):
    half = size // 2
    for g in range(GROUPS):
        yield g // 2, g % 2 * half, unpack_lanes(packed[:half], g)


def pack_corners(field, rows):
    width = field.shape[2]
    left = [field[k, rows, 0:LANES] for k in (0, 1)]
    right = [field[k, rows, width - LANES : width] for k in (0, 1)]
    lane = lane_index(HALO)
    low = jnp.where(lane < HALO, right[0], pltpu.roll(right[1], HALO, 1))
    high = jnp.where(lane < 3 * HALO, pltpu.roll(left[1], 3 * HALO, 1), left[0])
    packed = jnp.where(lane < 2 * HALO, low, high)
    return beside(*(packed[i : i + MARKS] for i in range(0, HALO, MARKS)))


def unpack_corners(packed):
    packed = below(*(packed[:, i : i + LANES] for i in range(0, GROUPS * LANES, LANES)))
    lane = lane_index(HALO)
    for k, left, right in ((0, 0, 0), (1, HALO, 3 * HALO)):
        yield (
            k,
            jnp.where(lane >= 3 * HALO, pltpu.roll(packed, left, 1) if left else packed, 0.0),
            jnp.where(lane < HALO, pltpu.roll(packed, right, 1) if right else packed, 0.0),
        )


def row_halos(cells_in, own, by_inner, by_outer, cells, marks, to_inner, to_outer):
    rows, width = cells.shape[1:]
    middle = slice(LANES, width - LANES)
    before, after = received(by_inner, by_outer, "row")
    for k in (0, 1):
        cells[k, 0:HALO, middle] = before[k * HALO : (k + 1) * HALO]
        cells[k, rows - HALO : rows, middle] = after[k * HALO : (k + 1) * HALO]
    first_mark = 2 * HALO
    for i, message in enumerate((own[...], before, after)):
        marks[2 * i : 2 * i + 2, :] = message[first_mark : first_mark + 2, 0:LANES]
    half = rows // 2
    to_left = pack_lanes(cells, 0, rows, slice(LANES, 2 * LANES), 0)
    to_right = pack_lanes(cells, 0, rows, slice(width - 2 * LANES, width - LANES), LANES - HALO)
    send_columns(to_left, to_right, to_inner, to_outer)
    to_inner[half:, :] = marks[...]
    to_outer[half:, :] = marks[...]


def live_slots(slots, cells):
    tile_r = cells.shape[1] - 2 * HALO
    count = jnp.int32(0)
    for slot in range(slots.shape[1]):
        count += (slots[0, slot] < tile_r).astype(jnp.int32)
    return count


FIRST, BEFORE, OVER, AFTER, LAST = range(5)


def run_windows(phase, slots, cells, acc, probe_re, probe_im, table, frames, order):
    tile_r, tile_c = cells.shape[1] - 2 * HALO, cells.shape[2] - 2 * LANES
    count = live_slots(slots, cells)
    kinds = []
    n_inside, n_row, n_col = jnp.int32(0), jnp.int32(0), jnp.int32(0)
    for slot in range(slots.shape[1]):
        row, col = slots[0, slot], slots[1, slot]
        live = slot < count
        over_col = (col < 0) | (col > tile_c - P_SIZE)
        over_row = (row < 0) | (row > tile_r - P_SIZE)
        inside, by_row = live & ~over_col & ~over_row, live & ~over_col & over_row
        by_col, by_both = live & over_col & ~over_row, live & over_col & over_row
        kinds.append((inside, by_row, by_col, by_both, n_inside, n_row))
        n_inside += inside.astype(jnp.int32)
        n_row += by_row.astype(jnp.int32)
        n_col += by_col.astype(jnp.int32)
    first = jnp.minimum(n_inside, PAIR)
    before = first + jnp.minimum(n_inside - first, PAIR - jnp.minimum(n_row, PAIR))
    rest = n_inside - before
    after = n_inside - jnp.clip(n_col + rest - 2 * PAIR, 0, jnp.minimum(rest, PAIR))
    found = jnp.int32(0)
    for slot, (inside, by_row, by_col, by_both, rank, row_rank) in enumerate(kinds):
        mine = {
            FIRST: lambda: inside & (rank < first),
            BEFORE: lambda: (by_row & (row_rank < PAIR)) | (inside & (rank >= first) & (rank < before)),
            OVER: lambda: by_both | (by_row & (row_rank >= PAIR)),
            AFTER: lambda: by_col | (inside & (rank >= before) & (rank < after)),
            LAST: lambda: inside & (rank >= after),
        }[phase]()

        @pl.when(mine)
        def _():
            order[found] = slot

        found += mine.astype(jnp.int32)

    lane = lane_index(P_SIZE)

    def load(slot):
        where = row, base, turn = window_place(slots, slot)
        keep = lane >= turn
        w_re = pltpu.roll(probe_re[...], turn, 1)
        w_im = pltpu.roll(probe_im[...], turn, 1)
        patch = []
        for k in (0, 1):
            block = cells[k, pl.ds(row, P_SIZE), pl.ds(base, 3 * LANES)]
            patch.append(
                beside(jnp.where(keep, block[:, :LANES], block[:, 2 * LANES :]), block[:, LANES : 2 * LANES])
            )
        exit_re = w_re * patch[0] - w_im * patch[1]
        exit_im = w_re * patch[1] + w_im * patch[0]
        return (where, keep, w_re, w_im), exit_re, exit_im

    def frame_of(slot):
        half = product(table[8], frames[slots[2, slot]]).astype(jnp.bfloat16)
        return product(half, table[9])

    def place(at, back_re, back_im):
        where, keep, w_re, w_im = at
        add_window(acc, 0, where, keep, w_re * back_re + w_im * back_im)
        add_window(acc, 1, where, keep, w_re * back_im - w_im * back_re)

    def step(group):
        frame = [frame_of(slot) for slot in group]
        loaded = [load(slot) for slot in group]
        state = [forward_columns(x[1], x[2], table) for x in loaded]
        state = [forward_rows(*x, table) for x in state]
        state = [residual(x, f) for x, f in zip(state, frame)]
        state = [back_rows(x, table) for x in state]
        state = [back_columns(x, table) for x in state]
        for x, back in zip(loaded, state):
            place(x[0], *back)

    def pair_step(pair, carry):
        step([order[pair * PAIR + i] for i in range(PAIR)])
        return carry

    lax.fori_loop(0, found // PAIR, pair_step, 0)

    @pl.when(found % PAIR == 1)
    def _():
        step([order[found - 1]])


def windows_first(
    slots, obj_re, obj_im, probe_re_far, probe_im_far, table_far, frames_far,
    cells, acc, probe_re, probe_im, table, frames, order, sems,
):
    tile_r, tile_c = obj_re.shape
    inner = slice(HALO, HALO + tile_r)
    middle = slice(LANES, LANES + tile_c)
    pairs = (
        (table_far, table),
        (frames_far, frames),
        (obj_re, cells.at[0, inner, middle]),
        (obj_im, cells.at[1, inner, middle]),
        (probe_re_far, probe_re),
        (probe_im_far, probe_im),
    )
    copies = fetch(pairs, sems)
    acc[...] = jnp.zeros_like(acc)
    finish_all(copies)
    run_windows(FIRST, slots, cells, acc, probe_re, probe_im, table, frames, order)


def windows_before(
    slots, cells, acc_in, probe_re, probe_im, table, frames, acc, order, power,
):
    power[...] = probe_re[...] * probe_re[...] + probe_im[...] * probe_im[...]
    lane = lane_index(P_SIZE)

    def step(slot, carry):
        where = window_place(slots, slot)
        add_window(acc, 2, where, lane >= where[2], pltpu.roll(power[...], where[2], 1))
        return carry

    lax.fori_loop(0, live_slots(slots, cells), step, 0)
    run_windows(BEFORE, slots, cells, acc, probe_re, probe_im, table, frames, order)


def reaching(place, right, tile_r, tile_c):
    shape = place.shape
    index = lax.broadcasted_iota(jnp.int32, shape, 0)
    lane = lax.broadcasted_iota(jnp.int32, shape, 1)
    col = pltpu.roll(place, shape[0] - 1, 0)
    low = jnp.where(index == 2, tile_r - P_SIZE, -tile_r).astype(jnp.float32)
    high = jnp.where(index == 4, 0, tile_r).astype(jnp.float32)
    reaches = (lane < MARKS) & (index % 2 == 0) & (index < 6) & (place > low) & (place < high)
    if right < 0:
        reaches &= col > tile_c - P_SIZE
    if right > 0:
        reaches &= col < 0
    bit = lax.shift_left(jnp.ones(shape, jnp.int32), jnp.minimum(lane, MARKS)).astype(jnp.float32)
    bits = jnp.sum(jnp.where(reaches, bit, 0.0), axis=1, keepdims=True)
    return jnp.where(lane < MARKS, place, bits).astype(jnp.int32)


def add_neighbours_light(places, acc, power):
    rows, width = acc.shape[1:]
    tile_r, tile_c = rows - 2 * HALO, width - 2 * LANES
    for right in (-1, 0, 1):
        for i, down in enumerate((0, -1, 1)):
            if not right and not down:
                continue
            first, last = {-1: (P_SIZE - HALO, P_SIZE), 0: (0, P_SIZE), 1: (0, HALO)}[down]
            tiles = {-1: (2,), 0: (0, 1, 2), 1: (0,)}[right]
            lane = lane_index(last - first)
            bits = places[right + 1, 2 * i, MARKS]

            def step(slot, carry):
                row, col = places[right + 1, 2 * i, slot], places[right + 1, 2 * i + 1, slot]

                @pl.when(lax.shift_right_logical(bits, slot) % 2 == 1)
                def _():
                    turn = lax.rem(col + LANES, LANES)
                    at = pl.multiple_of(row + HALO + (down * tile_r + first), 16)
                    base = pl.multiple_of(col + LANES - turn + right * tile_c, LANES)
                    part = pltpu.roll(power[first:last, :], turn, 1)
                    add_window(acc, 2, (at, base, turn), lane >= turn, part, tiles)

                return carry

            @pl.when(bits != 0)
            def _():
                lax.fori_loop(0, MARKS, step, 0)


def windows_after(
    slots, cells, acc_in, probe_re, probe_im, table, frames, marks, by_inner, by_outer,
    acc, order, power, whole, places, sem,
):
    rows, width = acc.shape[1:]
    before, after = received(by_inner, by_outer, "col")
    for i, part in enumerate((before[-MARKS:], marks[...], after[-MARKS:])):
        whole[i] = reaching(part, i - 1, rows - 2 * HALO, width - 2 * LANES)
    copy = pltpu.make_async_copy(whole, places, sem)
    copy.start()
    power[...] = probe_re[...] * probe_re[...] + probe_im[...] * probe_im[...]
    run_windows(AFTER, slots, cells, acc, probe_re, probe_im, table, frames, order)
    copy.wait()
    add_neighbours_light(places, acc, power)


def windows_over_edge(
    slots, cells_in, acc_in, probe_re, probe_im, table, frames, by_inner, by_outer,
    cells, acc, to_inner, to_outer, order,
):
    rows, width = acc.shape[1:]
    before, after = received(by_inner, by_outer, "col")
    for tile, packed in ((slice(0, LANES), before), (slice(width - LANES, width), after)):
        for layer, row, part in pieces(packed, rows):
            cells[layer, row : row + part.shape[0], tile] = part
    run_windows(OVER, slots, cells, acc, probe_re, probe_im, table, frames, order)
    odd = is_odd("row")
    strips = []
    for here in (slice(0, HALO), slice(rows - HALO, rows)):
        middle = [acc[k, here, LANES : width - LANES] for k in (0, 1)]
        strips.append(below(*middle, pack_corners(acc, here)))
    to_inner[...] = jnp.where(odd, strips[0], strips[1])
    to_outer[...] = jnp.where(odd, strips[1], strips[0])


def column_spill(acc_in, by_inner, by_outer, acc, to_inner, to_outer):
    rows, width = acc.shape[1:]
    before, after = received(by_inner, by_outer, "row")
    for start, came in ((HALO, before), (rows - 2 * HALO, after)):
        here = slice(start, start + HALO)
        for k in (0, 1):
            acc[k, here, LANES : width - LANES] += came[k * HALO : (k + 1) * HALO]
        for k, left, right in unpack_corners(came[2 * HALO :]):
            acc[k, here, 0:LANES] += left
            acc[k, here, width - LANES :] += right
    tile_r = rows - 2 * HALO
    to_left = pack_lanes(acc, HALO, tile_r, slice(0, LANES), LANES - HALO)
    to_right = pack_lanes(acc, HALO, tile_r, slice(width - LANES, width), 0)
    send_columns(to_left, to_right, to_inner, to_outer)


def new_columns(cells, acc, spill, start, size, near_re, near_im):
    rows = acc.shape[1]
    here, there = slice(HALO, rows - HALO), slice(LANES + start, LANES + start + size)
    part = [acc[k, here, there] for k in range(acc.shape[0])]
    if spill is not None:
        part[:2] = [part[k] + spill[k] for k in (0, 1)]
    scale = 1.0 / (part[2] + ridge)
    near_re[:, start : start + size] = cells[0, here, there] - part[0] * scale
    near_im[:, start : start + size] = cells[1, here, there] - part[1] * scale


def finish_inner(
    slots, cells, acc_in, probe_re, probe_im, table, frames, acc, new_re, new_im, order, near_re, near_im, sems,
):
    run_windows(LAST, slots, cells, acc, probe_re, probe_im, table, frames, order)
    size = near_re.shape[1] - 2 * LANES
    new_columns(cells, acc, None, LANES, size, near_re, near_im)
    there = slice(LANES, LANES + size)
    finish_all(fetch([(near_re.at[:, there], new_re.at[:, there]), (near_im.at[:, there], new_im.at[:, there])], sems))


def finish_edges(cells, acc, by_inner, by_outer, re_in, im_in, new_re, new_im, near_re, near_im, sems):
    tile_r, tile_c = near_re.shape
    lane = lane_index(tile_r)
    sides = ((0, lane < HALO), (tile_c - LANES, lane >= LANES - HALO))
    copies = []
    for i, ((start, mine), packed) in enumerate(zip(sides, received(by_inner, by_outer, "col"))):
        parts = [part for _, _, part in pieces(packed, tile_r)]
        spill = [jnp.where(mine, below(*parts[2 * k : 2 * k + 2]), 0.0) for k in (0, 1)]
        new_columns(cells, acc, spill, start, LANES, near_re, near_im)
        there = slice(start, start + LANES)
        pairs = ((near_re.at[:, there], new_re.at[:, there]), (near_im.at[:, there], new_im.at[:, there]))
        copies += fetch(pairs, sems.at[2 * i : 2 * i + 2])
    finish_all(copies)


def swap(to_inner, to_outer, axis):
    devices = lax.axis_size(axis)
    inner = [(i, i + 1) for i in range(0, devices, 2)]
    partner = {i: i + 1 if i % 2 else i - 1 for i in range(1, devices - 1)}
    n_row, n_col = lax.axis_size("row"), lax.axis_size("col")
    pairs = []
    for row in range(n_row):
        for col in range(n_col):
            if axis == "row":
                there = (partner[row], col) if row in partner else (row, col ^ 1)
            else:
                there = (row, partner[col]) if col in partner else (row ^ 1, col)
            pairs.append((row * n_col + col, there[0] * n_col + there[1]))
    by_outer = lax.ppermute(to_outer, ("row", "col"), pairs)
    by_inner = lax.ppermute(to_inner, axis, inner + [(j, i) for i, j in inner])
    return by_inner, by_outer


def far(x):
    return pltpu.with_memory_space_constraint(x, pltpu.HBM)


def f32(*shape):
    return jax.ShapeDtypeStruct(shape, jnp.float32)


def shards(object_re, object_im, probe_re, probe_im, frames, counts, offsets, frame_index):
    tile_r, tile_c = object_re.shape
    rows, width = tile_r + 2 * HALO, tile_c + 2 * LANES
    layers = 3
    slots = offsets.shape[2]
    table = jnp.asarray(transform_tables())
    frames = frames.reshape(frames.shape[2:])
    cells_shape, acc_shape = f32(2, rows, width), f32(layers, rows, width)
    dma = pltpu.SemaphoreType.DMA

    places = jnp.swapaxes(offsets, 2, 3)
    edge = f32(2 * HALO + MARKS, tile_c)
    to_inner, to_outer, marked = pl.pallas_call(
        row_edges,
        out_shape=(edge, edge, jax.ShapeDtypeStruct((3, slots), jnp.int32)),
        in_specs=[SMEM] + [HBM] * 4,
        out_specs=(VMEM, VMEM, VMEM),
        scratch_shapes=[
            pltpu.VMEM(places.shape, jnp.int32), pltpu.VMEM(frame_index.shape, jnp.int32), dma((6,)),
        ],
        compiler_params=SMALL,
        name="row_edges",
    )(counts, far(object_re), far(object_im), far(places), far(frame_index))
    by_inner, by_outer = swap(to_inner, to_outer, "row")

    order = pltpu.SMEM((slots,), jnp.int32)
    cells, acc, *fixed = pl.pallas_call(
        windows_first,
        out_shape=(
            cells_shape, acc_shape, f32(*probe_re.shape), f32(*probe_im.shape),
            jax.ShapeDtypeStruct(table.shape, table.dtype), jax.ShapeDtypeStruct(frames.shape, frames.dtype),
        ),
        in_specs=[SMEM] + [HBM] * 6,
        out_specs=(VMEM,) * 6,
        scratch_shapes=[order, dma((6,))],
        compiler_params=PARAMS,
        cost_estimate=BUSY,
        name="windows_first",
    )(marked, *map(far, (object_re, object_im, probe_re, probe_im, table, frames)))

    packed = f32(rows // 2 + MARKS, LANES)
    cells, marks, to_inner, to_outer = pl.pallas_call(
        row_halos,
        out_shape=(cells_shape, f32(MARKS, LANES), packed, packed),
        in_specs=[VMEM] * 4,
        out_specs=(VMEM,) * 4,
        input_output_aliases={0: 0},
        compiler_params=SMALL,
        name="row_halos",
    )(cells, to_outer, by_inner, by_outer)
    edges = swap(to_inner, to_outer, "col")

    acc = pl.pallas_call(
        windows_before,
        out_shape=acc_shape,
        in_specs=[SMEM] + [VMEM] * 6,
        out_specs=VMEM,
        scratch_shapes=[order, pltpu.VMEM(probe_re.shape, jnp.float32)],
        input_output_aliases={2: 0},
        compiler_params=PARAMS,
        cost_estimate=BUSY,
        name="windows_before",
    )(marked, cells, acc, *fixed)

    cells, acc, to_inner, to_outer = pl.pallas_call(
        windows_over_edge,
        out_shape=(cells_shape, acc_shape, edge, edge),
        in_specs=[SMEM] + [VMEM] * 8,
        out_specs=(VMEM,) * 4,
        scratch_shapes=[order],
        input_output_aliases={1: 0, 2: 1},
        compiler_params=PARAMS,
        cost_estimate=BUSY,
        name="windows_over_edge",
    )(marked, cells, acc, *fixed, *edges)
    by_inner, by_outer = swap(to_inner, to_outer, "row")

    acc = pl.pallas_call(
        windows_after,
        out_shape=acc_shape,
        in_specs=[SMEM] + [VMEM] * 9,
        out_specs=VMEM,
        scratch_shapes=[
            order, pltpu.VMEM(probe_re.shape, jnp.float32),
            pltpu.VMEM((3, MARKS, LANES), jnp.int32), pltpu.SMEM((3, MARKS, LANES), jnp.int32), dma(()),
        ],
        input_output_aliases={2: 0},
        compiler_params=PARAMS,
        cost_estimate=BUSY,
        name="windows_after",
    )(marked, cells, acc, *fixed, marks, *edges)

    packed = f32(tile_r // 2, LANES)
    acc, to_inner, to_outer = pl.pallas_call(
        column_spill,
        out_shape=(acc_shape, packed, packed),
        in_specs=[VMEM] * 3,
        out_specs=(VMEM,) * 3,
        input_output_aliases={0: 0},
        compiler_params=SMALL,
        name="column_spill",
    )(acc, by_inner, by_outer)
    by_inner, by_outer = swap(to_inner, to_outer, "col")

    near = [pltpu.VMEM((tile_r, tile_c), jnp.float32)] * 2
    new = (f32(tile_r, tile_c), f32(tile_r, tile_c))
    acc, new_re, new_im = pl.pallas_call(
        finish_inner,
        out_shape=(acc_shape, *new),
        in_specs=[SMEM] + [VMEM] * 6,
        out_specs=(VMEM, HBM, HBM),
        scratch_shapes=[order] + near + [dma((2,))],
        input_output_aliases={2: 0},
        compiler_params=PARAMS,
        cost_estimate=BUSY,
        name="finish_inner",
    )(marked, cells, acc, *fixed)
    return pl.pallas_call(
        finish_edges,
        out_shape=new,
        in_specs=[VMEM] * 4 + [HBM] * 2,
        out_specs=(HBM, HBM),
        scratch_shapes=near + [dma((4,))],
        input_output_aliases={4: 0, 5: 1},
        compiler_params=SMALL,
        name="finish_edges",
    )(cells, acc, by_inner, by_outer, far(new_re), far(new_im))


def solution(mesh):
    return jax.shard_map(
        shards,
        mesh=mesh,
        in_specs=(
            P("row", "col"),
            P("row", "col"),
            P(),
            P(),
            P("row", "col", None, None, None),
            P("row", "col"),
            P("row", "col", None, None),
            P("row", "col", None),
        ),
        out_specs=(P("row", "col"), P("row", "col")),
        check_vma=False,
    )
```

```python
import functools
import math

import jax
import jax.numpy as jnp
import ml_dtypes
import numpy as np
from jax import lax
from jax.experimental import pallas as pl
from jax.experimental.pallas import tpu as pltpu
from jax.sharding import PartitionSpec as P

P_SIZE = 256
HALF = P_SIZE // 2
HALO = 32
LANES = 128
GROUPS = LANES // HALO
MARKS = 8
PAIR = 2

floor_amp = 0.5
ridge = 1.0

VMEM = pl.BlockSpec(memory_space=pltpu.VMEM)
SMEM = pl.BlockSpec(memory_space=pltpu.SMEM)
HBM = pl.BlockSpec(memory_space=pltpu.HBM)
PARAMS = pltpu.CompilerParams(vmem_limit_bytes=32 * 1024 * 1024)
SMALL = pltpu.CompilerParams(vmem_limit_bytes=16 * 1024 * 1024)
BUSY = pl.CostEstimate(flops=4_000_000_000, bytes_accessed=8_000_000, transcendentals=0)


def transform_tables():
    index = np.arange(HALF)
    plain = []
    for parity in (0, 1):
        angle = 2.0 * math.pi / P_SIZE * (index[:, None] * (2 * index[None, :] + parity) % P_SIZE)
        cos, sin = np.cos(angle), np.sin(angle)
        plain.append(np.block([[cos, -sin], [sin, cos]]) / math.sqrt(P_SIZE))
    parts = []
    for table in plain + [t.T for t in plain]:
        high = table.astype(np.float32).astype(ml_dtypes.bfloat16)
        low = (table - high.astype(np.float64)).astype(np.float32).astype(ml_dtypes.bfloat16)
        parts += [high, low]
    order = np.concatenate([np.arange(0, P_SIZE, 2), np.arange(1, P_SIZE, 2)])
    sort = np.zeros((P_SIZE, P_SIZE), np.float32)
    sort[np.arange(P_SIZE), order] = 1.0
    parts += [sort.astype(ml_dtypes.bfloat16), sort.T.astype(ml_dtypes.bfloat16)]
    return np.stack(parts)


def lane_index(rows):
    return lax.broadcasted_iota(jnp.int32, (rows, LANES), 1)


def pack_lanes(field, top, size, tile, first):
    half = size // 2
    lane = lane_index(half)
    packed = None
    for g in range(GROUPS):
        start = top + g % 2 * half
        part = field[g // 2, start : start + half, tile]
        if g:
            part = pltpu.roll(part, HALO * g, 1)
        low = (first + HALO * g) % LANES
        mine = (lane >= low) & (lane < low + HALO)
        packed = part if packed is None else jnp.where(mine, part, packed)
    return packed


def unpack_lanes(packed, group):
    return pltpu.roll(packed, LANES - HALO * group, 1) if group else packed


def split(x):
    high = x.astype(jnp.bfloat16)
    return high, (x - high.astype(jnp.float32)).astype(jnp.bfloat16)


def product(left, right):
    return jnp.dot(left, right, preferred_element_type=jnp.float32)


def times_table(x, table, which):
    high, low = split(x)
    t_high, t_low = table[2 * which], table[2 * which + 1]
    return product(beside(high, high, low), below(t_high, t_low, t_high))


def table_times(table, which, x):
    high, low = split(x)
    t_high, t_low = table[2 * which], table[2 * which + 1]
    return product(beside(t_high, t_low, t_high), below(high, high, low))


def beside(*blocks):
    return jnp.concatenate(blocks, axis=1)


def below(*blocks):
    return jnp.concatenate(blocks, axis=0)


def ends(x):
    return x[:, :HALF], x[:, HALF:]


def forward_columns(exit_re, exit_im, table):
    re_lo, re_hi = ends(exit_re)
    im_lo, im_hi = ends(exit_im)
    even = times_table(beside(re_lo + re_hi, im_lo + im_hi), table, 0)
    odd = times_table(beside(re_lo - re_hi, im_lo - im_hi), table, 1)
    return even, odd


def forward_rows(even, odd, table):
    out = []
    for parity in (0, 1):
        if parity == 0:
            se, so = even[:HALF] + even[HALF:], odd[:HALF] + odd[HALF:]
        else:
            se, so = even[:HALF] - even[HALF:], odd[:HALF] - odd[HALF:]
        e_re, e_im = ends(se)
        o_re, o_im = ends(so)
        out.append(table_times(table, 2 + parity, below(beside(e_re, o_re), beside(e_im, o_im))))
    return out


def residual(far, frame):
    out = []
    for parity in (0, 1):
        re, im = far[parity][:HALF], far[parity][HALF:]
        level = jnp.maximum(re * re + im * im, floor_amp * floor_amp)
        inten = frame[parity * HALF : (parity + 1) * HALF]
        factor = 1.0 - inten * lax.rsqrt(inten * level)
        out.append(below(re * factor, im * factor))
    return out


def back_rows(res, table):
    first = table_times(table, 0, res[0])
    second = table_times(table, 1, res[1])
    upper, lower = first + second, first - second
    out = []
    for cols in (slice(0, HALF), slice(HALF, P_SIZE)):
        out.append(
            below(
                beside(upper[:HALF, cols], upper[HALF:, cols]),
                beside(lower[:HALF, cols], lower[HALF:, cols]),
            )
        )
    return out


def back_columns(parts, table):
    even = times_table(parts[0], table, 2)
    odd = times_table(parts[1], table, 3)
    lo, hi = even + odd, even - odd
    return beside(lo[:, :HALF], hi[:, :HALF]), beside(lo[:, HALF:], hi[:, HALF:])


def is_odd(axis):
    return lax.rem(lax.axis_index(axis), 2) == 1


def fetch(pairs, sems):
    copies = [pltpu.make_async_copy(far, near, sems.at[i]) for i, (far, near) in enumerate(pairs)]
    for copy in copies:
        copy.start()
    return copies


def finish_all(copies):
    for copy in copies:
        copy.wait()


def row_edges(counts, obj_re, obj_im, offsets, chosen, to_outer, to_inner, marked, places, frame_of, sems):
    tile_r = obj_re.shape[0]
    odd = is_odd("row")
    low = pl.multiple_of(jnp.where(odd, 0, tile_r - HALO), 16)
    high = pl.multiple_of(jnp.where(odd, tile_r - HALO, 0), 16)
    pairs = [(offsets, places), (chosen, frame_of)]
    tiles = obj_re.shape[1] // LANES
    for k, ref in enumerate((obj_re, obj_im)):
        for t in range(tiles):
            lanes = slice(t * LANES, (t + 1) * LANES)
            rows = slice((2 * t + k) * HALO, (2 * t + k + 1) * HALO)
            pairs.append((ref.at[pl.ds(high, HALO), lanes], to_outer.at[rows]))
            pairs.append((ref.at[pl.ds(low, HALO), lanes], to_inner.at[rows]))
    copies = fetch(pairs, sems)
    finish_all(copies[:2])
    place = places[0, 0]
    live = lax.broadcasted_iota(jnp.int32, place.shape, 1) < counts[0, 0]
    place = jnp.where(live, place, 2 * tile_r)
    marked[0:2, :] = place
    marked[2:3, :] = frame_of[0]
    for message in (to_inner, to_outer):
        first = 2 * HALO * tiles
        message[first : first + 2, 0 : place.shape[1]] = place.astype(jnp.float32)
    finish_all(copies[2:])


def window_place(slots, slot):
    row = pl.multiple_of(slots[0, slot] + HALO, 16)
    col = slots[1, slot] + LANES
    turn = lax.rem(col, LANES)
    return row, pl.multiple_of(col - turn, LANES), turn


def add_window(acc, layer, where, keep, term, tiles=(0, 1, 2)):
    row, base, _ = where
    lo, hi = ends(term)
    parts = (jnp.where(keep, lo, 0.0), hi, jnp.where(keep, 0.0, lo))
    for t in tiles:
        acc[layer, pl.ds(row, term.shape[0]), pl.ds(base + t * LANES, LANES)] += parts[t]


def send_columns(to_left, to_right, to_inner, to_outer):
    odd = is_odd("col")
    to_inner[0 : to_left.shape[0], :] = jnp.where(odd, to_left, to_right)
    to_outer[0 : to_left.shape[0], :] = jnp.where(odd, to_right, to_left)


def received(by_inner, by_outer, axis):
    odd = is_odd(axis)
    index = lax.axis_index(axis)
    inside = (index > 0) & (index < lax.axis_size(axis) - 1)
    by_outer = jnp.where(inside, by_outer[...], 0.0)
    by_inner = by_inner[...]
    return jnp.where(odd, by_inner, by_outer), jnp.where(odd, by_outer, by_inner)


def pieces(packed, size):
    half = size // 2
    for g in range(GROUPS):
        yield g // 2, g % 2 * half, unpack_lanes(packed[:half], g)


def pack_corners(field, rows):
    width = field.shape[2]
    left = [field[k, rows, 0:LANES] for k in (0, 1)]
    right = [field[k, rows, width - LANES : width] for k in (0, 1)]
    lane = lane_index(HALO)
    low = jnp.where(lane < HALO, right[0], pltpu.roll(right[1], HALO, 1))
    high = jnp.where(lane < 3 * HALO, pltpu.roll(left[1], 3 * HALO, 1), left[0])
    packed = jnp.where(lane < 2 * HALO, low, high)
    return beside(*(packed[i : i + MARKS] for i in range(0, HALO, MARKS)))


def unpack_corners(packed):
    packed = below(*(packed[:, i : i + LANES] for i in range(0, GROUPS * LANES, LANES)))
    lane = lane_index(HALO)
    for k, left, right in ((0, 0, 0), (1, HALO, 3 * HALO)):
        yield (
            k,
            jnp.where(lane >= 3 * HALO, pltpu.roll(packed, left, 1) if left else packed, 0.0),
            jnp.where(lane < HALO, pltpu.roll(packed, right, 1) if right else packed, 0.0),
        )


def row_halos(cells_in, own, by_outer, by_inner, cells, marks, to_inner, to_outer):
    rows, width = cells.shape[1:]
    before, after = received(by_inner, by_outer, "row")
    tiles = width // LANES - 2
    for k in (0, 1):
        for t in range(tiles):
            lanes = slice((t + 1) * LANES, (t + 2) * LANES)
            part = slice((2 * t + k) * HALO, (2 * t + k + 1) * HALO)
            cells[k, 0:HALO, lanes] = before[part]
            cells[k, rows - HALO : rows, lanes] = after[part]
    first = 2 * HALO * tiles
    for i, message in enumerate((own[...], before, after)):
        marks[2 * i : 2 * i + 2, :] = message[first : first + 2]
    half = rows // 2
    to_left = pack_lanes(cells, 0, rows, slice(LANES, 2 * LANES), 0)
    to_right = pack_lanes(cells, 0, rows, slice(width - 2 * LANES, width - LANES), LANES - HALO)
    send_columns(to_left, to_right, to_inner, to_outer)
    to_inner[half:, :] = marks[...]
    to_outer[half:, :] = marks[...]


def live_slots(slots, cells):
    tile_r = cells.shape[1] - 2 * HALO
    count = jnp.int32(0)
    for slot in range(slots.shape[1]):
        count += (slots[0, slot] < tile_r).astype(jnp.int32)
    return count


FIRST, BEFORE, OVER, AFTER, LAST = range(5)


def run_windows(phase, slots, cells, acc, probe_re, probe_im, table, frames, order):
    tile_r, tile_c = cells.shape[1] - 2 * HALO, cells.shape[2] - 2 * LANES
    count = live_slots(slots, cells)
    kinds = []
    n_inside, n_row, n_col = jnp.int32(0), jnp.int32(0), jnp.int32(0)
    for slot in range(slots.shape[1]):
        row, col = slots[0, slot], slots[1, slot]
        live = slot < count
        over_col = (col < 0) | (col > tile_c - P_SIZE)
        over_row = (row < 0) | (row > tile_r - P_SIZE)
        inside, by_row = live & ~over_col & ~over_row, live & ~over_col & over_row
        by_col, by_both = live & over_col & ~over_row, live & over_col & over_row
        kinds.append((inside, by_row, by_col, by_both, n_inside, n_row))
        n_inside += inside.astype(jnp.int32)
        n_row += by_row.astype(jnp.int32)
        n_col += by_col.astype(jnp.int32)
    first = jnp.minimum(n_inside, PAIR)
    before = first + jnp.minimum(n_inside - first, PAIR - jnp.minimum(n_row, PAIR))
    rest = n_inside - before
    after = n_inside - jnp.clip(n_col + rest - 2 * PAIR, 0, jnp.minimum(rest, PAIR))
    found = jnp.int32(0)
    for slot, (inside, by_row, by_col, by_both, rank, row_rank) in enumerate(kinds):
        mine = {
            FIRST: lambda: inside & (rank < first),
            BEFORE: lambda: (by_row & (row_rank < PAIR)) | (inside & (rank >= first) & (rank < before)),
            OVER: lambda: by_both | (by_row & (row_rank >= PAIR)),
            AFTER: lambda: by_col | (inside & (rank >= before) & (rank < after)),
            LAST: lambda: inside & (rank >= after),
        }[phase]()

        @pl.when(mine)
        def _():
            order[found] = slot

        found += mine.astype(jnp.int32)

    lane = lane_index(P_SIZE)

    def load(slot):
        where = row, base, turn = window_place(slots, slot)
        keep = lane >= turn
        w_re = pltpu.roll(probe_re[...], turn, 1)
        w_im = pltpu.roll(probe_im[...], turn, 1)
        patch = []
        for k in (0, 1):
            block = cells[k, pl.ds(row, P_SIZE), pl.ds(base, 3 * LANES)]
            patch.append(
                beside(jnp.where(keep, block[:, :LANES], block[:, 2 * LANES :]), block[:, LANES : 2 * LANES])
            )
        exit_re = w_re * patch[0] - w_im * patch[1]
        exit_im = w_re * patch[1] + w_im * patch[0]
        return (where, keep, w_re, w_im), exit_re, exit_im

    def frame_of(slot):
        half = product(table[8], frames[slots[2, slot]]).astype(jnp.bfloat16)
        return product(half, table[9])

    def place(at, back_re, back_im):
        where, keep, w_re, w_im = at
        add_window(acc, 0, where, keep, w_re * back_re + w_im * back_im)
        add_window(acc, 1, where, keep, w_re * back_im - w_im * back_re)

    def step(group):
        frame = [frame_of(slot) for slot in group]
        loaded = [load(slot) for slot in group]
        state = [forward_columns(x[1], x[2], table) for x in loaded]
        state = [forward_rows(*x, table) for x in state]
        state = [residual(x, f) for x, f in zip(state, frame)]
        state = [back_rows(x, table) for x in state]
        state = [back_columns(x, table) for x in state]
        for x, back in zip(loaded, state):
            place(x[0], *back)

    def pair_step(pair, carry):
        step([order[pair * PAIR + i] for i in range(PAIR)])
        return carry

    lax.fori_loop(0, found // PAIR, pair_step, 0)

    @pl.when(found % PAIR == 1)
    def _():
        step([order[found - 1]])


def windows_first(
    slots, obj_re, obj_im, probe_re_far, probe_im_far, table_far, frames_far,
    cells, acc, probe_re, probe_im, table, frames, order, sems,
):
    tile_r, tile_c = obj_re.shape
    inner = slice(HALO, HALO + tile_r)
    middle = slice(LANES, LANES + tile_c)
    pairs = (
        (table_far, table),
        (frames_far, frames),
        (obj_re, cells.at[0, inner, middle]),
        (obj_im, cells.at[1, inner, middle]),
        (probe_re_far, probe_re),
        (probe_im_far, probe_im),
    )
    copies = fetch(pairs, sems)
    acc[...] = jnp.zeros_like(acc)
    finish_all(copies)
    run_windows(FIRST, slots, cells, acc, probe_re, probe_im, table, frames, order)


def windows_before(
    slots, cells, acc_in, probe_re, probe_im, table, frames, acc, order, power,
):
    power[...] = probe_re[...] * probe_re[...] + probe_im[...] * probe_im[...]
    lane = lane_index(P_SIZE)

    def step(slot, carry):
        where = window_place(slots, slot)
        add_window(acc, 2, where, lane >= where[2], pltpu.roll(power[...], where[2], 1))
        return carry

    lax.fori_loop(0, live_slots(slots, cells), step, 0)
    run_windows(BEFORE, slots, cells, acc, probe_re, probe_im, table, frames, order)


def reaching(place, right, tile_r, tile_c):
    shape = place.shape
    index = lax.broadcasted_iota(jnp.int32, shape, 0)
    lane = lax.broadcasted_iota(jnp.int32, shape, 1)
    col = pltpu.roll(place, shape[0] - 1, 0)
    low = jnp.where(index == 2, tile_r - P_SIZE, -tile_r).astype(jnp.float32)
    high = jnp.where(index == 4, 0, tile_r).astype(jnp.float32)
    reaches = (lane < MARKS) & (index % 2 == 0) & (index < 6) & (place > low) & (place < high)
    if right < 0:
        reaches &= col > tile_c - P_SIZE
    if right > 0:
        reaches &= col < 0
    bit = lax.shift_left(jnp.ones(shape, jnp.int32), jnp.minimum(lane, MARKS)).astype(jnp.float32)
    bits = jnp.sum(jnp.where(reaches, bit, 0.0), axis=1, keepdims=True)
    return jnp.where(lane < MARKS, place, bits).astype(jnp.int32)


def add_neighbours_light(places, acc, power):
    rows, width = acc.shape[1:]
    tile_r, tile_c = rows - 2 * HALO, width - 2 * LANES
    for right in (-1, 0, 1):
        for i, down in enumerate((0, -1, 1)):
            if not right and not down:
                continue
            first, last = {-1: (P_SIZE - HALO, P_SIZE), 0: (0, P_SIZE), 1: (0, HALO)}[down]
            tiles = {-1: (2,), 0: (0, 1, 2), 1: (0,)}[right]
            lane = lane_index(last - first)
            bits = places[right + 1, 2 * i, MARKS]

            def step(slot, carry):
                row, col = places[right + 1, 2 * i, slot], places[right + 1, 2 * i + 1, slot]

                @pl.when(lax.shift_right_logical(bits, slot) % 2 == 1)
                def _():
                    turn = lax.rem(col + LANES, LANES)
                    at = pl.multiple_of(row + HALO + (down * tile_r + first), 16)
                    base = pl.multiple_of(col + LANES - turn + right * tile_c, LANES)
                    part = pltpu.roll(power[first:last, :], turn, 1)
                    add_window(acc, 2, (at, base, turn), lane >= turn, part, tiles)

                return carry

            @pl.when(bits != 0)
            def _():
                lax.fori_loop(0, MARKS, step, 0)


def windows_after(
    slots, cells, acc_in, probe_re, probe_im, table, frames, marks, by_inner, by_outer,
    acc, order, power, whole, places, sem,
):
    rows, width = acc.shape[1:]
    before, after = received(by_inner, by_outer, "col")
    for i, part in enumerate((before[-MARKS:], marks[...], after[-MARKS:])):
        whole[i] = reaching(part, i - 1, rows - 2 * HALO, width - 2 * LANES)
    copy = pltpu.make_async_copy(whole, places, sem)
    copy.start()
    power[...] = probe_re[...] * probe_re[...] + probe_im[...] * probe_im[...]
    run_windows(AFTER, slots, cells, acc, probe_re, probe_im, table, frames, order)
    copy.wait()
    add_neighbours_light(places, acc, power)


def windows_over_edge(
    marked, cells_in, acc_in, probe_re, probe_im, table, frames, by_inner, by_outer,
    cells, acc, to_outer, to_inner, order, slots, sem,
):
    scalars = pltpu.make_async_copy(marked, slots, sem)
    scalars.start()
    rows, width = acc.shape[1:]
    before, after = received(by_inner, by_outer, "col")
    for tile, packed in ((slice(0, LANES), before), (slice(width - LANES, width), after)):
        for layer, row, part in pieces(packed, rows):
            cells[layer, row : row + part.shape[0], tile] = part
    scalars.wait()
    run_windows(OVER, slots, cells, acc, probe_re, probe_im, table, frames, order)
    odd = is_odd("row")
    strips = []
    for here in (slice(0, HALO), slice(rows - HALO, rows)):
        middle = [acc[k, here, LANES : width - LANES] for k in (0, 1)]
        strips.append(below(*middle, pack_corners(acc, here)))
    to_inner[...] = jnp.where(odd, strips[0], strips[1])
    to_outer[...] = jnp.where(odd, strips[1], strips[0])


def column_spill(acc_in, by_outer, by_inner, acc, to_inner, to_outer):
    rows, width = acc.shape[1:]
    before, after = received(by_inner, by_outer, "row")
    for start, came in ((HALO, before), (rows - 2 * HALO, after)):
        here = slice(start, start + HALO)
        for k in (0, 1):
            acc[k, here, LANES : width - LANES] += came[k * HALO : (k + 1) * HALO]
        for k, left, right in unpack_corners(came[2 * HALO :]):
            acc[k, here, 0:LANES] += left
            acc[k, here, width - LANES :] += right
    tile_r = rows - 2 * HALO
    to_left = pack_lanes(acc, HALO, tile_r, slice(0, LANES), LANES - HALO)
    to_right = pack_lanes(acc, HALO, tile_r, slice(width - LANES, width), 0)
    send_columns(to_left, to_right, to_inner, to_outer)


def new_columns(cells, acc, spill, start, size, near_re, near_im):
    rows = acc.shape[1]
    here, there = slice(HALO, rows - HALO), slice(LANES + start, LANES + start + size)
    part = [acc[k, here, there] for k in range(acc.shape[0])]
    if spill is not None:
        part[:2] = [part[k] + spill[k] for k in (0, 1)]
    scale = 1.0 / (part[2] + ridge)
    near_re[:, start : start + size] = cells[0, here, there] - part[0] * scale
    near_im[:, start : start + size] = cells[1, here, there] - part[1] * scale


def finish_inner(
    slots, cells, acc_in, probe_re, probe_im, table, frames, acc, new_re, new_im, order, near_re, near_im, sems,
):
    run_windows(LAST, slots, cells, acc, probe_re, probe_im, table, frames, order)
    size = near_re.shape[1] - 2 * LANES
    new_columns(cells, acc, None, LANES, size, near_re, near_im)
    there = slice(LANES, LANES + size)
    finish_all(fetch([(near_re.at[:, there], new_re.at[:, there]), (near_im.at[:, there], new_im.at[:, there])], sems))


def finish_edges(cells, acc, by_inner, by_outer, re_in, im_in, new_re, new_im, near_re, near_im, sems):
    tile_r, tile_c = near_re.shape
    lane = lane_index(tile_r)
    sides = ((0, lane < HALO), (tile_c - LANES, lane >= LANES - HALO))
    copies = []
    for i, ((start, mine), packed) in enumerate(zip(sides, received(by_inner, by_outer, "col"))):
        parts = [part for _, _, part in pieces(packed, tile_r)]
        spill = [jnp.where(mine, below(*parts[2 * k : 2 * k + 2]), 0.0) for k in (0, 1)]
        new_columns(cells, acc, spill, start, LANES, near_re, near_im)
        there = slice(start, start + LANES)
        pairs = ((near_re.at[:, there], new_re.at[:, there]), (near_im.at[:, there], new_im.at[:, there]))
        copies += fetch(pairs, sems.at[2 * i : 2 * i + 2])
    finish_all(copies)


def swap(to_inner, to_outer, axis):
    devices = lax.axis_size(axis)
    inner = [(i, i + 1) for i in range(0, devices, 2)]
    partner = {i: i + 1 if i % 2 else i - 1 for i in range(1, devices - 1)}
    n_row, n_col = lax.axis_size("row"), lax.axis_size("col")
    pairs = []
    for row in range(n_row):
        for col in range(n_col):
            if axis == "row":
                there = (partner[row], col) if row in partner else (row, col ^ 1)
            else:
                there = (row, partner[col]) if col in partner else (row ^ 1, col)
            pairs.append((row * n_col + col, there[0] * n_col + there[1]))
    by_inner = lax.ppermute(to_inner, axis, inner + [(j, i) for i, j in inner])
    by_outer = lax.ppermute(to_outer, ("row", "col"), pairs)
    return by_inner, by_outer


def far(x):
    return pltpu.with_memory_space_constraint(x, pltpu.HBM)


def f32(*shape):
    return jax.ShapeDtypeStruct(shape, jnp.float32)


def shards(object_re, object_im, probe_re, probe_im, frames, counts, offsets, frame_index):
    tile_r, tile_c = object_re.shape
    rows, width = tile_r + 2 * HALO, tile_c + 2 * LANES
    layers = 3
    slots = offsets.shape[2]
    table = jnp.asarray(transform_tables())
    frames = frames.reshape(frames.shape[2:])
    cells_shape, acc_shape = f32(2, rows, width), f32(layers, rows, width)
    dma = pltpu.SemaphoreType.DMA

    places = jnp.swapaxes(offsets, 2, 3)
    edge = f32(2 * HALO * (tile_c // LANES) + MARKS, LANES)
    to_outer, to_inner, marked = pl.pallas_call(
        row_edges,
        out_shape=(edge, edge, jax.ShapeDtypeStruct((3, slots), jnp.int32)),
        in_specs=[SMEM] + [HBM] * 4,
        out_specs=(VMEM, VMEM, VMEM),
        scratch_shapes=[
            pltpu.VMEM(places.shape, jnp.int32), pltpu.VMEM(frame_index.shape, jnp.int32),
            dma((2 + 4 * (tile_c // LANES),)),
        ],
        compiler_params=SMALL,
        name="row_edges",
    )(counts, far(object_re), far(object_im), far(places), far(frame_index))
    by_inner, by_outer = swap(to_inner, to_outer, "row")

    order = pltpu.SMEM((slots,), jnp.int32)
    cells, acc, *fixed = pl.pallas_call(
        windows_first,
        out_shape=(
            cells_shape, acc_shape, f32(*probe_re.shape), f32(*probe_im.shape),
            jax.ShapeDtypeStruct(table.shape, table.dtype), jax.ShapeDtypeStruct(frames.shape, frames.dtype),
        ),
        in_specs=[SMEM] + [HBM] * 6,
        out_specs=(VMEM,) * 6,
        scratch_shapes=[order, dma((6,))],
        compiler_params=PARAMS,
        cost_estimate=BUSY,
        name="windows_first",
    )(marked, *map(far, (object_re, object_im, probe_re, probe_im, table, frames)))

    packed = f32(rows // 2 + MARKS, LANES)
    cells, marks, to_inner, to_outer = pl.pallas_call(
        row_halos,
        out_shape=(cells_shape, f32(MARKS, LANES), packed, packed),
        in_specs=[VMEM] * 4,
        out_specs=(VMEM,) * 4,
        input_output_aliases={0: 0},
        compiler_params=SMALL,
        name="row_halos",
    )(cells, to_outer, by_outer, by_inner)
    edges = swap(to_inner, to_outer, "col")

    acc = pl.pallas_call(
        windows_before,
        out_shape=acc_shape,
        in_specs=[SMEM] + [VMEM] * 6,
        out_specs=VMEM,
        scratch_shapes=[order, pltpu.VMEM(probe_re.shape, jnp.float32)],
        input_output_aliases={2: 0},
        compiler_params=PARAMS,
        cost_estimate=BUSY,
        name="windows_before",
    )(marked, cells, acc, *fixed)

    edge = f32(2 * HALO + MARKS, tile_c)
    cells, acc, to_outer, to_inner = pl.pallas_call(
        windows_over_edge,
        out_shape=(cells_shape, acc_shape, edge, edge),
        in_specs=[VMEM] * 9,
        out_specs=(VMEM,) * 4,
        scratch_shapes=[order, pltpu.SMEM((3, slots), jnp.int32), dma(())],
        input_output_aliases={1: 0, 2: 1},
        compiler_params=PARAMS,
        cost_estimate=BUSY,
        name="windows_over_edge",
    )(marked, cells, acc, *fixed, *edges)
    by_inner, by_outer = swap(to_inner, to_outer, "row")

    acc = pl.pallas_call(
        windows_after,
        out_shape=acc_shape,
        in_specs=[SMEM] + [VMEM] * 9,
        out_specs=VMEM,
        scratch_shapes=[
            order, pltpu.VMEM(probe_re.shape, jnp.float32),
            pltpu.VMEM((3, MARKS, LANES), jnp.int32), pltpu.SMEM((3, MARKS, LANES), jnp.int32), dma(()),
        ],
        input_output_aliases={2: 0},
        compiler_params=PARAMS,
        cost_estimate=BUSY,
        name="windows_after",
    )(marked, cells, acc, *fixed, marks, *edges)

    packed = f32(tile_r // 2, LANES)
    acc, to_inner, to_outer = pl.pallas_call(
        column_spill,
        out_shape=(acc_shape, packed, packed),
        in_specs=[VMEM] * 3,
        out_specs=(VMEM,) * 3,
        input_output_aliases={0: 0},
        compiler_params=SMALL,
        name="column_spill",
    )(acc, by_outer, by_inner)
    by_inner, by_outer = swap(to_inner, to_outer, "col")

    near = [pltpu.VMEM((tile_r, tile_c), jnp.float32)] * 2
    new = (f32(tile_r, tile_c), f32(tile_r, tile_c))
    acc, new_re, new_im = pl.pallas_call(
        finish_inner,
        out_shape=(acc_shape, *new),
        in_specs=[SMEM] + [VMEM] * 6,
        out_specs=(VMEM, HBM, HBM),
        scratch_shapes=[order] + near + [dma((2,))],
        input_output_aliases={2: 0},
        compiler_params=PARAMS,
        cost_estimate=BUSY,
        name="finish_inner",
    )(marked, cells, acc, *fixed)
    return pl.pallas_call(
        finish_edges,
        out_shape=new,
        in_specs=[VMEM] * 4 + [HBM] * 2,
        out_specs=(HBM, HBM),
        scratch_shapes=near + [dma((4,))],
        input_output_aliases={4: 0, 5: 1},
        compiler_params=SMALL,
        name="finish_edges",
    )(cells, acc, by_inner, by_outer, far(new_re), far(new_im))


def solution(mesh):
    return jax.shard_map(
        shards,
        mesh=mesh,
        in_specs=(
            P("row", "col"),
            P("row", "col"),
            P(),
            P(),
            P("row", "col", None, None, None),
            P("row", "col"),
            P("row", "col", None, None),
            P("row", "col", None),
        ),
        out_specs=(P("row", "col"), P("row", "col")),
        check_vma=False,
    )
```

```python
import functools
import math

import jax
import jax.numpy as jnp
import ml_dtypes
import numpy as np
from jax import lax
from jax.experimental import pallas as pl
from jax.experimental.pallas import tpu as pltpu
from jax.sharding import PartitionSpec as P

P_SIZE = 256
HALF = P_SIZE // 2
HALO = 32
LANES = 128
GROUPS = LANES // HALO
MARKS = 8
PAIR = 2

floor_amp = 0.5
ridge = 1.0

VMEM = pl.BlockSpec(memory_space=pltpu.VMEM)
SMEM = pl.BlockSpec(memory_space=pltpu.SMEM)
HBM = pl.BlockSpec(memory_space=pltpu.HBM)
PARAMS = pltpu.CompilerParams(vmem_limit_bytes=32 * 1024 * 1024)
SMALL = pltpu.CompilerParams(vmem_limit_bytes=16 * 1024 * 1024)
BUSY = pl.CostEstimate(flops=4_000_000_000, bytes_accessed=8_000_000, transcendentals=0)


def transform_tables():
    index = np.arange(HALF)
    plain = []
    for parity in (0, 1):
        angle = 2.0 * math.pi / P_SIZE * (index[:, None] * (2 * index[None, :] + parity) % P_SIZE)
        cos, sin = np.cos(angle), np.sin(angle)
        plain.append(np.block([[cos, -sin], [sin, cos]]) / math.sqrt(P_SIZE))
    parts = []
    for table in plain + [t.T for t in plain]:
        high = table.astype(np.float32).astype(ml_dtypes.bfloat16)
        low = (table - high.astype(np.float64)).astype(np.float32).astype(ml_dtypes.bfloat16)
        parts += [high, low]
    order = np.concatenate([np.arange(0, P_SIZE, 2), np.arange(1, P_SIZE, 2)])
    sort = np.zeros((P_SIZE, P_SIZE), np.float32)
    sort[np.arange(P_SIZE), order] = 1.0
    parts += [sort.astype(ml_dtypes.bfloat16), sort.T.astype(ml_dtypes.bfloat16)]
    return np.stack(parts)


def lane_index(rows):
    return lax.broadcasted_iota(jnp.int32, (rows, LANES), 1)


def pack_lanes(field, top, size, tile, first):
    half = size // 2
    lane = lane_index(half)
    packed = None
    for g in range(GROUPS):
        start = top + g % 2 * half
        part = field[g // 2, start : start + half, tile]
        if g:
            part = pltpu.roll(part, HALO * g, 1)
        low = (first + HALO * g) % LANES
        mine = (lane >= low) & (lane < low + HALO)
        packed = part if packed is None else jnp.where(mine, part, packed)
    return packed


def unpack_lanes(packed, group):
    return pltpu.roll(packed, LANES - HALO * group, 1) if group else packed


def split(x):
    high = x.astype(jnp.bfloat16)
    return high, (x - high.astype(jnp.float32)).astype(jnp.bfloat16)


def product(left, right):
    return jnp.dot(left, right, preferred_element_type=jnp.float32)


def times_table(x, table, which):
    high, low = split(x)
    t_high, t_low = table[2 * which], table[2 * which + 1]
    return product(beside(high, high, low), below(t_high, t_low, t_high))


def table_times(table, which, x):
    high, low = split(x)
    t_high, t_low = table[2 * which], table[2 * which + 1]
    return product(beside(t_high, t_low, t_high), below(high, high, low))


def beside(*blocks):
    return jnp.concatenate(blocks, axis=1)


def below(*blocks):
    return jnp.concatenate(blocks, axis=0)


def ends(x):
    return x[:, :HALF], x[:, HALF:]


def forward_columns(exit_re, exit_im, table):
    re_lo, re_hi = ends(exit_re)
    im_lo, im_hi = ends(exit_im)
    even = times_table(beside(re_lo + re_hi, im_lo + im_hi), table, 0)
    odd = times_table(beside(re_lo - re_hi, im_lo - im_hi), table, 1)
    return even, odd


def forward_rows(even, odd, table):
    out = []
    for parity in (0, 1):
        if parity == 0:
            se, so = even[:HALF] + even[HALF:], odd[:HALF] + odd[HALF:]
        else:
            se, so = even[:HALF] - even[HALF:], odd[:HALF] - odd[HALF:]
        e_re, e_im = ends(se)
        o_re, o_im = ends(so)
        out.append(table_times(table, 2 + parity, below(beside(e_re, o_re), beside(e_im, o_im))))
    return out


def residual(far, frame):
    out = []
    for parity in (0, 1):
        re, im = far[parity][:HALF], far[parity][HALF:]
        level = jnp.maximum(re * re + im * im, floor_amp * floor_amp)
        inten = frame[parity * HALF : (parity + 1) * HALF]
        factor = 1.0 - inten * lax.rsqrt(inten * level)
        out.append(below(re * factor, im * factor))
    return out


def back_rows(res, table):
    first = table_times(table, 0, res[0])
    second = table_times(table, 1, res[1])
    upper, lower = first + second, first - second
    out = []
    for cols in (slice(0, HALF), slice(HALF, P_SIZE)):
        out.append(
            below(
                beside(upper[:HALF, cols], upper[HALF:, cols]),
                beside(lower[:HALF, cols], lower[HALF:, cols]),
            )
        )
    return out


def back_columns(parts, table):
    even = times_table(parts[0], table, 2)
    odd = times_table(parts[1], table, 3)
    lo, hi = even + odd, even - odd
    return beside(lo[:, :HALF], hi[:, :HALF]), beside(lo[:, HALF:], hi[:, HALF:])


def is_odd(axis):
    return lax.rem(lax.axis_index(axis), 2) == 1


def fetch(pairs, sems):
    copies = [pltpu.make_async_copy(far, near, sems.at[i]) for i, (far, near) in enumerate(pairs)]
    for copy in copies:
        copy.start()
    return copies


def finish_all(copies):
    for copy in copies:
        copy.wait()


def row_edges(counts, obj_re, obj_im, offsets, chosen, to_outer, to_inner, marked, places, frame_of, sems):
    tile_r = obj_re.shape[0]
    odd = is_odd("row")
    low = pl.multiple_of(jnp.where(odd, 0, tile_r - HALO), 16)
    high = pl.multiple_of(jnp.where(odd, tile_r - HALO, 0), 16)
    pairs = [(offsets, places), (chosen, frame_of)]
    tiles = obj_re.shape[1] // LANES
    for k, ref in enumerate((obj_re, obj_im)):
        for t in range(tiles):
            lanes = slice(t * LANES, (t + 1) * LANES)
            rows = slice((2 * t + k) * HALO, (2 * t + k + 1) * HALO)
            pairs.append((ref.at[pl.ds(high, HALO), lanes], to_outer.at[rows]))
            pairs.append((ref.at[pl.ds(low, HALO), lanes], to_inner.at[rows]))
    copies = fetch(pairs, sems)
    finish_all(copies[:2])
    place = places[0, 0]
    live = lax.broadcasted_iota(jnp.int32, place.shape, 1) < counts[0, 0]
    place = jnp.where(live, place, 2 * tile_r)
    marked[0:2, :] = place
    marked[2:3, :] = frame_of[0]
    for message in (to_inner, to_outer):
        first = 2 * HALO * tiles
        message[first : first + 2, 0 : place.shape[1]] = place.astype(jnp.float32)
    finish_all(copies[2:])


def window_place(slots, slot):
    row = pl.multiple_of(slots[0, slot] + HALO, 16)
    col = slots[1, slot] + LANES
    turn = lax.rem(col, LANES)
    return row, pl.multiple_of(col - turn, LANES), turn


def add_window(acc, layer, where, keep, term, tiles=(0, 1, 2)):
    row, base, _ = where
    lo, hi = ends(term)
    parts = (jnp.where(keep, lo, 0.0), hi, jnp.where(keep, 0.0, lo))
    for t in tiles:
        acc[layer, pl.ds(row, term.shape[0]), pl.ds(base + t * LANES, LANES)] += parts[t]


def send_columns(to_left, to_right, to_inner, to_outer):
    odd = is_odd("col")
    to_inner[0 : to_left.shape[0], :] = jnp.where(odd, to_left, to_right)
    to_outer[0 : to_left.shape[0], :] = jnp.where(odd, to_right, to_left)


def received(by_inner, by_outer, axis):
    odd = is_odd(axis)
    index = lax.axis_index(axis)
    inside = (index > 0) & (index < lax.axis_size(axis) - 1)
    by_outer = jnp.where(inside, by_outer[...], 0.0)
    by_inner = by_inner[...]
    return jnp.where(odd, by_inner, by_outer), jnp.where(odd, by_outer, by_inner)


def pieces(packed, size):
    half = size // 2
    for g in range(GROUPS):
        yield g // 2, g % 2 * half, unpack_lanes(packed[:half], g)


def pack_corners(field, rows):
    width = field.shape[2]
    left = [field[k, rows, 0:LANES] for k in (0, 1)]
    right = [field[k, rows, width - LANES : width] for k in (0, 1)]
    lane = lane_index(HALO)
    low = jnp.where(lane < HALO, right[0], pltpu.roll(right[1], HALO, 1))
    high = jnp.where(lane < 3 * HALO, pltpu.roll(left[1], 3 * HALO, 1), left[0])
    packed = jnp.where(lane < 2 * HALO, low, high)
    return beside(*(packed[i : i + MARKS] for i in range(0, HALO, MARKS)))


def unpack_corners(packed):
    packed = below(*(packed[:, i : i + LANES] for i in range(0, GROUPS * LANES, LANES)))
    lane = lane_index(HALO)
    for k, left, right in ((0, 0, 0), (1, HALO, 3 * HALO)):
        yield (
            k,
            jnp.where(lane >= 3 * HALO, pltpu.roll(packed, left, 1) if left else packed, 0.0),
            jnp.where(lane < HALO, pltpu.roll(packed, right, 1) if right else packed, 0.0),
        )


def row_halos(cells_in, own, by_outer, by_inner, cells, marks, to_inner, to_outer):
    rows, width = cells.shape[1:]
    before, after = received(by_inner, by_outer, "row")
    tiles = width // LANES - 2
    for k in (0, 1):
        for t in range(tiles):
            lanes = slice((t + 1) * LANES, (t + 2) * LANES)
            part = slice((2 * t + k) * HALO, (2 * t + k + 1) * HALO)
            cells[k, 0:HALO, lanes] = before[part]
            cells[k, rows - HALO : rows, lanes] = after[part]
    first = 2 * HALO * tiles
    for i, message in enumerate((own[...], before, after)):
        marks[2 * i : 2 * i + 2, :] = message[first : first + 2]
    half = rows // 2
    to_left = pack_lanes(cells, 0, rows, slice(LANES, 2 * LANES), 0)
    to_right = pack_lanes(cells, 0, rows, slice(width - 2 * LANES, width - LANES), LANES - HALO)
    send_columns(to_left, to_right, to_inner, to_outer)
    to_inner[half:, :] = marks[...]
    to_outer[half:, :] = marks[...]


def live_slots(slots, cells):
    tile_r = cells.shape[1] - 2 * HALO
    count = jnp.int32(0)
    for slot in range(slots.shape[1]):
        count += (slots[0, slot] < tile_r).astype(jnp.int32)
    return count


FIRST, BEFORE, OVER, AFTER, LAST = range(5)


def run_windows(phase, slots, cells, acc, probe_re, probe_im, table, frames, order):
    tile_r, tile_c = cells.shape[1] - 2 * HALO, cells.shape[2] - 2 * LANES
    count = live_slots(slots, cells)
    kinds = []
    n_inside, n_row, n_col = jnp.int32(0), jnp.int32(0), jnp.int32(0)
    for slot in range(slots.shape[1]):
        row, col = slots[0, slot], slots[1, slot]
        live = slot < count
        over_col = (col < 0) | (col > tile_c - P_SIZE)
        over_row = (row < 0) | (row > tile_r - P_SIZE)
        inside, by_row = live & ~over_col & ~over_row, live & ~over_col & over_row
        by_col, by_both = live & over_col & ~over_row, live & over_col & over_row
        kinds.append((inside, by_row, by_col, by_both, n_inside, n_row))
        n_inside += inside.astype(jnp.int32)
        n_row += by_row.astype(jnp.int32)
        n_col += by_col.astype(jnp.int32)
    first = jnp.minimum(n_inside, PAIR)
    before = first + jnp.minimum(n_inside - first, PAIR - jnp.minimum(n_row, PAIR))
    rest = n_inside - before
    after = n_inside - jnp.clip(n_col + rest - 2 * PAIR, 0, jnp.minimum(rest, PAIR))
    found = jnp.int32(0)
    for slot, (inside, by_row, by_col, by_both, rank, row_rank) in enumerate(kinds):
        mine = {
            FIRST: lambda: inside & (rank < first),
            BEFORE: lambda: (by_row & (row_rank < PAIR)) | (inside & (rank >= first) & (rank < before)),
            OVER: lambda: by_both | (by_row & (row_rank >= PAIR)),
            AFTER: lambda: by_col | (inside & (rank >= before) & (rank < after)),
            LAST: lambda: inside & (rank >= after),
        }[phase]()

        @pl.when(mine)
        def _():
            order[found] = slot

        found += mine.astype(jnp.int32)

    lane = lane_index(P_SIZE)

    def load(slot):
        where = row, base, turn = window_place(slots, slot)
        keep = lane >= turn
        w_re = pltpu.roll(probe_re[...], turn, 1)
        w_im = pltpu.roll(probe_im[...], turn, 1)
        patch = []
        for k in (0, 1):
            block = cells[k, pl.ds(row, P_SIZE), pl.ds(base, 3 * LANES)]
            patch.append(
                beside(jnp.where(keep, block[:, :LANES], block[:, 2 * LANES :]), block[:, LANES : 2 * LANES])
            )
        exit_re = w_re * patch[0] - w_im * patch[1]
        exit_im = w_re * patch[1] + w_im * patch[0]
        return (where, keep, w_re, w_im), exit_re, exit_im

    def frame_of(slot):
        half = product(table[8], frames[slots[2, slot]]).astype(jnp.bfloat16)
        return product(half, table[9])

    def place(at, back_re, back_im):
        where, keep, w_re, w_im = at
        add_window(acc, 0, where, keep, w_re * back_re + w_im * back_im)
        add_window(acc, 1, where, keep, w_re * back_im - w_im * back_re)

    def rows_of(stacked):
        return [stacked[i : i + P_SIZE] for i in range(0, stacked.shape[0], P_SIZE)]

    def step(group):
        frame = [frame_of(slot) for slot in group]
        loaded = [load(slot) for slot in group]
        stacked = forward_columns(below(*(x[1] for x in loaded)), below(*(x[2] for x in loaded)), table)
        state = [forward_rows(*x, table) for x in zip(*map(rows_of, stacked))]
        state = [residual(x, f) for x, f in zip(state, frame)]
        state = [back_rows(x, table) for x in state]
        stacked = back_columns([below(*parts) for parts in zip(*state)], table)
        for x, back in zip(loaded, zip(*map(rows_of, stacked))):
            place(x[0], *back)

    def pair_step(pair, carry):
        step([order[pair * PAIR + i] for i in range(PAIR)])
        return carry

    lax.fori_loop(0, found // PAIR, pair_step, 0)

    @pl.when(found % PAIR == 1)
    def _():
        step([order[found - 1]])


def windows_first(
    slots, obj_re, obj_im, probe_re_far, probe_im_far, table_far, frames_far,
    cells, acc, probe_re, probe_im, table, frames, order, sems,
):
    tile_r, tile_c = obj_re.shape
    inner = slice(HALO, HALO + tile_r)
    middle = slice(LANES, LANES + tile_c)
    pairs = (
        (table_far, table),
        (frames_far, frames),
        (obj_re, cells.at[0, inner, middle]),
        (obj_im, cells.at[1, inner, middle]),
        (probe_re_far, probe_re),
        (probe_im_far, probe_im),
    )
    copies = fetch(pairs, sems)
    acc[...] = jnp.zeros_like(acc)
    finish_all(copies)
    run_windows(FIRST, slots, cells, acc, probe_re, probe_im, table, frames, order)


def windows_before(
    slots, cells, acc_in, probe_re, probe_im, table, frames, acc, order, power,
):
    power[...] = probe_re[...] * probe_re[...] + probe_im[...] * probe_im[...]
    lane = lane_index(P_SIZE)

    def step(slot, carry):
        where = window_place(slots, slot)
        add_window(acc, 2, where, lane >= where[2], pltpu.roll(power[...], where[2], 1))
        return carry

    lax.fori_loop(0, live_slots(slots, cells), step, 0)
    run_windows(BEFORE, slots, cells, acc, probe_re, probe_im, table, frames, order)


def reaching(place, right, tile_r, tile_c):
    shape = place.shape
    index = lax.broadcasted_iota(jnp.int32, shape, 0)
    lane = lax.broadcasted_iota(jnp.int32, shape, 1)
    col = pltpu.roll(place, shape[0] - 1, 0)
    low = jnp.where(index == 2, tile_r - P_SIZE, -tile_r).astype(jnp.float32)
    high = jnp.where(index == 4, 0, tile_r).astype(jnp.float32)
    reaches = (lane < MARKS) & (index % 2 == 0) & (index < 6) & (place > low) & (place < high)
    if right < 0:
        reaches &= col > tile_c - P_SIZE
    if right > 0:
        reaches &= col < 0
    bit = lax.shift_left(jnp.ones(shape, jnp.int32), jnp.minimum(lane, MARKS)).astype(jnp.float32)
    bits = jnp.sum(jnp.where(reaches, bit, 0.0), axis=1, keepdims=True)
    return jnp.where(lane < MARKS, place, bits).astype(jnp.int32)


def add_neighbours_light(places, acc, power):
    rows, width = acc.shape[1:]
    tile_r, tile_c = rows - 2 * HALO, width - 2 * LANES
    for right in (-1, 0, 1):
        for i, down in enumerate((0, -1, 1)):
            if not right and not down:
                continue
            first, last = {-1: (P_SIZE - HALO, P_SIZE), 0: (0, P_SIZE), 1: (0, HALO)}[down]
            tiles = {-1: (2,), 0: (0, 1, 2), 1: (0,)}[right]
            lane = lane_index(last - first)
            bits = places[right + 1, 2 * i, MARKS]

            def step(slot, carry):
                row, col = places[right + 1, 2 * i, slot], places[right + 1, 2 * i + 1, slot]

                @pl.when(lax.shift_right_logical(bits, slot) % 2 == 1)
                def _():
                    turn = lax.rem(col + LANES, LANES)
                    at = pl.multiple_of(row + HALO + (down * tile_r + first), 16)
                    base = pl.multiple_of(col + LANES - turn + right * tile_c, LANES)
                    part = pltpu.roll(power[first:last, :], turn, 1)
                    add_window(acc, 2, (at, base, turn), lane >= turn, part, tiles)

                return carry

            @pl.when(bits != 0)
            def _():
                lax.fori_loop(0, MARKS, step, 0)


def windows_after(
    slots, cells, acc_in, probe_re, probe_im, table, frames, marks, by_inner, by_outer,
    acc, order, power, whole, places, sem,
):
    rows, width = acc.shape[1:]
    before, after = received(by_inner, by_outer, "col")
    for i, part in enumerate((before[-MARKS:], marks[...], after[-MARKS:])):
        whole[i] = reaching(part, i - 1, rows - 2 * HALO, width - 2 * LANES)
    copy = pltpu.make_async_copy(whole, places, sem)
    copy.start()
    power[...] = probe_re[...] * probe_re[...] + probe_im[...] * probe_im[...]
    run_windows(AFTER, slots, cells, acc, probe_re, probe_im, table, frames, order)
    copy.wait()
    add_neighbours_light(places, acc, power)


def windows_over_edge(
    marked, cells_in, acc_in, probe_re, probe_im, table, frames, by_inner, by_outer,
    cells, acc, to_outer, to_inner, order, slots, sem,
):
    scalars = pltpu.make_async_copy(marked, slots, sem)
    scalars.start()
    rows, width = acc.shape[1:]
    before, after = received(by_inner, by_outer, "col")
    for tile, packed in ((slice(0, LANES), before), (slice(width - LANES, width), after)):
        for layer, row, part in pieces(packed, rows):
            cells[layer, row : row + part.shape[0], tile] = part
    scalars.wait()
    run_windows(OVER, slots, cells, acc, probe_re, probe_im, table, frames, order)
    odd = is_odd("row")
    strips = []
    for here in (slice(0, HALO), slice(rows - HALO, rows)):
        middle = [acc[k, here, LANES : width - LANES] for k in (0, 1)]
        strips.append(below(*middle, pack_corners(acc, here)))
    to_inner[...] = jnp.where(odd, strips[0], strips[1])
    to_outer[...] = jnp.where(odd, strips[1], strips[0])


def column_spill(acc_in, by_outer, by_inner, acc, to_inner, to_outer):
    rows, width = acc.shape[1:]
    before, after = received(by_inner, by_outer, "row")
    for start, came in ((HALO, before), (rows - 2 * HALO, after)):
        here = slice(start, start + HALO)
        for k in (0, 1):
            acc[k, here, LANES : width - LANES] += came[k * HALO : (k + 1) * HALO]
        for k, left, right in unpack_corners(came[2 * HALO :]):
            acc[k, here, 0:LANES] += left
            acc[k, here, width - LANES :] += right
    tile_r = rows - 2 * HALO
    to_left = pack_lanes(acc, HALO, tile_r, slice(0, LANES), LANES - HALO)
    to_right = pack_lanes(acc, HALO, tile_r, slice(width - LANES, width), 0)
    send_columns(to_left, to_right, to_inner, to_outer)


def new_columns(cells, acc, spill, start, size, near_re, near_im):
    rows = acc.shape[1]
    here, there = slice(HALO, rows - HALO), slice(LANES + start, LANES + start + size)
    part = [acc[k, here, there] for k in range(acc.shape[0])]
    if spill is not None:
        part[:2] = [part[k] + spill[k] for k in (0, 1)]
    scale = 1.0 / (part[2] + ridge)
    near_re[:, start : start + size] = cells[0, here, there] - part[0] * scale
    near_im[:, start : start + size] = cells[1, here, there] - part[1] * scale


def finish_inner(
    slots, cells, acc_in, probe_re, probe_im, table, frames, acc, new_re, new_im, order, near_re, near_im, sems,
):
    run_windows(LAST, slots, cells, acc, probe_re, probe_im, table, frames, order)
    size = near_re.shape[1] - 2 * LANES
    new_columns(cells, acc, None, LANES, size, near_re, near_im)
    there = slice(LANES, LANES + size)
    finish_all(fetch([(near_re.at[:, there], new_re.at[:, there]), (near_im.at[:, there], new_im.at[:, there])], sems))


def finish_edges(cells, acc, by_inner, by_outer, re_in, im_in, new_re, new_im, near_re, near_im, sems):
    tile_r, tile_c = near_re.shape
    lane = lane_index(tile_r)
    sides = ((0, lane < HALO), (tile_c - LANES, lane >= LANES - HALO))
    copies = []
    for i, ((start, mine), packed) in enumerate(zip(sides, received(by_inner, by_outer, "col"))):
        parts = [part for _, _, part in pieces(packed, tile_r)]
        spill = [jnp.where(mine, below(*parts[2 * k : 2 * k + 2]), 0.0) for k in (0, 1)]
        new_columns(cells, acc, spill, start, LANES, near_re, near_im)
        there = slice(start, start + LANES)
        pairs = ((near_re.at[:, there], new_re.at[:, there]), (near_im.at[:, there], new_im.at[:, there]))
        copies += fetch(pairs, sems.at[2 * i : 2 * i + 2])
    finish_all(copies)


def swap(to_inner, to_outer, axis):
    devices = lax.axis_size(axis)
    inner = [(i, i + 1) for i in range(0, devices, 2)]
    partner = {i: i + 1 if i % 2 else i - 1 for i in range(1, devices - 1)}
    n_row, n_col = lax.axis_size("row"), lax.axis_size("col")
    pairs = []
    for row in range(n_row):
        for col in range(n_col):
            if axis == "row":
                there = (partner[row], col) if row in partner else (row, col ^ 1)
            else:
                there = (row, partner[col]) if col in partner else (row ^ 1, col)
            pairs.append((row * n_col + col, there[0] * n_col + there[1]))
    by_inner = lax.ppermute(to_inner, axis, inner + [(j, i) for i, j in inner])
    by_outer = lax.ppermute(to_outer, ("row", "col"), pairs)
    return by_inner, by_outer


def far(x):
    return pltpu.with_memory_space_constraint(x, pltpu.HBM)


def f32(*shape):
    return jax.ShapeDtypeStruct(shape, jnp.float32)


def shards(object_re, object_im, probe_re, probe_im, frames, counts, offsets, frame_index):
    tile_r, tile_c = object_re.shape
    rows, width = tile_r + 2 * HALO, tile_c + 2 * LANES
    layers = 3
    slots = offsets.shape[2]
    table = jnp.asarray(transform_tables())
    frames = frames.reshape(frames.shape[2:])
    cells_shape, acc_shape = f32(2, rows, width), f32(layers, rows, width)
    dma = pltpu.SemaphoreType.DMA

    places = jnp.swapaxes(offsets, 2, 3)
    edge = f32(2 * HALO * (tile_c // LANES) + MARKS, LANES)
    to_outer, to_inner, marked = pl.pallas_call(
        row_edges,
        out_shape=(edge, edge, jax.ShapeDtypeStruct((3, slots), jnp.int32)),
        in_specs=[SMEM] + [HBM] * 4,
        out_specs=(VMEM, VMEM, VMEM),
        scratch_shapes=[
            pltpu.VMEM(places.shape, jnp.int32), pltpu.VMEM(frame_index.shape, jnp.int32),
            dma((2 + 4 * (tile_c // LANES),)),
        ],
        compiler_params=SMALL,
        name="row_edges",
    )(counts, far(object_re), far(object_im), far(places), far(frame_index))
    by_inner, by_outer = swap(to_inner, to_outer, "row")

    order = pltpu.SMEM((slots,), jnp.int32)
    cells, acc, *fixed = pl.pallas_call(
        windows_first,
        out_shape=(
            cells_shape, acc_shape, f32(*probe_re.shape), f32(*probe_im.shape),
            jax.ShapeDtypeStruct(table.shape, table.dtype), jax.ShapeDtypeStruct(frames.shape, frames.dtype),
        ),
        in_specs=[SMEM] + [HBM] * 6,
        out_specs=(VMEM,) * 6,
        scratch_shapes=[order, dma((6,))],
        compiler_params=PARAMS,
        cost_estimate=BUSY,
        name="windows_first",
    )(marked, *map(far, (object_re, object_im, probe_re, probe_im, table, frames)))

    packed = f32(rows // 2 + MARKS, LANES)
    cells, marks, to_inner, to_outer = pl.pallas_call(
        row_halos,
        out_shape=(cells_shape, f32(MARKS, LANES), packed, packed),
        in_specs=[VMEM] * 4,
        out_specs=(VMEM,) * 4,
        input_output_aliases={0: 0},
        compiler_params=SMALL,
        name="row_halos",
    )(cells, to_outer, by_outer, by_inner)
    edges = swap(to_inner, to_outer, "col")

    acc = pl.pallas_call(
        windows_before,
        out_shape=acc_shape,
        in_specs=[SMEM] + [VMEM] * 6,
        out_specs=VMEM,
        scratch_shapes=[order, pltpu.VMEM(probe_re.shape, jnp.float32)],
        input_output_aliases={2: 0},
        compiler_params=PARAMS,
        cost_estimate=BUSY,
        name="windows_before",
    )(marked, cells, acc, *fixed)

    edge = f32(2 * HALO + MARKS, tile_c)
    cells, acc, to_outer, to_inner = pl.pallas_call(
        windows_over_edge,
        out_shape=(cells_shape, acc_shape, edge, edge),
        in_specs=[VMEM] * 9,
        out_specs=(VMEM,) * 4,
        scratch_shapes=[order, pltpu.SMEM((3, slots), jnp.int32), dma(())],
        input_output_aliases={1: 0, 2: 1},
        compiler_params=PARAMS,
        cost_estimate=BUSY,
        name="windows_over_edge",
    )(marked, cells, acc, *fixed, *edges)
    by_inner, by_outer = swap(to_inner, to_outer, "row")

    acc = pl.pallas_call(
        windows_after,
        out_shape=acc_shape,
        in_specs=[SMEM] + [VMEM] * 9,
        out_specs=VMEM,
        scratch_shapes=[
            order, pltpu.VMEM(probe_re.shape, jnp.float32),
            pltpu.VMEM((3, MARKS, LANES), jnp.int32), pltpu.SMEM((3, MARKS, LANES), jnp.int32), dma(()),
        ],
        input_output_aliases={2: 0},
        compiler_params=PARAMS,
        cost_estimate=BUSY,
        name="windows_after",
    )(marked, cells, acc, *fixed, marks, *edges)

    packed = f32(tile_r // 2, LANES)
    acc, to_inner, to_outer = pl.pallas_call(
        column_spill,
        out_shape=(acc_shape, packed, packed),
        in_specs=[VMEM] * 3,
        out_specs=(VMEM,) * 3,
        input_output_aliases={0: 0},
        compiler_params=SMALL,
        name="column_spill",
    )(acc, by_outer, by_inner)
    by_inner, by_outer = swap(to_inner, to_outer, "col")

    near = [pltpu.VMEM((tile_r, tile_c), jnp.float32)] * 2
    new = (f32(tile_r, tile_c), f32(tile_r, tile_c))
    acc, new_re, new_im = pl.pallas_call(
        finish_inner,
        out_shape=(acc_shape, *new),
        in_specs=[SMEM] + [VMEM] * 6,
        out_specs=(VMEM, HBM, HBM),
        scratch_shapes=[order] + near + [dma((2,))],
        input_output_aliases={2: 0},
        compiler_params=PARAMS,
        cost_estimate=BUSY,
        name="finish_inner",
    )(marked, cells, acc, *fixed)
    return pl.pallas_call(
        finish_edges,
        out_shape=new,
        in_specs=[VMEM] * 4 + [HBM] * 2,
        out_specs=(HBM, HBM),
        scratch_shapes=near + [dma((4,))],
        input_output_aliases={4: 0, 5: 1},
        compiler_params=SMALL,
        name="finish_edges",
    )(cells, acc, by_inner, by_outer, far(new_re), far(new_im))


def solution(mesh):
    return jax.shard_map(
        shards,
        mesh=mesh,
        in_specs=(
            P("row", "col"),
            P("row", "col"),
            P(),
            P(),
            P("row", "col", None, None, None),
            P("row", "col"),
            P("row", "col", None, None),
            P("row", "col", None),
        ),
        out_specs=(P("row", "col"), P("row", "col")),
        check_vma=False,
    )
```

```python
import functools
import math

import jax
import jax.numpy as jnp
import ml_dtypes
import numpy as np
from jax import lax
from jax.experimental import pallas as pl
from jax.experimental.pallas import tpu as pltpu
from jax.sharding import PartitionSpec as P

P_SIZE = 256
HALF = P_SIZE // 2
HALO = 32
LANES = 128
GROUPS = LANES // HALO
MARKS = 8
PAIR = 2

floor_amp = 0.5
ridge = 1.0

VMEM = pl.BlockSpec(memory_space=pltpu.VMEM)
SMEM = pl.BlockSpec(memory_space=pltpu.SMEM)
HBM = pl.BlockSpec(memory_space=pltpu.HBM)
PARAMS = pltpu.CompilerParams(vmem_limit_bytes=32 * 1024 * 1024)
SMALL = pltpu.CompilerParams(vmem_limit_bytes=16 * 1024 * 1024)
BUSY = pl.CostEstimate(flops=4_000_000_000, bytes_accessed=8_000_000, transcendentals=0)


def transform_tables():
    index = np.arange(HALF)
    plain = []
    for parity in (0, 1):
        angle = 2.0 * math.pi / P_SIZE * (index[:, None] * (2 * index[None, :] + parity) % P_SIZE)
        cos, sin = np.cos(angle), np.sin(angle)
        plain.append(np.block([[cos, -sin], [sin, cos]]) / math.sqrt(P_SIZE))
    parts = []
    for table in plain + [t.T for t in plain]:
        high = table.astype(np.float32).astype(ml_dtypes.bfloat16)
        low = (table - high.astype(np.float64)).astype(np.float32).astype(ml_dtypes.bfloat16)
        parts += [high, low]
    order = np.concatenate([np.arange(0, P_SIZE, 2), np.arange(1, P_SIZE, 2)])
    sort = np.zeros((P_SIZE, P_SIZE), np.float32)
    sort[np.arange(P_SIZE), order] = 1.0
    parts += [sort.astype(ml_dtypes.bfloat16), sort.T.astype(ml_dtypes.bfloat16)]
    return np.stack(parts)


def lane_index(rows):
    return lax.broadcasted_iota(jnp.int32, (rows, LANES), 1)


def pack_lanes(field, top, size, tile, first):
    half = size // 2
    lane = lane_index(half)
    packed = None
    for g in range(GROUPS):
        start = top + g % 2 * half
        part = field[g // 2, start : start + half, tile]
        if g:
            part = pltpu.roll(part, HALO * g, 1)
        low = (first + HALO * g) % LANES
        mine = (lane >= low) & (lane < low + HALO)
        packed = part if packed is None else jnp.where(mine, part, packed)
    return packed


def unpack_lanes(packed, group):
    return pltpu.roll(packed, LANES - HALO * group, 1) if group else packed


def split(x):
    high = x.astype(jnp.bfloat16)
    return high, (x - high.astype(jnp.float32)).astype(jnp.bfloat16)


def product(left, right):
    return jnp.dot(left, right, preferred_element_type=jnp.float32)


def times_table(x, table, which):
    high, low = split(x)
    t_high, t_low = table[2 * which], table[2 * which + 1]
    return product(beside(high, high, low), below(t_high, t_low, t_high))


def table_times(table, which, x):
    high, low = split(x)
    t_high, t_low = table[2 * which], table[2 * which + 1]
    return product(beside(t_high, t_low, t_high), below(high, high, low))


def beside(*blocks):
    return jnp.concatenate(blocks, axis=1)


def below(*blocks):
    return jnp.concatenate(blocks, axis=0)


def ends(x):
    return x[:, :HALF], x[:, HALF:]


def forward_columns(exit_re, exit_im, table):
    re_lo, re_hi = ends(exit_re)
    im_lo, im_hi = ends(exit_im)
    even = times_table(beside(re_lo + re_hi, im_lo + im_hi), table, 0)
    odd = times_table(beside(re_lo - re_hi, im_lo - im_hi), table, 1)
    return even, odd


def forward_rows(even, odd, table):
    out = []
    for parity in (0, 1):
        if parity == 0:
            se, so = even[:HALF] + even[HALF:], odd[:HALF] + odd[HALF:]
        else:
            se, so = even[:HALF] - even[HALF:], odd[:HALF] - odd[HALF:]
        e_re, e_im = ends(se)
        o_re, o_im = ends(so)
        out.append(table_times(table, 2 + parity, below(beside(e_re, o_re), beside(e_im, o_im))))
    return out


def residual(far, frame):
    out = []
    for parity in (0, 1):
        re, im = far[parity][:HALF], far[parity][HALF:]
        level = jnp.maximum(re * re + im * im, floor_amp * floor_amp)
        inten = frame[parity * HALF : (parity + 1) * HALF]
        factor = 1.0 - inten * lax.rsqrt(inten * level)
        out.append(below(re * factor, im * factor))
    return out


def back_rows(res, table):
    first = table_times(table, 0, res[0])
    second = table_times(table, 1, res[1])
    upper, lower = first + second, first - second
    out = []
    for cols in (slice(0, HALF), slice(HALF, P_SIZE)):
        out.append(
            below(
                beside(upper[:HALF, cols], upper[HALF:, cols]),
                beside(lower[:HALF, cols], lower[HALF:, cols]),
            )
        )
    return out


def back_columns(parts, table):
    even = times_table(parts[0], table, 2)
    odd = times_table(parts[1], table, 3)
    lo, hi = even + odd, even - odd
    return beside(lo[:, :HALF], hi[:, :HALF]), beside(lo[:, HALF:], hi[:, HALF:])


def is_odd(axis):
    return lax.rem(lax.axis_index(axis), 2) == 1


def fetch(pairs, sems):
    copies = [pltpu.make_async_copy(far, near, sems.at[i]) for i, (far, near) in enumerate(pairs)]
    for copy in copies:
        copy.start()
    return copies


def finish_all(copies):
    for copy in copies:
        copy.wait()


def row_edges(counts, obj_re, obj_im, offsets, chosen, to_outer, to_inner, marked, places, frame_of, sems):
    tile_r = obj_re.shape[0]
    odd = is_odd("row")
    low = pl.multiple_of(jnp.where(odd, 0, tile_r - HALO), 16)
    high = pl.multiple_of(jnp.where(odd, tile_r - HALO, 0), 16)
    pairs = [(offsets, places), (chosen, frame_of)]
    tiles = obj_re.shape[1] // LANES
    for k, ref in enumerate((obj_re, obj_im)):
        for t in range(tiles):
            lanes = slice(t * LANES, (t + 1) * LANES)
            rows = slice((2 * t + k) * HALO, (2 * t + k + 1) * HALO)
            pairs.append((ref.at[pl.ds(high, HALO), lanes], to_outer.at[rows]))
            pairs.append((ref.at[pl.ds(low, HALO), lanes], to_inner.at[rows]))
    copies = fetch(pairs, sems)
    finish_all(copies[:2])
    place = places[0, 0]
    live = lax.broadcasted_iota(jnp.int32, place.shape, 1) < counts[0, 0]
    place = jnp.where(live, place, 2 * tile_r)
    marked[0:2, :] = place
    marked[2:3, :] = frame_of[0]
    for message in (to_inner, to_outer):
        first = 2 * HALO * tiles
        message[first : first + 2, 0 : place.shape[1]] = place.astype(jnp.float32)
    finish_all(copies[2:])


def window_place(slots, slot):
    row = pl.multiple_of(slots[0, slot] + HALO, 16)
    col = slots[1, slot] + LANES
    turn = lax.rem(col, LANES)
    return row, pl.multiple_of(col - turn, LANES), turn


def add_window(acc, layer, where, keep, term, tiles=(0, 1, 2)):
    row, base, _ = where
    lo, hi = ends(term)
    parts = (jnp.where(keep, lo, 0.0), hi, jnp.where(keep, 0.0, lo))
    for t in tiles:
        acc[layer, pl.ds(row, term.shape[0]), pl.ds(base + t * LANES, LANES)] += parts[t]


def send_columns(to_left, to_right, to_inner, to_outer):
    odd = is_odd("col")
    to_inner[0 : to_left.shape[0], :] = jnp.where(odd, to_left, to_right)
    to_outer[0 : to_left.shape[0], :] = jnp.where(odd, to_right, to_left)


def received(by_inner, by_outer, axis):
    odd = is_odd(axis)
    index = lax.axis_index(axis)
    inside = (index > 0) & (index < lax.axis_size(axis) - 1)
    by_outer = jnp.where(inside, by_outer[...], 0.0)
    by_inner = by_inner[...]
    return jnp.where(odd, by_inner, by_outer), jnp.where(odd, by_outer, by_inner)


def pieces(packed, size):
    half = size // 2
    for g in range(GROUPS):
        yield g // 2, g % 2 * half, unpack_lanes(packed[:half], g)


def pack_corners(field, rows):
    width = field.shape[2]
    left = [field[k, rows, 0:LANES] for k in (0, 1)]
    right = [field[k, rows, width - LANES : width] for k in (0, 1)]
    lane = lane_index(HALO)
    low = jnp.where(lane < HALO, right[0], pltpu.roll(right[1], HALO, 1))
    high = jnp.where(lane < 3 * HALO, pltpu.roll(left[1], 3 * HALO, 1), left[0])
    packed = jnp.where(lane < 2 * HALO, low, high)
    return beside(*(packed[i : i + MARKS] for i in range(0, HALO, MARKS)))


def unpack_corners(packed):
    packed = below(*(packed[:, i : i + LANES] for i in range(0, GROUPS * LANES, LANES)))
    lane = lane_index(HALO)
    for k, left, right in ((0, 0, 0), (1, HALO, 3 * HALO)):
        yield (
            k,
            jnp.where(lane >= 3 * HALO, pltpu.roll(packed, left, 1) if left else packed, 0.0),
            jnp.where(lane < HALO, pltpu.roll(packed, right, 1) if right else packed, 0.0),
        )


def row_halos(cells_in, own, by_outer, by_inner, cells, marks, to_inner, to_outer):
    rows, width = cells.shape[1:]
    before, after = received(by_inner, by_outer, "row")
    tiles = width // LANES - 2
    for k in (0, 1):
        for t in range(tiles):
            lanes = slice((t + 1) * LANES, (t + 2) * LANES)
            part = slice((2 * t + k) * HALO, (2 * t + k + 1) * HALO)
            cells[k, 0:HALO, lanes] = before[part]
            cells[k, rows - HALO : rows, lanes] = after[part]
    first = 2 * HALO * tiles
    for i, message in enumerate((own[...], before, after)):
        marks[2 * i : 2 * i + 2, :] = message[first : first + 2]
    half = rows // 2
    to_left = pack_lanes(cells, 0, rows, slice(LANES, 2 * LANES), 0)
    to_right = pack_lanes(cells, 0, rows, slice(width - 2 * LANES, width - LANES), LANES - HALO)
    send_columns(to_left, to_right, to_inner, to_outer)
    to_inner[half:, :] = marks[...]
    to_outer[half:, :] = marks[...]


def live_slots(slots, cells):
    tile_r = cells.shape[1] - 2 * HALO
    count = jnp.int32(0)
    for slot in range(slots.shape[1]):
        count += (slots[0, slot] < tile_r).astype(jnp.int32)
    return count


FIRST, BEFORE, OVER, AFTER, LAST = range(5)


def run_windows(phase, slots, cells, acc, probe_re, probe_im, table, frames, order, largest=PAIR):
    tile_r, tile_c = cells.shape[1] - 2 * HALO, cells.shape[2] - 2 * LANES
    count = live_slots(slots, cells)
    kinds = []
    n_inside, n_row, n_col = jnp.int32(0), jnp.int32(0), jnp.int32(0)
    for slot in range(slots.shape[1]):
        row, col = slots[0, slot], slots[1, slot]
        live = slot < count
        over_col = (col < 0) | (col > tile_c - P_SIZE)
        over_row = (row < 0) | (row > tile_r - P_SIZE)
        inside, by_row = live & ~over_col & ~over_row, live & ~over_col & over_row
        by_col, by_both = live & over_col & ~over_row, live & over_col & over_row
        kinds.append((inside, by_row, by_col, by_both, n_inside, n_row))
        n_inside += inside.astype(jnp.int32)
        n_row += by_row.astype(jnp.int32)
        n_col += by_col.astype(jnp.int32)
    first = jnp.minimum(n_inside, PAIR)
    before = first + jnp.minimum(n_inside - first, PAIR - jnp.minimum(n_row, PAIR))
    rest = n_inside - before
    after = n_inside - jnp.clip(n_col + rest - 2 * PAIR, 0, jnp.minimum(rest, PAIR))
    found = jnp.int32(0)
    for slot, (inside, by_row, by_col, by_both, rank, row_rank) in enumerate(kinds):
        mine = {
            FIRST: lambda: inside & (rank < first),
            BEFORE: lambda: (by_row & (row_rank < PAIR)) | (inside & (rank >= first) & (rank < before)),
            OVER: lambda: by_both | (by_row & (row_rank >= PAIR)),
            AFTER: lambda: by_col | (inside & (rank >= before) & (rank < after)),
            LAST: lambda: inside & (rank >= after),
        }[phase]()

        @pl.when(mine)
        def _():
            order[found] = slot

        found += mine.astype(jnp.int32)

    lane = lane_index(P_SIZE)

    def load(slot):
        where = row, base, turn = window_place(slots, slot)
        keep = lane >= turn
        w_re = pltpu.roll(probe_re[...], turn, 1)
        w_im = pltpu.roll(probe_im[...], turn, 1)
        patch = []
        for k in (0, 1):
            block = cells[k, pl.ds(row, P_SIZE), pl.ds(base, 3 * LANES)]
            patch.append(
                beside(jnp.where(keep, block[:, :LANES], block[:, 2 * LANES :]), block[:, LANES : 2 * LANES])
            )
        exit_re = w_re * patch[0] - w_im * patch[1]
        exit_im = w_re * patch[1] + w_im * patch[0]
        return (where, keep, w_re, w_im), exit_re, exit_im

    def frame_of(slot):
        half = product(table[8], frames[slots[2, slot]]).astype(jnp.bfloat16)
        return product(half, table[9])

    def place(at, back_re, back_im):
        where, keep, w_re, w_im = at
        add_window(acc, 0, where, keep, w_re * back_re + w_im * back_im)
        add_window(acc, 1, where, keep, w_re * back_im - w_im * back_re)

    def step(group):
        frame = [frame_of(slot) for slot in group]
        loaded = [load(slot) for slot in group]
        state = [forward_columns(x[1], x[2], table) for x in loaded]
        state = [forward_rows(*x, table) for x in state]
        state = [residual(x, f) for x, f in zip(state, frame)]
        state = [back_rows(x, table) for x in state]
        state = [back_columns(x, table) for x in state]
        for x, back in zip(loaded, state):
            place(x[0], *back)

    def group_step(group, carry):
        step([order[group * largest + i] for i in range(largest)])
        return carry

    lax.fori_loop(0, found // largest, group_step, 0)
    for left in range(1, largest):

        @pl.when(found % largest == left)
        def _():
            step([order[found - left + i] for i in range(left)])


def windows_first(
    slots, obj_re, obj_im, probe_re_far, probe_im_far, table_far, frames_far,
    cells, acc, probe_re, probe_im, table, frames, order, sems,
):
    tile_r, tile_c = obj_re.shape
    inner = slice(HALO, HALO + tile_r)
    middle = slice(LANES, LANES + tile_c)
    pairs = (
        (table_far, table),
        (frames_far, frames),
        (obj_re, cells.at[0, inner, middle]),
        (obj_im, cells.at[1, inner, middle]),
        (probe_re_far, probe_re),
        (probe_im_far, probe_im),
    )
    copies = fetch(pairs, sems)
    acc[...] = jnp.zeros_like(acc)
    finish_all(copies)
    run_windows(FIRST, slots, cells, acc, probe_re, probe_im, table, frames, order)


def windows_before(
    slots, cells, acc_in, probe_re, probe_im, table, frames, acc, order, power,
):
    power[...] = probe_re[...] * probe_re[...] + probe_im[...] * probe_im[...]
    lane = lane_index(P_SIZE)

    def step(slot, carry):
        where = window_place(slots, slot)
        add_window(acc, 2, where, lane >= where[2], pltpu.roll(power[...], where[2], 1))
        return carry

    lax.fori_loop(0, live_slots(slots, cells), step, 0)
    run_windows(BEFORE, slots, cells, acc, probe_re, probe_im, table, frames, order)


def reaching(place, right, tile_r, tile_c):
    shape = place.shape
    index = lax.broadcasted_iota(jnp.int32, shape, 0)
    lane = lax.broadcasted_iota(jnp.int32, shape, 1)
    col = pltpu.roll(place, shape[0] - 1, 0)
    low = jnp.where(index == 2, tile_r - P_SIZE, -tile_r).astype(jnp.float32)
    high = jnp.where(index == 4, 0, tile_r).astype(jnp.float32)
    reaches = (lane < MARKS) & (index % 2 == 0) & (index < 6) & (place > low) & (place < high)
    if right < 0:
        reaches &= col > tile_c - P_SIZE
    if right > 0:
        reaches &= col < 0
    bit = lax.shift_left(jnp.ones(shape, jnp.int32), jnp.minimum(lane, MARKS)).astype(jnp.float32)
    bits = jnp.sum(jnp.where(reaches, bit, 0.0), axis=1, keepdims=True)
    return jnp.where(lane < MARKS, place, bits).astype(jnp.int32)


def add_neighbours_light(places, acc, power):
    rows, width = acc.shape[1:]
    tile_r, tile_c = rows - 2 * HALO, width - 2 * LANES
    for right in (-1, 0, 1):
        for i, down in enumerate((0, -1, 1)):
            if not right and not down:
                continue
            first, last = {-1: (P_SIZE - HALO, P_SIZE), 0: (0, P_SIZE), 1: (0, HALO)}[down]
            tiles = {-1: (2,), 0: (0, 1, 2), 1: (0,)}[right]
            lane = lane_index(last - first)
            bits = places[right + 1, 2 * i, MARKS]

            def step(slot, carry):
                row, col = places[right + 1, 2 * i, slot], places[right + 1, 2 * i + 1, slot]

                @pl.when(lax.shift_right_logical(bits, slot) % 2 == 1)
                def _():
                    turn = lax.rem(col + LANES, LANES)
                    at = pl.multiple_of(row + HALO + (down * tile_r + first), 16)
                    base = pl.multiple_of(col + LANES - turn + right * tile_c, LANES)
                    part = pltpu.roll(power[first:last, :], turn, 1)
                    add_window(acc, 2, (at, base, turn), lane >= turn, part, tiles)

                return carry

            @pl.when(bits != 0)
            def _():
                lax.fori_loop(0, MARKS, step, 0)


def windows_after(
    slots, cells, acc_in, probe_re, probe_im, table, frames, marks, by_inner, by_outer,
    acc, order, power, whole, places, sem,
):
    rows, width = acc.shape[1:]
    before, after = received(by_inner, by_outer, "col")
    for i, part in enumerate((before[-MARKS:], marks[...], after[-MARKS:])):
        whole[i] = reaching(part, i - 1, rows - 2 * HALO, width - 2 * LANES)
    copy = pltpu.make_async_copy(whole, places, sem)
    copy.start()
    power[...] = probe_re[...] * probe_re[...] + probe_im[...] * probe_im[...]
    run_windows(AFTER, slots, cells, acc, probe_re, probe_im, table, frames, order, 2 * PAIR)
    copy.wait()
    add_neighbours_light(places, acc, power)


def windows_over_edge(
    marked, cells_in, acc_in, probe_re, probe_im, table, frames, by_inner, by_outer,
    cells, acc, to_outer, to_inner, order, slots, sem,
):
    scalars = pltpu.make_async_copy(marked, slots, sem)
    scalars.start()
    rows, width = acc.shape[1:]
    before, after = received(by_inner, by_outer, "col")
    for tile, packed in ((slice(0, LANES), before), (slice(width - LANES, width), after)):
        for layer, row, part in pieces(packed, rows):
            cells[layer, row : row + part.shape[0], tile] = part
    scalars.wait()
    run_windows(OVER, slots, cells, acc, probe_re, probe_im, table, frames, order)
    odd = is_odd("row")
    strips = []
    for here in (slice(0, HALO), slice(rows - HALO, rows)):
        middle = [acc[k, here, LANES : width - LANES] for k in (0, 1)]
        strips.append(below(*middle, pack_corners(acc, here)))
    to_inner[...] = jnp.where(odd, strips[0], strips[1])
    to_outer[...] = jnp.where(odd, strips[1], strips[0])


def column_spill(acc_in, by_outer, by_inner, acc, to_inner, to_outer):
    rows, width = acc.shape[1:]
    before, after = received(by_inner, by_outer, "row")
    for start, came in ((HALO, before), (rows - 2 * HALO, after)):
        here = slice(start, start + HALO)
        for k in (0, 1):
            acc[k, here, LANES : width - LANES] += came[k * HALO : (k + 1) * HALO]
        for k, left, right in unpack_corners(came[2 * HALO :]):
            acc[k, here, 0:LANES] += left
            acc[k, here, width - LANES :] += right
    tile_r = rows - 2 * HALO
    to_left = pack_lanes(acc, HALO, tile_r, slice(0, LANES), LANES - HALO)
    to_right = pack_lanes(acc, HALO, tile_r, slice(width - LANES, width), 0)
    send_columns(to_left, to_right, to_inner, to_outer)


def new_columns(cells, acc, spill, start, size, near_re, near_im):
    rows = acc.shape[1]
    here, there = slice(HALO, rows - HALO), slice(LANES + start, LANES + start + size)
    part = [acc[k, here, there] for k in range(acc.shape[0])]
    if spill is not None:
        part[:2] = [part[k] + spill[k] for k in (0, 1)]
    scale = 1.0 / (part[2] + ridge)
    near_re[:, start : start + size] = cells[0, here, there] - part[0] * scale
    near_im[:, start : start + size] = cells[1, here, there] - part[1] * scale


def finish_inner(
    slots, cells, acc_in, probe_re, probe_im, table, frames, acc, new_re, new_im, order, near_re, near_im, sems,
):
    run_windows(LAST, slots, cells, acc, probe_re, probe_im, table, frames, order)
    size = near_re.shape[1] - 2 * LANES
    new_columns(cells, acc, None, LANES, size, near_re, near_im)
    there = slice(LANES, LANES + size)
    finish_all(fetch([(near_re.at[:, there], new_re.at[:, there]), (near_im.at[:, there], new_im.at[:, there])], sems))


def finish_edges(cells, acc, by_inner, by_outer, re_in, im_in, new_re, new_im, near_re, near_im, sems):
    tile_r, tile_c = near_re.shape
    lane = lane_index(tile_r)
    sides = ((0, lane < HALO), (tile_c - LANES, lane >= LANES - HALO))
    copies = []
    for i, ((start, mine), packed) in enumerate(zip(sides, received(by_inner, by_outer, "col"))):
        parts = [part for _, _, part in pieces(packed, tile_r)]
        spill = [jnp.where(mine, below(*parts[2 * k : 2 * k + 2]), 0.0) for k in (0, 1)]
        new_columns(cells, acc, spill, start, LANES, near_re, near_im)
        there = slice(start, start + LANES)
        pairs = ((near_re.at[:, there], new_re.at[:, there]), (near_im.at[:, there], new_im.at[:, there]))
        copies += fetch(pairs, sems.at[2 * i : 2 * i + 2])
    finish_all(copies)


def swap(to_inner, to_outer, axis):
    devices = lax.axis_size(axis)
    inner = [(i, i + 1) for i in range(0, devices, 2)]
    partner = {i: i + 1 if i % 2 else i - 1 for i in range(1, devices - 1)}
    n_row, n_col = lax.axis_size("row"), lax.axis_size("col")
    pairs = []
    for row in range(n_row):
        for col in range(n_col):
            if axis == "row":
                there = (partner[row], col) if row in partner else (row, col ^ 1)
            else:
                there = (row, partner[col]) if col in partner else (row ^ 1, col)
            pairs.append((row * n_col + col, there[0] * n_col + there[1]))
    by_inner = lax.ppermute(to_inner, axis, inner + [(j, i) for i, j in inner])
    by_outer = lax.ppermute(to_outer, ("row", "col"), pairs)
    return by_inner, by_outer


def far(x):
    return pltpu.with_memory_space_constraint(x, pltpu.HBM)


def f32(*shape):
    return jax.ShapeDtypeStruct(shape, jnp.float32)


def shards(object_re, object_im, probe_re, probe_im, frames, counts, offsets, frame_index):
    tile_r, tile_c = object_re.shape
    rows, width = tile_r + 2 * HALO, tile_c + 2 * LANES
    layers = 3
    slots = offsets.shape[2]
    table = jnp.asarray(transform_tables())
    frames = frames.reshape(frames.shape[2:])
    cells_shape, acc_shape = f32(2, rows, width), f32(layers, rows, width)
    dma = pltpu.SemaphoreType.DMA

    places = jnp.swapaxes(offsets, 2, 3)
    edge = f32(2 * HALO * (tile_c // LANES) + MARKS, LANES)
    to_outer, to_inner, marked = pl.pallas_call(
        row_edges,
        out_shape=(edge, edge, jax.ShapeDtypeStruct((3, slots), jnp.int32)),
        in_specs=[SMEM] + [HBM] * 4,
        out_specs=(VMEM, VMEM, VMEM),
        scratch_shapes=[
            pltpu.VMEM(places.shape, jnp.int32), pltpu.VMEM(frame_index.shape, jnp.int32),
            dma((2 + 4 * (tile_c // LANES),)),
        ],
        compiler_params=SMALL,
        name="row_edges",
    )(counts, far(object_re), far(object_im), far(places), far(frame_index))
    by_inner, by_outer = swap(to_inner, to_outer, "row")

    order = pltpu.SMEM((slots,), jnp.int32)
    cells, acc, *fixed = pl.pallas_call(
        windows_first,
        out_shape=(
            cells_shape, acc_shape, f32(*probe_re.shape), f32(*probe_im.shape),
            jax.ShapeDtypeStruct(table.shape, table.dtype), jax.ShapeDtypeStruct(frames.shape, frames.dtype),
        ),
        in_specs=[SMEM] + [HBM] * 6,
        out_specs=(VMEM,) * 6,
        scratch_shapes=[order, dma((6,))],
        compiler_params=PARAMS,
        cost_estimate=BUSY,
        name="windows_first",
    )(marked, *map(far, (object_re, object_im, probe_re, probe_im, table, frames)))

    packed = f32(rows // 2 + MARKS, LANES)
    cells, marks, to_inner, to_outer = pl.pallas_call(
        row_halos,
        out_shape=(cells_shape, f32(MARKS, LANES), packed, packed),
        in_specs=[VMEM] * 4,
        out_specs=(VMEM,) * 4,
        input_output_aliases={0: 0},
        compiler_params=SMALL,
        name="row_halos",
    )(cells, to_outer, by_outer, by_inner)
    edges = swap(to_inner, to_outer, "col")

    acc = pl.pallas_call(
        windows_before,
        out_shape=acc_shape,
        in_specs=[SMEM] + [VMEM] * 6,
        out_specs=VMEM,
        scratch_shapes=[order, pltpu.VMEM(probe_re.shape, jnp.float32)],
        input_output_aliases={2: 0},
        compiler_params=PARAMS,
        cost_estimate=BUSY,
        name="windows_before",
    )(marked, cells, acc, *fixed)

    edge = f32(2 * HALO + MARKS, tile_c)
    cells, acc, to_outer, to_inner = pl.pallas_call(
        windows_over_edge,
        out_shape=(cells_shape, acc_shape, edge, edge),
        in_specs=[VMEM] * 9,
        out_specs=(VMEM,) * 4,
        scratch_shapes=[order, pltpu.SMEM((3, slots), jnp.int32), dma(())],
        input_output_aliases={1: 0, 2: 1},
        compiler_params=PARAMS,
        cost_estimate=BUSY,
        name="windows_over_edge",
    )(marked, cells, acc, *fixed, *edges)
    by_inner, by_outer = swap(to_inner, to_outer, "row")

    acc = pl.pallas_call(
        windows_after,
        out_shape=acc_shape,
        in_specs=[SMEM] + [VMEM] * 9,
        out_specs=VMEM,
        scratch_shapes=[
            order, pltpu.VMEM(probe_re.shape, jnp.float32),
            pltpu.VMEM((3, MARKS, LANES), jnp.int32), pltpu.SMEM((3, MARKS, LANES), jnp.int32), dma(()),
        ],
        input_output_aliases={2: 0},
        compiler_params=PARAMS,
        cost_estimate=BUSY,
        name="windows_after",
    )(marked, cells, acc, *fixed, marks, *edges)

    packed = f32(tile_r // 2, LANES)
    acc, to_inner, to_outer = pl.pallas_call(
        column_spill,
        out_shape=(acc_shape, packed, packed),
        in_specs=[VMEM] * 3,
        out_specs=(VMEM,) * 3,
        input_output_aliases={0: 0},
        compiler_params=SMALL,
        name="column_spill",
    )(acc, by_outer, by_inner)
    by_inner, by_outer = swap(to_inner, to_outer, "col")

    near = [pltpu.VMEM((tile_r, tile_c), jnp.float32)] * 2
    new = (f32(tile_r, tile_c), f32(tile_r, tile_c))
    acc, new_re, new_im = pl.pallas_call(
        finish_inner,
        out_shape=(acc_shape, *new),
        in_specs=[SMEM] + [VMEM] * 6,
        out_specs=(VMEM, HBM, HBM),
        scratch_shapes=[order] + near + [dma((2,))],
        input_output_aliases={2: 0},
        compiler_params=PARAMS,
        cost_estimate=BUSY,
        name="finish_inner",
    )(marked, cells, acc, *fixed)
    return pl.pallas_call(
        finish_edges,
        out_shape=new,
        in_specs=[VMEM] * 4 + [HBM] * 2,
        out_specs=(HBM, HBM),
        scratch_shapes=near + [dma((4,))],
        input_output_aliases={4: 0, 5: 1},
        compiler_params=SMALL,
        name="finish_edges",
    )(cells, acc, by_inner, by_outer, far(new_re), far(new_im))


def solution(mesh):
    return jax.shard_map(
        shards,
        mesh=mesh,
        in_specs=(
            P("row", "col"),
            P("row", "col"),
            P(),
            P(),
            P("row", "col", None, None, None),
            P("row", "col"),
            P("row", "col", None, None),
            P("row", "col", None),
        ),
        out_specs=(P("row", "col"), P("row", "col")),
        check_vma=False,
    )
```

```python
import functools
import math

import jax
import jax.numpy as jnp
import ml_dtypes
import numpy as np
from jax import lax
from jax.experimental import pallas as pl
from jax.experimental.pallas import tpu as pltpu
from jax.sharding import PartitionSpec as P

P_SIZE = 256
HALF = P_SIZE // 2
HALO = 32
LANES = 128
GROUPS = LANES // HALO
MARKS = 8
PAIR = 2

floor_amp = 0.5
ridge = 1.0

VMEM = pl.BlockSpec(memory_space=pltpu.VMEM)
SMEM = pl.BlockSpec(memory_space=pltpu.SMEM)
HBM = pl.BlockSpec(memory_space=pltpu.HBM)
PARAMS = pltpu.CompilerParams(vmem_limit_bytes=32 * 1024 * 1024)
SMALL = pltpu.CompilerParams(vmem_limit_bytes=16 * 1024 * 1024)
BUSY = pl.CostEstimate(flops=4_000_000_000, bytes_accessed=8_000_000, transcendentals=0)


def transform_tables():
    index = np.arange(HALF)
    plain = []
    for parity in (0, 1):
        angle = 2.0 * math.pi / P_SIZE * (index[:, None] * (2 * index[None, :] + parity) % P_SIZE)
        cos, sin = np.cos(angle), np.sin(angle)
        plain.append(np.block([[cos, -sin], [sin, cos]]) / math.sqrt(P_SIZE))
    parts = []
    for table in plain + [t.T for t in plain]:
        high = table.astype(np.float32).astype(ml_dtypes.bfloat16)
        low = (table - high.astype(np.float64)).astype(np.float32).astype(ml_dtypes.bfloat16)
        parts += [high, low]
    order = np.concatenate([np.arange(0, P_SIZE, 2), np.arange(1, P_SIZE, 2)])
    sort = np.zeros((P_SIZE, P_SIZE), np.float32)
    sort[np.arange(P_SIZE), order] = 1.0
    parts += [sort.astype(ml_dtypes.bfloat16), sort.T.astype(ml_dtypes.bfloat16)]
    return np.stack(parts)


def lane_index(rows):
    return lax.broadcasted_iota(jnp.int32, (rows, LANES), 1)


def pack_lanes(field, top, size, tile, first):
    half = size // 2
    lane = lane_index(half)
    packed = None
    for g in range(GROUPS):
        start = top + g % 2 * half
        part = field[g // 2, start : start + half, tile]
        if g:
            part = pltpu.roll(part, HALO * g, 1)
        low = (first + HALO * g) % LANES
        mine = (lane >= low) & (lane < low + HALO)
        packed = part if packed is None else jnp.where(mine, part, packed)
    return packed


def unpack_lanes(packed, group):
    return pltpu.roll(packed, LANES - HALO * group, 1) if group else packed


def split(x):
    high = x.astype(jnp.bfloat16)
    return high, (x - high.astype(jnp.float32)).astype(jnp.bfloat16)


def product(left, right):
    return jnp.dot(left, right, preferred_element_type=jnp.float32)


def times_table(x, table, which):
    high, low = split(x)
    t_high, t_low = table[2 * which], table[2 * which + 1]
    return product(beside(high, high, low), below(t_high, t_low, t_high))


def table_times(table, which, x):
    high, low = split(x)
    t_high, t_low = table[2 * which], table[2 * which + 1]
    return product(beside(t_high, t_low, t_high), below(high, high, low))


def beside(*blocks):
    return jnp.concatenate(blocks, axis=1)


def below(*blocks):
    return jnp.concatenate(blocks, axis=0)


def ends(x):
    return x[:, :HALF], x[:, HALF:]


def forward_columns(exit_re, exit_im, table):
    re_lo, re_hi = ends(exit_re)
    im_lo, im_hi = ends(exit_im)
    even = times_table(beside(re_lo + re_hi, im_lo + im_hi), table, 0)
    odd = times_table(beside(re_lo - re_hi, im_lo - im_hi), table, 1)
    return even, odd


def forward_rows(even, odd, table):
    out = []
    for parity in (0, 1):
        if parity == 0:
            se, so = even[:HALF] + even[HALF:], odd[:HALF] + odd[HALF:]
        else:
            se, so = even[:HALF] - even[HALF:], odd[:HALF] - odd[HALF:]
        e_re, e_im = ends(se)
        o_re, o_im = ends(so)
        out.append(table_times(table, 2 + parity, below(beside(e_re, o_re), beside(e_im, o_im))))
    return out


def residual(far, frame):
    out = []
    for parity in (0, 1):
        re, im = far[parity][:HALF], far[parity][HALF:]
        level = jnp.maximum(re * re + im * im, floor_amp * floor_amp)
        inten = frame[parity * HALF : (parity + 1) * HALF]
        factor = 1.0 - inten * lax.rsqrt(inten * level)
        out.append(below(re * factor, im * factor))
    return out


def back_rows(res, table):
    first = table_times(table, 0, res[0])
    second = table_times(table, 1, res[1])
    upper, lower = first + second, first - second
    out = []
    for cols in (slice(0, HALF), slice(HALF, P_SIZE)):
        out.append(
            below(
                beside(upper[:HALF, cols], upper[HALF:, cols]),
                beside(lower[:HALF, cols], lower[HALF:, cols]),
            )
        )
    return out


def back_columns(parts, table):
    even = times_table(parts[0], table, 2)
    odd = times_table(parts[1], table, 3)
    lo, hi = even + odd, even - odd
    return beside(lo[:, :HALF], hi[:, :HALF]), beside(lo[:, HALF:], hi[:, HALF:])


def is_odd(axis):
    return lax.rem(lax.axis_index(axis), 2) == 1


def fetch(pairs, sems):
    copies = [pltpu.make_async_copy(far, near, sems.at[i]) for i, (far, near) in enumerate(pairs)]
    for copy in copies:
        copy.start()
    return copies


def finish_all(copies):
    for copy in copies:
        copy.wait()


def row_edges(
    counts, obj_re, obj_im, offsets, chosen,
    small_outer, small_inner, to_outer, to_inner, marked, places, frame_of, sems,
):
    tile_r = obj_re.shape[0]
    odd = is_odd("row")
    low = pl.multiple_of(jnp.where(odd, 0, tile_r - HALO), 16)
    high = pl.multiple_of(jnp.where(odd, tile_r - HALO, 0), 16)
    pairs = [(offsets, places), (chosen, frame_of)]
    tiles = obj_re.shape[1] // LANES
    for k, ref in enumerate((obj_re, obj_im)):
        for t in range(tiles):
            lanes = slice(t * LANES, (t + 1) * LANES)
            rows = slice((2 * t + k) * HALO, (2 * t + k + 1) * HALO)
            pairs.append((ref.at[pl.ds(high, HALO), lanes], to_outer.at[rows]))
            pairs.append((ref.at[pl.ds(low, HALO), lanes], to_inner.at[rows]))
    copies = fetch(pairs, sems)
    finish_all(copies[:2])
    place = places[0, 0]
    live = lax.broadcasted_iota(jnp.int32, place.shape, 1) < counts[0, 0]
    place = jnp.where(live, place, 2 * tile_r)
    marked[0:2, :] = place
    marked[2:3, :] = frame_of[0]
    finish_all(copies[2:])
    for small, message in ((small_inner, to_inner), (small_outer, to_outer)):
        first = [message[k * HALO : (k + 1) * HALO, :] for k in (0, 1)]
        last = [message[(2 * tiles - 2 + k) * HALO : (2 * tiles - 1 + k) * HALO, :] for k in (0, 1)]
        small[0:HALO, :] = pack_four(first, last)
        small[HALO : HALO + 2, 0 : place.shape[1]] = place.astype(jnp.float32)


def load_object(obj_re, obj_im, cells, sems):
    tile_r, tile_c = obj_re.shape
    inner = slice(HALO, HALO + tile_r)
    middle = slice(LANES, LANES + tile_c)
    finish_all(fetch([(ref, cells.at[k, inner, middle]) for k, ref in enumerate((obj_re, obj_im))], sems))


def window_place(slots, slot):
    row = pl.multiple_of(slots[0, slot] + HALO, 16)
    col = slots[1, slot] + LANES
    turn = lax.rem(col, LANES)
    return row, pl.multiple_of(col - turn, LANES), turn


def add_window(acc, layer, where, keep, term, tiles=(0, 1, 2)):
    row, base, _ = where
    lo, hi = ends(term)
    parts = (jnp.where(keep, lo, 0.0), hi, jnp.where(keep, 0.0, lo))
    for t in tiles:
        acc[layer, pl.ds(row, term.shape[0]), pl.ds(base + t * LANES, LANES)] += parts[t]


def send_columns(to_left, to_right, to_inner, to_outer):
    odd = is_odd("col")
    to_inner[0 : to_left.shape[0], :] = jnp.where(odd, to_left, to_right)
    to_outer[0 : to_left.shape[0], :] = jnp.where(odd, to_right, to_left)


def received(by_inner, by_outer, axis):
    odd = is_odd(axis)
    index = lax.axis_index(axis)
    inside = (index > 0) & (index < lax.axis_size(axis) - 1)
    by_outer = jnp.where(inside, by_outer[...], 0.0)
    by_inner = by_inner[...]
    return jnp.where(odd, by_inner, by_outer), jnp.where(odd, by_outer, by_inner)


def pieces(packed, size):
    half = size // 2
    for g in range(GROUPS):
        yield g // 2, g % 2 * half, unpack_lanes(packed[:half], g)


def pack_four(low, high):
    lane = lane_index(HALO)
    first = jnp.where(lane < HALO, low[0], pltpu.roll(low[1], HALO, 1))
    second = jnp.where(lane < 3 * HALO, pltpu.roll(high[1], 3 * HALO, 1), high[0])
    return jnp.where(lane < 2 * HALO, first, second)


def unpack_four(packed):
    lane = lane_index(HALO)
    for k, low, high in ((0, 0, 0), (1, 3 * HALO, HALO)):
        yield (
            k,
            jnp.where(lane < HALO, pltpu.roll(packed, low, 1) if low else packed, 0.0),
            jnp.where(lane >= 3 * HALO, pltpu.roll(packed, high, 1) if high else packed, 0.0),
        )


def row_corners(cells_in, own, by_outer, by_inner, cells, marks, to_inner, to_outer):
    rows, width = cells.shape[1:]
    first, last = slice(LANES, 2 * LANES), slice(width - 2 * LANES, width - LANES)
    before, after = received(by_inner, by_outer, "row")
    for here, came in ((slice(0, HALO), before), (slice(rows - HALO, rows), after)):
        for k, low, high in unpack_four(came[0:HALO]):
            cells[k, here, first] = low
            cells[k, here, last] = high
    for i, message in enumerate((own[...], before, after)):
        marks[2 * i : 2 * i + 2, :] = message[HALO : HALO + 2]
    half = rows // 2
    to_left = pack_lanes(cells, 0, rows, first, 0)
    to_right = pack_lanes(cells, 0, rows, last, LANES - HALO)
    send_columns(to_left, to_right, to_inner, to_outer)
    to_inner[half:, :] = marks[...]
    to_outer[half:, :] = marks[...]


def live_slots(slots, cells):
    tile_r = cells.shape[1] - 2 * HALO
    count = jnp.int32(0)
    for slot in range(slots.shape[1]):
        count += (slots[0, slot] < tile_r).astype(jnp.int32)
    return count


FIRST, BEFORE, OVER, AFTER, LAST = range(5)


def run_windows(phase, slots, cells, acc, probe_re, probe_im, table, frames, order, largest=PAIR):
    tile_r, tile_c = cells.shape[1] - 2 * HALO, cells.shape[2] - 2 * LANES
    count = live_slots(slots, cells)
    kinds = []
    n_inside, n_row = jnp.int32(0), jnp.int32(0)
    for slot in range(slots.shape[1]):
        row, col = slots[0, slot], slots[1, slot]
        live = slot < count
        over_col = (col < 0) | (col > tile_c - P_SIZE)
        over_row = (row < 0) | (row > tile_r - P_SIZE)
        inside, by_row = live & ~over_col & ~over_row, live & ~over_col & over_row
        by_col, by_both = live & over_col & ~over_row, live & over_col & over_row
        kinds.append((inside, by_row, by_col, by_both, n_inside, n_row))
        n_inside += inside.astype(jnp.int32)
        n_row += by_row.astype(jnp.int32)
    first = jnp.clip(n_inside - 2 * PAIR, 0, PAIR)
    found = jnp.int32(0)
    for slot, (inside, by_row, by_col, by_both, rank, row_rank) in enumerate(kinds):
        mine = {
            FIRST: lambda: inside & (rank < first),
            BEFORE: lambda: by_row & (row_rank < PAIR),
            OVER: lambda: by_both | (by_row & (row_rank >= PAIR)),
            AFTER: lambda: by_col,
            LAST: lambda: inside & (rank >= first),
        }[phase]()

        @pl.when(mine)
        def _():
            order[found] = slot

        found += mine.astype(jnp.int32)

    lane = lane_index(P_SIZE)

    def load(slot):
        where = row, base, turn = window_place(slots, slot)
        keep = lane >= turn
        w_re = pltpu.roll(probe_re[...], turn, 1)
        w_im = pltpu.roll(probe_im[...], turn, 1)
        patch = []
        for k in (0, 1):
            block = cells[k, pl.ds(row, P_SIZE), pl.ds(base, 3 * LANES)]
            patch.append(
                beside(jnp.where(keep, block[:, :LANES], block[:, 2 * LANES :]), block[:, LANES : 2 * LANES])
            )
        exit_re = w_re * patch[0] - w_im * patch[1]
        exit_im = w_re * patch[1] + w_im * patch[0]
        return (where, keep, w_re, w_im), exit_re, exit_im

    def frame_of(slot):
        half = product(table[8], frames[slots[2, slot]]).astype(jnp.bfloat16)
        return product(half, table[9])

    def place(at, back_re, back_im):
        where, keep, w_re, w_im = at
        add_window(acc, 0, where, keep, w_re * back_re + w_im * back_im)
        add_window(acc, 1, where, keep, w_re * back_im - w_im * back_re)

    def step(group):
        frame = [frame_of(slot) for slot in group]
        loaded = [load(slot) for slot in group]
        state = [forward_columns(x[1], x[2], table) for x in loaded]
        state = [forward_rows(*x, table) for x in state]
        state = [residual(x, f) for x, f in zip(state, frame)]
        state = [back_rows(x, table) for x in state]
        state = [back_columns(x, table) for x in state]
        for x, back in zip(loaded, state):
            place(x[0], *back)

    def group_step(group, carry):
        step([order[group * largest + i] for i in range(largest)])
        return carry

    lax.fori_loop(0, found // largest, group_step, 0)
    for left in range(1, largest):

        @pl.when(found % largest == left)
        def _():
            step([order[found - left + i] for i in range(left)])


def windows_first(
    slots, cells, probe_re_far, probe_im_far, table_far, frames_far,
    acc, probe_re, probe_im, table, frames, order, sems,
):
    pairs = ((table_far, table), (frames_far, frames), (probe_re_far, probe_re), (probe_im_far, probe_im))
    copies = fetch(pairs, sems)
    acc[...] = jnp.zeros_like(acc)
    finish_all(copies)
    run_windows(FIRST, slots, cells, acc, probe_re, probe_im, table, frames, order)


def windows_before(
    slots, cells_in, acc_in, probe_re, probe_im, table, frames, by_outer, by_inner,
    cells, acc, order, power,
):
    rows, width = cells.shape[1:]
    before, after = received(by_inner, by_outer, "row")
    for k in (0, 1):
        for t in range(width // LANES - 2):
            lanes = slice((t + 1) * LANES, (t + 2) * LANES)
            part = slice((2 * t + k) * HALO, (2 * t + k + 1) * HALO)
            cells[k, 0:HALO, lanes] = before[part]
            cells[k, rows - HALO : rows, lanes] = after[part]
    power[...] = probe_re[...] * probe_re[...] + probe_im[...] * probe_im[...]
    lane = lane_index(P_SIZE)

    def step(slot, carry):
        where = window_place(slots, slot)
        add_window(acc, 2, where, lane >= where[2], pltpu.roll(power[...], where[2], 1))
        return carry

    lax.fori_loop(0, live_slots(slots, cells), step, 0)
    run_windows(BEFORE, slots, cells, acc, probe_re, probe_im, table, frames, order)


def reaching(place, right, tile_r, tile_c):
    shape = place.shape
    index = lax.broadcasted_iota(jnp.int32, shape, 0)
    lane = lax.broadcasted_iota(jnp.int32, shape, 1)
    col = pltpu.roll(place, shape[0] - 1, 0)
    low = jnp.where(index == 2, tile_r - P_SIZE, -tile_r).astype(jnp.float32)
    high = jnp.where(index == 4, 0, tile_r).astype(jnp.float32)
    reaches = (lane < MARKS) & (index % 2 == 0) & (index < 6) & (place > low) & (place < high)
    if right < 0:
        reaches &= col > tile_c - P_SIZE
    if right > 0:
        reaches &= col < 0
    bit = lax.shift_left(jnp.ones(shape, jnp.int32), jnp.minimum(lane, MARKS)).astype(jnp.float32)
    bits = jnp.sum(jnp.where(reaches, bit, 0.0), axis=1, keepdims=True)
    return jnp.where(lane < MARKS, place, bits).astype(jnp.int32)


def add_neighbours_light(places, acc, power):
    rows, width = acc.shape[1:]
    tile_r, tile_c = rows - 2 * HALO, width - 2 * LANES
    for right in (-1, 0, 1):
        for i, down in enumerate((0, -1, 1)):
            if not right and not down:
                continue
            first, last = {-1: (P_SIZE - HALO, P_SIZE), 0: (0, P_SIZE), 1: (0, HALO)}[down]
            tiles = {-1: (2,), 0: (0, 1, 2), 1: (0,)}[right]
            lane = lane_index(last - first)
            bits = places[right + 1, 2 * i, MARKS]

            def step(slot, carry):
                row, col = places[right + 1, 2 * i, slot], places[right + 1, 2 * i + 1, slot]

                @pl.when(lax.shift_right_logical(bits, slot) % 2 == 1)
                def _():
                    turn = lax.rem(col + LANES, LANES)
                    at = pl.multiple_of(row + HALO + (down * tile_r + first), 16)
                    base = pl.multiple_of(col + LANES - turn + right * tile_c, LANES)
                    part = pltpu.roll(power[first:last, :], turn, 1)
                    add_window(acc, 2, (at, base, turn), lane >= turn, part, tiles)

                return carry

            @pl.when(bits != 0)
            def _():
                lax.fori_loop(0, MARKS, step, 0)


def windows_over_columns(slots, cells, acc_in, probe_re, probe_im, table, frames, acc, order):
    run_windows(AFTER, slots, cells, acc, probe_re, probe_im, table, frames, order)


def windows_over_edge(
    marked, cells_in, acc_in, probe_re, probe_im, table, frames, by_inner, by_outer,
    cells, acc, small_outer, small_inner, to_outer, to_inner, order, slots, sem,
):
    scalars = pltpu.make_async_copy(marked, slots, sem)
    scalars.start()
    rows, width = acc.shape[1:]
    before, after = received(by_inner, by_outer, "col")
    for tile, packed in ((slice(0, LANES), before), (slice(width - LANES, width), after)):
        for layer, row, part in pieces(packed, rows):
            cells[layer, row : row + part.shape[0], tile] = part
    scalars.wait()
    run_windows(OVER, slots, cells, acc, probe_re, probe_im, table, frames, order)
    odd = is_odd("row")
    corners, strips = [], []
    for here in (slice(0, HALO), slice(rows - HALO, rows)):
        right = [acc[k, here, width - LANES : width] for k in (0, 1)]
        corners.append(pack_four(right, [acc[k, here, 0:LANES] for k in (0, 1)]))
        strips.append(below(*(acc[k, here, LANES : width - LANES] for k in (0, 1))))
    for inner, outer, (up, down) in ((small_inner, small_outer, corners), (to_inner, to_outer, strips)):
        inner[...] = jnp.where(odd, up, down)
        outer[...] = jnp.where(odd, down, up)


def column_spill(acc_in, by_outer, by_inner, acc, to_inner, to_outer):
    rows, width = acc.shape[1:]
    before, after = received(by_inner, by_outer, "row")
    for start, came in ((HALO, before), (rows - 2 * HALO, after)):
        here = slice(start, start + HALO)
        for k, low, high in unpack_four(came):
            acc[k, here, 0:LANES] += high
            acc[k, here, width - LANES :] += low
    tile_r = rows - 2 * HALO
    to_left = pack_lanes(acc, HALO, tile_r, slice(0, LANES), LANES - HALO)
    to_right = pack_lanes(acc, HALO, tile_r, slice(width - LANES, width), 0)
    send_columns(to_left, to_right, to_inner, to_outer)


def new_columns(cells, acc, spill, start, size, near_re, near_im):
    rows = acc.shape[1]
    here, there = slice(HALO, rows - HALO), slice(LANES + start, LANES + start + size)
    part = [acc[k, here, there] for k in range(acc.shape[0])]
    if spill is not None:
        part[:2] = [part[k] + spill[k] for k in (0, 1)]
    scale = 1.0 / (part[2] + ridge)
    near_re[:, start : start + size] = cells[0, here, there] - part[0] * scale
    near_im[:, start : start + size] = cells[1, here, there] - part[1] * scale


def finish_inner(
    slots, cells, acc_in, probe_re, probe_im, table, frames, marks, col_inner, col_outer, by_outer, by_inner,
    acc, new_re, new_im, order, power, whole, places, near_re, near_im, sems,
):
    rows, width = acc.shape[1:]
    before, after = received(col_inner, col_outer, "col")
    for i, part in enumerate((before[-MARKS:], marks[...], after[-MARKS:])):
        whole[i] = reaching(part, i - 1, rows - 2 * HALO, width - 2 * LANES)
    copy = pltpu.make_async_copy(whole, places, sems.at[0])
    copy.start()
    power[...] = probe_re[...] * probe_re[...] + probe_im[...] * probe_im[...]
    run_windows(LAST, slots, cells, acc, probe_re, probe_im, table, frames, order, 2 * PAIR)
    copy.wait()
    add_neighbours_light(places, acc, power)
    before, after = received(by_inner, by_outer, "row")
    for start, came in ((HALO, before), (rows - 2 * HALO, after)):
        for k in (0, 1):
            acc[k, start : start + HALO, LANES : width - LANES] += came[k * HALO : (k + 1) * HALO]
    size = near_re.shape[1] - 2 * LANES
    new_columns(cells, acc, None, LANES, size, near_re, near_im)
    there = slice(LANES, LANES + size)
    pairs = [(near_re.at[:, there], new_re.at[:, there]), (near_im.at[:, there], new_im.at[:, there])]
    finish_all(fetch(pairs, sems.at[1:3]))


def finish_edges(cells, acc, by_inner, by_outer, re_in, im_in, new_re, new_im, near_re, near_im, sems):
    tile_r, tile_c = near_re.shape
    lane = lane_index(tile_r)
    sides = ((0, lane < HALO), (tile_c - LANES, lane >= LANES - HALO))
    copies = []
    for i, ((start, mine), packed) in enumerate(zip(sides, received(by_inner, by_outer, "col"))):
        parts = [part for _, _, part in pieces(packed, tile_r)]
        spill = [jnp.where(mine, below(*parts[2 * k : 2 * k + 2]), 0.0) for k in (0, 1)]
        new_columns(cells, acc, spill, start, LANES, near_re, near_im)
        there = slice(start, start + LANES)
        pairs = ((near_re.at[:, there], new_re.at[:, there]), (near_im.at[:, there], new_im.at[:, there]))
        copies += fetch(pairs, sems.at[2 * i : 2 * i + 2])
    finish_all(copies)


def swap(to_inner, to_outer, axis):
    devices = lax.axis_size(axis)
    inner = [(i, i + 1) for i in range(0, devices, 2)]
    partner = {i: i + 1 if i % 2 else i - 1 for i in range(1, devices - 1)}
    n_row, n_col = lax.axis_size("row"), lax.axis_size("col")
    pairs = []
    for row in range(n_row):
        for col in range(n_col):
            if axis == "row":
                there = (partner[row], col) if row in partner else (row, col ^ 1)
            else:
                there = (row, partner[col]) if col in partner else (row ^ 1, col)
            pairs.append((row * n_col + col, there[0] * n_col + there[1]))
    by_inner = lax.ppermute(to_inner, axis, inner + [(j, i) for i, j in inner])
    by_outer = lax.ppermute(to_outer, ("row", "col"), pairs)
    return by_inner, by_outer


def far(x):
    return pltpu.with_memory_space_constraint(x, pltpu.HBM)


def f32(*shape):
    return jax.ShapeDtypeStruct(shape, jnp.float32)


def shards(object_re, object_im, probe_re, probe_im, frames, counts, offsets, frame_index):
    tile_r, tile_c = object_re.shape
    rows, width = tile_r + 2 * HALO, tile_c + 2 * LANES
    layers = 3
    slots = offsets.shape[2]
    table = jnp.asarray(transform_tables())
    frames = frames.reshape(frames.shape[2:])
    cells_shape, acc_shape = f32(2, rows, width), f32(layers, rows, width)
    dma = pltpu.SemaphoreType.DMA

    places = jnp.swapaxes(offsets, 2, 3)
    small = f32(HALO + MARKS, LANES)
    edge = f32(2 * HALO * (tile_c // LANES), LANES)
    small_outer, small_inner, to_outer, to_inner, marked = pl.pallas_call(
        row_edges,
        out_shape=(small, small, edge, edge, jax.ShapeDtypeStruct((3, slots), jnp.int32)),
        in_specs=[SMEM] + [HBM] * 4,
        out_specs=(VMEM,) * 5,
        scratch_shapes=[
            pltpu.VMEM(places.shape, jnp.int32), pltpu.VMEM(frame_index.shape, jnp.int32),
            dma((2 + 4 * (tile_c // LANES),)),
        ],
        compiler_params=SMALL,
        name="row_edges",
    )(counts, far(object_re), far(object_im), far(places), far(frame_index))
    by_inner, by_outer = swap(small_inner, small_outer, "row")
    row_inner, row_outer = swap(to_inner, to_outer, "row")

    cells = pl.pallas_call(
        load_object,
        out_shape=cells_shape,
        in_specs=[HBM] * 2,
        out_specs=VMEM,
        scratch_shapes=[dma((2,))],
        compiler_params=SMALL,
        name="load_object",
    )(far(object_re), far(object_im))

    packed = f32(rows // 2 + MARKS, LANES)
    cells, marks, to_inner, to_outer = pl.pallas_call(
        row_corners,
        out_shape=(cells_shape, f32(MARKS, LANES), packed, packed),
        in_specs=[VMEM] * 4,
        out_specs=(VMEM,) * 4,
        input_output_aliases={0: 0},
        compiler_params=SMALL,
        name="row_corners",
    )(cells, small_outer, by_outer, by_inner)
    edges = swap(to_inner, to_outer, "col")

    order = pltpu.SMEM((slots,), jnp.int32)
    acc, *fixed = pl.pallas_call(
        windows_first,
        out_shape=(
            acc_shape, f32(*probe_re.shape), f32(*probe_im.shape),
            jax.ShapeDtypeStruct(table.shape, table.dtype), jax.ShapeDtypeStruct(frames.shape, frames.dtype),
        ),
        in_specs=[SMEM, VMEM] + [HBM] * 4,
        out_specs=(VMEM,) * 5,
        scratch_shapes=[order, dma((4,))],
        compiler_params=PARAMS,
        cost_estimate=BUSY,
        name="windows_first",
    )(marked, cells, *map(far, (probe_re, probe_im, table, frames)))

    cells, acc = pl.pallas_call(
        windows_before,
        out_shape=(cells_shape, acc_shape),
        in_specs=[SMEM] + [VMEM] * 8,
        out_specs=(VMEM, VMEM),
        scratch_shapes=[order, pltpu.VMEM(probe_re.shape, jnp.float32)],
        input_output_aliases={1: 0, 2: 1},
        compiler_params=PARAMS,
        cost_estimate=BUSY,
        name="windows_before",
    )(marked, cells, acc, *fixed, row_outer, row_inner)

    small, edge = f32(HALO, LANES), f32(2 * HALO, tile_c)
    cells, acc, small_outer, small_inner, to_outer, to_inner = pl.pallas_call(
        windows_over_edge,
        out_shape=(cells_shape, acc_shape, small, small, edge, edge),
        in_specs=[VMEM] * 9,
        out_specs=(VMEM,) * 6,
        scratch_shapes=[order, pltpu.SMEM((3, slots), jnp.int32), dma(())],
        input_output_aliases={1: 0, 2: 1},
        compiler_params=PARAMS,
        cost_estimate=BUSY,
        name="windows_over_edge",
    )(marked, cells, acc, *fixed, *edges)
    by_inner, by_outer = swap(small_inner, small_outer, "row")
    row_inner, row_outer = swap(to_inner, to_outer, "row")

    acc = pl.pallas_call(
        windows_over_columns,
        out_shape=acc_shape,
        in_specs=[SMEM] + [VMEM] * 6,
        out_specs=VMEM,
        scratch_shapes=[order],
        input_output_aliases={2: 0},
        compiler_params=PARAMS,
        cost_estimate=BUSY,
        name="windows_over_columns",
    )(marked, cells, acc, *fixed)

    packed = f32(tile_r // 2, LANES)
    acc, to_inner, to_outer = pl.pallas_call(
        column_spill,
        out_shape=(acc_shape, packed, packed),
        in_specs=[VMEM] * 3,
        out_specs=(VMEM,) * 3,
        input_output_aliases={0: 0},
        compiler_params=SMALL,
        name="column_spill",
    )(acc, by_outer, by_inner)
    by_inner, by_outer = swap(to_inner, to_outer, "col")

    near = [pltpu.VMEM((tile_r, tile_c), jnp.float32)] * 2
    new = (f32(tile_r, tile_c), f32(tile_r, tile_c))
    acc, new_re, new_im = pl.pallas_call(
        finish_inner,
        out_shape=(acc_shape, *new),
        in_specs=[SMEM] + [VMEM] * 11,
        out_specs=(VMEM, HBM, HBM),
        scratch_shapes=[
            order, pltpu.VMEM(probe_re.shape, jnp.float32),
            pltpu.VMEM((3, MARKS, LANES), jnp.int32), pltpu.SMEM((3, MARKS, LANES), jnp.int32),
            *near, dma((3,)),
        ],
        input_output_aliases={2: 0},
        compiler_params=PARAMS,
        cost_estimate=BUSY,
        name="finish_inner",
    )(marked, cells, acc, *fixed, marks, *edges, row_outer, row_inner)
    return pl.pallas_call(
        finish_edges,
        out_shape=new,
        in_specs=[VMEM] * 4 + [HBM] * 2,
        out_specs=(HBM, HBM),
        scratch_shapes=near + [dma((4,))],
        input_output_aliases={4: 0, 5: 1},
        compiler_params=SMALL,
        name="finish_edges",
    )(cells, acc, by_inner, by_outer, far(new_re), far(new_im))


def solution(mesh):
    return jax.shard_map(
        shards,
        mesh=mesh,
        in_specs=(
            P("row", "col"),
            P("row", "col"),
            P(),
            P(),
            P("row", "col", None, None, None),
            P("row", "col"),
            P("row", "col", None, None),
            P("row", "col", None),
        ),
        out_specs=(P("row", "col"), P("row", "col")),
        check_vma=False,
    )
```

```python
import functools
import math

import jax
import jax.numpy as jnp
import ml_dtypes
import numpy as np
from jax import lax
from jax.experimental import pallas as pl
from jax.experimental.pallas import tpu as pltpu
from jax.sharding import PartitionSpec as P

P_SIZE = 256
HALF = P_SIZE // 2
HALO = 32
LANES = 128
GROUPS = LANES // HALO
MARKS = 8
PAIR = 2

floor_amp = 0.5
ridge = 1.0

VMEM = pl.BlockSpec(memory_space=pltpu.VMEM)
SMEM = pl.BlockSpec(memory_space=pltpu.SMEM)
HBM = pl.BlockSpec(memory_space=pltpu.HBM)
PARAMS = pltpu.CompilerParams(vmem_limit_bytes=32 * 1024 * 1024)
SMALL = pltpu.CompilerParams(vmem_limit_bytes=16 * 1024 * 1024)
BUSY = pl.CostEstimate(flops=4_000_000_000, bytes_accessed=8_000_000, transcendentals=0)


def transform_tables():
    index = np.arange(HALF)
    plain = []
    for parity in (0, 1):
        angle = 2.0 * math.pi / P_SIZE * (index[:, None] * (2 * index[None, :] + parity) % P_SIZE)
        cos, sin = np.cos(angle), np.sin(angle)
        plain.append(np.block([[cos, -sin], [sin, cos]]) / math.sqrt(P_SIZE))
    parts = []
    for table in plain + [t.T for t in plain]:
        high = table.astype(np.float32).astype(ml_dtypes.bfloat16)
        low = (table - high.astype(np.float64)).astype(np.float32).astype(ml_dtypes.bfloat16)
        parts += [high, low]
    order = np.concatenate([np.arange(0, P_SIZE, 2), np.arange(1, P_SIZE, 2)])
    sort = np.zeros((P_SIZE, P_SIZE), np.float32)
    sort[np.arange(P_SIZE), order] = 1.0
    parts += [sort.astype(ml_dtypes.bfloat16), sort.T.astype(ml_dtypes.bfloat16)]
    return np.stack(parts)


def lane_index(rows):
    return lax.broadcasted_iota(jnp.int32, (rows, LANES), 1)


def pack_lanes(field, top, size, tile, first):
    half = size // 2
    lane = lane_index(half)
    packed = None
    for g in range(GROUPS):
        start = top + g % 2 * half
        part = field[g // 2, start : start + half, tile]
        if g:
            part = pltpu.roll(part, HALO * g, 1)
        low = (first + HALO * g) % LANES
        mine = (lane >= low) & (lane < low + HALO)
        packed = part if packed is None else jnp.where(mine, part, packed)
    return packed


def unpack_lanes(packed, group):
    return pltpu.roll(packed, LANES - HALO * group, 1) if group else packed


def split(x):
    high = x.astype(jnp.bfloat16)
    return high, (x - high.astype(jnp.float32)).astype(jnp.bfloat16)


def product(left, right):
    return jnp.dot(left, right, preferred_element_type=jnp.float32)


def times_table(x, table, which):
    high, low = split(x)
    t_high, t_low = table[2 * which], table[2 * which + 1]
    return product(beside(high, high, low), below(t_high, t_low, t_high))


def table_times(table, which, x):
    high, low = split(x)
    t_high, t_low = table[2 * which], table[2 * which + 1]
    return product(beside(t_high, t_low, t_high), below(high, high, low))


def beside(*blocks):
    return jnp.concatenate(blocks, axis=1)


def below(*blocks):
    return jnp.concatenate(blocks, axis=0)


def ends(x):
    return x[:, :HALF], x[:, HALF:]


def forward_columns(exit_re, exit_im, table):
    re_lo, re_hi = ends(exit_re)
    im_lo, im_hi = ends(exit_im)
    even = times_table(beside(re_lo + re_hi, im_lo + im_hi), table, 0)
    odd = times_table(beside(re_lo - re_hi, im_lo - im_hi), table, 1)
    return even, odd


def forward_rows(even, odd, table):
    out = []
    for parity in (0, 1):
        if parity == 0:
            se, so = even[:HALF] + even[HALF:], odd[:HALF] + odd[HALF:]
        else:
            se, so = even[:HALF] - even[HALF:], odd[:HALF] - odd[HALF:]
        e_re, e_im = ends(se)
        o_re, o_im = ends(so)
        out.append(table_times(table, 2 + parity, below(beside(e_re, o_re), beside(e_im, o_im))))
    return out


def residual(far, frame):
    out = []
    for parity in (0, 1):
        re, im = far[parity][:HALF], far[parity][HALF:]
        level = jnp.maximum(re * re + im * im, floor_amp * floor_amp)
        inten = frame[parity * HALF : (parity + 1) * HALF]
        factor = 1.0 - inten * lax.rsqrt(inten * level)
        out.append(below(re * factor, im * factor))
    return out


def back_rows(res, table):
    first = table_times(table, 0, res[0])
    second = table_times(table, 1, res[1])
    upper, lower = first + second, first - second
    out = []
    for cols in (slice(0, HALF), slice(HALF, P_SIZE)):
        out.append(
            below(
                beside(upper[:HALF, cols], upper[HALF:, cols]),
                beside(lower[:HALF, cols], lower[HALF:, cols]),
            )
        )
    return out


def back_columns(parts, table):
    even = times_table(parts[0], table, 2)
    odd = times_table(parts[1], table, 3)
    lo, hi = even + odd, even - odd
    return beside(lo[:, :HALF], hi[:, :HALF]), beside(lo[:, HALF:], hi[:, HALF:])


def is_odd(axis):
    return lax.rem(lax.axis_index(axis), 2) == 1


def fetch(pairs, sems):
    copies = [pltpu.make_async_copy(far, near, sems.at[i]) for i, (far, near) in enumerate(pairs)]
    for copy in copies:
        copy.start()
    return copies


def finish_all(copies):
    for copy in copies:
        copy.wait()


def row_edges(
    counts, obj_re, obj_im, offsets, chosen,
    small_outer, small_inner, to_outer, to_inner, marked, places, frame_of, sems,
):
    tile_r = obj_re.shape[0]
    odd = is_odd("row")
    low = pl.multiple_of(jnp.where(odd, 0, tile_r - HALO), 16)
    high = pl.multiple_of(jnp.where(odd, tile_r - HALO, 0), 16)
    pairs = [(offsets, places), (chosen, frame_of)]
    tiles = obj_re.shape[1] // LANES
    for k, ref in enumerate((obj_re, obj_im)):
        for t in range(tiles):
            lanes = slice(t * LANES, (t + 1) * LANES)
            rows = slice((2 * t + k) * HALO, (2 * t + k + 1) * HALO)
            pairs.append((ref.at[pl.ds(high, HALO), lanes], to_outer.at[rows]))
            pairs.append((ref.at[pl.ds(low, HALO), lanes], to_inner.at[rows]))
    copies = fetch(pairs, sems)
    finish_all(copies[:2])
    place = places[0, 0]
    live = lax.broadcasted_iota(jnp.int32, place.shape, 1) < counts[0, 0]
    place = jnp.where(live, place, 2 * tile_r)
    marked[0:2, :] = place
    marked[2:3, :] = frame_of[0]
    finish_all(copies[2:])
    for small, message in ((small_inner, to_inner), (small_outer, to_outer)):
        first = [message[k * HALO : (k + 1) * HALO, :] for k in (0, 1)]
        last = [message[(2 * tiles - 2 + k) * HALO : (2 * tiles - 1 + k) * HALO, :] for k in (0, 1)]
        small[0:HALO, :] = pack_four(first, last)
        small[HALO : HALO + 2, 0 : place.shape[1]] = place.astype(jnp.float32)


def load_object(obj_re, obj_im, cells, sems):
    tile_r, tile_c = obj_re.shape
    inner = slice(HALO, HALO + tile_r)
    middle = slice(LANES, LANES + tile_c)
    finish_all(fetch([(ref, cells.at[k, inner, middle]) for k, ref in enumerate((obj_re, obj_im))], sems))


def window_place(slots, slot):
    row = pl.multiple_of(slots[0, slot] + HALO, 16)
    col = slots[1, slot] + LANES
    turn = lax.rem(col, LANES)
    return row, pl.multiple_of(col - turn, LANES), turn


def add_window(acc, layer, where, keep, term, tiles=(0, 1, 2)):
    row, base, _ = where
    lo, hi = ends(term)
    parts = (jnp.where(keep, lo, 0.0), hi, jnp.where(keep, 0.0, lo))
    for t in tiles:
        acc[layer, pl.ds(row, term.shape[0]), pl.ds(base + t * LANES, LANES)] += parts[t]


def send_columns(to_left, to_right, to_inner, to_outer):
    odd = is_odd("col")
    to_inner[0 : to_left.shape[0], :] = jnp.where(odd, to_left, to_right)
    to_outer[0 : to_left.shape[0], :] = jnp.where(odd, to_right, to_left)


def received(by_inner, by_outer, axis):
    odd = is_odd(axis)
    index = lax.axis_index(axis)
    inside = (index > 0) & (index < lax.axis_size(axis) - 1)
    by_outer = jnp.where(inside, by_outer[...], 0.0)
    by_inner = by_inner[...]
    return jnp.where(odd, by_inner, by_outer), jnp.where(odd, by_outer, by_inner)


def pieces(packed, size):
    half = size // 2
    for g in range(GROUPS):
        yield g // 2, g % 2 * half, unpack_lanes(packed[:half], g)


def pack_four(low, high):
    lane = lane_index(HALO)
    first = jnp.where(lane < HALO, low[0], pltpu.roll(low[1], HALO, 1))
    second = jnp.where(lane < 3 * HALO, pltpu.roll(high[1], 3 * HALO, 1), high[0])
    return jnp.where(lane < 2 * HALO, first, second)


def unpack_four(packed):
    lane = lane_index(HALO)
    for k, low, high in ((0, 0, 0), (1, 3 * HALO, HALO)):
        yield (
            k,
            jnp.where(lane < HALO, pltpu.roll(packed, low, 1) if low else packed, 0.0),
            jnp.where(lane >= 3 * HALO, pltpu.roll(packed, high, 1) if high else packed, 0.0),
        )


def row_corners(cells_in, own, by_outer, by_inner, cells, marks, to_inner, to_outer):
    rows, width = cells.shape[1:]
    first, last = slice(LANES, 2 * LANES), slice(width - 2 * LANES, width - LANES)
    before, after = received(by_inner, by_outer, "row")
    for here, came in ((slice(0, HALO), before), (slice(rows - HALO, rows), after)):
        for k, low, high in unpack_four(came[0:HALO]):
            cells[k, here, first] = low
            cells[k, here, last] = high
    for i, message in enumerate((own[...], before, after)):
        marks[2 * i : 2 * i + 2, :] = message[HALO : HALO + 2]
    half = rows // 2
    to_left = pack_lanes(cells, 0, rows, first, 0)
    to_right = pack_lanes(cells, 0, rows, last, LANES - HALO)
    send_columns(to_left, to_right, to_inner, to_outer)
    to_inner[half:, :] = marks[...]
    to_outer[half:, :] = marks[...]


def live_slots(slots, cells):
    tile_r = cells.shape[1] - 2 * HALO
    count = jnp.int32(0)
    for slot in range(slots.shape[1]):
        count += (slots[0, slot] < tile_r).astype(jnp.int32)
    return count


FIRST, BEFORE, OVER, AFTER, LAST = range(5)


def run_windows(phase, slots, cells, acc, probe_re, probe_im, table, frames, order, largest=PAIR):
    tile_r, tile_c = cells.shape[1] - 2 * HALO, cells.shape[2] - 2 * LANES
    count = live_slots(slots, cells)
    kinds = []
    n_inside, n_row, n_col = jnp.int32(0), jnp.int32(0), jnp.int32(0)
    for slot in range(slots.shape[1]):
        row, col = slots[0, slot], slots[1, slot]
        live = slot < count
        over_col = (col < 0) | (col > tile_c - P_SIZE)
        over_row = (row < 0) | (row > tile_r - P_SIZE)
        inside, by_row = live & ~over_col & ~over_row, live & ~over_col & over_row
        by_col, by_both = live & over_col & ~over_row, live & over_col & over_row
        kinds.append((inside, by_row, by_col, by_both, n_inside, n_row))
        n_inside += inside.astype(jnp.int32)
        n_row += by_row.astype(jnp.int32)
        n_col += by_col.astype(jnp.int32)
    first = jnp.minimum(jnp.clip(n_inside + n_col - 2 * PAIR, 0, PAIR), n_inside)
    rest = n_inside - first
    after = n_inside - jnp.clip(n_col + rest - 2 * PAIR, 0, jnp.minimum(rest, PAIR))
    found = jnp.int32(0)
    for slot, (inside, by_row, by_col, by_both, rank, row_rank) in enumerate(kinds):
        mine = {
            FIRST: lambda: inside & (rank < first),
            BEFORE: lambda: by_row & (row_rank < PAIR),
            OVER: lambda: by_both | (by_row & (row_rank >= PAIR)),
            AFTER: lambda: by_col | (inside & (rank >= first) & (rank < after)),
            LAST: lambda: inside & (rank >= after),
        }[phase]()

        @pl.when(mine)
        def _():
            order[found] = slot

        found += mine.astype(jnp.int32)

    lane = lane_index(P_SIZE)

    def load(slot):
        where = row, base, turn = window_place(slots, slot)
        keep = lane >= turn
        w_re = pltpu.roll(probe_re[...], turn, 1)
        w_im = pltpu.roll(probe_im[...], turn, 1)
        patch = []
        for k in (0, 1):
            block = cells[k, pl.ds(row, P_SIZE), pl.ds(base, 3 * LANES)]
            patch.append(
                beside(jnp.where(keep, block[:, :LANES], block[:, 2 * LANES :]), block[:, LANES : 2 * LANES])
            )
        exit_re = w_re * patch[0] - w_im * patch[1]
        exit_im = w_re * patch[1] + w_im * patch[0]
        return (where, keep, w_re, w_im), exit_re, exit_im

    def frame_of(slot):
        half = product(table[8], frames[slots[2, slot]]).astype(jnp.bfloat16)
        return product(half, table[9])

    def place(at, back_re, back_im):
        where, keep, w_re, w_im = at
        add_window(acc, 0, where, keep, w_re * back_re + w_im * back_im)
        add_window(acc, 1, where, keep, w_re * back_im - w_im * back_re)

    def step(group):
        frame = [frame_of(slot) for slot in group]
        loaded = [load(slot) for slot in group]
        state = [forward_columns(x[1], x[2], table) for x in loaded]
        state = [forward_rows(*x, table) for x in state]
        state = [residual(x, f) for x, f in zip(state, frame)]
        state = [back_rows(x, table) for x in state]
        state = [back_columns(x, table) for x in state]
        for x, back in zip(loaded, state):
            place(x[0], *back)

    def group_step(group, carry):
        step([order[group * largest + i] for i in range(largest)])
        return carry

    lax.fori_loop(0, found // largest, group_step, 0)
    for left in range(1, largest):

        @pl.when(found % largest == left)
        def _():
            step([order[found - left + i] for i in range(left)])


def windows_first(
    slots, cells, probe_re_far, probe_im_far, table_far, frames_far,
    acc, probe_re, probe_im, table, frames, order, sems,
):
    pairs = ((table_far, table), (frames_far, frames), (probe_re_far, probe_re), (probe_im_far, probe_im))
    copies = fetch(pairs, sems)
    acc[...] = jnp.zeros_like(acc)
    finish_all(copies)
    run_windows(FIRST, slots, cells, acc, probe_re, probe_im, table, frames, order)


def windows_before(
    slots, cells_in, acc_in, probe_re, probe_im, table, frames, by_outer, by_inner,
    cells, acc, order, power,
):
    rows, width = cells.shape[1:]
    before, after = received(by_inner, by_outer, "row")
    for k in (0, 1):
        for t in range(width // LANES - 2):
            lanes = slice((t + 1) * LANES, (t + 2) * LANES)
            part = slice((2 * t + k) * HALO, (2 * t + k + 1) * HALO)
            cells[k, 0:HALO, lanes] = before[part]
            cells[k, rows - HALO : rows, lanes] = after[part]
    power[...] = probe_re[...] * probe_re[...] + probe_im[...] * probe_im[...]
    lane = lane_index(P_SIZE)

    def step(slot, carry):
        where = window_place(slots, slot)
        add_window(acc, 2, where, lane >= where[2], pltpu.roll(power[...], where[2], 1))
        return carry

    lax.fori_loop(0, live_slots(slots, cells), step, 0)
    run_windows(BEFORE, slots, cells, acc, probe_re, probe_im, table, frames, order)


def reaching(place, right, tile_r, tile_c):
    shape = place.shape
    index = lax.broadcasted_iota(jnp.int32, shape, 0)
    lane = lax.broadcasted_iota(jnp.int32, shape, 1)
    col = pltpu.roll(place, shape[0] - 1, 0)
    low = jnp.where(index == 2, tile_r - P_SIZE, -tile_r).astype(jnp.float32)
    high = jnp.where(index == 4, 0, tile_r).astype(jnp.float32)
    reaches = (lane < MARKS) & (index % 2 == 0) & (index < 6) & (place > low) & (place < high)
    if right < 0:
        reaches &= col > tile_c - P_SIZE
    if right > 0:
        reaches &= col < 0
    bit = lax.shift_left(jnp.ones(shape, jnp.int32), jnp.minimum(lane, MARKS)).astype(jnp.float32)
    bits = jnp.sum(jnp.where(reaches, bit, 0.0), axis=1, keepdims=True)
    return jnp.where(lane < MARKS, place, bits).astype(jnp.int32)


def add_neighbours_light(places, acc, power):
    rows, width = acc.shape[1:]
    tile_r, tile_c = rows - 2 * HALO, width - 2 * LANES
    for right in (-1, 0, 1):
        for i, down in enumerate((0, -1, 1)):
            if not right and not down:
                continue
            first, last = {-1: (P_SIZE - HALO, P_SIZE), 0: (0, P_SIZE), 1: (0, HALO)}[down]
            tiles = {-1: (2,), 0: (0, 1, 2), 1: (0,)}[right]
            lane = lane_index(last - first)
            bits = places[right + 1, 2 * i, MARKS]

            def step(slot, carry):
                row, col = places[right + 1, 2 * i, slot], places[right + 1, 2 * i + 1, slot]

                @pl.when(lax.shift_right_logical(bits, slot) % 2 == 1)
                def _():
                    turn = lax.rem(col + LANES, LANES)
                    at = pl.multiple_of(row + HALO + (down * tile_r + first), 16)
                    base = pl.multiple_of(col + LANES - turn + right * tile_c, LANES)
                    part = pltpu.roll(power[first:last, :], turn, 1)
                    add_window(acc, 2, (at, base, turn), lane >= turn, part, tiles)

                return carry

            @pl.when(bits != 0)
            def _():
                lax.fori_loop(0, MARKS, step, 0)


def windows_after(
    slots, cells, acc_in, probe_re, probe_im, table, frames, marks, by_inner, by_outer,
    acc, order, power, whole, places, sem,
):
    rows, width = acc.shape[1:]
    before, after = received(by_inner, by_outer, "col")
    for i, part in enumerate((before[-MARKS:], marks[...], after[-MARKS:])):
        whole[i] = reaching(part, i - 1, rows - 2 * HALO, width - 2 * LANES)
    copy = pltpu.make_async_copy(whole, places, sem)
    copy.start()
    power[...] = probe_re[...] * probe_re[...] + probe_im[...] * probe_im[...]
    run_windows(AFTER, slots, cells, acc, probe_re, probe_im, table, frames, order, 2 * PAIR)
    copy.wait()
    add_neighbours_light(places, acc, power)


def windows_over_edge(
    marked, cells_in, acc_in, probe_re, probe_im, table, frames, by_inner, by_outer,
    cells, acc, to_outer, to_inner, order, slots, sem,
):
    scalars = pltpu.make_async_copy(marked, slots, sem)
    scalars.start()
    rows, width = acc.shape[1:]
    before, after = received(by_inner, by_outer, "col")
    for tile, packed in ((slice(0, LANES), before), (slice(width - LANES, width), after)):
        for layer, row, part in pieces(packed, rows):
            cells[layer, row : row + part.shape[0], tile] = part
    scalars.wait()
    run_windows(OVER, slots, cells, acc, probe_re, probe_im, table, frames, order)
    odd = is_odd("row")
    strips = []
    for here in (slice(0, HALO), slice(rows - HALO, rows)):
        middle = [acc[k, here, LANES : width - LANES] for k in (0, 1)]
        right = [acc[k, here, width - LANES : width] for k in (0, 1)]
        corners = pack_four(right, [acc[k, here, 0:LANES] for k in (0, 1)])
        corners = beside(*(corners[i : i + MARKS] for i in range(0, HALO, MARKS)))
        strips.append(below(*middle, corners))
    to_inner[...] = jnp.where(odd, strips[0], strips[1])
    to_outer[...] = jnp.where(odd, strips[1], strips[0])


def column_spill(acc_in, by_outer, by_inner, acc, to_inner, to_outer):
    rows, width = acc.shape[1:]
    before, after = received(by_inner, by_outer, "row")
    for start, came in ((HALO, before), (rows - 2 * HALO, after)):
        here = slice(start, start + HALO)
        for k in (0, 1):
            acc[k, here, LANES : width - LANES] += came[k * HALO : (k + 1) * HALO]
        corners = came[2 * HALO :]
        corners = below(*(corners[:, i : i + LANES] for i in range(0, GROUPS * LANES, LANES)))
        for k, low, high in unpack_four(corners):
            acc[k, here, 0:LANES] += high
            acc[k, here, width - LANES :] += low
    tile_r = rows - 2 * HALO
    to_left = pack_lanes(acc, HALO, tile_r, slice(0, LANES), LANES - HALO)
    to_right = pack_lanes(acc, HALO, tile_r, slice(width - LANES, width), 0)
    send_columns(to_left, to_right, to_inner, to_outer)


def new_columns(cells, acc, spill, start, size, near_re, near_im):
    rows = acc.shape[1]
    here, there = slice(HALO, rows - HALO), slice(LANES + start, LANES + start + size)
    part = [acc[k, here, there] for k in range(acc.shape[0])]
    if spill is not None:
        part[:2] = [part[k] + spill[k] for k in (0, 1)]
    scale = 1.0 / (part[2] + ridge)
    near_re[:, start : start + size] = cells[0, here, there] - part[0] * scale
    near_im[:, start : start + size] = cells[1, here, there] - part[1] * scale


def finish_inner(
    slots, cells, acc_in, probe_re, probe_im, table, frames, acc, new_re, new_im, order, near_re, near_im, sems,
):
    run_windows(LAST, slots, cells, acc, probe_re, probe_im, table, frames, order)
    size = near_re.shape[1] - 2 * LANES
    new_columns(cells, acc, None, LANES, size, near_re, near_im)
    there = slice(LANES, LANES + size)
    finish_all(fetch([(near_re.at[:, there], new_re.at[:, there]), (near_im.at[:, there], new_im.at[:, there])], sems))


def finish_edges(cells, acc, by_inner, by_outer, re_in, im_in, new_re, new_im, near_re, near_im, sems):
    tile_r, tile_c = near_re.shape
    lane = lane_index(tile_r)
    sides = ((0, lane < HALO), (tile_c - LANES, lane >= LANES - HALO))
    copies = []
    for i, ((start, mine), packed) in enumerate(zip(sides, received(by_inner, by_outer, "col"))):
        parts = [part for _, _, part in pieces(packed, tile_r)]
        spill = [jnp.where(mine, below(*parts[2 * k : 2 * k + 2]), 0.0) for k in (0, 1)]
        new_columns(cells, acc, spill, start, LANES, near_re, near_im)
        there = slice(start, start + LANES)
        pairs = ((near_re.at[:, there], new_re.at[:, there]), (near_im.at[:, there], new_im.at[:, there]))
        copies += fetch(pairs, sems.at[2 * i : 2 * i + 2])
    finish_all(copies)


def swap(to_inner, to_outer, axis):
    devices = lax.axis_size(axis)
    inner = [(i, i + 1) for i in range(0, devices, 2)]
    partner = {i: i + 1 if i % 2 else i - 1 for i in range(1, devices - 1)}
    n_row, n_col = lax.axis_size("row"), lax.axis_size("col")
    pairs = []
    for row in range(n_row):
        for col in range(n_col):
            if axis == "row":
                there = (partner[row], col) if row in partner else (row, col ^ 1)
            else:
                there = (row, partner[col]) if col in partner else (row ^ 1, col)
            pairs.append((row * n_col + col, there[0] * n_col + there[1]))
    by_inner = lax.ppermute(to_inner, axis, inner + [(j, i) for i, j in inner])
    by_outer = lax.ppermute(to_outer, ("row", "col"), pairs)
    return by_inner, by_outer


def far(x):
    return pltpu.with_memory_space_constraint(x, pltpu.HBM)


def f32(*shape):
    return jax.ShapeDtypeStruct(shape, jnp.float32)


def shards(object_re, object_im, probe_re, probe_im, frames, counts, offsets, frame_index):
    tile_r, tile_c = object_re.shape
    rows, width = tile_r + 2 * HALO, tile_c + 2 * LANES
    layers = 3
    slots = offsets.shape[2]
    table = jnp.asarray(transform_tables())
    frames = frames.reshape(frames.shape[2:])
    cells_shape, acc_shape = f32(2, rows, width), f32(layers, rows, width)
    dma = pltpu.SemaphoreType.DMA

    places = jnp.swapaxes(offsets, 2, 3)
    small = f32(HALO + MARKS, LANES)
    edge = f32(2 * HALO * (tile_c // LANES), LANES)
    small_outer, small_inner, to_outer, to_inner, marked = pl.pallas_call(
        row_edges,
        out_shape=(small, small, edge, edge, jax.ShapeDtypeStruct((3, slots), jnp.int32)),
        in_specs=[SMEM] + [HBM] * 4,
        out_specs=(VMEM,) * 5,
        scratch_shapes=[
            pltpu.VMEM(places.shape, jnp.int32), pltpu.VMEM(frame_index.shape, jnp.int32),
            dma((2 + 4 * (tile_c // LANES),)),
        ],
        compiler_params=SMALL,
        name="row_edges",
    )(counts, far(object_re), far(object_im), far(places), far(frame_index))
    by_inner, by_outer = swap(small_inner, small_outer, "row")
    row_inner, row_outer = swap(to_inner, to_outer, "row")

    cells = pl.pallas_call(
        load_object,
        out_shape=cells_shape,
        in_specs=[HBM] * 2,
        out_specs=VMEM,
        scratch_shapes=[dma((2,))],
        compiler_params=SMALL,
        name="load_object",
    )(far(object_re), far(object_im))

    packed = f32(rows // 2 + MARKS, LANES)
    cells, marks, to_inner, to_outer = pl.pallas_call(
        row_corners,
        out_shape=(cells_shape, f32(MARKS, LANES), packed, packed),
        in_specs=[VMEM] * 4,
        out_specs=(VMEM,) * 4,
        input_output_aliases={0: 0},
        compiler_params=SMALL,
        name="row_corners",
    )(cells, small_outer, by_outer, by_inner)
    edges = swap(to_inner, to_outer, "col")

    order = pltpu.SMEM((slots,), jnp.int32)
    acc, *fixed = pl.pallas_call(
        windows_first,
        out_shape=(
            acc_shape, f32(*probe_re.shape), f32(*probe_im.shape),
            jax.ShapeDtypeStruct(table.shape, table.dtype), jax.ShapeDtypeStruct(frames.shape, frames.dtype),
        ),
        in_specs=[SMEM, VMEM] + [HBM] * 4,
        out_specs=(VMEM,) * 5,
        scratch_shapes=[order, dma((4,))],
        compiler_params=PARAMS,
        cost_estimate=BUSY,
        name="windows_first",
    )(marked, cells, *map(far, (probe_re, probe_im, table, frames)))

    cells, acc = pl.pallas_call(
        windows_before,
        out_shape=(cells_shape, acc_shape),
        in_specs=[SMEM] + [VMEM] * 8,
        out_specs=(VMEM, VMEM),
        scratch_shapes=[order, pltpu.VMEM(probe_re.shape, jnp.float32)],
        input_output_aliases={1: 0, 2: 1},
        compiler_params=PARAMS,
        cost_estimate=BUSY,
        name="windows_before",
    )(marked, cells, acc, *fixed, row_outer, row_inner)

    edge = f32(2 * HALO + MARKS, tile_c)
    cells, acc, to_outer, to_inner = pl.pallas_call(
        windows_over_edge,
        out_shape=(cells_shape, acc_shape, edge, edge),
        in_specs=[VMEM] * 9,
        out_specs=(VMEM,) * 4,
        scratch_shapes=[order, pltpu.SMEM((3, slots), jnp.int32), dma(())],
        input_output_aliases={1: 0, 2: 1},
        compiler_params=PARAMS,
        cost_estimate=BUSY,
        name="windows_over_edge",
    )(marked, cells, acc, *fixed, *edges)
    by_inner, by_outer = swap(to_inner, to_outer, "row")

    acc = pl.pallas_call(
        windows_after,
        out_shape=acc_shape,
        in_specs=[SMEM] + [VMEM] * 9,
        out_specs=VMEM,
        scratch_shapes=[
            order, pltpu.VMEM(probe_re.shape, jnp.float32),
            pltpu.VMEM((3, MARKS, LANES), jnp.int32), pltpu.SMEM((3, MARKS, LANES), jnp.int32), dma(()),
        ],
        input_output_aliases={2: 0},
        compiler_params=PARAMS,
        cost_estimate=BUSY,
        name="windows_after",
    )(marked, cells, acc, *fixed, marks, *edges)

    packed = f32(tile_r // 2, LANES)
    acc, to_inner, to_outer = pl.pallas_call(
        column_spill,
        out_shape=(acc_shape, packed, packed),
        in_specs=[VMEM] * 3,
        out_specs=(VMEM,) * 3,
        input_output_aliases={0: 0},
        compiler_params=SMALL,
        name="column_spill",
    )(acc, by_outer, by_inner)
    by_inner, by_outer = swap(to_inner, to_outer, "col")

    near = [pltpu.VMEM((tile_r, tile_c), jnp.float32)] * 2
    new = (f32(tile_r, tile_c), f32(tile_r, tile_c))
    acc, new_re, new_im = pl.pallas_call(
        finish_inner,
        out_shape=(acc_shape, *new),
        in_specs=[SMEM] + [VMEM] * 6,
        out_specs=(VMEM, HBM, HBM),
        scratch_shapes=[order] + near + [dma((2,))],
        input_output_aliases={2: 0},
        compiler_params=PARAMS,
        cost_estimate=BUSY,
        name="finish_inner",
    )(marked, cells, acc, *fixed)
    return pl.pallas_call(
        finish_edges,
        out_shape=new,
        in_specs=[VMEM] * 4 + [HBM] * 2,
        out_specs=(HBM, HBM),
        scratch_shapes=near + [dma((4,))],
        input_output_aliases={4: 0, 5: 1},
        compiler_params=SMALL,
        name="finish_edges",
    )(cells, acc, by_inner, by_outer, far(new_re), far(new_im))


def solution(mesh):
    return jax.shard_map(
        shards,
        mesh=mesh,
        in_specs=(
            P("row", "col"),
            P("row", "col"),
            P(),
            P(),
            P("row", "col", None, None, None),
            P("row", "col"),
            P("row", "col", None, None),
            P("row", "col", None),
        ),
        out_specs=(P("row", "col"), P("row", "col")),
        check_vma=False,
    )
```

```python
import functools
import math

import jax
import jax.numpy as jnp
import ml_dtypes
import numpy as np
from jax import lax
from jax.experimental import pallas as pl
from jax.experimental.pallas import tpu as pltpu
from jax.sharding import PartitionSpec as P

P_SIZE = 256
HALF = P_SIZE // 2
HALO = 32
LANES = 128
GROUPS = LANES // HALO
MARKS = 8
PAIR = 2

floor_amp = 0.5
ridge = 1.0

VMEM = pl.BlockSpec(memory_space=pltpu.VMEM)
SMEM = pl.BlockSpec(memory_space=pltpu.SMEM)
HBM = pl.BlockSpec(memory_space=pltpu.HBM)
PARAMS = pltpu.CompilerParams(vmem_limit_bytes=32 * 1024 * 1024)
SMALL = pltpu.CompilerParams(vmem_limit_bytes=16 * 1024 * 1024)
BUSY = pl.CostEstimate(flops=4_000_000_000, bytes_accessed=8_000_000, transcendentals=0)


def transform_tables():
    index = np.arange(HALF)
    plain = []
    for parity in (0, 1):
        angle = 2.0 * math.pi / P_SIZE * (index[:, None] * (2 * index[None, :] + parity) % P_SIZE)
        cos, sin = np.cos(angle), np.sin(angle)
        plain.append(np.block([[cos, -sin], [sin, cos]]) / math.sqrt(P_SIZE))
    parts = []
    for table in plain + [t.T for t in plain]:
        high = table.astype(np.float32).astype(ml_dtypes.bfloat16)
        low = (table - high.astype(np.float64)).astype(np.float32).astype(ml_dtypes.bfloat16)
        parts += [high, low]
    order = np.concatenate([np.arange(0, P_SIZE, 2), np.arange(1, P_SIZE, 2)])
    sort = np.zeros((P_SIZE, P_SIZE), np.float32)
    sort[np.arange(P_SIZE), order] = 1.0
    parts += [sort.astype(ml_dtypes.bfloat16), sort.T.astype(ml_dtypes.bfloat16)]
    return np.stack(parts)


def lane_index(rows):
    return lax.broadcasted_iota(jnp.int32, (rows, LANES), 1)


def pack_lanes(field, top, size, tile, first):
    half = size // 2
    lane = lane_index(half)
    packed = None
    for g in range(GROUPS):
        start = top + g % 2 * half
        part = field[g // 2, start : start + half, tile]
        if g:
            part = pltpu.roll(part, HALO * g, 1)
        low = (first + HALO * g) % LANES
        mine = (lane >= low) & (lane < low + HALO)
        packed = part if packed is None else jnp.where(mine, part, packed)
    return packed


def unpack_lanes(packed, group):
    return pltpu.roll(packed, LANES - HALO * group, 1) if group else packed


def split(x):
    high = x.astype(jnp.bfloat16)
    return high, (x - high.astype(jnp.float32)).astype(jnp.bfloat16)


def product(left, right):
    return jnp.dot(left, right, preferred_element_type=jnp.float32)


def times_table(x, table, which):
    high, low = split(x)
    t_high, t_low = table[2 * which], table[2 * which + 1]
    return product(beside(high, high, low), below(t_high, t_low, t_high))


def table_times(table, which, x):
    high, low = split(x)
    t_high, t_low = table[2 * which], table[2 * which + 1]
    return product(beside(t_high, t_low, t_high), below(high, high, low))


def beside(*blocks):
    return jnp.concatenate(blocks, axis=1)


def below(*blocks):
    return jnp.concatenate(blocks, axis=0)


def ends(x):
    return x[:, :HALF], x[:, HALF:]


def forward_columns(exit_re, exit_im, table):
    re_lo, re_hi = ends(exit_re)
    im_lo, im_hi = ends(exit_im)
    even = times_table(beside(re_lo + re_hi, im_lo + im_hi), table, 0)
    odd = times_table(beside(re_lo - re_hi, im_lo - im_hi), table, 1)
    return even, odd


def forward_rows(even, odd, table):
    out = []
    for parity in (0, 1):
        if parity == 0:
            se, so = even[:HALF] + even[HALF:], odd[:HALF] + odd[HALF:]
        else:
            se, so = even[:HALF] - even[HALF:], odd[:HALF] - odd[HALF:]
        e_re, e_im = ends(se)
        o_re, o_im = ends(so)
        out.append(table_times(table, 2 + parity, below(beside(e_re, o_re), beside(e_im, o_im))))
    return out


def residual(far, frame):
    out = []
    for parity in (0, 1):
        re, im = far[parity][:HALF], far[parity][HALF:]
        level = jnp.maximum(re * re + im * im, floor_amp * floor_amp)
        inten = frame[parity * HALF : (parity + 1) * HALF]
        factor = 1.0 - inten * lax.rsqrt(inten * level)
        out.append(below(re * factor, im * factor))
    return out


def back_rows(res, table):
    first = table_times(table, 0, res[0])
    second = table_times(table, 1, res[1])
    upper, lower = first + second, first - second
    out = []
    for cols in (slice(0, HALF), slice(HALF, P_SIZE)):
        out.append(
            below(
                beside(upper[:HALF, cols], upper[HALF:, cols]),
                beside(lower[:HALF, cols], lower[HALF:, cols]),
            )
        )
    return out


def back_columns(parts, table):
    even = times_table(parts[0], table, 2)
    odd = times_table(parts[1], table, 3)
    lo, hi = even + odd, even - odd
    return beside(lo[:, :HALF], hi[:, :HALF]), beside(lo[:, HALF:], hi[:, HALF:])


def is_odd(axis):
    return lax.rem(lax.axis_index(axis), 2) == 1


def fetch(pairs, sems):
    copies = [pltpu.make_async_copy(far, near, sems.at[i]) for i, (far, near) in enumerate(pairs)]
    for copy in copies:
        copy.start()
    return copies


def finish_all(copies):
    for copy in copies:
        copy.wait()


def row_edges(
    counts, obj_re, obj_im, offsets, chosen,
    small_outer, small_inner, to_outer, to_inner, marked, places, frame_of, sems,
):
    tile_r = obj_re.shape[0]
    odd = is_odd("row")
    low = pl.multiple_of(jnp.where(odd, 0, tile_r - HALO), 16)
    high = pl.multiple_of(jnp.where(odd, tile_r - HALO, 0), 16)
    pairs = [(offsets, places), (chosen, frame_of)]
    tiles = obj_re.shape[1] // LANES
    for k, ref in enumerate((obj_re, obj_im)):
        for t in range(tiles):
            lanes = slice(t * LANES, (t + 1) * LANES)
            rows = slice((2 * t + k) * HALO, (2 * t + k + 1) * HALO)
            pairs.append((ref.at[pl.ds(high, HALO), lanes], to_outer.at[rows]))
            pairs.append((ref.at[pl.ds(low, HALO), lanes], to_inner.at[rows]))
    copies = fetch(pairs, sems)
    finish_all(copies[:2])
    place = places[0, 0]
    live = lax.broadcasted_iota(jnp.int32, place.shape, 1) < counts[0, 0]
    place = jnp.where(live, place, 2 * tile_r)
    marked[0:2, :] = place
    marked[2:3, :] = frame_of[0]
    finish_all(copies[2:])
    for small, message in ((small_inner, to_inner), (small_outer, to_outer)):
        first = [message[k * HALO : (k + 1) * HALO, :] for k in (0, 1)]
        last = [message[(2 * tiles - 2 + k) * HALO : (2 * tiles - 1 + k) * HALO, :] for k in (0, 1)]
        small[0:HALO, :] = pack_four(first, last)
        small[HALO : HALO + 2, 0 : place.shape[1]] = place.astype(jnp.float32)


def load_object(obj_re, obj_im, cells, sems):
    tile_r, tile_c = obj_re.shape
    inner = slice(HALO, HALO + tile_r)
    middle = slice(LANES, LANES + tile_c)
    finish_all(fetch([(ref, cells.at[k, inner, middle]) for k, ref in enumerate((obj_re, obj_im))], sems))


def window_place(slots, slot):
    row = pl.multiple_of(slots[0, slot] + HALO, 16)
    col = slots[1, slot] + LANES
    turn = lax.rem(col, LANES)
    return row, pl.multiple_of(col - turn, LANES), turn


def add_window(acc, layer, where, keep, term, tiles=(0, 1, 2)):
    row, base, _ = where
    lo, hi = ends(term)
    parts = (jnp.where(keep, lo, 0.0), hi, jnp.where(keep, 0.0, lo))
    for t in tiles:
        acc[layer, pl.ds(row, term.shape[0]), pl.ds(base + t * LANES, LANES)] += parts[t]


def send_columns(to_left, to_right, to_inner, to_outer):
    odd = is_odd("col")
    to_inner[0 : to_left.shape[0], :] = jnp.where(odd, to_left, to_right)
    to_outer[0 : to_left.shape[0], :] = jnp.where(odd, to_right, to_left)


def received(by_inner, by_outer, axis):
    odd = is_odd(axis)
    index = lax.axis_index(axis)
    inside = (index > 0) & (index < lax.axis_size(axis) - 1)
    by_outer = jnp.where(inside, by_outer[...], 0.0)
    by_inner = by_inner[...]
    return jnp.where(odd, by_inner, by_outer), jnp.where(odd, by_outer, by_inner)


def pieces(packed, size):
    half = size // 2
    for g in range(GROUPS):
        yield g // 2, g % 2 * half, unpack_lanes(packed[:half], g)


def pack_four(low, high):
    lane = lane_index(HALO)
    first = jnp.where(lane < HALO, low[0], pltpu.roll(low[1], HALO, 1))
    second = jnp.where(lane < 3 * HALO, pltpu.roll(high[1], 3 * HALO, 1), high[0])
    return jnp.where(lane < 2 * HALO, first, second)


def unpack_four(packed):
    lane = lane_index(HALO)
    for k, low, high in ((0, 0, 0), (1, 3 * HALO, HALO)):
        yield (
            k,
            jnp.where(lane < HALO, pltpu.roll(packed, low, 1) if low else packed, 0.0),
            jnp.where(lane >= 3 * HALO, pltpu.roll(packed, high, 1) if high else packed, 0.0),
        )


def row_corners(cells_in, own, by_outer, by_inner, cells, marks, to_inner, to_outer):
    rows, width = cells.shape[1:]
    first, last = slice(LANES, 2 * LANES), slice(width - 2 * LANES, width - LANES)
    before, after = received(by_inner, by_outer, "row")
    for here, came in ((slice(0, HALO), before), (slice(rows - HALO, rows), after)):
        for k, low, high in unpack_four(came[0:HALO]):
            cells[k, here, first] = low
            cells[k, here, last] = high
    for i, message in enumerate((own[...], before, after)):
        marks[2 * i : 2 * i + 2, :] = message[HALO : HALO + 2]
    half = rows // 2
    to_left = pack_lanes(cells, 0, rows, first, 0)
    to_right = pack_lanes(cells, 0, rows, last, LANES - HALO)
    send_columns(to_left, to_right, to_inner, to_outer)
    to_inner[half:, :] = marks[...]
    to_outer[half:, :] = marks[...]


def live_slots(slots, cells):
    tile_r = cells.shape[1] - 2 * HALO
    count = jnp.int32(0)
    for slot in range(slots.shape[1]):
        count += (slots[0, slot] < tile_r).astype(jnp.int32)
    return count


FIRST, BEFORE, OVER, AFTER, LAST = range(5)


def run_windows(phase, slots, cells, acc, probe_re, probe_im, table, frames, order, largest=PAIR):
    tile_r, tile_c = cells.shape[1] - 2 * HALO, cells.shape[2] - 2 * LANES
    count = live_slots(slots, cells)
    kinds = []
    n_inside, n_row, n_col = jnp.int32(0), jnp.int32(0), jnp.int32(0)
    for slot in range(slots.shape[1]):
        row, col = slots[0, slot], slots[1, slot]
        live = slot < count
        over_col = (col < 0) | (col > tile_c - P_SIZE)
        over_row = (row < 0) | (row > tile_r - P_SIZE)
        inside, by_row = live & ~over_col & ~over_row, live & ~over_col & over_row
        by_col, by_both = live & over_col & ~over_row, live & over_col & over_row
        kinds.append((inside, by_row, by_col, by_both, n_inside, n_row))
        n_inside += inside.astype(jnp.int32)
        n_row += by_row.astype(jnp.int32)
        n_col += by_col.astype(jnp.int32)
    first = jnp.minimum(jnp.clip(n_inside + n_col - 2 * PAIR, 0, PAIR), n_inside)
    rest = n_inside - first
    after = n_inside - jnp.clip(n_col + rest - PAIR, 0, jnp.minimum(rest, PAIR))
    found = jnp.int32(0)
    for slot, (inside, by_row, by_col, by_both, rank, row_rank) in enumerate(kinds):
        mine = {
            FIRST: lambda: inside & (rank < first),
            BEFORE: lambda: by_row & (row_rank < PAIR),
            OVER: lambda: by_both | (by_row & (row_rank >= PAIR)),
            AFTER: lambda: by_col | (inside & (rank >= first) & (rank < after)),
            LAST: lambda: inside & (rank >= after),
        }[phase]()

        @pl.when(mine)
        def _():
            order[found] = slot

        found += mine.astype(jnp.int32)

    lane = lane_index(P_SIZE)

    def load(slot):
        where = row, base, turn = window_place(slots, slot)
        keep = lane >= turn
        w_re = pltpu.roll(probe_re[...], turn, 1)
        w_im = pltpu.roll(probe_im[...], turn, 1)
        patch = []
        for k in (0, 1):
            block = cells[k, pl.ds(row, P_SIZE), pl.ds(base, 3 * LANES)]
            patch.append(
                beside(jnp.where(keep, block[:, :LANES], block[:, 2 * LANES :]), block[:, LANES : 2 * LANES])
            )
        exit_re = w_re * patch[0] - w_im * patch[1]
        exit_im = w_re * patch[1] + w_im * patch[0]
        return (where, keep, w_re, w_im), exit_re, exit_im

    def frame_of(slot):
        half = product(table[8], frames[slots[2, slot]]).astype(jnp.bfloat16)
        return product(half, table[9])

    def place(at, back_re, back_im):
        where, keep, w_re, w_im = at
        add_window(acc, 0, where, keep, w_re * back_re + w_im * back_im)
        add_window(acc, 1, where, keep, w_re * back_im - w_im * back_re)

    def step(group):
        frame = [frame_of(slot) for slot in group]
        loaded = [load(slot) for slot in group]
        state = [forward_columns(x[1], x[2], table) for x in loaded]
        state = [forward_rows(*x, table) for x in state]
        state = [residual(x, f) for x, f in zip(state, frame)]
        state = [back_rows(x, table) for x in state]
        state = [back_columns(x, table) for x in state]
        for x, back in zip(loaded, state):
            place(x[0], *back)

    def group_step(group, carry):
        step([order[group * largest + i] for i in range(largest)])
        return carry

    lax.fori_loop(0, found // largest, group_step, 0)
    for left in range(1, largest):

        @pl.when(found % largest == left)
        def _():
            step([order[found - left + i] for i in range(left)])


def windows_first(
    slots, cells, probe_re_far, probe_im_far, table_far, frames_far,
    acc, probe_re, probe_im, table, frames, order, sems,
):
    pairs = ((table_far, table), (frames_far, frames), (probe_re_far, probe_re), (probe_im_far, probe_im))
    copies = fetch(pairs, sems)
    acc[...] = jnp.zeros_like(acc)
    finish_all(copies)
    run_windows(FIRST, slots, cells, acc, probe_re, probe_im, table, frames, order)


def windows_before(
    slots, cells_in, acc_in, probe_re, probe_im, table, frames, by_outer, by_inner,
    cells, acc, order, power,
):
    rows, width = cells.shape[1:]
    before, after = received(by_inner, by_outer, "row")
    for k in (0, 1):
        for t in range(width // LANES - 2):
            lanes = slice((t + 1) * LANES, (t + 2) * LANES)
            part = slice((2 * t + k) * HALO, (2 * t + k + 1) * HALO)
            cells[k, 0:HALO, lanes] = before[part]
            cells[k, rows - HALO : rows, lanes] = after[part]
    power[...] = probe_re[...] * probe_re[...] + probe_im[...] * probe_im[...]
    lane = lane_index(P_SIZE)

    def step(slot, carry):
        where = window_place(slots, slot)
        add_window(acc, 2, where, lane >= where[2], pltpu.roll(power[...], where[2], 1))
        return carry

    lax.fori_loop(0, live_slots(slots, cells), step, 0)
    run_windows(BEFORE, slots, cells, acc, probe_re, probe_im, table, frames, order)


def reaching(place, right, tile_r, tile_c):
    shape = place.shape
    index = lax.broadcasted_iota(jnp.int32, shape, 0)
    lane = lax.broadcasted_iota(jnp.int32, shape, 1)
    col = pltpu.roll(place, shape[0] - 1, 0)
    low = jnp.where(index == 2, tile_r - P_SIZE, -tile_r).astype(jnp.float32)
    high = jnp.where(index == 4, 0, tile_r).astype(jnp.float32)
    reaches = (lane < MARKS) & (index % 2 == 0) & (index < 6) & (place > low) & (place < high)
    if right < 0:
        reaches &= col > tile_c - P_SIZE
    if right > 0:
        reaches &= col < 0
    bit = lax.shift_left(jnp.ones(shape, jnp.int32), jnp.minimum(lane, MARKS)).astype(jnp.float32)
    bits = jnp.sum(jnp.where(reaches, bit, 0.0), axis=1, keepdims=True)
    return jnp.where(lane < MARKS, place, bits).astype(jnp.int32)


def add_neighbours_light(places, acc, power):
    rows, width = acc.shape[1:]
    tile_r, tile_c = rows - 2 * HALO, width - 2 * LANES
    for right in (-1, 0, 1):
        for i, down in enumerate((0, -1, 1)):
            if not right and not down:
                continue
            first, last = {-1: (P_SIZE - HALO, P_SIZE), 0: (0, P_SIZE), 1: (0, HALO)}[down]
            tiles = {-1: (2,), 0: (0, 1, 2), 1: (0,)}[right]
            lane = lane_index(last - first)
            bits = places[right + 1, 2 * i, MARKS]

            def step(slot, carry):
                row, col = places[right + 1, 2 * i, slot], places[right + 1, 2 * i + 1, slot]

                @pl.when(lax.shift_right_logical(bits, slot) % 2 == 1)
                def _():
                    turn = lax.rem(col + LANES, LANES)
                    at = pl.multiple_of(row + HALO + (down * tile_r + first), 16)
                    base = pl.multiple_of(col + LANES - turn + right * tile_c, LANES)
                    part = pltpu.roll(power[first:last, :], turn, 1)
                    add_window(acc, 2, (at, base, turn), lane >= turn, part, tiles)

                return carry

            @pl.when(bits != 0)
            def _():
                lax.fori_loop(0, MARKS, step, 0)


def windows_after(
    slots, cells, acc_in, probe_re, probe_im, table, frames, marks, by_inner, by_outer,
    acc, order, power, whole, places, sem,
):
    rows, width = acc.shape[1:]
    before, after = received(by_inner, by_outer, "col")
    for i, part in enumerate((before[-MARKS:], marks[...], after[-MARKS:])):
        whole[i] = reaching(part, i - 1, rows - 2 * HALO, width - 2 * LANES)
    copy = pltpu.make_async_copy(whole, places, sem)
    copy.start()
    power[...] = probe_re[...] * probe_re[...] + probe_im[...] * probe_im[...]
    run_windows(AFTER, slots, cells, acc, probe_re, probe_im, table, frames, order)
    copy.wait()
    add_neighbours_light(places, acc, power)


def windows_over_edge(
    marked, cells_in, acc_in, probe_re, probe_im, table, frames, by_inner, by_outer,
    cells, acc, to_outer, to_inner, order, slots, sem,
):
    scalars = pltpu.make_async_copy(marked, slots, sem)
    scalars.start()
    rows, width = acc.shape[1:]
    before, after = received(by_inner, by_outer, "col")
    for tile, packed in ((slice(0, LANES), before), (slice(width - LANES, width), after)):
        for layer, row, part in pieces(packed, rows):
            cells[layer, row : row + part.shape[0], tile] = part
    scalars.wait()
    run_windows(OVER, slots, cells, acc, probe_re, probe_im, table, frames, order)
    odd = is_odd("row")
    strips = []
    for here in (slice(0, HALO), slice(rows - HALO, rows)):
        middle = [acc[k, here, LANES : width - LANES] for k in (0, 1)]
        right = [acc[k, here, width - LANES : width] for k in (0, 1)]
        corners = pack_four(right, [acc[k, here, 0:LANES] for k in (0, 1)])
        corners = beside(*(corners[i : i + MARKS] for i in range(0, HALO, MARKS)))
        strips.append(below(*middle, corners))
    to_inner[...] = jnp.where(odd, strips[0], strips[1])
    to_outer[...] = jnp.where(odd, strips[1], strips[0])


def column_spill(acc_in, by_outer, by_inner, acc, to_inner, to_outer):
    rows, width = acc.shape[1:]
    before, after = received(by_inner, by_outer, "row")
    for start, came in ((HALO, before), (rows - 2 * HALO, after)):
        here = slice(start, start + HALO)
        for k in (0, 1):
            acc[k, here, LANES : width - LANES] += came[k * HALO : (k + 1) * HALO]
        corners = came[2 * HALO :]
        corners = below(*(corners[:, i : i + LANES] for i in range(0, GROUPS * LANES, LANES)))
        for k, low, high in unpack_four(corners):
            acc[k, here, 0:LANES] += high
            acc[k, here, width - LANES :] += low
    tile_r = rows - 2 * HALO
    to_left = pack_lanes(acc, HALO, tile_r, slice(0, LANES), LANES - HALO)
    to_right = pack_lanes(acc, HALO, tile_r, slice(width - LANES, width), 0)
    send_columns(to_left, to_right, to_inner, to_outer)


def new_columns(cells, acc, spill, start, size, near_re, near_im):
    rows = acc.shape[1]
    here, there = slice(HALO, rows - HALO), slice(LANES + start, LANES + start + size)
    part = [acc[k, here, there] for k in range(acc.shape[0])]
    if spill is not None:
        part[:2] = [part[k] + spill[k] for k in (0, 1)]
    scale = 1.0 / (part[2] + ridge)
    near_re[:, start : start + size] = cells[0, here, there] - part[0] * scale
    near_im[:, start : start + size] = cells[1, here, there] - part[1] * scale


def finish_inner(
    slots, cells, acc_in, probe_re, probe_im, table, frames, acc, new_re, new_im, order, near_re, near_im, sems,
):
    run_windows(LAST, slots, cells, acc, probe_re, probe_im, table, frames, order)
    size = near_re.shape[1] - 2 * LANES
    new_columns(cells, acc, None, LANES, size, near_re, near_im)
    there = slice(LANES, LANES + size)
    finish_all(fetch([(near_re.at[:, there], new_re.at[:, there]), (near_im.at[:, there], new_im.at[:, there])], sems))


def finish_edges(cells, acc, by_inner, by_outer, re_in, im_in, new_re, new_im, near_re, near_im, sems):
    tile_r, tile_c = near_re.shape
    lane = lane_index(tile_r)
    sides = ((0, lane < HALO), (tile_c - LANES, lane >= LANES - HALO))
    copies = []
    for i, ((start, mine), packed) in enumerate(zip(sides, received(by_inner, by_outer, "col"))):
        parts = [part for _, _, part in pieces(packed, tile_r)]
        spill = [jnp.where(mine, below(*parts[2 * k : 2 * k + 2]), 0.0) for k in (0, 1)]
        new_columns(cells, acc, spill, start, LANES, near_re, near_im)
        there = slice(start, start + LANES)
        pairs = ((near_re.at[:, there], new_re.at[:, there]), (near_im.at[:, there], new_im.at[:, there]))
        copies += fetch(pairs, sems.at[2 * i : 2 * i + 2])
    finish_all(copies)


def swap(to_inner, to_outer, axis):
    devices = lax.axis_size(axis)
    inner = [(i, i + 1) for i in range(0, devices, 2)]
    partner = {i: i + 1 if i % 2 else i - 1 for i in range(1, devices - 1)}
    n_row, n_col = lax.axis_size("row"), lax.axis_size("col")
    pairs = []
    for row in range(n_row):
        for col in range(n_col):
            if axis == "row":
                there = (partner[row], col) if row in partner else (row, col ^ 1)
            else:
                there = (row, partner[col]) if col in partner else (row ^ 1, col)
            pairs.append((row * n_col + col, there[0] * n_col + there[1]))
    by_inner = lax.ppermute(to_inner, axis, inner + [(j, i) for i, j in inner])
    by_outer = lax.ppermute(to_outer, ("row", "col"), pairs)
    return by_inner, by_outer


def far(x):
    return pltpu.with_memory_space_constraint(x, pltpu.HBM)


def f32(*shape):
    return jax.ShapeDtypeStruct(shape, jnp.float32)


def shards(object_re, object_im, probe_re, probe_im, frames, counts, offsets, frame_index):
    tile_r, tile_c = object_re.shape
    rows, width = tile_r + 2 * HALO, tile_c + 2 * LANES
    layers = 3
    slots = offsets.shape[2]
    table = jnp.asarray(transform_tables())
    frames = frames.reshape(frames.shape[2:])
    cells_shape, acc_shape = f32(2, rows, width), f32(layers, rows, width)
    dma = pltpu.SemaphoreType.DMA

    places = jnp.swapaxes(offsets, 2, 3)
    small = f32(HALO + MARKS, LANES)
    edge = f32(2 * HALO * (tile_c // LANES), LANES)
    small_outer, small_inner, to_outer, to_inner, marked = pl.pallas_call(
        row_edges,
        out_shape=(small, small, edge, edge, jax.ShapeDtypeStruct((3, slots), jnp.int32)),
        in_specs=[SMEM] + [HBM] * 4,
        out_specs=(VMEM,) * 5,
        scratch_shapes=[
            pltpu.VMEM(places.shape, jnp.int32), pltpu.VMEM(frame_index.shape, jnp.int32),
            dma((2 + 4 * (tile_c // LANES),)),
        ],
        compiler_params=SMALL,
        name="row_edges",
    )(counts, far(object_re), far(object_im), far(places), far(frame_index))
    by_inner, by_outer = swap(small_inner, small_outer, "row")
    row_inner, row_outer = swap(to_inner, to_outer, "row")

    cells = pl.pallas_call(
        load_object,
        out_shape=cells_shape,
        in_specs=[HBM] * 2,
        out_specs=VMEM,
        scratch_shapes=[dma((2,))],
        compiler_params=SMALL,
        name="load_object",
    )(far(object_re), far(object_im))

    packed = f32(rows // 2 + MARKS, LANES)
    cells, marks, to_inner, to_outer = pl.pallas_call(
        row_corners,
        out_shape=(cells_shape, f32(MARKS, LANES), packed, packed),
        in_specs=[VMEM] * 4,
        out_specs=(VMEM,) * 4,
        input_output_aliases={0: 0},
        compiler_params=SMALL,
        name="row_corners",
    )(cells, small_outer, by_outer, by_inner)
    edges = swap(to_inner, to_outer, "col")

    order = pltpu.SMEM((slots,), jnp.int32)
    acc, *fixed = pl.pallas_call(
        windows_first,
        out_shape=(
            acc_shape, f32(*probe_re.shape), f32(*probe_im.shape),
            jax.ShapeDtypeStruct(table.shape, table.dtype), jax.ShapeDtypeStruct(frames.shape, frames.dtype),
        ),
        in_specs=[SMEM, VMEM] + [HBM] * 4,
        out_specs=(VMEM,) * 5,
        scratch_shapes=[order, dma((4,))],
        compiler_params=PARAMS,
        cost_estimate=BUSY,
        name="windows_first",
    )(marked, cells, *map(far, (probe_re, probe_im, table, frames)))

    cells, acc = pl.pallas_call(
        windows_before,
        out_shape=(cells_shape, acc_shape),
        in_specs=[SMEM] + [VMEM] * 8,
        out_specs=(VMEM, VMEM),
        scratch_shapes=[order, pltpu.VMEM(probe_re.shape, jnp.float32)],
        input_output_aliases={1: 0, 2: 1},
        compiler_params=PARAMS,
        cost_estimate=BUSY,
        name="windows_before",
    )(marked, cells, acc, *fixed, row_outer, row_inner)

    edge = f32(2 * HALO + MARKS, tile_c)
    cells, acc, to_outer, to_inner = pl.pallas_call(
        windows_over_edge,
        out_shape=(cells_shape, acc_shape, edge, edge),
        in_specs=[VMEM] * 9,
        out_specs=(VMEM,) * 4,
        scratch_shapes=[order, pltpu.SMEM((3, slots), jnp.int32), dma(())],
        input_output_aliases={1: 0, 2: 1},
        compiler_params=PARAMS,
        cost_estimate=BUSY,
        name="windows_over_edge",
    )(marked, cells, acc, *fixed, *edges)
    by_inner, by_outer = swap(to_inner, to_outer, "row")

    acc = pl.pallas_call(
        windows_after,
        out_shape=acc_shape,
        in_specs=[SMEM] + [VMEM] * 9,
        out_specs=VMEM,
        scratch_shapes=[
            order, pltpu.VMEM(probe_re.shape, jnp.float32),
            pltpu.VMEM((3, MARKS, LANES), jnp.int32), pltpu.SMEM((3, MARKS, LANES), jnp.int32), dma(()),
        ],
        input_output_aliases={2: 0},
        compiler_params=PARAMS,
        cost_estimate=BUSY,
        name="windows_after",
    )(marked, cells, acc, *fixed, marks, *edges)

    packed = f32(tile_r // 2, LANES)
    acc, to_inner, to_outer = pl.pallas_call(
        column_spill,
        out_shape=(acc_shape, packed, packed),
        in_specs=[VMEM] * 3,
        out_specs=(VMEM,) * 3,
        input_output_aliases={0: 0},
        compiler_params=SMALL,
        name="column_spill",
    )(acc, by_outer, by_inner)
    by_inner, by_outer = swap(to_inner, to_outer, "col")

    near = [pltpu.VMEM((tile_r, tile_c), jnp.float32)] * 2
    new = (f32(tile_r, tile_c), f32(tile_r, tile_c))
    acc, new_re, new_im = pl.pallas_call(
        finish_inner,
        out_shape=(acc_shape, *new),
        in_specs=[SMEM] + [VMEM] * 6,
        out_specs=(VMEM, HBM, HBM),
        scratch_shapes=[order] + near + [dma((2,))],
        input_output_aliases={2: 0},
        compiler_params=PARAMS,
        cost_estimate=BUSY,
        name="finish_inner",
    )(marked, cells, acc, *fixed)
    return pl.pallas_call(
        finish_edges,
        out_shape=new,
        in_specs=[VMEM] * 4 + [HBM] * 2,
        out_specs=(HBM, HBM),
        scratch_shapes=near + [dma((4,))],
        input_output_aliases={4: 0, 5: 1},
        compiler_params=SMALL,
        name="finish_edges",
    )(cells, acc, by_inner, by_outer, far(new_re), far(new_im))


def solution(mesh):
    return jax.shard_map(
        shards,
        mesh=mesh,
        in_specs=(
            P("row", "col"),
            P("row", "col"),
            P(),
            P(),
            P("row", "col", None, None, None),
            P("row", "col"),
            P("row", "col", None, None),
            P("row", "col", None),
        ),
        out_specs=(P("row", "col"), P("row", "col")),
        check_vma=False,
    )
```

```python
import functools
import math

import jax
import jax.numpy as jnp
import ml_dtypes
import numpy as np
from jax import lax
from jax.experimental import pallas as pl
from jax.experimental.pallas import tpu as pltpu
from jax.sharding import PartitionSpec as P

P_SIZE = 256
HALF = P_SIZE // 2
HALO = 32
LANES = 128
GROUPS = LANES // HALO
MARKS = 8
PAIR = 2

floor_amp = 0.5
ridge = 1.0

VMEM = pl.BlockSpec(memory_space=pltpu.VMEM)
SMEM = pl.BlockSpec(memory_space=pltpu.SMEM)
HBM = pl.BlockSpec(memory_space=pltpu.HBM)
PARAMS = pltpu.CompilerParams(vmem_limit_bytes=32 * 1024 * 1024)
SMALL = pltpu.CompilerParams(vmem_limit_bytes=16 * 1024 * 1024)
BUSY = pl.CostEstimate(flops=4_000_000_000, bytes_accessed=8_000_000, transcendentals=0)


def transform_tables():
    index = np.arange(HALF)
    plain = []
    for parity in (0, 1):
        angle = 2.0 * math.pi / P_SIZE * (index[:, None] * (2 * index[None, :] + parity) % P_SIZE)
        cos, sin = np.cos(angle), np.sin(angle)
        plain.append(np.block([[cos, -sin], [sin, cos]]) / math.sqrt(P_SIZE))
    parts = []
    for table in plain + [t.T for t in plain]:
        high = table.astype(np.float32).astype(ml_dtypes.bfloat16)
        low = (table - high.astype(np.float64)).astype(np.float32).astype(ml_dtypes.bfloat16)
        parts += [high, low]
    order = np.concatenate([np.arange(0, P_SIZE, 2), np.arange(1, P_SIZE, 2)])
    sort = np.zeros((P_SIZE, P_SIZE), np.float32)
    sort[np.arange(P_SIZE), order] = 1.0
    parts += [sort.astype(ml_dtypes.bfloat16), sort.T.astype(ml_dtypes.bfloat16)]
    return np.stack(parts)


def lane_index(rows):
    return lax.broadcasted_iota(jnp.int32, (rows, LANES), 1)


def pack_lanes(field, top, size, tile, first):
    half = size // 2
    lane = lane_index(half)
    packed = None
    for g in range(GROUPS):
        start = top + g % 2 * half
        part = field[g // 2, start : start + half, tile]
        if g:
            part = pltpu.roll(part, HALO * g, 1)
        low = (first + HALO * g) % LANES
        mine = (lane >= low) & (lane < low + HALO)
        packed = part if packed is None else jnp.where(mine, part, packed)
    return packed


def unpack_lanes(packed, group):
    return pltpu.roll(packed, LANES - HALO * group, 1) if group else packed


def split(x):
    high = x.astype(jnp.bfloat16)
    return high, (x - high.astype(jnp.float32)).astype(jnp.bfloat16)


def product(left, right):
    return jnp.dot(left, right, preferred_element_type=jnp.float32)


def times_table(x, table, which):
    high, low = split(x)
    t_high, t_low = table[2 * which], table[2 * which + 1]
    return product(beside(high, high, low), below(t_high, t_low, t_high))


def table_times(table, which, x):
    high, low = split(x)
    t_high, t_low = table[2 * which], table[2 * which + 1]
    return product(beside(t_high, t_low, t_high), below(high, high, low))


def beside(*blocks):
    return jnp.concatenate(blocks, axis=1)


def below(*blocks):
    return jnp.concatenate(blocks, axis=0)


def ends(x):
    return x[:, :HALF], x[:, HALF:]


def forward_columns(exit_re, exit_im, table):
    re_lo, re_hi = ends(exit_re)
    im_lo, im_hi = ends(exit_im)
    even = times_table(beside(re_lo + re_hi, im_lo + im_hi), table, 0)
    odd = times_table(beside(re_lo - re_hi, im_lo - im_hi), table, 1)
    return even, odd


def forward_rows(even, odd, table):
    out = []
    for parity in (0, 1):
        if parity == 0:
            se, so = even[:HALF] + even[HALF:], odd[:HALF] + odd[HALF:]
        else:
            se, so = even[:HALF] - even[HALF:], odd[:HALF] - odd[HALF:]
        e_re, e_im = ends(se)
        o_re, o_im = ends(so)
        out.append(table_times(table, 2 + parity, below(beside(e_re, o_re), beside(e_im, o_im))))
    return out


def residual(far, frame):
    out = []
    for parity in (0, 1):
        re, im = far[parity][:HALF], far[parity][HALF:]
        level = jnp.maximum(re * re + im * im, floor_amp * floor_amp)
        inten = frame[parity * HALF : (parity + 1) * HALF]
        factor = 1.0 - inten * lax.rsqrt(inten * level)
        out.append(below(re * factor, im * factor))
    return out


def back_rows(res, table):
    first = table_times(table, 0, res[0])
    second = table_times(table, 1, res[1])
    upper, lower = first + second, first - second
    out = []
    for cols in (slice(0, HALF), slice(HALF, P_SIZE)):
        out.append(
            below(
                beside(upper[:HALF, cols], upper[HALF:, cols]),
                beside(lower[:HALF, cols], lower[HALF:, cols]),
            )
        )
    return out


def back_columns(parts, table):
    even = times_table(parts[0], table, 2)
    odd = times_table(parts[1], table, 3)
    lo, hi = even + odd, even - odd
    return beside(lo[:, :HALF], hi[:, :HALF]), beside(lo[:, HALF:], hi[:, HALF:])


def is_odd(axis):
    return lax.rem(lax.axis_index(axis), 2) == 1


def fetch(pairs, sems):
    copies = [pltpu.make_async_copy(far, near, sems.at[i]) for i, (far, near) in enumerate(pairs)]
    for copy in copies:
        copy.start()
    return copies


def finish_all(copies):
    for copy in copies:
        copy.wait()


def row_edges(counts, obj_re, obj_im, offsets, chosen, to_outer, to_inner, marked, places, frame_of, sems):
    tile_r = obj_re.shape[0]
    odd = is_odd("row")
    low = pl.multiple_of(jnp.where(odd, 0, tile_r - HALO), 16)
    high = pl.multiple_of(jnp.where(odd, tile_r - HALO, 0), 16)
    pairs = [(offsets, places), (chosen, frame_of)]
    tiles = obj_re.shape[1] // LANES
    for k, ref in enumerate((obj_re, obj_im)):
        for t in range(tiles):
            lanes = slice(t * LANES, (t + 1) * LANES)
            rows = slice((2 * t + k) * HALO, (2 * t + k + 1) * HALO)
            pairs.append((ref.at[pl.ds(high, HALO), lanes], to_outer.at[rows]))
            pairs.append((ref.at[pl.ds(low, HALO), lanes], to_inner.at[rows]))
    copies = fetch(pairs, sems)
    finish_all(copies[:2])
    place = places[0, 0]
    live = lax.broadcasted_iota(jnp.int32, place.shape, 1) < counts[0, 0]
    place = jnp.where(live, place, 2 * tile_r)
    marked[0:2, :] = place
    marked[2:3, :] = frame_of[0]
    for message in (to_inner, to_outer):
        first = 2 * HALO * tiles
        message[first : first + 2, 0 : place.shape[1]] = place.astype(jnp.float32)
    finish_all(copies[2:])


def window_place(slots, slot):
    row = pl.multiple_of(slots[0, slot] + HALO, 16)
    col = slots[1, slot] + LANES
    turn = lax.rem(col, LANES)
    return row, pl.multiple_of(col - turn, LANES), turn


def add_window(acc, layer, where, keep, term, tiles=(0, 1, 2)):
    row, base, _ = where
    lo, hi = ends(term)
    parts = (jnp.where(keep, lo, 0.0), hi, jnp.where(keep, 0.0, lo))
    for t in tiles:
        acc[layer, pl.ds(row, term.shape[0]), pl.ds(base + t * LANES, LANES)] += parts[t]


def send_columns(to_left, to_right, to_inner, to_outer):
    odd = is_odd("col")
    to_inner[0 : to_left.shape[0], :] = jnp.where(odd, to_left, to_right)
    to_outer[0 : to_left.shape[0], :] = jnp.where(odd, to_right, to_left)


def received(by_inner, by_outer, axis):
    odd = is_odd(axis)
    index = lax.axis_index(axis)
    inside = (index > 0) & (index < lax.axis_size(axis) - 1)
    by_outer = jnp.where(inside, by_outer[...], 0.0)
    by_inner = by_inner[...]
    return jnp.where(odd, by_inner, by_outer), jnp.where(odd, by_outer, by_inner)


def pieces(packed, size):
    half = size // 2
    for g in range(GROUPS):
        yield g // 2, g % 2 * half, unpack_lanes(packed[:half], g)


def pack_corners(field, rows):
    width = field.shape[2]
    left = [field[k, rows, 0:LANES] for k in (0, 1)]
    right = [field[k, rows, width - LANES : width] for k in (0, 1)]
    lane = lane_index(HALO)
    low = jnp.where(lane < HALO, right[0], pltpu.roll(right[1], HALO, 1))
    high = jnp.where(lane < 3 * HALO, pltpu.roll(left[1], 3 * HALO, 1), left[0])
    packed = jnp.where(lane < 2 * HALO, low, high)
    return beside(*(packed[i : i + MARKS] for i in range(0, HALO, MARKS)))


def unpack_corners(packed):
    packed = below(*(packed[:, i : i + LANES] for i in range(0, GROUPS * LANES, LANES)))
    lane = lane_index(HALO)
    for k, left, right in ((0, 0, 0), (1, HALO, 3 * HALO)):
        yield (
            k,
            jnp.where(lane >= 3 * HALO, pltpu.roll(packed, left, 1) if left else packed, 0.0),
            jnp.where(lane < HALO, pltpu.roll(packed, right, 1) if right else packed, 0.0),
        )


def row_halos(cells_in, own, by_outer, by_inner, cells, marks, to_inner, to_outer):
    rows, width = cells.shape[1:]
    before, after = received(by_inner, by_outer, "row")
    tiles = width // LANES - 2
    for k in (0, 1):
        for t in range(tiles):
            lanes = slice((t + 1) * LANES, (t + 2) * LANES)
            part = slice((2 * t + k) * HALO, (2 * t + k + 1) * HALO)
            cells[k, 0:HALO, lanes] = before[part]
            cells[k, rows - HALO : rows, lanes] = after[part]
    first = 2 * HALO * tiles
    for i, message in enumerate((own[...], before, after)):
        marks[2 * i : 2 * i + 2, :] = message[first : first + 2]
    half = rows // 2
    to_left = pack_lanes(cells, 0, rows, slice(LANES, 2 * LANES), 0)
    to_right = pack_lanes(cells, 0, rows, slice(width - 2 * LANES, width - LANES), LANES - HALO)
    send_columns(to_left, to_right, to_inner, to_outer)
    to_inner[half:, :] = marks[...]
    to_outer[half:, :] = marks[...]


def live_slots(slots, cells):
    tile_r = cells.shape[1] - 2 * HALO
    count = jnp.int32(0)
    for slot in range(slots.shape[1]):
        count += (slots[0, slot] < tile_r).astype(jnp.int32)
    return count


FIRST, BEFORE, OVER, AFTER, LAST = range(5)


def run_windows(phase, slots, cells, acc, probe_re, probe_im, table, frames, order):
    tile_r, tile_c = cells.shape[1] - 2 * HALO, cells.shape[2] - 2 * LANES
    count = live_slots(slots, cells)
    kinds = []
    n_inside, n_row, n_col = jnp.int32(0), jnp.int32(0), jnp.int32(0)
    for slot in range(slots.shape[1]):
        row, col = slots[0, slot], slots[1, slot]
        live = slot < count
        over_col = (col < 0) | (col > tile_c - P_SIZE)
        over_row = (row < 0) | (row > tile_r - P_SIZE)
        inside, by_row = live & ~over_col & ~over_row, live & ~over_col & over_row
        by_col, by_both = live & over_col & ~over_row, live & over_col & over_row
        kinds.append((inside, by_row, by_col, by_both, n_inside, n_row))
        n_inside += inside.astype(jnp.int32)
        n_row += by_row.astype(jnp.int32)
        n_col += by_col.astype(jnp.int32)
    first = jnp.where(count > 2 * PAIR, jnp.minimum(n_inside, PAIR), 0)
    before = first + jnp.minimum(n_inside - first, PAIR - jnp.minimum(n_row, PAIR))
    rest = n_inside - before
    after = n_inside - jnp.clip(n_col + rest - 2 * PAIR, 0, jnp.minimum(rest, PAIR))
    found = jnp.int32(0)
    for slot, (inside, by_row, by_col, by_both, rank, row_rank) in enumerate(kinds):
        mine = {
            FIRST: lambda: inside & (rank < first),
            BEFORE: lambda: (by_row & (row_rank < PAIR)) | (inside & (rank >= first) & (rank < before)),
            OVER: lambda: by_both | (by_row & (row_rank >= PAIR)),
            AFTER: lambda: by_col | (inside & (rank >= before) & (rank < after)),
            LAST: lambda: inside & (rank >= after),
        }[phase]()

        @pl.when(mine)
        def _():
            order[found] = slot

        found += mine.astype(jnp.int32)

    lane = lane_index(P_SIZE)

    def load(slot):
        where = row, base, turn = window_place(slots, slot)
        keep = lane >= turn
        w_re = pltpu.roll(probe_re[...], turn, 1)
        w_im = pltpu.roll(probe_im[...], turn, 1)
        patch = []
        for k in (0, 1):
            block = cells[k, pl.ds(row, P_SIZE), pl.ds(base, 3 * LANES)]
            patch.append(
                beside(jnp.where(keep, block[:, :LANES], block[:, 2 * LANES :]), block[:, LANES : 2 * LANES])
            )
        exit_re = w_re * patch[0] - w_im * patch[1]
        exit_im = w_re * patch[1] + w_im * patch[0]
        return (where, keep, w_re, w_im), exit_re, exit_im

    def frame_of(slot):
        half = product(table[8], frames[slots[2, slot]]).astype(jnp.bfloat16)
        return product(half, table[9])

    def place(at, back_re, back_im):
        where, keep, w_re, w_im = at
        add_window(acc, 0, where, keep, w_re * back_re + w_im * back_im)
        add_window(acc, 1, where, keep, w_re * back_im - w_im * back_re)

    def step(group):
        frame = [frame_of(slot) for slot in group]
        loaded = [load(slot) for slot in group]
        state = [forward_columns(x[1], x[2], table) for x in loaded]
        state = [forward_rows(*x, table) for x in state]
        state = [residual(x, f) for x, f in zip(state, frame)]
        state = [back_rows(x, table) for x in state]
        state = [back_columns(x, table) for x in state]
        for x, back in zip(loaded, state):
            place(x[0], *back)

    def pair_step(pair, carry):
        step([order[pair * PAIR + i] for i in range(PAIR)])
        return carry

    lax.fori_loop(0, found // PAIR, pair_step, 0)

    @pl.when(found % PAIR == 1)
    def _():
        step([order[found - 1]])


def windows_first(
    slots, obj_re, obj_im, probe_re_far, probe_im_far, table_far, frames_far,
    cells, acc, probe_re, probe_im, table, frames, order, sems,
):
    tile_r, tile_c = obj_re.shape
    inner = slice(HALO, HALO + tile_r)
    middle = slice(LANES, LANES + tile_c)
    pairs = (
        (table_far, table),
        (frames_far, frames),
        (obj_re, cells.at[0, inner, middle]),
        (obj_im, cells.at[1, inner, middle]),
        (probe_re_far, probe_re),
        (probe_im_far, probe_im),
    )
    copies = fetch(pairs, sems)
    acc[...] = jnp.zeros_like(acc)
    finish_all(copies)
    run_windows(FIRST, slots, cells, acc, probe_re, probe_im, table, frames, order)


def windows_before(
    slots, cells, acc_in, probe_re, probe_im, table, frames, acc, order, power,
):
    power[...] = probe_re[...] * probe_re[...] + probe_im[...] * probe_im[...]
    lane = lane_index(P_SIZE)

    def step(slot, carry):
        where = window_place(slots, slot)
        add_window(acc, 2, where, lane >= where[2], pltpu.roll(power[...], where[2], 1))
        return carry

    lax.fori_loop(0, live_slots(slots, cells), step, 0)
    run_windows(BEFORE, slots, cells, acc, probe_re, probe_im, table, frames, order)


def reaching(place, right, tile_r, tile_c):
    shape = place.shape
    index = lax.broadcasted_iota(jnp.int32, shape, 0)
    lane = lax.broadcasted_iota(jnp.int32, shape, 1)
    col = pltpu.roll(place, shape[0] - 1, 0)
    low = jnp.where(index == 2, tile_r - P_SIZE, -tile_r).astype(jnp.float32)
    high = jnp.where(index == 4, 0, tile_r).astype(jnp.float32)
    reaches = (lane < MARKS) & (index % 2 == 0) & (index < 6) & (place > low) & (place < high)
    if right < 0:
        reaches &= col > tile_c - P_SIZE
    if right > 0:
        reaches &= col < 0
    bit = lax.shift_left(jnp.ones(shape, jnp.int32), jnp.minimum(lane, MARKS)).astype(jnp.float32)
    bits = jnp.sum(jnp.where(reaches, bit, 0.0), axis=1, keepdims=True)
    return jnp.where(lane < MARKS, place, bits).astype(jnp.int32)


def add_neighbours_light(places, acc, power):
    rows, width = acc.shape[1:]
    tile_r, tile_c = rows - 2 * HALO, width - 2 * LANES
    for right in (-1, 0, 1):
        for i, down in enumerate((0, -1, 1)):
            if not right and not down:
                continue
            first, last = {-1: (P_SIZE - HALO, P_SIZE), 0: (0, P_SIZE), 1: (0, HALO)}[down]
            tiles = {-1: (2,), 0: (0, 1, 2), 1: (0,)}[right]
            lane = lane_index(last - first)
            bits = places[right + 1, 2 * i, MARKS]

            def step(slot, carry):
                row, col = places[right + 1, 2 * i, slot], places[right + 1, 2 * i + 1, slot]

                @pl.when(lax.shift_right_logical(bits, slot) % 2 == 1)
                def _():
                    turn = lax.rem(col + LANES, LANES)
                    at = pl.multiple_of(row + HALO + (down * tile_r + first), 16)
                    base = pl.multiple_of(col + LANES - turn + right * tile_c, LANES)
                    part = pltpu.roll(power[first:last, :], turn, 1)
                    add_window(acc, 2, (at, base, turn), lane >= turn, part, tiles)

                return carry

            @pl.when(bits != 0)
            def _():
                lax.fori_loop(0, MARKS, step, 0)


def windows_after(
    slots, cells, acc_in, probe_re, probe_im, table, frames, marks, by_inner, by_outer,
    acc, order, power, whole, places, sem,
):
    rows, width = acc.shape[1:]
    before, after = received(by_inner, by_outer, "col")
    for i, part in enumerate((before[-MARKS:], marks[...], after[-MARKS:])):
        whole[i] = reaching(part, i - 1, rows - 2 * HALO, width - 2 * LANES)
    copy = pltpu.make_async_copy(whole, places, sem)
    copy.start()
    power[...] = probe_re[...] * probe_re[...] + probe_im[...] * probe_im[...]
    run_windows(AFTER, slots, cells, acc, probe_re, probe_im, table, frames, order)
    copy.wait()
    add_neighbours_light(places, acc, power)


def windows_over_edge(
    marked, cells_in, acc_in, probe_re, probe_im, table, frames, by_inner, by_outer,
    cells, acc, to_outer, to_inner, order, slots, sem,
):
    scalars = pltpu.make_async_copy(marked, slots, sem)
    scalars.start()
    rows, width = acc.shape[1:]
    before, after = received(by_inner, by_outer, "col")
    for tile, packed in ((slice(0, LANES), before), (slice(width - LANES, width), after)):
        for layer, row, part in pieces(packed, rows):
            cells[layer, row : row + part.shape[0], tile] = part
    scalars.wait()
    run_windows(OVER, slots, cells, acc, probe_re, probe_im, table, frames, order)
    odd = is_odd("row")
    strips = []
    for here in (slice(0, HALO), slice(rows - HALO, rows)):
        middle = [acc[k, here, LANES : width - LANES] for k in (0, 1)]
        strips.append(below(*middle, pack_corners(acc, here)))
    to_inner[...] = jnp.where(odd, strips[0], strips[1])
    to_outer[...] = jnp.where(odd, strips[1], strips[0])


def column_spill(acc_in, by_outer, by_inner, acc, to_inner, to_outer):
    rows, width = acc.shape[1:]
    before, after = received(by_inner, by_outer, "row")
    for start, came in ((HALO, before), (rows - 2 * HALO, after)):
        here = slice(start, start + HALO)
        for k in (0, 1):
            acc[k, here, LANES : width - LANES] += came[k * HALO : (k + 1) * HALO]
        for k, left, right in unpack_corners(came[2 * HALO :]):
            acc[k, here, 0:LANES] += left
            acc[k, here, width - LANES :] += right
    tile_r = rows - 2 * HALO
    to_left = pack_lanes(acc, HALO, tile_r, slice(0, LANES), LANES - HALO)
    to_right = pack_lanes(acc, HALO, tile_r, slice(width - LANES, width), 0)
    send_columns(to_left, to_right, to_inner, to_outer)


def new_columns(cells, acc, spill, start, size, near_re, near_im):
    rows = acc.shape[1]
    here, there = slice(HALO, rows - HALO), slice(LANES + start, LANES + start + size)
    part = [acc[k, here, there] for k in range(acc.shape[0])]
    if spill is not None:
        part[:2] = [part[k] + spill[k] for k in (0, 1)]
    scale = 1.0 / (part[2] + ridge)
    near_re[:, start : start + size] = cells[0, here, there] - part[0] * scale
    near_im[:, start : start + size] = cells[1, here, there] - part[1] * scale


def finish_inner(
    slots, cells, acc_in, probe_re, probe_im, table, frames, acc, new_re, new_im, order, near_re, near_im, sems,
):
    run_windows(LAST, slots, cells, acc, probe_re, probe_im, table, frames, order)
    size = near_re.shape[1] - 2 * LANES
    new_columns(cells, acc, None, LANES, size, near_re, near_im)
    there = slice(LANES, LANES + size)
    finish_all(fetch([(near_re.at[:, there], new_re.at[:, there]), (near_im.at[:, there], new_im.at[:, there])], sems))


def finish_edges(cells, acc, by_inner, by_outer, re_in, im_in, new_re, new_im, near_re, near_im, sems):
    tile_r, tile_c = near_re.shape
    lane = lane_index(tile_r)
    sides = ((0, lane < HALO), (tile_c - LANES, lane >= LANES - HALO))
    copies = []
    for i, ((start, mine), packed) in enumerate(zip(sides, received(by_inner, by_outer, "col"))):
        parts = [part for _, _, part in pieces(packed, tile_r)]
        spill = [jnp.where(mine, below(*parts[2 * k : 2 * k + 2]), 0.0) for k in (0, 1)]
        new_columns(cells, acc, spill, start, LANES, near_re, near_im)
        there = slice(start, start + LANES)
        pairs = ((near_re.at[:, there], new_re.at[:, there]), (near_im.at[:, there], new_im.at[:, there]))
        copies += fetch(pairs, sems.at[2 * i : 2 * i + 2])
    finish_all(copies)


def swap(to_inner, to_outer, axis):
    devices = lax.axis_size(axis)
    inner = [(i, i + 1) for i in range(0, devices, 2)]
    partner = {i: i + 1 if i % 2 else i - 1 for i in range(1, devices - 1)}
    n_row, n_col = lax.axis_size("row"), lax.axis_size("col")
    pairs = []
    for row in range(n_row):
        for col in range(n_col):
            if axis == "row":
                there = (partner[row], col) if row in partner else (row, col ^ 1)
            else:
                there = (row, partner[col]) if col in partner else (row ^ 1, col)
            pairs.append((row * n_col + col, there[0] * n_col + there[1]))
    by_inner = lax.ppermute(to_inner, axis, inner + [(j, i) for i, j in inner])
    by_outer = lax.ppermute(to_outer, ("row", "col"), pairs)
    return by_inner, by_outer


def far(x):
    return pltpu.with_memory_space_constraint(x, pltpu.HBM)


def f32(*shape):
    return jax.ShapeDtypeStruct(shape, jnp.float32)


def shards(object_re, object_im, probe_re, probe_im, frames, counts, offsets, frame_index):
    tile_r, tile_c = object_re.shape
    rows, width = tile_r + 2 * HALO, tile_c + 2 * LANES
    layers = 3
    slots = offsets.shape[2]
    table = jnp.asarray(transform_tables())
    frames = frames.reshape(frames.shape[2:])
    cells_shape, acc_shape = f32(2, rows, width), f32(layers, rows, width)
    dma = pltpu.SemaphoreType.DMA

    places = jnp.swapaxes(offsets, 2, 3)
    edge = f32(2 * HALO * (tile_c // LANES) + MARKS, LANES)
    to_outer, to_inner, marked = pl.pallas_call(
        row_edges,
        out_shape=(edge, edge, jax.ShapeDtypeStruct((3, slots), jnp.int32)),
        in_specs=[SMEM] + [HBM] * 4,
        out_specs=(VMEM, VMEM, VMEM),
        scratch_shapes=[
            pltpu.VMEM(places.shape, jnp.int32), pltpu.VMEM(frame_index.shape, jnp.int32),
            dma((2 + 4 * (tile_c // LANES),)),
        ],
        compiler_params=SMALL,
        name="row_edges",
    )(counts, far(object_re), far(object_im), far(places), far(frame_index))
    by_inner, by_outer = swap(to_inner, to_outer, "row")

    order = pltpu.SMEM((slots,), jnp.int32)
    cells, acc, *fixed = pl.pallas_call(
        windows_first,
        out_shape=(
            cells_shape, acc_shape, f32(*probe_re.shape), f32(*probe_im.shape),
            jax.ShapeDtypeStruct(table.shape, table.dtype), jax.ShapeDtypeStruct(frames.shape, frames.dtype),
        ),
        in_specs=[SMEM] + [HBM] * 6,
        out_specs=(VMEM,) * 6,
        scratch_shapes=[order, dma((6,))],
        compiler_params=PARAMS,
        cost_estimate=BUSY,
        name="windows_first",
    )(marked, *map(far, (object_re, object_im, probe_re, probe_im, table, frames)))

    packed = f32(rows // 2 + MARKS, LANES)
    cells, marks, to_inner, to_outer = pl.pallas_call(
        row_halos,
        out_shape=(cells_shape, f32(MARKS, LANES), packed, packed),
        in_specs=[VMEM] * 4,
        out_specs=(VMEM,) * 4,
        input_output_aliases={0: 0},
        compiler_params=SMALL,
        name="row_halos",
    )(cells, to_outer, by_outer, by_inner)
    edges = swap(to_inner, to_outer, "col")

    acc = pl.pallas_call(
        windows_before,
        out_shape=acc_shape,
        in_specs=[SMEM] + [VMEM] * 6,
        out_specs=VMEM,
        scratch_shapes=[order, pltpu.VMEM(probe_re.shape, jnp.float32)],
        input_output_aliases={2: 0},
        compiler_params=PARAMS,
        cost_estimate=BUSY,
        name="windows_before",
    )(marked, cells, acc, *fixed)

    edge = f32(2 * HALO + MARKS, tile_c)
    cells, acc, to_outer, to_inner = pl.pallas_call(
        windows_over_edge,
        out_shape=(cells_shape, acc_shape, edge, edge),
        in_specs=[VMEM] * 9,
        out_specs=(VMEM,) * 4,
        scratch_shapes=[order, pltpu.SMEM((3, slots), jnp.int32), dma(())],
        input_output_aliases={1: 0, 2: 1},
        compiler_params=PARAMS,
        cost_estimate=BUSY,
        name="windows_over_edge",
    )(marked, cells, acc, *fixed, *edges)
    by_inner, by_outer = swap(to_inner, to_outer, "row")

    acc = pl.pallas_call(
        windows_after,
        out_shape=acc_shape,
        in_specs=[SMEM] + [VMEM] * 9,
        out_specs=VMEM,
        scratch_shapes=[
            order, pltpu.VMEM(probe_re.shape, jnp.float32),
            pltpu.VMEM((3, MARKS, LANES), jnp.int32), pltpu.SMEM((3, MARKS, LANES), jnp.int32), dma(()),
        ],
        input_output_aliases={2: 0},
        compiler_params=PARAMS,
        cost_estimate=BUSY,
        name="windows_after",
    )(marked, cells, acc, *fixed, marks, *edges)

    packed = f32(tile_r // 2, LANES)
    acc, to_inner, to_outer = pl.pallas_call(
        column_spill,
        out_shape=(acc_shape, packed, packed),
        in_specs=[VMEM] * 3,
        out_specs=(VMEM,) * 3,
        input_output_aliases={0: 0},
        compiler_params=SMALL,
        name="column_spill",
    )(acc, by_outer, by_inner)
    by_inner, by_outer = swap(to_inner, to_outer, "col")

    near = [pltpu.VMEM((tile_r, tile_c), jnp.float32)] * 2
    new = (f32(tile_r, tile_c), f32(tile_r, tile_c))
    acc, new_re, new_im = pl.pallas_call(
        finish_inner,
        out_shape=(acc_shape, *new),
        in_specs=[SMEM] + [VMEM] * 6,
        out_specs=(VMEM, HBM, HBM),
        scratch_shapes=[order] + near + [dma((2,))],
        input_output_aliases={2: 0},
        compiler_params=PARAMS,
        cost_estimate=BUSY,
        name="finish_inner",
    )(marked, cells, acc, *fixed)
    return pl.pallas_call(
        finish_edges,
        out_shape=new,
        in_specs=[VMEM] * 4 + [HBM] * 2,
        out_specs=(HBM, HBM),
        scratch_shapes=near + [dma((4,))],
        input_output_aliases={4: 0, 5: 1},
        compiler_params=SMALL,
        name="finish_edges",
    )(cells, acc, by_inner, by_outer, far(new_re), far(new_im))


def solution(mesh):
    return jax.shard_map(
        shards,
        mesh=mesh,
        in_specs=(
            P("row", "col"),
            P("row", "col"),
            P(),
            P(),
            P("row", "col", None, None, None),
            P("row", "col"),
            P("row", "col", None, None),
            P("row", "col", None),
        ),
        out_specs=(P("row", "col"), P("row", "col")),
        check_vma=False,
    )
```

```python
import functools
import math

import jax
import jax.numpy as jnp
import ml_dtypes
import numpy as np
from jax import lax
from jax.experimental import pallas as pl
from jax.experimental.pallas import tpu as pltpu
from jax.sharding import PartitionSpec as P

P_SIZE = 256
HALF = P_SIZE // 2
HALO = 32
LANES = 128
GROUPS = LANES // HALO
MARKS = 8
PAIR = 2

floor_amp = 0.5
ridge = 1.0

VMEM = pl.BlockSpec(memory_space=pltpu.VMEM)
SMEM = pl.BlockSpec(memory_space=pltpu.SMEM)
HBM = pl.BlockSpec(memory_space=pltpu.HBM)
PARAMS = pltpu.CompilerParams(vmem_limit_bytes=32 * 1024 * 1024)
SMALL = pltpu.CompilerParams(vmem_limit_bytes=16 * 1024 * 1024)
BUSY = pl.CostEstimate(flops=4_000_000_000, bytes_accessed=8_000_000, transcendentals=0)


def transform_tables():
    index = np.arange(HALF)
    plain = []
    for parity in (0, 1):
        angle = 2.0 * math.pi / P_SIZE * (index[:, None] * (2 * index[None, :] + parity) % P_SIZE)
        cos, sin = np.cos(angle), np.sin(angle)
        plain.append(np.block([[cos, -sin], [sin, cos]]) / math.sqrt(P_SIZE))
    parts = []
    for table in plain + [t.T for t in plain]:
        high = table.astype(np.float32).astype(ml_dtypes.bfloat16)
        low = (table - high.astype(np.float64)).astype(np.float32).astype(ml_dtypes.bfloat16)
        parts += [high, low]
    order = np.concatenate([np.arange(0, P_SIZE, 2), np.arange(1, P_SIZE, 2)])
    sort = np.zeros((P_SIZE, P_SIZE), np.float32)
    sort[np.arange(P_SIZE), order] = 1.0
    parts += [sort.astype(ml_dtypes.bfloat16), sort.T.astype(ml_dtypes.bfloat16)]
    return np.stack(parts)


def lane_index(rows):
    return lax.broadcasted_iota(jnp.int32, (rows, LANES), 1)


def pack_lanes(field, top, size, tile, first):
    half = size // 2
    lane = lane_index(half)
    packed = None
    for g in range(GROUPS):
        start = top + g % 2 * half
        part = field[g // 2, start : start + half, tile]
        if g:
            part = pltpu.roll(part, HALO * g, 1)
        low = (first + HALO * g) % LANES
        mine = (lane >= low) & (lane < low + HALO)
        packed = part if packed is None else jnp.where(mine, part, packed)
    return packed


def unpack_lanes(packed, group):
    return pltpu.roll(packed, LANES - HALO * group, 1) if group else packed


def split(x):
    high = x.astype(jnp.bfloat16)
    return high, (x - high.astype(jnp.float32)).astype(jnp.bfloat16)


def product(left, right):
    return jnp.dot(left, right, preferred_element_type=jnp.float32)


def times_table(x, table, which):
    high, low = split(x)
    t_high, t_low = table[2 * which], table[2 * which + 1]
    return product(beside(high, high, low), below(t_high, t_low, t_high))


def table_times(table, which, x):
    high, low = split(x)
    t_high, t_low = table[2 * which], table[2 * which + 1]
    return product(beside(t_high, t_low, t_high), below(high, high, low))


def beside(*blocks):
    return jnp.concatenate(blocks, axis=1)


def below(*blocks):
    return jnp.concatenate(blocks, axis=0)


def ends(x):
    return x[:, :HALF], x[:, HALF:]


def forward_columns(exit_re, exit_im, table):
    re_lo, re_hi = ends(exit_re)
    im_lo, im_hi = ends(exit_im)
    even = times_table(beside(re_lo + re_hi, im_lo + im_hi), table, 0)
    odd = times_table(beside(re_lo - re_hi, im_lo - im_hi), table, 1)
    return even, odd


def forward_rows(even, odd, table):
    out = []
    for parity in (0, 1):
        if parity == 0:
            se, so = even[:HALF] + even[HALF:], odd[:HALF] + odd[HALF:]
        else:
            se, so = even[:HALF] - even[HALF:], odd[:HALF] - odd[HALF:]
        e_re, e_im = ends(se)
        o_re, o_im = ends(so)
        out.append(table_times(table, 2 + parity, below(beside(e_re, o_re), beside(e_im, o_im))))
    return out


def residual(far, frame):
    out = []
    for parity in (0, 1):
        re, im = far[parity][:HALF], far[parity][HALF:]
        level = jnp.maximum(re * re + im * im, floor_amp * floor_amp)
        inten = frame[parity * HALF : (parity + 1) * HALF]
        factor = 1.0 - inten * lax.rsqrt(inten * level)
        out.append(below(re * factor, im * factor))
    return out


def back_rows(res, table):
    first = table_times(table, 0, res[0])
    second = table_times(table, 1, res[1])
    upper, lower = first + second, first - second
    out = []
    for cols in (slice(0, HALF), slice(HALF, P_SIZE)):
        out.append(
            below(
                beside(upper[:HALF, cols], upper[HALF:, cols]),
                beside(lower[:HALF, cols], lower[HALF:, cols]),
            )
        )
    return out


def back_columns(parts, table):
    even = times_table(parts[0], table, 2)
    odd = times_table(parts[1], table, 3)
    lo, hi = even + odd, even - odd
    return beside(lo[:, :HALF], hi[:, :HALF]), beside(lo[:, HALF:], hi[:, HALF:])


def is_odd(axis):
    return lax.rem(lax.axis_index(axis), 2) == 1


def fetch(pairs, sems):
    copies = [pltpu.make_async_copy(far, near, sems.at[i]) for i, (far, near) in enumerate(pairs)]
    for copy in copies:
        copy.start()
    return copies


def finish_all(copies):
    for copy in copies:
        copy.wait()


def row_edges(counts, obj_re, obj_im, offsets, chosen, to_outer, to_inner, marked, places, frame_of, sems):
    tile_r = obj_re.shape[0]
    odd = is_odd("row")
    low = pl.multiple_of(jnp.where(odd, 0, tile_r - HALO), 16)
    high = pl.multiple_of(jnp.where(odd, tile_r - HALO, 0), 16)
    pairs = [(offsets, places), (chosen, frame_of)]
    tiles = obj_re.shape[1] // LANES
    for k, ref in enumerate((obj_re, obj_im)):
        for t in range(tiles):
            lanes = slice(t * LANES, (t + 1) * LANES)
            rows = slice((2 * t + k) * HALO, (2 * t + k + 1) * HALO)
            pairs.append((ref.at[pl.ds(high, HALO), lanes], to_outer.at[rows]))
            pairs.append((ref.at[pl.ds(low, HALO), lanes], to_inner.at[rows]))
    copies = fetch(pairs, sems)
    finish_all(copies[:2])
    place = places[0, 0]
    live = lax.broadcasted_iota(jnp.int32, place.shape, 1) < counts[0, 0]
    place = jnp.where(live, place, 2 * tile_r)
    marked[0:2, :] = place
    marked[2:3, :] = frame_of[0]
    for message in (to_inner, to_outer):
        first = 2 * HALO * tiles
        message[first : first + 2, 0 : place.shape[1]] = place.astype(jnp.float32)
    finish_all(copies[2:])


def window_place(slots, slot):
    row = pl.multiple_of(slots[0, slot] + HALO, 16)
    col = slots[1, slot] + LANES
    turn = lax.rem(col, LANES)
    return row, pl.multiple_of(col - turn, LANES), turn


def add_window(acc, layer, where, keep, term, tiles=(0, 1, 2)):
    row, base, _ = where
    lo, hi = ends(term)
    parts = (jnp.where(keep, lo, 0.0), hi, jnp.where(keep, 0.0, lo))
    for t in tiles:
        acc[layer, pl.ds(row, term.shape[0]), pl.ds(base + t * LANES, LANES)] += parts[t]


def send_columns(to_left, to_right, to_inner, to_outer):
    odd = is_odd("col")
    to_inner[0 : to_left.shape[0], :] = jnp.where(odd, to_left, to_right)
    to_outer[0 : to_left.shape[0], :] = jnp.where(odd, to_right, to_left)


def received(by_inner, by_outer, axis):
    odd = is_odd(axis)
    index = lax.axis_index(axis)
    inside = (index > 0) & (index < lax.axis_size(axis) - 1)
    by_outer = jnp.where(inside, by_outer[...], 0.0)
    by_inner = by_inner[...]
    return jnp.where(odd, by_inner, by_outer), jnp.where(odd, by_outer, by_inner)


def pieces(packed, size):
    half = size // 2
    for g in range(GROUPS):
        yield g // 2, g % 2 * half, unpack_lanes(packed[:half], g)


def pack_corners(field, rows):
    width = field.shape[2]
    left = [field[k, rows, 0:LANES] for k in (0, 1)]
    right = [field[k, rows, width - LANES : width] for k in (0, 1)]
    lane = lane_index(HALO)
    low = jnp.where(lane < HALO, right[0], pltpu.roll(right[1], HALO, 1))
    high = jnp.where(lane < 3 * HALO, pltpu.roll(left[1], 3 * HALO, 1), left[0])
    packed = jnp.where(lane < 2 * HALO, low, high)
    return beside(*(packed[i : i + MARKS] for i in range(0, HALO, MARKS)))


def unpack_corners(packed):
    packed = below(*(packed[:, i : i + LANES] for i in range(0, GROUPS * LANES, LANES)))
    lane = lane_index(HALO)
    for k, left, right in ((0, 0, 0), (1, HALO, 3 * HALO)):
        yield (
            k,
            jnp.where(lane >= 3 * HALO, pltpu.roll(packed, left, 1) if left else packed, 0.0),
            jnp.where(lane < HALO, pltpu.roll(packed, right, 1) if right else packed, 0.0),
        )


def row_halos(cells_in, own, by_outer, by_inner, cells, marks, to_inner, to_outer):
    rows, width = cells.shape[1:]
    before, after = received(by_inner, by_outer, "row")
    tiles = width // LANES - 2
    for k in (0, 1):
        for t in range(tiles):
            lanes = slice((t + 1) * LANES, (t + 2) * LANES)
            part = slice((2 * t + k) * HALO, (2 * t + k + 1) * HALO)
            cells[k, 0:HALO, lanes] = before[part]
            cells[k, rows - HALO : rows, lanes] = after[part]
    first = 2 * HALO * tiles
    for i, message in enumerate((own[...], before, after)):
        marks[2 * i : 2 * i + 2, :] = message[first : first + 2]
    half = rows // 2
    to_left = pack_lanes(cells, 0, rows, slice(LANES, 2 * LANES), 0)
    to_right = pack_lanes(cells, 0, rows, slice(width - 2 * LANES, width - LANES), LANES - HALO)
    send_columns(to_left, to_right, to_inner, to_outer)
    to_inner[half:, :] = marks[...]
    to_outer[half:, :] = marks[...]


def live_slots(slots, cells):
    tile_r = cells.shape[1] - 2 * HALO
    count = jnp.int32(0)
    for slot in range(slots.shape[1]):
        count += (slots[0, slot] < tile_r).astype(jnp.int32)
    return count


FIRST, BEFORE, OVER, AFTER, LAST = range(5)


def run_windows(phase, slots, cells, acc, probe_re, probe_im, table, frames, order):
    tile_r, tile_c = cells.shape[1] - 2 * HALO, cells.shape[2] - 2 * LANES
    count = live_slots(slots, cells)
    kinds = []
    n_inside, n_row, n_col = jnp.int32(0), jnp.int32(0), jnp.int32(0)
    for slot in range(slots.shape[1]):
        row, col = slots[0, slot], slots[1, slot]
        live = slot < count
        over_col = (col < 0) | (col > tile_c - P_SIZE)
        over_row = (row < 0) | (row > tile_r - P_SIZE)
        inside, by_row = live & ~over_col & ~over_row, live & ~over_col & over_row
        by_col, by_both = live & over_col & ~over_row, live & over_col & over_row
        kinds.append((inside, by_row, by_col, by_both, n_inside, n_row))
        n_inside += inside.astype(jnp.int32)
        n_row += by_row.astype(jnp.int32)
        n_col += by_col.astype(jnp.int32)
    first = jnp.minimum(n_inside, PAIR)
    before = first + jnp.minimum(n_inside - first, PAIR - jnp.minimum(n_row, PAIR))
    rest = n_inside - before
    after = n_inside - jnp.clip(n_col + rest - 2 * PAIR, 0, jnp.minimum(rest, PAIR))
    found = jnp.int32(0)
    for slot, (inside, by_row, by_col, by_both, rank, row_rank) in enumerate(kinds):
        mine = {
            FIRST: lambda: inside & (rank < first),
            BEFORE: lambda: (by_row & (row_rank < PAIR)) | (inside & (rank >= first) & (rank < before)),
            OVER: lambda: by_both | (by_row & (row_rank >= PAIR)),
            AFTER: lambda: by_col | (inside & (rank >= before) & (rank < after)),
            LAST: lambda: inside & (rank >= after),
        }[phase]()

        @pl.when(mine)
        def _():
            order[found] = slot

        found += mine.astype(jnp.int32)

    lane = lane_index(P_SIZE)

    def load(slot):
        where = row, base, turn = window_place(slots, slot)
        keep = lane >= turn
        w_re = pltpu.roll(probe_re[...], turn, 1)
        w_im = pltpu.roll(probe_im[...], turn, 1)
        patch = []
        for k in (0, 1):
            block = cells[k, pl.ds(row, P_SIZE), pl.ds(base, 3 * LANES)]
            patch.append(
                beside(jnp.where(keep, block[:, :LANES], block[:, 2 * LANES :]), block[:, LANES : 2 * LANES])
            )
        exit_re = w_re * patch[0] - w_im * patch[1]
        exit_im = w_re * patch[1] + w_im * patch[0]
        return (where, keep, w_re, w_im), exit_re, exit_im

    def frame_of(slot):
        half = product(table[8], frames[slots[2, slot]]).astype(jnp.bfloat16)
        return product(half, table[9])

    def place(at, back_re, back_im):
        where, keep, w_re, w_im = at
        add_window(acc, 0, where, keep, w_re * back_re + w_im * back_im)
        add_window(acc, 1, where, keep, w_re * back_im - w_im * back_re)

    def rows_of(stacked):
        return [stacked[i : i + P_SIZE] for i in range(0, stacked.shape[0], P_SIZE)]

    def step(group):
        frame = [frame_of(slot) for slot in group]
        loaded = [load(slot) for slot in group]
        stacked = forward_columns(below(*(x[1] for x in loaded)), below(*(x[2] for x in loaded)), table)
        state = [forward_rows(*x, table) for x in zip(*map(rows_of, stacked))]
        state = [residual(x, f) for x, f in zip(state, frame)]
        state = [back_rows(x, table) for x in state]
        stacked = back_columns([below(*parts) for parts in zip(*state)], table)
        for x, back in zip(loaded, zip(*map(rows_of, stacked))):
            place(x[0], *back)

    def pair_step(pair, carry):
        step([order[pair * PAIR + i] for i in range(PAIR)])
        return carry

    lax.fori_loop(0, found // PAIR, pair_step, 0)

    @pl.when(found % PAIR == 1)
    def _():
        step([order[found - 1]])


def windows_first(
    slots, obj_re, obj_im, probe_re_far, probe_im_far, table_far, frames_far,
    cells, acc, probe_re, probe_im, table, frames, order, sems,
):
    tile_r, tile_c = obj_re.shape
    inner = slice(HALO, HALO + tile_r)
    middle = slice(LANES, LANES + tile_c)
    pairs = (
        (table_far, table),
        (frames_far, frames),
        (obj_re, cells.at[0, inner, middle]),
        (obj_im, cells.at[1, inner, middle]),
        (probe_re_far, probe_re),
        (probe_im_far, probe_im),
    )
    copies = fetch(pairs, sems)
    acc[...] = jnp.zeros_like(acc)
    finish_all(copies)
    run_windows(FIRST, slots, cells, acc, probe_re, probe_im, table, frames, order)


def windows_before(
    slots, cells, acc_in, probe_re, probe_im, table, frames, acc, order, power,
):
    power[...] = probe_re[...] * probe_re[...] + probe_im[...] * probe_im[...]
    lane = lane_index(P_SIZE)

    def step(slot, carry):
        where = window_place(slots, slot)
        add_window(acc, 2, where, lane >= where[2], pltpu.roll(power[...], where[2], 1))
        return carry

    lax.fori_loop(0, live_slots(slots, cells), step, 0)
    run_windows(BEFORE, slots, cells, acc, probe_re, probe_im, table, frames, order)


def reaching(place, right, tile_r, tile_c):
    shape = place.shape
    index = lax.broadcasted_iota(jnp.int32, shape, 0)
    lane = lax.broadcasted_iota(jnp.int32, shape, 1)
    col = pltpu.roll(place, shape[0] - 1, 0)
    low = jnp.where(index == 2, tile_r - P_SIZE, -tile_r).astype(jnp.float32)
    high = jnp.where(index == 4, 0, tile_r).astype(jnp.float32)
    reaches = (lane < MARKS) & (index % 2 == 0) & (index < 6) & (place > low) & (place < high)
    if right < 0:
        reaches &= col > tile_c - P_SIZE
    if right > 0:
        reaches &= col < 0
    bit = lax.shift_left(jnp.ones(shape, jnp.int32), jnp.minimum(lane, MARKS)).astype(jnp.float32)
    bits = jnp.sum(jnp.where(reaches, bit, 0.0), axis=1, keepdims=True)
    return jnp.where(lane < MARKS, place, bits).astype(jnp.int32)


def add_neighbours_light(places, acc, power):
    rows, width = acc.shape[1:]
    tile_r, tile_c = rows - 2 * HALO, width - 2 * LANES
    for right in (-1, 0, 1):
        for i, down in enumerate((0, -1, 1)):
            if not right and not down:
                continue
            first, last = {-1: (P_SIZE - HALO, P_SIZE), 0: (0, P_SIZE), 1: (0, HALO)}[down]
            tiles = {-1: (2,), 0: (0, 1, 2), 1: (0,)}[right]
            lane = lane_index(last - first)
            bits = places[right + 1, 2 * i, MARKS]

            def step(slot, carry):
                row, col = places[right + 1, 2 * i, slot], places[right + 1, 2 * i + 1, slot]

                @pl.when(lax.shift_right_logical(bits, slot) % 2 == 1)
                def _():
                    turn = lax.rem(col + LANES, LANES)
                    at = pl.multiple_of(row + HALO + (down * tile_r + first), 16)
                    base = pl.multiple_of(col + LANES - turn + right * tile_c, LANES)
                    part = pltpu.roll(power[first:last, :], turn, 1)
                    add_window(acc, 2, (at, base, turn), lane >= turn, part, tiles)

                return carry

            @pl.when(bits != 0)
            def _():
                lax.fori_loop(0, MARKS, step, 0)


def windows_after(
    slots, cells, acc_in, probe_re, probe_im, table, frames, marks, by_inner, by_outer,
    acc, order, power, whole, places, sem,
):
    rows, width = acc.shape[1:]
    before, after = received(by_inner, by_outer, "col")
    for i, part in enumerate((before[-MARKS:], marks[...], after[-MARKS:])):
        whole[i] = reaching(part, i - 1, rows - 2 * HALO, width - 2 * LANES)
    copy = pltpu.make_async_copy(whole, places, sem)
    copy.start()
    power[...] = probe_re[...] * probe_re[...] + probe_im[...] * probe_im[...]
    run_windows(AFTER, slots, cells, acc, probe_re, probe_im, table, frames, order)
    copy.wait()
    add_neighbours_light(places, acc, power)


def windows_over_edge(
    marked, cells_in, acc_in, probe_re, probe_im, table, frames, by_inner, by_outer,
    cells, acc, to_outer, to_inner, order, slots, sem,
):
    scalars = pltpu.make_async_copy(marked, slots, sem)
    scalars.start()
    rows, width = acc.shape[1:]
    before, after = received(by_inner, by_outer, "col")
    for tile, packed in ((slice(0, LANES), before), (slice(width - LANES, width), after)):
        for layer, row, part in pieces(packed, rows):
            cells[layer, row : row + part.shape[0], tile] = part
    scalars.wait()
    run_windows(OVER, slots, cells, acc, probe_re, probe_im, table, frames, order)
    odd = is_odd("row")
    strips = []
    for here in (slice(0, HALO), slice(rows - HALO, rows)):
        middle = [acc[k, here, LANES : width - LANES] for k in (0, 1)]
        strips.append(below(*middle, pack_corners(acc, here)))
    to_inner[...] = jnp.where(odd, strips[0], strips[1])
    to_outer[...] = jnp.where(odd, strips[1], strips[0])


def column_spill(acc_in, by_outer, by_inner, acc, to_inner, to_outer):
    rows, width = acc.shape[1:]
    before, after = received(by_inner, by_outer, "row")
    for start, came in ((HALO, before), (rows - 2 * HALO, after)):
        here = slice(start, start + HALO)
        for k in (0, 1):
            acc[k, here, LANES : width - LANES] += came[k * HALO : (k + 1) * HALO]
        for k, left, right in unpack_corners(came[2 * HALO :]):
            acc[k, here, 0:LANES] += left
            acc[k, here, width - LANES :] += right
    tile_r = rows - 2 * HALO
    to_left = pack_lanes(acc, HALO, tile_r, slice(0, LANES), LANES - HALO)
    to_right = pack_lanes(acc, HALO, tile_r, slice(width - LANES, width), 0)
    send_columns(to_left, to_right, to_inner, to_outer)


def new_columns(cells, acc, spill, top, tall, start, size, near_re, near_im):
    here, there = slice(HALO + top, HALO + top + tall), slice(LANES + start, LANES + start + size)
    part = [acc[k, here, there] for k in range(acc.shape[0])]
    if spill is not None:
        part[:2] = [part[k] + spill[k] for k in (0, 1)]
    scale = 1.0 / (part[2] + ridge)
    near_re[top : top + tall, start : start + size] = cells[0, here, there] - part[0] * scale
    near_im[top : top + tall, start : start + size] = cells[1, here, there] - part[1] * scale


def finish_inner(
    slots, cells, acc_in, probe_re, probe_im, table, frames, acc, new_re, new_im, order, near_re, near_im, sems,
):
    run_windows(LAST, slots, cells, acc, probe_re, probe_im, table, frames, order)
    size = near_re.shape[1] - 2 * LANES
    new_columns(cells, acc, None, 0, near_re.shape[0], LANES, size, near_re, near_im)
    there = slice(LANES, LANES + size)
    finish_all(fetch([(near_re.at[:, there], new_re.at[:, there]), (near_im.at[:, there], new_im.at[:, there])], sems))


def finish_edges(cells, acc, by_inner, by_outer, re_in, im_in, new_re, new_im, near_re, near_im, sems):
    tile_r, tile_c = near_re.shape
    half = tile_r // 2
    lane = lane_index(half)
    sides = ((0, lane < HALO), (tile_c - LANES, lane >= LANES - HALO))
    copies = []
    for i, ((start, mine), packed) in enumerate(zip(sides, received(by_inner, by_outer, "col"))):
        parts = [jnp.where(mine, part, 0.0) for _, _, part in pieces(packed, tile_r)]
        there = slice(start, start + LANES)
        for j in (0, 1):
            new_columns(cells, acc, (parts[j], parts[2 + j]), j * half, half, start, LANES, near_re, near_im)
            rows = slice(j * half, (j + 1) * half)
            pairs = ((near_re.at[rows, there], new_re.at[rows, there]), (near_im.at[rows, there], new_im.at[rows, there]))
            copies += fetch(pairs, sems.at[4 * i + 2 * j : 4 * i + 2 * j + 2])
    finish_all(copies)


def swap(to_inner, to_outer, axis):
    devices = lax.axis_size(axis)
    inner = [(i, i + 1) for i in range(0, devices, 2)]
    partner = {i: i + 1 if i % 2 else i - 1 for i in range(1, devices - 1)}
    n_row, n_col = lax.axis_size("row"), lax.axis_size("col")
    pairs = []
    for row in range(n_row):
        for col in range(n_col):
            if axis == "row":
                there = (partner[row], col) if row in partner else (row, col ^ 1)
            else:
                there = (row, partner[col]) if col in partner else (row ^ 1, col)
            pairs.append((row * n_col + col, there[0] * n_col + there[1]))
    by_inner = lax.ppermute(to_inner, axis, inner + [(j, i) for i, j in inner])
    by_outer = lax.ppermute(to_outer, ("row", "col"), pairs)
    return by_inner, by_outer


def far(x):
    return pltpu.with_memory_space_constraint(x, pltpu.HBM)


def f32(*shape):
    return jax.ShapeDtypeStruct(shape, jnp.float32)


def shards(object_re, object_im, probe_re, probe_im, frames, counts, offsets, frame_index):
    tile_r, tile_c = object_re.shape
    rows, width = tile_r + 2 * HALO, tile_c + 2 * LANES
    layers = 3
    slots = offsets.shape[2]
    table = jnp.asarray(transform_tables())
    frames = frames.reshape(frames.shape[2:])
    cells_shape, acc_shape = f32(2, rows, width), f32(layers, rows, width)
    dma = pltpu.SemaphoreType.DMA

    places = jnp.swapaxes(offsets, 2, 3)
    edge = f32(2 * HALO * (tile_c // LANES) + MARKS, LANES)
    to_outer, to_inner, marked = pl.pallas_call(
        row_edges,
        out_shape=(edge, edge, jax.ShapeDtypeStruct((3, slots), jnp.int32)),
        in_specs=[SMEM] + [HBM] * 4,
        out_specs=(VMEM, VMEM, VMEM),
        scratch_shapes=[
            pltpu.VMEM(places.shape, jnp.int32), pltpu.VMEM(frame_index.shape, jnp.int32),
            dma((2 + 4 * (tile_c // LANES),)),
        ],
        compiler_params=SMALL,
        name="row_edges",
    )(counts, far(object_re), far(object_im), far(places), far(frame_index))
    by_inner, by_outer = swap(to_inner, to_outer, "row")

    order = pltpu.SMEM((slots,), jnp.int32)
    cells, acc, *fixed = pl.pallas_call(
        windows_first,
        out_shape=(
            cells_shape, acc_shape, f32(*probe_re.shape), f32(*probe_im.shape),
            jax.ShapeDtypeStruct(table.shape, table.dtype), jax.ShapeDtypeStruct(frames.shape, frames.dtype),
        ),
        in_specs=[SMEM] + [HBM] * 6,
        out_specs=(VMEM,) * 6,
        scratch_shapes=[order, dma((6,))],
        compiler_params=PARAMS,
        cost_estimate=BUSY,
        name="windows_first",
    )(marked, *map(far, (object_re, object_im, probe_re, probe_im, table, frames)))

    packed = f32(rows // 2 + MARKS, LANES)
    cells, marks, to_inner, to_outer = pl.pallas_call(
        row_halos,
        out_shape=(cells_shape, f32(MARKS, LANES), packed, packed),
        in_specs=[VMEM] * 4,
        out_specs=(VMEM,) * 4,
        input_output_aliases={0: 0},
        compiler_params=SMALL,
        name="row_halos",
    )(cells, to_outer, by_outer, by_inner)
    edges = swap(to_inner, to_outer, "col")

    acc = pl.pallas_call(
        windows_before,
        out_shape=acc_shape,
        in_specs=[SMEM] + [VMEM] * 6,
        out_specs=VMEM,
        scratch_shapes=[order, pltpu.VMEM(probe_re.shape, jnp.float32)],
        input_output_aliases={2: 0},
        compiler_params=PARAMS,
        cost_estimate=BUSY,
        name="windows_before",
    )(marked, cells, acc, *fixed)

    edge = f32(2 * HALO + MARKS, tile_c)
    cells, acc, to_outer, to_inner = pl.pallas_call(
        windows_over_edge,
        out_shape=(cells_shape, acc_shape, edge, edge),
        in_specs=[VMEM] * 9,
        out_specs=(VMEM,) * 4,
        scratch_shapes=[order, pltpu.SMEM((3, slots), jnp.int32), dma(())],
        input_output_aliases={1: 0, 2: 1},
        compiler_params=PARAMS,
        cost_estimate=BUSY,
        name="windows_over_edge",
    )(marked, cells, acc, *fixed, *edges)
    by_inner, by_outer = swap(to_inner, to_outer, "row")

    acc = pl.pallas_call(
        windows_after,
        out_shape=acc_shape,
        in_specs=[SMEM] + [VMEM] * 9,
        out_specs=VMEM,
        scratch_shapes=[
            order, pltpu.VMEM(probe_re.shape, jnp.float32),
            pltpu.VMEM((3, MARKS, LANES), jnp.int32), pltpu.SMEM((3, MARKS, LANES), jnp.int32), dma(()),
        ],
        input_output_aliases={2: 0},
        compiler_params=PARAMS,
        cost_estimate=BUSY,
        name="windows_after",
    )(marked, cells, acc, *fixed, marks, *edges)

    packed = f32(tile_r // 2, LANES)
    acc, to_inner, to_outer = pl.pallas_call(
        column_spill,
        out_shape=(acc_shape, packed, packed),
        in_specs=[VMEM] * 3,
        out_specs=(VMEM,) * 3,
        input_output_aliases={0: 0},
        compiler_params=SMALL,
        name="column_spill",
    )(acc, by_outer, by_inner)
    by_inner, by_outer = swap(to_inner, to_outer, "col")

    near = [pltpu.VMEM((tile_r, tile_c), jnp.float32)] * 2
    new = (f32(tile_r, tile_c), f32(tile_r, tile_c))
    acc, new_re, new_im = pl.pallas_call(
        finish_inner,
        out_shape=(acc_shape, *new),
        in_specs=[SMEM] + [VMEM] * 6,
        out_specs=(VMEM, HBM, HBM),
        scratch_shapes=[order] + near + [dma((2,))],
        input_output_aliases={2: 0},
        compiler_params=PARAMS,
        cost_estimate=BUSY,
        name="finish_inner",
    )(marked, cells, acc, *fixed)
    return pl.pallas_call(
        finish_edges,
        out_shape=new,
        in_specs=[VMEM] * 4 + [HBM] * 2,
        out_specs=(HBM, HBM),
        scratch_shapes=near + [dma((8,))],
        input_output_aliases={4: 0, 5: 1},
        compiler_params=SMALL,
        name="finish_edges",
    )(cells, acc, by_inner, by_outer, far(new_re), far(new_im))


def solution(mesh):
    return jax.shard_map(
        shards,
        mesh=mesh,
        in_specs=(
            P("row", "col"),
            P("row", "col"),
            P(),
            P(),
            P("row", "col", None, None, None),
            P("row", "col"),
            P("row", "col", None, None),
            P("row", "col", None),
        ),
        out_specs=(P("row", "col"), P("row", "col")),
        check_vma=False,
    )
```

```python
import functools
import math

import jax
import jax.numpy as jnp
import ml_dtypes
import numpy as np
from jax import lax
from jax.experimental import pallas as pl
from jax.experimental.pallas import tpu as pltpu
from jax.sharding import PartitionSpec as P

P_SIZE = 256
HALF = P_SIZE // 2
HALO = 32
LANES = 128
GROUPS = LANES // HALO
MARKS = 8
PAIR = 2

floor_amp = 0.5
ridge = 1.0

VMEM = pl.BlockSpec(memory_space=pltpu.VMEM)
SMEM = pl.BlockSpec(memory_space=pltpu.SMEM)
HBM = pl.BlockSpec(memory_space=pltpu.HBM)
PARAMS = pltpu.CompilerParams(vmem_limit_bytes=32 * 1024 * 1024)
SMALL = pltpu.CompilerParams(vmem_limit_bytes=16 * 1024 * 1024)
BUSY = pl.CostEstimate(flops=4_000_000_000, bytes_accessed=8_000_000, transcendentals=0)


def transform_tables():
    index = np.arange(HALF)
    plain = []
    for parity in (0, 1):
        angle = 2.0 * math.pi / P_SIZE * (index[:, None] * (2 * index[None, :] + parity) % P_SIZE)
        cos, sin = np.cos(angle), np.sin(angle)
        plain.append(np.block([[cos, -sin], [sin, cos]]) / math.sqrt(P_SIZE))
    parts = []
    for table in plain + [t.T for t in plain]:
        high = table.astype(np.float32).astype(ml_dtypes.bfloat16)
        low = (table - high.astype(np.float64)).astype(np.float32).astype(ml_dtypes.bfloat16)
        parts += [high, low]
    order = np.concatenate([np.arange(0, P_SIZE, 2), np.arange(1, P_SIZE, 2)])
    sort = np.zeros((P_SIZE, P_SIZE), np.float32)
    sort[np.arange(P_SIZE), order] = 1.0
    parts += [sort.astype(ml_dtypes.bfloat16), sort.T.astype(ml_dtypes.bfloat16)]
    return np.stack(parts)


def lane_index(rows):
    return lax.broadcasted_iota(jnp.int32, (rows, LANES), 1)


def pack_lanes(field, top, size, tile, first):
    half = size // 2
    lane = lane_index(half)
    packed = None
    for g in range(GROUPS):
        start = top + g % 2 * half
        part = field[g // 2, start : start + half, tile]
        if g:
            part = pltpu.roll(part, HALO * g, 1)
        low = (first + HALO * g) % LANES
        mine = (lane >= low) & (lane < low + HALO)
        packed = part if packed is None else jnp.where(mine, part, packed)
    return packed


def unpack_lanes(packed, group):
    return pltpu.roll(packed, LANES - HALO * group, 1) if group else packed


def split(x):
    high = x.astype(jnp.bfloat16)
    return high, (x - high.astype(jnp.float32)).astype(jnp.bfloat16)


def product(left, right):
    return jnp.dot(left, right, preferred_element_type=jnp.float32)


def times_table(x, table, which):
    high, low = split(x)
    t_high, t_low = table[2 * which], table[2 * which + 1]
    return product(beside(high, high, low), below(t_high, t_low, t_high))


def table_times(table, which, x):
    high, low = split(x)
    t_high, t_low = table[2 * which], table[2 * which + 1]
    return product(beside(t_high, t_low, t_high), below(high, high, low))


def beside(*blocks):
    return jnp.concatenate(blocks, axis=1)


def below(*blocks):
    return jnp.concatenate(blocks, axis=0)


def ends(x):
    return x[:, :HALF], x[:, HALF:]


def forward_columns(exit_re, exit_im, table):
    re_lo, re_hi = ends(exit_re)
    im_lo, im_hi = ends(exit_im)
    even = times_table(beside(re_lo + re_hi, im_lo + im_hi), table, 0)
    odd = times_table(beside(re_lo - re_hi, im_lo - im_hi), table, 1)
    return even, odd


def forward_rows(even, odd, table):
    out = []
    for parity in (0, 1):
        if parity == 0:
            se, so = even[:HALF] + even[HALF:], odd[:HALF] + odd[HALF:]
        else:
            se, so = even[:HALF] - even[HALF:], odd[:HALF] - odd[HALF:]
        e_re, e_im = ends(se)
        o_re, o_im = ends(so)
        out.append(table_times(table, 2 + parity, below(beside(e_re, o_re), beside(e_im, o_im))))
    return out


def residual(far, frame):
    out = []
    for parity in (0, 1):
        re, im = far[parity][:HALF], far[parity][HALF:]
        level = jnp.maximum(re * re + im * im, floor_amp * floor_amp)
        inten = frame[parity * HALF : (parity + 1) * HALF]
        factor = 1.0 - inten * lax.rsqrt(inten * level)
        out.append(below(re * factor, im * factor))
    return out


def back_rows(res, table):
    first = table_times(table, 0, res[0])
    second = table_times(table, 1, res[1])
    upper, lower = first + second, first - second
    out = []
    for cols in (slice(0, HALF), slice(HALF, P_SIZE)):
        out.append(
            below(
                beside(upper[:HALF, cols], upper[HALF:, cols]),
                beside(lower[:HALF, cols], lower[HALF:, cols]),
            )
        )
    return out


def back_columns(parts, table):
    even = times_table(parts[0], table, 2)
    odd = times_table(parts[1], table, 3)
    lo, hi = even + odd, even - odd
    return beside(lo[:, :HALF], hi[:, :HALF]), beside(lo[:, HALF:], hi[:, HALF:])


def is_odd(axis):
    return lax.rem(lax.axis_index(axis), 2) == 1


def fetch(pairs, sems):
    copies = [pltpu.make_async_copy(far, near, sems.at[i]) for i, (far, near) in enumerate(pairs)]
    for copy in copies:
        copy.start()
    return copies


def finish_all(copies):
    for copy in copies:
        copy.wait()


def row_edges(counts, obj_re, obj_im, offsets, chosen, to_outer, to_inner, marked, places, frame_of, sems):
    tile_r = obj_re.shape[0]
    odd = is_odd("row")
    low = pl.multiple_of(jnp.where(odd, 0, tile_r - HALO), 16)
    high = pl.multiple_of(jnp.where(odd, tile_r - HALO, 0), 16)
    pairs = [(offsets, places), (chosen, frame_of)]
    tiles = obj_re.shape[1] // LANES
    for k, ref in enumerate((obj_re, obj_im)):
        for t in range(tiles):
            lanes = slice(t * LANES, (t + 1) * LANES)
            rows = slice((2 * t + k) * HALO, (2 * t + k + 1) * HALO)
            pairs.append((ref.at[pl.ds(high, HALO), lanes], to_outer.at[rows]))
            pairs.append((ref.at[pl.ds(low, HALO), lanes], to_inner.at[rows]))
    copies = fetch(pairs, sems)
    finish_all(copies[:2])
    place = places[0, 0]
    live = lax.broadcasted_iota(jnp.int32, place.shape, 1) < counts[0, 0]
    place = jnp.where(live, place, 2 * tile_r)
    marked[0:2, :] = place
    marked[2:3, :] = frame_of[0]
    for message in (to_inner, to_outer):
        first = 2 * HALO * tiles
        message[first : first + 2, 0 : place.shape[1]] = place.astype(jnp.float32)
    finish_all(copies[2:])


def window_place(slots, slot):
    row = pl.multiple_of(slots[0, slot] + HALO, 16)
    col = slots[1, slot] + LANES
    turn = lax.rem(col, LANES)
    return row, pl.multiple_of(col - turn, LANES), turn


def add_window(acc, layer, where, keep, term, tiles=(0, 1, 2)):
    row, base, _ = where
    lo, hi = ends(term)
    parts = (jnp.where(keep, lo, 0.0), hi, jnp.where(keep, 0.0, lo))
    for t in tiles:
        acc[layer, pl.ds(row, term.shape[0]), pl.ds(base + t * LANES, LANES)] += parts[t]


def send_columns(to_left, to_right, to_inner, to_outer):
    odd = is_odd("col")
    to_inner[0 : to_left.shape[0], :] = jnp.where(odd, to_left, to_right)
    to_outer[0 : to_left.shape[0], :] = jnp.where(odd, to_right, to_left)


def received(by_inner, by_outer, axis):
    odd = is_odd(axis)
    index = lax.axis_index(axis)
    inside = (index > 0) & (index < lax.axis_size(axis) - 1)
    by_outer = jnp.where(inside, by_outer[...], 0.0)
    by_inner = by_inner[...]
    return jnp.where(odd, by_inner, by_outer), jnp.where(odd, by_outer, by_inner)


def pieces(packed, size):
    half = size // 2
    for g in range(GROUPS):
        yield g // 2, g % 2 * half, unpack_lanes(packed[:half], g)


def pack_corners(field, rows):
    width = field.shape[2]
    left = [field[k, rows, 0:LANES] for k in (0, 1)]
    right = [field[k, rows, width - LANES : width] for k in (0, 1)]
    lane = lane_index(HALO)
    low = jnp.where(lane < HALO, right[0], pltpu.roll(right[1], HALO, 1))
    high = jnp.where(lane < 3 * HALO, pltpu.roll(left[1], 3 * HALO, 1), left[0])
    packed = jnp.where(lane < 2 * HALO, low, high)
    return beside(*(packed[i : i + MARKS] for i in range(0, HALO, MARKS)))


def unpack_corners(packed):
    packed = below(*(packed[:, i : i + LANES] for i in range(0, GROUPS * LANES, LANES)))
    lane = lane_index(HALO)
    for k, left, right in ((0, 0, 0), (1, HALO, 3 * HALO)):
        yield (
            k,
            jnp.where(lane >= 3 * HALO, pltpu.roll(packed, left, 1) if left else packed, 0.0),
            jnp.where(lane < HALO, pltpu.roll(packed, right, 1) if right else packed, 0.0),
        )


def row_halos(cells_in, own, by_outer, by_inner, cells, marks, to_inner, to_outer):
    rows, width = cells.shape[1:]
    before, after = received(by_inner, by_outer, "row")
    tiles = width // LANES - 2
    for k in (0, 1):
        for t in range(tiles):
            lanes = slice((t + 1) * LANES, (t + 2) * LANES)
            part = slice((2 * t + k) * HALO, (2 * t + k + 1) * HALO)
            cells[k, 0:HALO, lanes] = before[part]
            cells[k, rows - HALO : rows, lanes] = after[part]
    first = 2 * HALO * tiles
    for i, message in enumerate((own[...], before, after)):
        marks[2 * i : 2 * i + 2, :] = message[first : first + 2]
    half = rows // 2
    to_left = pack_lanes(cells, 0, rows, slice(LANES, 2 * LANES), 0)
    to_right = pack_lanes(cells, 0, rows, slice(width - 2 * LANES, width - LANES), LANES - HALO)
    send_columns(to_left, to_right, to_inner, to_outer)
    to_inner[half:, :] = marks[...]
    to_outer[half:, :] = marks[...]


def live_slots(slots, cells):
    tile_r = cells.shape[1] - 2 * HALO
    count = jnp.int32(0)
    for slot in range(slots.shape[1]):
        count += (slots[0, slot] < tile_r).astype(jnp.int32)
    return count


FIRST, BEFORE, OVER, AFTER, LAST = range(5)


def run_windows(phase, slots, cells, acc, probe_re, probe_im, table, frames, order):
    tile_r, tile_c = cells.shape[1] - 2 * HALO, cells.shape[2] - 2 * LANES
    count = live_slots(slots, cells)
    kinds = []
    n_inside, n_row, n_col = jnp.int32(0), jnp.int32(0), jnp.int32(0)
    for slot in range(slots.shape[1]):
        row, col = slots[0, slot], slots[1, slot]
        live = slot < count
        over_col = (col < 0) | (col > tile_c - P_SIZE)
        over_row = (row < 0) | (row > tile_r - P_SIZE)
        inside, by_row = live & ~over_col & ~over_row, live & ~over_col & over_row
        by_col, by_both = live & over_col & ~over_row, live & over_col & over_row
        kinds.append((inside, by_row, by_col, by_both, n_inside, n_row))
        n_inside += inside.astype(jnp.int32)
        n_row += by_row.astype(jnp.int32)
        n_col += by_col.astype(jnp.int32)
    first = jnp.where(count > PAIR, jnp.minimum(n_inside, PAIR), 0)
    before = first + jnp.minimum(n_inside - first, PAIR - jnp.minimum(n_row, PAIR))
    rest = n_inside - before
    after = n_inside - jnp.clip(n_col + rest - 2 * PAIR, 0, jnp.minimum(rest, PAIR))
    found = jnp.int32(0)
    for slot, (inside, by_row, by_col, by_both, rank, row_rank) in enumerate(kinds):
        mine = {
            FIRST: lambda: inside & (rank < first),
            BEFORE: lambda: (by_row & (row_rank < PAIR)) | (inside & (rank >= first) & (rank < before)),
            OVER: lambda: by_both | (by_row & (row_rank >= PAIR)),
            AFTER: lambda: by_col | (inside & (rank >= before) & (rank < after)),
            LAST: lambda: inside & (rank >= after),
        }[phase]()

        @pl.when(mine)
        def _():
            order[found] = slot

        found += mine.astype(jnp.int32)

    lane = lane_index(P_SIZE)

    def load(slot):
        where = row, base, turn = window_place(slots, slot)
        keep = lane >= turn
        w_re = pltpu.roll(probe_re[...], turn, 1)
        w_im = pltpu.roll(probe_im[...], turn, 1)
        patch = []
        for k in (0, 1):
            block = cells[k, pl.ds(row, P_SIZE), pl.ds(base, 3 * LANES)]
            patch.append(
                beside(jnp.where(keep, block[:, :LANES], block[:, 2 * LANES :]), block[:, LANES : 2 * LANES])
            )
        exit_re = w_re * patch[0] - w_im * patch[1]
        exit_im = w_re * patch[1] + w_im * patch[0]
        return (where, keep, w_re, w_im), exit_re, exit_im

    def frame_of(slot):
        half = product(table[8], frames[slots[2, slot]]).astype(jnp.bfloat16)
        return product(half, table[9])

    def place(at, back_re, back_im):
        where, keep, w_re, w_im = at
        add_window(acc, 0, where, keep, w_re * back_re + w_im * back_im)
        add_window(acc, 1, where, keep, w_re * back_im - w_im * back_re)

    def rows_of(stacked):
        return [stacked[i : i + P_SIZE] for i in range(0, stacked.shape[0], P_SIZE)]

    def step(group):
        frame = [frame_of(slot) for slot in group]
        loaded = [load(slot) for slot in group]
        stacked = forward_columns(below(*(x[1] for x in loaded)), below(*(x[2] for x in loaded)), table)
        state = [forward_rows(*x, table) for x in zip(*map(rows_of, stacked))]
        state = [residual(x, f) for x, f in zip(state, frame)]
        state = [back_rows(x, table) for x in state]
        stacked = back_columns([below(*parts) for parts in zip(*state)], table)
        for x, back in zip(loaded, zip(*map(rows_of, stacked))):
            place(x[0], *back)

    def pair_step(pair, carry):
        step([order[pair * PAIR + i] for i in range(PAIR)])
        return carry

    lax.fori_loop(0, found // PAIR, pair_step, 0)

    @pl.when(found % PAIR == 1)
    def _():
        step([order[found - 1]])


def windows_first(
    slots, obj_re, obj_im, probe_re_far, probe_im_far, table_far, frames_far,
    cells, acc, probe_re, probe_im, table, frames, order, sems,
):
    tile_r, tile_c = obj_re.shape
    inner = slice(HALO, HALO + tile_r)
    middle = slice(LANES, LANES + tile_c)
    pairs = (
        (table_far, table),
        (frames_far, frames),
        (obj_re, cells.at[0, inner, middle]),
        (obj_im, cells.at[1, inner, middle]),
        (probe_re_far, probe_re),
        (probe_im_far, probe_im),
    )
    copies = fetch(pairs, sems)
    acc[...] = jnp.zeros_like(acc)
    finish_all(copies)
    run_windows(FIRST, slots, cells, acc, probe_re, probe_im, table, frames, order)


def windows_before(
    slots, cells, acc_in, probe_re, probe_im, table, frames, acc, order, power,
):
    power[...] = probe_re[...] * probe_re[...] + probe_im[...] * probe_im[...]
    lane = lane_index(P_SIZE)

    def step(slot, carry):
        where = window_place(slots, slot)
        add_window(acc, 2, where, lane >= where[2], pltpu.roll(power[...], where[2], 1))
        return carry

    lax.fori_loop(0, live_slots(slots, cells), step, 0)
    run_windows(BEFORE, slots, cells, acc, probe_re, probe_im, table, frames, order)


def reaching(place, right, tile_r, tile_c):
    shape = place.shape
    index = lax.broadcasted_iota(jnp.int32, shape, 0)
    lane = lax.broadcasted_iota(jnp.int32, shape, 1)
    col = pltpu.roll(place, shape[0] - 1, 0)
    low = jnp.where(index == 2, tile_r - P_SIZE, -tile_r).astype(jnp.float32)
    high = jnp.where(index == 4, 0, tile_r).astype(jnp.float32)
    reaches = (lane < MARKS) & (index % 2 == 0) & (index < 6) & (place > low) & (place < high)
    if right < 0:
        reaches &= col > tile_c - P_SIZE
    if right > 0:
        reaches &= col < 0
    bit = lax.shift_left(jnp.ones(shape, jnp.int32), jnp.minimum(lane, MARKS)).astype(jnp.float32)
    bits = jnp.sum(jnp.where(reaches, bit, 0.0), axis=1, keepdims=True)
    return jnp.where(lane < MARKS, place, bits).astype(jnp.int32)


def add_neighbours_light(places, acc, power):
    rows, width = acc.shape[1:]
    tile_r, tile_c = rows - 2 * HALO, width - 2 * LANES
    for right in (-1, 0, 1):
        for i, down in enumerate((0, -1, 1)):
            if not right and not down:
                continue
            first, last = {-1: (P_SIZE - HALO, P_SIZE), 0: (0, P_SIZE), 1: (0, HALO)}[down]
            tiles = {-1: (2,), 0: (0, 1, 2), 1: (0,)}[right]
            lane = lane_index(last - first)
            bits = places[right + 1, 2 * i, MARKS]

            def step(slot, carry):
                row, col = places[right + 1, 2 * i, slot], places[right + 1, 2 * i + 1, slot]

                @pl.when(lax.shift_right_logical(bits, slot) % 2 == 1)
                def _():
                    turn = lax.rem(col + LANES, LANES)
                    at = pl.multiple_of(row + HALO + (down * tile_r + first), 16)
                    base = pl.multiple_of(col + LANES - turn + right * tile_c, LANES)
                    part = pltpu.roll(power[first:last, :], turn, 1)
                    add_window(acc, 2, (at, base, turn), lane >= turn, part, tiles)

                return carry

            @pl.when(bits != 0)
            def _():
                lax.fori_loop(0, MARKS, step, 0)


def windows_after(
    slots, cells, acc_in, probe_re, probe_im, table, frames, marks, by_inner, by_outer,
    acc, order, power, whole, places, sem,
):
    rows, width = acc.shape[1:]
    before, after = received(by_inner, by_outer, "col")
    for i, part in enumerate((before[-MARKS:], marks[...], after[-MARKS:])):
        whole[i] = reaching(part, i - 1, rows - 2 * HALO, width - 2 * LANES)
    copy = pltpu.make_async_copy(whole, places, sem)
    copy.start()
    power[...] = probe_re[...] * probe_re[...] + probe_im[...] * probe_im[...]
    run_windows(AFTER, slots, cells, acc, probe_re, probe_im, table, frames, order)
    copy.wait()
    add_neighbours_light(places, acc, power)


def windows_over_edge(
    marked, cells_in, acc_in, probe_re, probe_im, table, frames, by_inner, by_outer,
    cells, acc, to_outer, to_inner, order, slots, sem,
):
    scalars = pltpu.make_async_copy(marked, slots, sem)
    scalars.start()
    rows, width = acc.shape[1:]
    before, after = received(by_inner, by_outer, "col")
    for tile, packed in ((slice(0, LANES), before), (slice(width - LANES, width), after)):
        for layer, row, part in pieces(packed, rows):
            cells[layer, row : row + part.shape[0], tile] = part
    scalars.wait()
    run_windows(OVER, slots, cells, acc, probe_re, probe_im, table, frames, order)
    odd = is_odd("row")
    strips = []
    for here in (slice(0, HALO), slice(rows - HALO, rows)):
        middle = [acc[k, here, LANES : width - LANES] for k in (0, 1)]
        strips.append(below(*middle, pack_corners(acc, here)))
    to_inner[...] = jnp.where(odd, strips[0], strips[1])
    to_outer[...] = jnp.where(odd, strips[1], strips[0])


def column_spill(acc_in, by_outer, by_inner, acc, to_inner, to_outer):
    rows, width = acc.shape[1:]
    before, after = received(by_inner, by_outer, "row")
    for start, came in ((HALO, before), (rows - 2 * HALO, after)):
        here = slice(start, start + HALO)
        for k in (0, 1):
            acc[k, here, LANES : width - LANES] += came[k * HALO : (k + 1) * HALO]
        for k, left, right in unpack_corners(came[2 * HALO :]):
            acc[k, here, 0:LANES] += left
            acc[k, here, width - LANES :] += right
    tile_r = rows - 2 * HALO
    to_left = pack_lanes(acc, HALO, tile_r, slice(0, LANES), LANES - HALO)
    to_right = pack_lanes(acc, HALO, tile_r, slice(width - LANES, width), 0)
    send_columns(to_left, to_right, to_inner, to_outer)


def new_columns(cells, acc, spill, start, size, near_re, near_im):
    rows = acc.shape[1]
    here, there = slice(HALO, rows - HALO), slice(LANES + start, LANES + start + size)
    part = [acc[k, here, there] for k in range(acc.shape[0])]
    if spill is not None:
        part[:2] = [part[k] + spill[k] for k in (0, 1)]
    scale = 1.0 / (part[2] + ridge)
    near_re[:, start : start + size] = cells[0, here, there] - part[0] * scale
    near_im[:, start : start + size] = cells[1, here, there] - part[1] * scale


def finish_inner(
    slots, cells, acc_in, probe_re, probe_im, table, frames, acc, new_re, new_im, order, near_re, near_im, sems,
):
    run_windows(LAST, slots, cells, acc, probe_re, probe_im, table, frames, order)
    size = near_re.shape[1] - 2 * LANES
    new_columns(cells, acc, None, LANES, size, near_re, near_im)
    there = slice(LANES, LANES + size)
    finish_all(fetch([(near_re.at[:, there], new_re.at[:, there]), (near_im.at[:, there], new_im.at[:, there])], sems))


def finish_edges(cells, acc, by_inner, by_outer, re_in, im_in, new_re, new_im, near_re, near_im, sems):
    tile_r, tile_c = near_re.shape
    lane = lane_index(tile_r)
    sides = ((0, lane < HALO), (tile_c - LANES, lane >= LANES - HALO))
    copies = []
    for i, ((start, mine), packed) in enumerate(zip(sides, received(by_inner, by_outer, "col"))):
        parts = [part for _, _, part in pieces(packed, tile_r)]
        spill = [jnp.where(mine, below(*parts[2 * k : 2 * k + 2]), 0.0) for k in (0, 1)]
        new_columns(cells, acc, spill, start, LANES, near_re, near_im)
        there = slice(start, start + LANES)
        pairs = ((near_re.at[:, there], new_re.at[:, there]), (near_im.at[:, there], new_im.at[:, there]))
        copies += fetch(pairs, sems.at[2 * i : 2 * i + 2])
    finish_all(copies)


def swap(to_inner, to_outer, axis):
    devices = lax.axis_size(axis)
    inner = [(i, i + 1) for i in range(0, devices, 2)]
    partner = {i: i + 1 if i % 2 else i - 1 for i in range(1, devices - 1)}
    n_row, n_col = lax.axis_size("row"), lax.axis_size("col")
    pairs = []
    for row in range(n_row):
        for col in range(n_col):
            if axis == "row":
                there = (partner[row], col) if row in partner else (row, col ^ 1)
            else:
                there = (row, partner[col]) if col in partner else (row ^ 1, col)
            pairs.append((row * n_col + col, there[0] * n_col + there[1]))
    by_inner = lax.ppermute(to_inner, axis, inner + [(j, i) for i, j in inner])
    by_outer = lax.ppermute(to_outer, ("row", "col"), pairs)
    return by_inner, by_outer


def far(x):
    return pltpu.with_memory_space_constraint(x, pltpu.HBM)


def f32(*shape):
    return jax.ShapeDtypeStruct(shape, jnp.float32)


def shards(object_re, object_im, probe_re, probe_im, frames, counts, offsets, frame_index):
    tile_r, tile_c = object_re.shape
    rows, width = tile_r + 2 * HALO, tile_c + 2 * LANES
    layers = 3
    slots = offsets.shape[2]
    table = jnp.asarray(transform_tables())
    frames = frames.reshape(frames.shape[2:])
    cells_shape, acc_shape = f32(2, rows, width), f32(layers, rows, width)
    dma = pltpu.SemaphoreType.DMA

    places = jnp.swapaxes(offsets, 2, 3)
    edge = f32(2 * HALO * (tile_c // LANES) + MARKS, LANES)
    to_outer, to_inner, marked = pl.pallas_call(
        row_edges,
        out_shape=(edge, edge, jax.ShapeDtypeStruct((3, slots), jnp.int32)),
        in_specs=[SMEM] + [HBM] * 4,
        out_specs=(VMEM, VMEM, VMEM),
        scratch_shapes=[
            pltpu.VMEM(places.shape, jnp.int32), pltpu.VMEM(frame_index.shape, jnp.int32),
            dma((2 + 4 * (tile_c // LANES),)),
        ],
        compiler_params=SMALL,
        name="row_edges",
    )(counts, far(object_re), far(object_im), far(places), far(frame_index))
    by_inner, by_outer = swap(to_inner, to_outer, "row")

    order = pltpu.SMEM((slots,), jnp.int32)
    cells, acc, *fixed = pl.pallas_call(
        windows_first,
        out_shape=(
            cells_shape, acc_shape, f32(*probe_re.shape), f32(*probe_im.shape),
            jax.ShapeDtypeStruct(table.shape, table.dtype), jax.ShapeDtypeStruct(frames.shape, frames.dtype),
        ),
        in_specs=[SMEM] + [HBM] * 6,
        out_specs=(VMEM,) * 6,
        scratch_shapes=[order, dma((6,))],
        compiler_params=PARAMS,
        cost_estimate=BUSY,
        name="windows_first",
    )(marked, *map(far, (object_re, object_im, probe_re, probe_im, table, frames)))

    packed = f32(rows // 2 + MARKS, LANES)
    cells, marks, to_inner, to_outer = pl.pallas_call(
        row_halos,
        out_shape=(cells_shape, f32(MARKS, LANES), packed, packed),
        in_specs=[VMEM] * 4,
        out_specs=(VMEM,) * 4,
        input_output_aliases={0: 0},
        compiler_params=SMALL,
        name="row_halos",
    )(cells, to_outer, by_outer, by_inner)
    edges = swap(to_inner, to_outer, "col")

    acc = pl.pallas_call(
        windows_before,
        out_shape=acc_shape,
        in_specs=[SMEM] + [VMEM] * 6,
        out_specs=VMEM,
        scratch_shapes=[order, pltpu.VMEM(probe_re.shape, jnp.float32)],
        input_output_aliases={2: 0},
        compiler_params=PARAMS,
        cost_estimate=BUSY,
        name="windows_before",
    )(marked, cells, acc, *fixed)

    edge = f32(2 * HALO + MARKS, tile_c)
    cells, acc, to_outer, to_inner = pl.pallas_call(
        windows_over_edge,
        out_shape=(cells_shape, acc_shape, edge, edge),
        in_specs=[VMEM] * 9,
        out_specs=(VMEM,) * 4,
        scratch_shapes=[order, pltpu.SMEM((3, slots), jnp.int32), dma(())],
        input_output_aliases={1: 0, 2: 1},
        compiler_params=PARAMS,
        cost_estimate=BUSY,
        name="windows_over_edge",
    )(marked, cells, acc, *fixed, *edges)
    by_inner, by_outer = swap(to_inner, to_outer, "row")

    acc = pl.pallas_call(
        windows_after,
        out_shape=acc_shape,
        in_specs=[SMEM] + [VMEM] * 9,
        out_specs=VMEM,
        scratch_shapes=[
            order, pltpu.VMEM(probe_re.shape, jnp.float32),
            pltpu.VMEM((3, MARKS, LANES), jnp.int32), pltpu.SMEM((3, MARKS, LANES), jnp.int32), dma(()),
        ],
        input_output_aliases={2: 0},
        compiler_params=PARAMS,
        cost_estimate=BUSY,
        name="windows_after",
    )(marked, cells, acc, *fixed, marks, *edges)

    packed = f32(tile_r // 2, LANES)
    acc, to_inner, to_outer = pl.pallas_call(
        column_spill,
        out_shape=(acc_shape, packed, packed),
        in_specs=[VMEM] * 3,
        out_specs=(VMEM,) * 3,
        input_output_aliases={0: 0},
        compiler_params=SMALL,
        name="column_spill",
    )(acc, by_outer, by_inner)
    by_inner, by_outer = swap(to_inner, to_outer, "col")

    near = [pltpu.VMEM((tile_r, tile_c), jnp.float32)] * 2
    new = (f32(tile_r, tile_c), f32(tile_r, tile_c))
    acc, new_re, new_im = pl.pallas_call(
        finish_inner,
        out_shape=(acc_shape, *new),
        in_specs=[SMEM] + [VMEM] * 6,
        out_specs=(VMEM, HBM, HBM),
        scratch_shapes=[order] + near + [dma((2,))],
        input_output_aliases={2: 0},
        compiler_params=PARAMS,
        cost_estimate=BUSY,
        name="finish_inner",
    )(marked, cells, acc, *fixed)
    return pl.pallas_call(
        finish_edges,
        out_shape=new,
        in_specs=[VMEM] * 4 + [HBM] * 2,
        out_specs=(HBM, HBM),
        scratch_shapes=near + [dma((4,))],
        input_output_aliases={4: 0, 5: 1},
        compiler_params=SMALL,
        name="finish_edges",
    )(cells, acc, by_inner, by_outer, far(new_re), far(new_im))


def solution(mesh):
    return jax.shard_map(
        shards,
        mesh=mesh,
        in_specs=(
            P("row", "col"),
            P("row", "col"),
            P(),
            P(),
            P("row", "col", None, None, None),
            P("row", "col"),
            P("row", "col", None, None),
            P("row", "col", None),
        ),
        out_specs=(P("row", "col"), P("row", "col")),
        check_vma=False,
    )
```
